32 devices in a mesh: dp: 2 (over y), ctx: 4 (over z), head: 4 (over x, core).
Axes of the slice: x: 2, y: 2, z: 4, core: 2. Of those that a mesh axis runs over, the one named last changes fastest.
Arguments:
- queries: bfloat16 [2, 1024, 8192], P('dp', 'ctx', 'head'), may hold values from -45 to 45
- keys: bfloat16 [2, 1024, 1024], P('dp', 'ctx', 'head'), may hold values from -6 to 6
- values: bfloat16 [2, 1024, 1024], P('dp', 'ctx', 'head'), may hold values from -6 to 6
- doc_ids: int32 [2, 1024], P('dp'), may hold values from 0 to 2, never falling along the last dimension, each value on 1 to 768 neighbouring positions
- inputs: bfloat16 [2, 1024, 8192], P('dp', 'ctx', 'head'), may hold values from -6 to 6
- gate_input: bfloat16 [2, 1024, 8192], P('dp', 'ctx', 'head'), may hold values from -40 to 40
- b_input: bfloat16 [2, 1024, 1024], P('dp', 'ctx', 'head'), may hold values from -0.0625 to 0.0625
- c_input: bfloat16 [2, 1024, 1024], P('dp', 'ctx', 'head'), may hold values from -6 to 6
- dt_raw: float32 [2, 1024, 128], P('dp', 'ctx', 'head'), may hold values from -2 to 2
- dt_bias: float32 [128], P('head'), may hold values from -1 to 1
- decay_log: float32 [128], P('head'), may hold values from -12 to -2
- skip: float32 [128], P('head'), may hold values from 0.5 to 2
- gain: float32 [8192], P('head'), may hold values from 0.5 to 1.5
Outputs:
- teacher_out: bfloat16 [2, 1024, 8192], P('dp', 'ctx', 'head')
- student_out: bfloat16 [2, 1024, 8192], P('dp', 'ctx', 'head')
- grad_gain: float32 [8192], P('head')
- grad_skip: float32 [128], P('head')
The draws below stay inside these ranges and needn't reach their ends.
Inputs may be any that keep to these rules, and one draw needn't show every extreme that they name: `doc_ids`: three or fewer documents a sequence, numbered from 0 in order; one of them has 768 positions.
All inputs are finite; a program needn't handle non-finite values.
Results may differ from the reference program's by a relative error of at most 0.012.
Values may be sent and summed in bfloat16 or wider, within the bound.
No kernel may reach another device: no remote copies, remote signals or barrier semaphores. Data moves between devices by JAX's collectives and lax.ppermute only.
A program may use at most 64 MiB of HBM per device.

```python
import math
import jax
import jax.numpy as jnp
import numpy as np
from jax import lax

DH = 128
HQ = 64
KVH = 8
HS = 128
P_SIZE = 64
N = 128
GROUPS = 8
TOK_DEV = 256
STRETCH = 128
LENGTH = 1024
SEQS = 2
DM = 8192


def shared_keys(key):
    shape = (SEQS, LENGTH, KVH * DH)
    return jnp.clip(jax.random.normal(jax.random.fold_in(key, 11), shape, jnp.float32), -6.0, 6.0)


def draw_keys(key, part):
    return shared_keys(key).astype(jnp.bfloat16)


def draw_queries(key, part):
    shape = (SEQS, LENGTH, HQ * DH)
    return jnp.clip(jax.random.normal(jax.random.fold_in(key, 21), shape, jnp.float32), -6.0, 6.0).astype(jnp.bfloat16)


def draw_gate_input(key, part):
    shape = (SEQS, LENGTH, HS * P_SIZE)
    base = jnp.clip(jax.random.normal(jax.random.fold_in(key, 31), shape, jnp.float32), -4.0, 4.0)
    row_scale = jnp.exp(jax.random.uniform(jax.random.fold_in(key, 32), (SEQS, LENGTH, 1), jnp.float32, -1.2, 1.1))
    col_scale = jnp.exp(jax.random.uniform(jax.random.fold_in(key, 33), (1, 1, HS * P_SIZE), jnp.float32, -1.2, 1.1))
    return (base * row_scale * col_scale).astype(jnp.bfloat16)


def draw_dt_raw(key, part):
    blocks = LENGTH // TOK_DEV
    offset = jax.random.uniform(jax.random.fold_in(key, 41), (SEQS, blocks, 1, HS), jnp.float32, -1.0, 1.0)
    noise = jnp.clip(0.3 * jax.random.normal(jax.random.fold_in(key, 42), (SEQS, blocks, TOK_DEV, HS), jnp.float32), -0.9, 0.9)
    return (offset + noise).reshape(SEQS, LENGTH, HS)


def draw_decay_log(key, part):
    share = 0.4
    fast = jax.random.uniform(jax.random.fold_in(key, 51), (HS,), jnp.float32) < share
    quick = jax.random.uniform(jax.random.fold_in(key, 52), (HS,), jnp.float32, jnp.log(1.0 / 30.0), jnp.log(1.0 / 15.0))
    slow = jax.random.uniform(jax.random.fold_in(key, 53), (HS,), jnp.float32, jnp.log(0.3), jnp.log(1.5)) - jnp.log(jnp.float32(LENGTH))
    return jnp.where(fast, quick, slow)


def level_of(stream_key, extent, shards, smallest, largest):
    def one(position, shards_of):
        heights = jax.random.uniform(jax.random.fold_in(jax.random.fold_in(stream_key, 6), position), (shards_of,), jnp.float32, smallest / len(shards), largest / len(shards))
        return jnp.repeat(jnp.exp(heights), extent[position] // shards_of).reshape((-1,) + (1,) * (len(extent) - position - 1))

    loudness = one(*shards[0])
    for cut in shards[1:]:
        loudness = loudness * one(*cut)
    return loudness


def length_profile(amount, total, limit, slope):
    loads = [(1 << 20) // math.isqrt(grade ** slope) + 1 for grade in range(2, amount + 1)]
    rest, holding = total - limit - (amount - 1), [1] * (amount - 1)
    while rest > 0:
        candidates = [i for i in range(amount - 1) if holding[i] < limit]
        mass, budget = sum([loads[i] for i in candidates]), rest
        for i in candidates:
            more = min(limit - holding[i], max(1, budget * loads[i] // mass), rest)
            holding[i] = holding[i] + more
            rest = rest - more
    return np.array([limit] + holding)


def ragged_sizes(own_key, count, total, bound, slope):
    if count == 2:
        one = jax.random.randint(own_key, (), max(1, total - bound), min(bound, total - 1) + 1)
        return jnp.stack([one, total - one])
    sizes = jnp.asarray(length_profile(count, total, bound, slope), jnp.int32)
    pairs = (count - 1) // 2
    donor, sink = sizes[1:1 + 2 * pairs:2], sizes[2:2 + 2 * pairs:2]
    margin = jnp.minimum(donor - 1, bound - sink)
    moved = jax.random.randint(jax.random.fold_in(own_key, 1), (pairs,), 0, 1 << 20) % (margin + 1)
    sizes = sizes.at[1:1 + 2 * pairs:2].set(donor - moved).at[2:2 + 2 * pairs:2].set(sink + moved)
    return sizes[jax.random.permutation(jax.random.fold_in(own_key, 2), count)]


def bell_draw(stream_key, shape, deviation, bound, pieces=(), held_as=jnp.bfloat16):
    loudness = level_of(stream_key, shape, pieces, -0.22, 0.18) if pieces else 1.0
    entries = jax.random.normal(stream_key, shape, jnp.float32) * deviation * loudness
    return jnp.minimum(jnp.maximum(entries, -bound), bound).astype(held_as)


def setup_inputs(seed: int = 0) -> dict:
    splits = jax.random.split(jax.random.key(seed), 14)
    queries = draw_queries(jax.random.fold_in(splits[13], 71), 0)
    keys = draw_keys(jax.random.fold_in(splits[13], 71), 0)
    values = bell_draw(splits[2], (SEQS, LENGTH, KVH * DH), 1.0, 6.0, ((0, 2), (1, 4), (2, 4)))
    doc_ids = jax.vmap(lambda own: jnp.searchsorted(jnp.cumsum(ragged_sizes(own, 3, LENGTH, LENGTH * 3 // 4, 0)), jnp.arange(LENGTH), side="right"))(jax.random.split(splits[3], SEQS)).reshape((SEQS, LENGTH)).astype(jnp.int32)
    inputs = bell_draw(splits[4], (SEQS, LENGTH, HS * P_SIZE), 1.0, 6.0, ((0, 2), (1, 4), (2, 4)))
    gate_input = draw_gate_input(jax.random.fold_in(splits[13], 71), 0)
    b_input = bell_draw(splits[6], (SEQS, LENGTH, GROUPS * N), (N * 64) ** -0.5, 0.0625, ((0, 2), (1, 4), (2, 4)))
    c_input = bell_draw(splits[7], (SEQS, LENGTH, GROUPS * N), 1.0, 6.0, ((0, 2), (1, 4), (2, 4)))
    dt_raw = draw_dt_raw(jax.random.fold_in(splits[13], 71), 0)
    dt_bias = jnp.clip(jax.random.uniform(splits[9], (HS,), jnp.float32, -1.0, 1.0) * level_of(splits[9], (HS,), ((0, 4),), -0.4, 0.0), -1.0, 1.0)
    decay_log = draw_decay_log(jax.random.fold_in(splits[13], 71), 0)
    skip = jnp.clip(0.5 + 1.5 * jax.random.uniform(splits[11], (HS,), jnp.float32) ** level_of(splits[11], (HS,), ((0, 4),), -0.2, 0.2), 0.5, 2.0)
    gain = jnp.clip(1.0 + 0.1 * jax.random.normal(splits[12], (DM,), jnp.float32), 0.5, 1.5)
    return {"queries": queries, "keys": keys, "values": values, "doc_ids": doc_ids, "inputs": inputs, "gate_input": gate_input, "b_input": b_input, "c_input": c_input, "dt_raw": dt_raw, "dt_bias": dt_bias, "decay_log": decay_log, "skip": skip, "gain": gain}


def natural_rows(length, stretch, tok_dev):
    count = length // tok_dev
    place = jnp.arange(length, dtype=jnp.int32)
    block = place // stretch
    front = block < count
    device = jnp.where(front, block, 2 * count - 1 - block)
    offset = jnp.where(front, place % stretch, stretch + place % stretch)
    return (device * tok_dev + offset).astype(jnp.int32)

def stored_positions(length, stretch, tok_dev):
    count = length // tok_dev
    rows = jnp.arange(length, dtype=jnp.int32)
    device = rows // tok_dev
    offset = rows % tok_dev
    block = jnp.where(offset < stretch, device, 2 * count - 1 - device)
    return (block * stretch + offset % stretch).astype(jnp.int32)

def teacher_one(query_rows, key_part, value_part, docs):
    length = query_rows.shape[0]
    per_kv = HQ // KVH
    query_heads = query_rows.reshape(length, HQ, DH).transpose(1, 0, 2)
    key_heads = key_part.reshape(length, KVH, DH).transpose(1, 0, 2)
    value_heads = value_part.reshape(length, KVH, DH).transpose(1, 0, 2)
    place = jnp.arange(length, dtype=jnp.int32)
    allowed = (place[:, None] >= place[None, :]) & (docs[:, None] == docs[None, :])
    scale = 1.0 / jnp.sqrt(jnp.float32(DH))

    def one_head(head):
        query = query_heads[head]
        key = key_heads[head // per_kv]
        value = value_heads[head // per_kv]
        scores = jnp.dot(query, key.T, preferred_element_type=jnp.float32) * scale
        top = lax.optimization_barrier(jnp.max(jnp.where(allowed, scores, -jnp.inf), axis=1, keepdims=True))
        weights = jnp.where(allowed, jnp.exp(scores - top), 0.0)
        total = lax.optimization_barrier(jnp.sum(weights, axis=1, keepdims=True))
        summed = jnp.dot(weights.astype(jnp.bfloat16), value, preferred_element_type=jnp.float32)
        return (summed / total).astype(jnp.bfloat16)
    result = lax.map(one_head, jnp.arange(HQ, dtype=jnp.int32))
    return result.transpose(1, 0, 2).reshape(length, HQ * DH)

def block_terms(xs, bmat, cmat, dt, rate, docs, prior):
    rows, heads, width = xs.shape
    groups, state = (bmat.shape[1], bmat.shape[2])
    per = heads // groups
    cum = jnp.cumsum(rate, axis=0)
    order = jnp.arange(rows, dtype=jnp.int32)
    allowed = (order[:, None] >= order[None, :]) & (docs[:, None] == docs[None, :])
    gram = jnp.einsum('tgn,sgn->gts', cmat.astype(jnp.float32), bmat.astype(jnp.float32))
    spans = cum.T[:, :, None] - cum.T[:, None, :]
    fading = jnp.exp(jnp.where(allowed[None], spans, -jnp.inf))
    mixing = (fading.reshape(groups, per, rows, rows) * gram[:, None] * dt.T.reshape(groups, per, 1, rows)).astype(jnp.bfloat16)
    grouped = xs.reshape(rows, groups, per, width)
    intra = jnp.einsum('gjts,sgjp->tgjp', mixing.astype(jnp.float32), grouped.astype(jnp.float32)).reshape(rows, heads, width)
    final = cum[-1]
    decay = jnp.where(docs[-1] == prior, jnp.exp(final), 0.0)
    tail = jnp.exp(final[None, :] - cum) * dt * (docs == docs[-1]).astype(jnp.float32)[:, None]
    loaded = (tail.reshape(rows, groups, per)[..., None] * bmat[:, :, None, :].astype(jnp.float32)).astype(jnp.bfloat16)
    summary = jnp.einsum('sgjp,sgjn->gjpn', grouped.astype(jnp.float32), loaded.astype(jnp.float32)).reshape(heads, width, state)
    reach = jnp.exp(cum) * (docs == prior).astype(jnp.float32)[:, None]
    return (intra, decay, summary, reach)

def inflow(cmat, state, reach):
    rows, groups, width_n = cmat.shape
    heads = state.shape[0]
    per = heads // groups
    grouped = state.reshape(groups, per, state.shape[1], width_n)
    flow = jnp.einsum('tgn,gjpn->tgjp', cmat.astype(jnp.float32), grouped, precision=lax.Precision.HIGHEST)
    return flow.reshape(rows, heads, state.shape[1]) * reach[:, :, None]

def student_one(xs, bmat, cmat, dt_raw, dt_bias, decay_log, docs):
    length = xs.shape[0]
    count = length // STRETCH
    dt = jax.nn.softplus(dt_raw + dt_bias)
    rate = -dt * jnp.exp(decay_log)
    x_blocks = xs.reshape(count, STRETCH, HS, P_SIZE)
    b_blocks = bmat.reshape(count, STRETCH, GROUPS, N)
    c_blocks = cmat.reshape(count, STRETCH, GROUPS, N)
    dt_blocks = dt.reshape(count, STRETCH, HS)
    rate_blocks = rate.reshape(count, STRETCH, HS)
    doc_blocks = docs.reshape(count, STRETCH)
    priors = jnp.concatenate([jnp.full((1,), -1, jnp.int32), doc_blocks[:-1, -1].astype(jnp.int32)])

    def step(state, items):
        x_b, b_b, c_b, dt_b, rate_b, doc_b, prior_b = items
        intra, decay, summary, reach = block_terms(x_b, b_b, c_b, dt_b, rate_b, doc_b, prior_b)
        inner = intra + inflow(c_b, state, reach)
        state = decay[:, None, None] * state + summary
        return (state, inner)
    start = jnp.zeros((HS, P_SIZE, N), jnp.float32)
    _, mixed = lax.scan(step, start, (x_blocks, b_blocks, c_blocks, dt_blocks, rate_blocks, doc_blocks, priors))
    return mixed.reshape(length, HS, P_SIZE)

def gated_norm(mixed, xs, gate, skip, gain, groups):
    rows, heads, width = mixed.shape
    values_out = mixed + skip[None, :, None] * xs.astype(jnp.float32)
    gated = values_out.reshape(rows, heads * width) * jax.nn.silu(gate.astype(jnp.float32))
    gated = gated.reshape(rows, groups, -1)
    normed = gated * lax.rsqrt(lax.optimization_barrier(jnp.mean(gated * gated, axis=2, keepdims=True)) + 1e-05)
    return normed.reshape(rows, heads * width) * gain

def reference(queries, keys, values, doc_ids, inputs, gate_input, b_input, c_input, dt_raw, dt_bias, decay_log, skip, gain):
    natural = natural_rows(LENGTH, STRETCH, TOK_DEV)
    stored = stored_positions(LENGTH, STRETCH, TOK_DEV)

    def to_natural(array):
        return jnp.take(array, natural, axis=1)
    q_nat, k_nat, v_nat = (to_natural(queries), to_natural(keys), to_natural(values))
    x_nat, g_nat = (to_natural(inputs), to_natural(gate_input))
    b_nat, c_nat, dt_nat = (to_natural(b_input), to_natural(c_input), to_natural(dt_raw))
    teachers = []
    mixes = []
    for seq in range(SEQS):
        teachers.append(teacher_one(q_nat[seq], k_nat[seq], v_nat[seq], doc_ids[seq]))
        mixes.append(student_one(x_nat[seq], b_nat[seq], c_nat[seq], dt_nat[seq], dt_bias, decay_log, doc_ids[seq]))
    teacher_nat = jnp.stack(teachers)
    mixed = jnp.stack(mixes).reshape(SEQS * LENGTH, HS, P_SIZE)
    x_rows = x_nat.reshape(SEQS * LENGTH, HS, P_SIZE)
    g_rows = g_nat.reshape(SEQS * LENGTH, HS * P_SIZE)
    target = teacher_nat.reshape(SEQS * LENGTH, HS * P_SIZE).astype(jnp.float32)

    def loss_fn(gain_p, skip_p):
        normed = gated_norm(mixed, x_rows, g_rows, skip_p, gain_p, GROUPS)
        diff = normed - target
        return (jnp.sum(diff * diff) / (SEQS * LENGTH), normed)
    (grad_gain, grad_skip), normed = jax.grad(loss_fn, argnums=(0, 1), has_aux=True)(gain, skip)
    student_nat = normed.astype(jnp.bfloat16).reshape(SEQS, LENGTH, HS * P_SIZE)
    teacher_out = jnp.take(teacher_nat, stored, axis=1)
    student_out = jnp.take(student_nat, stored, axis=1)
    return (teacher_out, student_out, grad_gain, grad_skip)
```

```python
import functools
import math

import jax
import jax.numpy as jnp
from jax import lax
from jax.experimental import pallas as pl
from jax.experimental.pallas import tpu as pltpu
from jax.sharding import PartitionSpec as P

DH = 128
P_SIZE = 64
N = 128
EXTRA = 16
EPS = 1e-05
MASKED = -1e30
F32 = jnp.float32
BF16 = jnp.bfloat16
VMEM = pl.BlockSpec(memory_space=pltpu.VMEM)


def params(mib):
    return pltpu.CompilerParams(vmem_limit_bytes=mib << 20)


def cost(flops, size):
    return pl.CostEstimate(flops=flops, bytes_accessed=size, transcendentals=0)


def parts(v):
    hi = v.astype(BF16)
    return hi, (v - hi.astype(F32)).astype(BF16)


def spread_matrix(heads, width, first):
    row = lax.broadcasted_iota(jnp.int32, (heads, width), 0)
    lane = lax.broadcasted_iota(jnp.int32, (heads, width), 1)
    return jnp.where(row == (lane // P_SIZE) + first, 1.0, 0.0).astype(BF16)


def spread(v, matrix):
    hi, lo = parts(v)
    return jnp.dot(hi, matrix, preferred_element_type=F32) + jnp.dot(
        lo, matrix, preferred_element_type=F32
    )


def dot_nt(a, b):
    return lax.dot_general(a, b, (((1,), (1,)), ((), ())), preferred_element_type=F32)


def dot_tn(a, b):
    return lax.dot_general(a, b, (((0,), (0,)), ((), ())), preferred_element_type=F32)


def doc_row(docs_ref, block, stretch):
    return docs_ref[:, pl.ds(pl.multiple_of(block * stretch, stretch), stretch)]


def as_column(row):
    size = row.shape[1]
    r = lax.broadcasted_iota(jnp.int32, (size, size), 0)
    c = lax.broadcasted_iota(jnp.int32, (size, size), 1)
    return jnp.sum(jnp.where(r == c, row.astype(F32), 0.0), axis=1, keepdims=True)


def lower_triangle(size):
    r = lax.broadcasted_iota(jnp.int32, (size, size), 0)
    c = lax.broadcasted_iota(jnp.int32, (size, size), 1)
    return r >= c


def prior_doc(docs_ref, block, stretch):
    before = doc_row(docs_ref, jnp.maximum(block - 1, 0), stretch)[:, stretch - 1 :]
    return jnp.where(block > 0, before, -1)


def pack_kernel(k_ref, v_ref, full_ref, front_ref):
    width = k_ref.shape[1]
    rows = front_ref.shape[0]
    full_ref[:, :width] = k_ref[...]
    full_ref[:, width:] = v_ref[...]
    front_ref[:, :width] = k_ref[:rows, :]
    front_ref[:, width:] = v_ref[:rows, :]


def summary_kernel(
    count, groups, docs_ref, x_ref, b_ref, dt_ref, bias_ref, log_ref, xw_ref, ec_ref, dec_ref, *outs
):
    f_refs, b_refs, q_refs = outs[:groups], outs[groups : 2 * groups], outs[2 * groups :]
    rows, heads = dt_ref.shape
    stretch = rows // 2
    width = x_ref.shape[1] // groups
    index = lax.axis_index("ctx")
    triangle = jnp.where(lower_triangle(stretch), 1.0, 0.0)
    slope = jnp.exp(log_ref[...])
    decays = []
    sums = []
    for half in range(2):
        block = index if half == 0 else 2 * count - 1 - index
        sl = slice(half * stretch, (half + 1) * stretch)
        raw = dt_ref[sl, :] + bias_ref[...]
        dt = jnp.maximum(raw, 0.0) + jnp.log1p(jnp.exp(-jnp.abs(raw)))
        cum = jnp.dot(
            triangle, -dt * slope, precision=lax.Precision.HIGHEST, preferred_element_type=F32
        )
        ec_ref[sl, :] = jnp.exp(cum)
        load = jnp.exp(-cum) * dt
        final = jnp.exp(cum[stretch - 1 :, :])
        row = doc_row(docs_ref, block, stretch)
        last = row[:, stretch - 1 :]
        decays.append(jnp.where(last == prior_doc(docs_ref, block, stretch), final, 0.0))
        same = jnp.where(as_column(row) == last.astype(F32), 1.0, 0.0)
        here = []
        for g in range(groups):
            cols = slice(g * width, (g + 1) * width)
            matrix = spread_matrix(heads, width, g * (heads // groups))
            xw = (x_ref[sl, cols].astype(F32) * spread(load, matrix)).astype(BF16)
            xw_ref[sl, cols] = xw
            proj = (b_ref[sl, g * N : (g + 1) * N].astype(F32) * same).astype(BF16)
            here.append(dot_tn(proj, xw) * spread(final, matrix))
        sums.append(here)
    for g in range(groups):
        cols = slice(g * width, (g + 1) * width)
        matrix = spread_matrix(heads, width, g * (heads // groups))
        both = jnp.concatenate([decays[0], decays[1]], axis=0)
        wide = spread(both, matrix)
        dec_ref[0:2, cols] = wide
        f_refs[g][...] = sums[0][g].astype(BF16)
        b_refs[g][...] = sums[1][g].astype(BF16)
        q_refs[g][:N, :] = (wide[1:2] * sums[0][g] + sums[1][g]).astype(BF16)
        hi, lo = parts(wide[0:1] * wide[1:2])
        q_refs[g][N : N + 1, :] = hi
        q_refs[g][N + 1 : N + 2, :] = lo
        q_refs[g][N + 2 :, :] = jnp.zeros((EXTRA - 2, width), BF16)


def chain_kernel(p_ref, q_ref, f_ref, b_ref, dec_ref, p_out, q_out):
    d_front, d_back = dec_ref[0:1, :], dec_ref[1:2, :]
    f = f_ref[...].astype(F32)
    d_in = q_ref[N : N + 1, :].astype(F32) + q_ref[N + 1 : N + 2, :].astype(F32)
    p_out[...] = (d_front * p_ref[...].astype(F32) + f).astype(BF16)
    q_out[:N, :] = (
        d_back * (d_in * f + q_ref[:N, :].astype(F32)) + b_ref[...].astype(F32)
    ).astype(BF16)
    hi, lo = parts(d_back * d_in * d_front)
    q_out[N : N + 1, :] = hi
    q_out[N + 1 : N + 2, :] = lo
    q_out[N + 2 :, :] = jnp.zeros((EXTRA - 2, p_ref.shape[1]), BF16)


def local_kernel(
    count, docs_ref, x_ref, xw_ref, b_ref, c_ref, ec_ref, skip_ref, pre_ref, reach_ref
):
    rows, heads = ec_ref.shape
    stretch = rows // 2
    width = x_ref.shape[1]
    index = lax.axis_index("ctx")
    g = pl.program_id(0)
    matrix = spread_matrix(heads, width, g * (width // P_SIZE))
    wide_skip = spread(skip_ref[...], matrix)
    triangle = lower_triangle(stretch)
    for half in range(2):
        block = index if half == 0 else 2 * count - 1 - index
        sl = slice(half * stretch, (half + 1) * stretch)
        row = doc_row(docs_ref, block, stretch)
        column = as_column(row)
        gram = dot_nt(c_ref[sl, :], b_ref[sl, :])
        gram = jnp.where(triangle & (column == row.astype(F32)), gram, 0.0).astype(BF16)
        wide = spread(ec_ref[sl, :], matrix)
        inner = jnp.dot(gram, xw_ref[sl, :], preferred_element_type=F32)
        pre_ref[sl, :] = inner * wide + wide_skip * x_ref[sl, :].astype(F32)
        reached = column == prior_doc(docs_ref, block, stretch).astype(F32)
        reach_ref[sl, :] = jnp.where(reached, wide, 0.0)


def attention_kernel(count, per, unroll, docs_ref, q_ref, k_ref, v_ref, *refs):
    others = count - 1
    ups, downs = refs[:others], refs[others : 2 * others]
    out_ref = refs[2 * others]
    kb, vb, ka, va, bias_b, bias_f, bias_a = refs[2 * others + 1 :]
    rows = q_ref.shape[0]
    stretch = rows // 2
    index = lax.axis_index("ctx")
    g = pl.program_id(0)
    kv_width = ups[0].shape[1] // 2
    k_cols = pl.ds(pl.multiple_of(g * DH, DH), DH)
    v_cols = pl.ds(pl.multiple_of(kv_width + g * DH, DH), DH)
    kb[: 2 * stretch, :] = k_ref[...]
    vb[: 2 * stretch, :] = v_ref[...]
    for r in range(1, count):
        at_b = slice((r + 1) * stretch, (r + 2) * stretch)
        at_a = slice((r - 1) * stretch, r * stretch)
        up, down = ups[r - 1], downs[count - r - 1]

        @pl.when(index >= r)
        def _():
            kb[at_b, :] = up[:, k_cols]
            ka[at_a, :] = up[:, k_cols]
            vb[at_b, :] = up[:, v_cols]
            va[at_a, :] = up[:, v_cols]

        @pl.when(index < r)
        def _():
            kb[at_b, :] = down[:stretch, k_cols]
            ka[at_a, :] = down[stretch:, k_cols]
            vb[at_b, :] = down[:stretch, v_cols]
            va[at_a, :] = down[stretch:, v_cols]

    @pl.when(g == 0)
    def _():
        last = 2 * count - 1
        row_f = doc_row(docs_ref, index, stretch).astype(F32)
        row_b = doc_row(docs_ref, last - index, stretch).astype(F32)
        col_f = as_column(row_f)
        col_b = as_column(row_b)
        triangle = lower_triangle(stretch)
        bias_f[...] = jnp.where(triangle & (col_f == row_f), 0.0, MASKED)
        bias_b[:, :stretch] = jnp.where(col_b == row_f, 0.0, MASKED)
        bias_b[:, stretch : 2 * stretch] = jnp.where(triangle & (col_b == row_b), 0.0, MASKED)
        for r in range(1, count):
            up = index >= r
            source = jnp.where(up, index - r, index + count - r)
            key_f = doc_row(docs_ref, source, stretch).astype(F32)
            key_a = doc_row(docs_ref, jnp.where(up, source, last - source), stretch).astype(F32)
            col_a = jnp.where(up, col_f, col_b)
            bias_b[:, (r + 1) * stretch : (r + 2) * stretch] = jnp.where(
                col_b == key_f, 0.0, MASKED
            )
            bias_a[:, (r - 1) * stretch : r * stretch] = jnp.where(col_a == key_a, 0.0, MASKED)

    factor = math.log2(math.e) / math.sqrt(DH)

    def one_head(h):
        cols = pl.ds(pl.multiple_of(h * DH, DH), DH)
        q_f = q_ref[:stretch, cols]
        q_b = q_ref[stretch:, cols]
        s_f = dot_nt(q_f, kb[:stretch, :]) + bias_f[...]
        s_b = dot_nt(q_b, kb[...]) + bias_b[...]
        top_f = jnp.max(s_f, axis=1, keepdims=True)
        top_b = jnp.max(s_b, axis=1, keepdims=True)
        s_a = []
        for r in range(1, count):
            at_a = slice((r - 1) * stretch, r * stretch)
            first = pl.multiple_of(jnp.where(index >= r, 0, stretch), stretch)
            score = dot_nt(q_ref[pl.ds(first, stretch), cols], ka[at_a, :]) + bias_a[:, at_a]
            top = jnp.max(score, axis=1, keepdims=True)
            top_f = jnp.maximum(top_f, jnp.where(index >= r, top, MASKED))
            top_b = jnp.maximum(top_b, jnp.where(index >= r, MASKED, top))
            s_a.append(score)
        w_f = jnp.exp2((s_f - top_f) * factor)
        w_b = jnp.exp2((s_b - top_b) * factor)
        sum_f = jnp.sum(w_f, axis=1, keepdims=True)
        sum_b = jnp.sum(w_b, axis=1, keepdims=True)
        out_f = jnp.dot(w_f.astype(BF16), vb[:stretch, :], preferred_element_type=F32)
        out_b = jnp.dot(w_b.astype(BF16), vb[...], preferred_element_type=F32)
        for r in range(1, count):
            at_a = slice((r - 1) * stretch, r * stretch)
            up = index >= r
            w = jnp.exp2((s_a[r - 1] - jnp.where(up, top_f, top_b)) * factor)
            total = jnp.sum(w, axis=1, keepdims=True)
            out = jnp.dot(w.astype(BF16), va[at_a, :], preferred_element_type=F32)
            sum_f += jnp.where(up, total, 0.0)
            sum_b += jnp.where(up, 0.0, total)
            out_f += jnp.where(up, out, 0.0)
            out_b += jnp.where(up, 0.0, out)
        out_ref[:stretch, cols] = (out_f / sum_f).astype(BF16)
        out_ref[stretch:, cols] = (out_b / sum_b).astype(BF16)

    if unroll:
        for h in range(per):
            one_head(h)
    else:

        @pl.loop(0, per)
        def _(h):
            one_head(h)


def final_kernel(
    count,
    g,
    loss_scale,
    pre_ref,
    reach_ref,
    c_ref,
    x_ref,
    gate_ref,
    teacher_ref,
    gain_ref,
    f_ref,
    dec_ref,
    *refs,
):
    others = count - 1
    p_refs, q_refs = refs[:others], refs[others : 2 * others]
    out_ref, grad_ref, flow_ref, gain_acc, skip_acc = refs[-5:]
    rows, width = pre_ref.shape
    stretch = rows // 2
    index = lax.axis_index("ctx")
    state = p_refs[0][...].astype(F32)
    back = q_refs[0][...].astype(F32)
    for r in range(1, others):
        state += p_refs[r][...].astype(F32)
        back += q_refs[r][...].astype(F32)
    d_in = jnp.where(index == count - 1, 1.0, back[N : N + 1] + back[N + 1 : N + 2])
    after = d_in * (dec_ref[0:1, :] * state + f_ref[...].astype(F32)) + back[:N]
    flow_ref[:stretch, :] = jnp.dot(
        c_ref[:stretch, :], state.astype(BF16), preferred_element_type=F32
    )
    flow_ref[stretch:, :] = jnp.dot(
        c_ref[stretch:, :], after.astype(BF16), preferred_element_type=F32
    )
    gain_acc[...] = jnp.zeros_like(gain_acc)
    skip_acc[...] = jnp.zeros_like(skip_acc)
    gain = gain_ref[...]
    step = 16

    @pl.loop(0, rows // step)
    def _(k):
        sl = pl.ds(pl.multiple_of(k * step, step), step)
        gate = gate_ref[sl, :].astype(F32)
        silu = gate / (1.0 + jnp.exp(-gate))
        gated = (pre_ref[sl, :] + reach_ref[sl, :] * flow_ref[sl, :]) * silu
        scale = lax.rsqrt(jnp.mean(gated * gated, axis=1, keepdims=True) + EPS)
        unit = gated * scale
        normed = unit * gain
        out_ref[sl, :] = normed.astype(BF16)
        push = (normed - teacher_ref[sl, :].astype(F32)) * (2.0 * loss_scale)
        by_gain = push * unit
        pulled = push * gain
        mean = jnp.mean(by_gain * gain, axis=1, keepdims=True)
        by_skip = scale * (pulled - unit * mean) * silu * x_ref[sl, :].astype(F32)
        gain_acc[...] += by_gain[:8] + by_gain[8:]
        skip_acc[...] += by_skip[:8] + by_skip[8:]

    grad_ref[0:1, :] = jnp.sum(gain_acc[...], axis=0, keepdims=True)
    heads = width // P_SIZE
    row = lax.broadcasted_iota(jnp.int32, (128, width), 0)
    lane = lax.broadcasted_iota(jnp.int32, (128, width), 1)
    matrix = jnp.where(row == lane // P_SIZE, 1.0, 0.0).astype(BF16)
    hi, lo = parts(skip_acc[...])
    by_head = jnp.sum(dot_nt(hi, matrix) + dot_nt(lo, matrix), axis=0, keepdims=True)
    grad_ref[1:2, :] = jnp.zeros((1, width), F32)
    grad_ref[1:2, :128] = by_head


def exchange_sum(part, axis):
    size = lax.axis_size(axis)
    step = 1
    while step < size:
        span = 4 if (size // step) % 4 == 0 else 2
        got = [part]
        for k in range(1, span):
            pairs = [(d, d ^ (k * step)) for d in range(size)]
            got.append(lax.ppermute(part, axis, pairs))
        if span == 4:
            part = (got[0] + got[1]) + (got[2] + got[3])
        else:
            part = got[0] + got[1]
        step *= span
    return part


def body(
    queries,
    keys,
    values,
    doc_ids,
    inputs,
    gate_input,
    b_input,
    c_input,
    dt_raw,
    dt_bias,
    decay_log,
    skip,
    gain,
):
    count = lax.axis_size("ctx")
    rows, features = queries.shape[1:]
    stretch = rows // 2
    kv_dev = keys.shape[2] // DH
    per_kv = queries.shape[2] // keys.shape[2]
    groups = b_input.shape[2] // N
    heads = features // P_SIZE
    width = features // groups
    length = doc_ids.shape[1]
    others = count - 1
    last = count - 1
    loss_scale = 1.0 / (lax.axis_size("dp") * count * rows)
    x, gate, bmat, cmat = inputs[0], gate_input[0], b_input[0], c_input[0]
    struct = jax.ShapeDtypeStruct

    full, front = pl.pallas_call(
        pack_kernel,
        out_shape=(
            struct((rows, 2 * kv_dev * DH), BF16),
            struct((stretch, 2 * kv_dev * DH), BF16),
        ),
        in_specs=[VMEM] * 2,
        out_specs=(VMEM,) * 2,
        cost_estimate=cost(0, 3 * keys.size * 2),
        name="pack_kv",
    )(keys[0], values[0])
    ups, downs = [], []
    up, down = front, full
    for r in range(1, count):
        up = lax.ppermute(up, "ctx", [(d, d + 1) for d in range(r - 1, last)])
        down = lax.ppermute(down, "ctx", [(d, d - 1) for d in range(1, count - r + 1)])
        ups.append(up)
        downs.append(down)

    state = struct((N, width), BF16)
    composite = struct((N + EXTRA, width), BF16)
    outs = pl.pallas_call(
        functools.partial(summary_kernel, count, groups),
        out_shape=(
            struct((rows, features), BF16),
            struct((rows, heads), F32),
            struct((8, features), F32),
            *([state] * (2 * groups)),
            *([composite] * groups),
        ),
        in_specs=[VMEM] * 6,
        out_specs=(VMEM,) * (3 + 3 * groups),
        compiler_params=params(32),
        cost_estimate=cost(4 * rows * features * N, 8 * rows * features),
        name="summaries",
    )(doc_ids, x, bmat, dt_raw[0], dt_bias.reshape(1, heads), decay_log.reshape(1, heads))
    xw, ec, dec = outs[:3]
    f_parts, b_parts, q_parts = (
        outs[3 : 3 + groups],
        outs[3 + groups : 3 + 2 * groups],
        outs[3 + 2 * groups :],
    )

    chain = [
        pl.pallas_call(
            chain_kernel,
            out_shape=(state, composite),
            grid=(1,),
            in_specs=[
                pl.BlockSpec((N, width), lambda k: (0, 0)),
                pl.BlockSpec((N + EXTRA, width), lambda k: (0, 0)),
                pl.BlockSpec((N, width), lambda k: (0, 0)),
                pl.BlockSpec((N, width), lambda k: (0, 0)),
                pl.BlockSpec((8, width), lambda k, g=g: (0, g)),
            ],
            out_specs=(
                pl.BlockSpec((N, width), lambda k: (0, 0)),
                pl.BlockSpec((N + EXTRA, width), lambda k: (0, 0)),
            ),
            cost_estimate=cost(8 * N * width, 12 * N * width),
            compiler_params=params(16),
            name="chain",
        )
        for g in range(groups)
    ]
    p_got = [[] for _ in range(groups)]
    q_got = [[] for _ in range(groups)]
    p_send, q_send = list(f_parts), list(q_parts)
    for r in range(1, count):
        for g in range(groups):
            if r > 1:
                p_send[g], q_send[g] = chain[g](
                    p_got[g][-1], q_got[g][-1], f_parts[g], b_parts[g], dec
                )
            p_got[g].append(lax.ppermute(p_send[g], "ctx", [(r - 1, r)]))
            q_got[g].append(lax.ppermute(q_send[g], "ctx", [(count - r, count - r - 1)]))

    by_group = pl.BlockSpec((rows, width), lambda g: (0, g))
    by_proj = pl.BlockSpec((rows, N), lambda g: (0, g))
    pre, reach = pl.pallas_call(
        functools.partial(local_kernel, count),
        out_shape=(struct((rows, features), F32), struct((rows, features), F32)),
        grid=(groups,),
        in_specs=[
            pl.BlockSpec((1, length), lambda g: (0, 0)),
            by_group,
            by_group,
            by_proj,
            by_proj,
            pl.BlockSpec((rows, heads), lambda g: (0, 0)),
            pl.BlockSpec((1, heads), lambda g: (0, 0)),
        ],
        out_specs=(by_group, by_group),
        compiler_params=params(32),
        cost_estimate=cost(4 * rows * features * N, 12 * rows * features),
        name="local",
    )(doc_ids, x, xw, bmat, cmat, ec, skip.reshape(1, heads))

    by_kv = pl.BlockSpec((rows, per_kv * DH), lambda g: (0, g))
    by_key = pl.BlockSpec((rows, DH), lambda g: (0, g))
    teacher = pl.pallas_call(
        functools.partial(attention_kernel, count, per_kv, count <= 4),
        out_shape=struct((rows, features), BF16),
        grid=(kv_dev,),
        in_specs=[
            pl.BlockSpec((1, length), lambda g: (0, 0)),
            by_kv,
            by_key,
            by_key,
            *[pl.BlockSpec((stretch, 2 * kv_dev * DH), lambda g: (0, 0))] * others,
            *[pl.BlockSpec((rows, 2 * kv_dev * DH), lambda g: (0, 0))] * others,
        ],
        out_specs=by_kv,
        scratch_shapes=[
            pltpu.VMEM(((count + 1) * stretch, DH), BF16),
            pltpu.VMEM(((count + 1) * stretch, DH), BF16),
            pltpu.VMEM((others * stretch, DH), BF16),
            pltpu.VMEM((others * stretch, DH), BF16),
            pltpu.VMEM((stretch, (count + 1) * stretch), F32),
            pltpu.VMEM((stretch, stretch), F32),
            pltpu.VMEM((stretch, others * stretch), F32),
        ],
        compiler_params=params(40),
        cost_estimate=cost(
            4 * (2 * count + 1) * stretch * stretch * features, 8 * rows * features
        ),
        name="attention",
    )(doc_ids, queries[0], keys[0], values[0], *ups, *downs)

    student = None
    reduced = []
    for g in range(groups):
        at = lambda k, g=g: (0, g)
        whole = lambda k: (0, 0)
        more = [] if student is None else [student]
        fixed = 9 + 2 * others
        student, grads = pl.pallas_call(
            functools.partial(final_kernel, count, g, loss_scale),
            out_shape=(struct((rows, features), BF16), struct((2, width), F32)),
            grid=(1,),
            in_specs=[
                pl.BlockSpec((rows, width), at),
                pl.BlockSpec((rows, width), at),
                pl.BlockSpec((rows, N), at),
                pl.BlockSpec((rows, width), at),
                pl.BlockSpec((rows, width), at),
                pl.BlockSpec((rows, width), at),
                pl.BlockSpec((1, width), at),
                pl.BlockSpec((N, width), whole),
                pl.BlockSpec((8, width), at),
                *[pl.BlockSpec((N, width), whole)] * others,
                *[pl.BlockSpec((N + EXTRA, width), whole)] * others,
                *[pl.BlockSpec(memory_space=pl.ANY)] * len(more),
            ],
            out_specs=(pl.BlockSpec((rows, width), at), pl.BlockSpec((2, width), whole)),
            scratch_shapes=[
                pltpu.VMEM((rows, width), F32),
                pltpu.VMEM((8, width), F32),
                pltpu.VMEM((8, width), F32),
            ],
            input_output_aliases={fixed: 0} if more else {},
            compiler_params=params(40),
            cost_estimate=cost(2 * rows * width * N, 20 * rows * width),
            name="final",
        )(
            pre,
            reach,
            cmat,
            x,
            gate,
            teacher,
            gain.reshape(1, features),
            f_parts[g],
            dec,
            *p_got[g],
            *q_got[g],
            *more,
        )
        reduced.append(exchange_sum(exchange_sum(grads, "ctx"), "dp"))
    grad_gain = jnp.concatenate([part[0] for part in reduced])
    grad_skip = jnp.concatenate([part[1, : heads // groups] for part in reduced])
    return (teacher[None], student[None], grad_gain, grad_skip)


def solution(mesh):
    rows = P("dp", "ctx", "head")
    in_specs = (
        rows,
        rows,
        rows,
        P("dp", None),
        rows,
        rows,
        rows,
        rows,
        rows,
        P("head"),
        P("head"),
        P("head"),
        P("head"),
    )
    out_specs = (rows, rows, P("head"), P("head"))
    return jax.shard_map(body, mesh=mesh, in_specs=in_specs, out_specs=out_specs, check_vma=False)
```

```python
import functools
import math

import jax
import jax.numpy as jnp
from jax import lax
from jax.experimental import pallas as pl
from jax.experimental.pallas import tpu as pltpu
from jax.sharding import PartitionSpec as P

DH = 128
P_SIZE = 64
N = 128
EXTRA = 16
EPS = 1e-05
MASKED = -1e30
F32 = jnp.float32
BF16 = jnp.bfloat16
VMEM = pl.BlockSpec(memory_space=pltpu.VMEM)


def params(mib):
    return pltpu.CompilerParams(vmem_limit_bytes=mib << 20)


def cost(flops, size):
    return pl.CostEstimate(flops=flops, bytes_accessed=size, transcendentals=0)


def parts(v):
    hi = v.astype(BF16)
    return hi, (v - hi.astype(F32)).astype(BF16)


def spread_matrix(heads, width, first):
    row = lax.broadcasted_iota(jnp.int32, (heads, width), 0)
    lane = lax.broadcasted_iota(jnp.int32, (heads, width), 1)
    return jnp.where(row == (lane // P_SIZE) + first, 1.0, 0.0).astype(BF16)


def dot_nt(a, b):
    return lax.dot_general(a, b, (((1,), (1,)), ((), ())), preferred_element_type=F32)


def dot_tn(a, b):
    return lax.dot_general(a, b, (((0,), (0,)), ((), ())), preferred_element_type=F32)


def spread(v, matrix):
    hi, lo = parts(v)
    return dot_tn(hi, matrix) + dot_tn(lo, matrix)


def doc_row(docs_ref, block, stretch):
    return docs_ref[:, pl.ds(pl.multiple_of(block * stretch, stretch), stretch)]


def as_column(row):
    size = row.shape[1]
    r = lax.broadcasted_iota(jnp.int32, (size, size), 0)
    c = lax.broadcasted_iota(jnp.int32, (size, size), 1)
    return jnp.sum(jnp.where(r == c, row.astype(F32), 0.0), axis=1, keepdims=True)


def lower_triangle(size):
    r = lax.broadcasted_iota(jnp.int32, (size, size), 0)
    c = lax.broadcasted_iota(jnp.int32, (size, size), 1)
    return r >= c


def prior_doc(docs_ref, block, stretch):
    before = doc_row(docs_ref, jnp.maximum(block - 1, 0), stretch)[:, stretch - 1 :]
    return jnp.where(block > 0, before, -1)


def own_block(index, count, half):
    return index if half == 0 else 2 * count - 1 - index


def ring_order(count):
    return [0] + list(range(1, count, 2)) + list(range(2, count, 2))[::-1]


def ring_source(index, count, steps):
    order = ring_order(count)
    source = jnp.int32(0)
    for place, member in enumerate(order):
        source = jnp.where(index == member, order[(place - steps) % count], source)
    return source


def put_state(ref, state):
    ref[:N, :] = state.astype(BF16)
    ref[N:, :] = jnp.zeros((EXTRA, ref.shape[1]), BF16)


def put_composite(ref, state, decay):
    hi, lo = parts(decay)
    ref[:N, :] = state.astype(BF16)
    ref[N:, :] = jnp.concatenate(
        [hi, lo, jnp.zeros((EXTRA - 2, ref.shape[1]), BF16)], axis=0
    )


def opening_kernel(
    count,
    groups,
    docs_ref,
    k_ref,
    v_ref,
    x_ref,
    b_ref,
    dt_ref,
    bias_ref,
    log_ref,
    kv_ref,
    ec_ref,
    *outs,
):
    xw_refs, dec_refs, f_refs, b_refs, send_refs = (
        outs[k * groups : (k + 1) * groups] for k in range(5)
    )
    heads, rows = dt_ref.shape
    stretch = rows // 2
    width = x_ref.shape[1] // groups
    kv_width = k_ref.shape[1]
    index = lax.axis_index("ctx")
    kv_ref[:, :kv_width] = k_ref[...]
    kv_ref[:, kv_width:] = v_ref[...]
    triangle = jnp.where(lower_triangle(stretch), 1.0, 0.0)
    slope = jnp.exp(as_column(log_ref[...]))
    bias = as_column(bias_ref[...])
    lane = lax.broadcasted_iota(jnp.int32, (heads, 8), 1)
    ends = jnp.zeros((heads, 8), F32)
    loads = []
    projs = []
    for half in range(2):
        block = own_block(index, count, half)
        sl = slice(half * stretch, (half + 1) * stretch)
        raw = dt_ref[:, sl] + bias
        dt = jnp.maximum(raw, 0.0) + jnp.log1p(jnp.exp(-jnp.abs(raw)))
        cum = lax.dot_general(
            -dt * slope,
            triangle,
            (((1,), (1,)), ((), ())),
            precision=lax.Precision.HIGHEST,
            preferred_element_type=F32,
        )
        ec_ref[:, sl] = jnp.exp(cum)
        loads.append(jnp.exp(-cum) * dt)
        final = jnp.exp(cum[:, stretch - 1 :])
        row = doc_row(docs_ref, block, stretch)
        last = row[:, stretch - 1 :]
        kept = jnp.where(last == prior_doc(docs_ref, block, stretch), 1.0, 0.0)
        ends = jnp.where(lane == half, final * kept, ends)
        ends = jnp.where(lane == 2 + half, final, ends)
        same = jnp.where(as_column(row) == last.astype(F32), 1.0, 0.0)
        projs.append((b_ref[sl, :].astype(F32) * same).astype(BF16))
    for g in range(groups):
        cols = slice(g * width, (g + 1) * width)
        matrix = spread_matrix(heads, width, g * (heads // groups))
        wide = spread(ends, matrix)
        dec_refs[g][...] = wide
        sums = []
        for half in range(2):
            sl = slice(half * stretch, (half + 1) * stretch)
            xw = (x_ref[sl, cols].astype(F32) * spread(loads[half], matrix)).astype(BF16)
            xw_refs[g][sl, :] = xw
            sums.append(dot_tn(projs[half][:, g * N : (g + 1) * N], xw) * wide[2 + half : 3 + half])
        f_refs[g][...] = sums[0].astype(BF16)
        b_refs[g][...] = sums[1].astype(BF16)

        @pl.when(index == 0)
        def _():
            put_state(send_refs[g], sums[0])

        @pl.when(index != 0)
        def _():
            put_composite(send_refs[g], wide[1:2] * sums[0] + sums[1], wide[0:1] * wide[1:2])


def chain_kernel(count, stage, got_ref, f_ref, b_ref, dec_ref, send_ref):
    index = lax.axis_index("ctx")

    @pl.when(index == stage)
    def _():
        state = dec_ref[0:1, :] * got_ref[:N, :].astype(F32) + f_ref[...].astype(F32)
        put_state(send_ref, state)

    @pl.when(index == count - 1 - stage)
    def _():
        decay = got_ref[N : N + 1, :].astype(F32) + got_ref[N + 1 : N + 2, :].astype(F32)
        inner = decay * f_ref[...].astype(F32) + got_ref[:N, :].astype(F32)
        state = dec_ref[1:2, :] * inner + b_ref[...].astype(F32)
        put_composite(send_ref, state, dec_ref[1:2, :] * decay * dec_ref[0:1, :])


def local_kernel(
    count,
    first,
    docs_ref,
    x_ref,
    gate_ref,
    b_ref,
    c_ref,
    ec_ref,
    skip_ref,
    xw_ref,
    pre_ref,
    reach_ref,
    sx_ref,
):
    heads, rows = ec_ref.shape
    stretch = rows // 2
    width = x_ref.shape[1]
    index = lax.axis_index("ctx")
    matrix = spread_matrix(heads, width, first)
    wide_skip = spread(as_column(skip_ref[...]), matrix)
    triangle = lower_triangle(stretch)
    step = 16
    for half in range(2):
        block = own_block(index, count, half)
        sl = slice(half * stretch, (half + 1) * stretch)
        row = doc_row(docs_ref, block, stretch)
        column = as_column(row)
        gram = dot_nt(c_ref[sl, :], b_ref[sl, :])
        gram = jnp.where(triangle & (column == row.astype(F32)), gram, 0.0).astype(BF16)
        wide = spread(ec_ref[:, sl], matrix)
        inner = jnp.dot(gram, xw_ref[sl, :], preferred_element_type=F32)
        reached = jnp.where(column == prior_doc(docs_ref, block, stretch).astype(F32), 1.0, 0.0)
        for k in range(0, stretch, step):
            at = slice(half * stretch + k, half * stretch + k + step)
            here = slice(k, k + step)
            x = x_ref[at, :].astype(F32)
            gate = gate_ref[at, :].astype(F32)
            silu = gate / (1.0 + jnp.exp(-gate))
            fade = wide[here] * silu
            sx = silu * x
            sx_ref[at, :] = sx
            pre_ref[at, :] = inner[here] * fade + wide_skip * sx
            reach_ref[at, :] = reached[here] * fade


def attention_kernel(count, per, stack, g, docs_ref, q_ref, k_ref, v_ref, *refs):
    others = count - 1
    got = refs[:others]
    out_ref, copy_ref = refs[-10:-8]
    kb, vb, ka, va, bias_b, bias_f, bias_a, best = refs[-8:]
    rows = q_ref.shape[0]
    stretch = rows // 2
    index = lax.axis_index("ctx")
    last = 2 * count - 1
    kv_width = got[0].shape[1] // 2
    k_cols = slice(g * DH, (g + 1) * DH)
    v_cols = slice(kv_width + g * DH, kv_width + (g + 1) * DH)
    row_f = doc_row(docs_ref, index, stretch).astype(F32)
    row_b = doc_row(docs_ref, last - index, stretch).astype(F32)
    col_f = as_column(row_f)
    col_b = as_column(row_b)
    triangle = lower_triangle(stretch)
    bias_f[...] = jnp.where(triangle & (col_f == row_f), 0.0, MASKED)
    bias_b[:, :stretch] = jnp.where(col_b == row_f, 0.0, MASKED)
    bias_b[:, stretch:rows] = jnp.where(triangle & (col_b == row_b), 0.0, MASKED)
    vb[:, DH:] = jnp.ones((vb.shape[0], DH), BF16)
    va[:, DH:] = jnp.ones((va.shape[0], DH), BF16)
    kb[:rows, :] = k_ref[...]
    vb[:rows, :DH] = v_ref[...]
    lower, at_a, picks = [], [], []
    for r in range(others):
        at_b = slice(rows + r * stretch, rows + (r + 1) * stretch)
        at_a.append(slice(r * stretch, (r + 1) * stretch))
        source = ring_source(index, count, r + 1)
        lower.append(source < index)
        picks.append(jnp.where(lower[r], 0, 1))
        own = pl.ds(pl.multiple_of(picks[r] * stretch, stretch), stretch)
        kb[at_b, :] = got[r][:stretch, k_cols]
        vb[at_b, :DH] = got[r][:stretch, v_cols]
        ka[at_a[r], :] = got[r][own, k_cols]
        va[at_a[r], :DH] = got[r][own, v_cols]
        key_f = doc_row(docs_ref, source, stretch).astype(F32)
        key_a = doc_row(docs_ref, jnp.where(lower[r], source, last - source), stretch).astype(F32)
        bias_b[:, at_b] = jnp.where(col_b == key_f, 0.0, MASKED)
        bias_a[:, at_a[r]] = jnp.where(
            jnp.where(lower[r], col_f, col_b) == key_a, 0.0, MASKED
        )

    factor = math.log2(math.e) / math.sqrt(DH)
    tall = stack * stretch

    def stacked(first, base):
        return jnp.concatenate(
            [q_ref[pl.ds(base, stretch), (first + j) * DH : (first + j + 1) * DH] for j in range(stack)],
            axis=0,
        )

    def biased(score, bias):
        size = score.shape[1]
        return (score.reshape(stack, stretch, size) + bias[None]).reshape(tall, size)

    for first in range(0, per, stack):
        s_f = biased(dot_nt(stacked(first, 0), kb[:stretch, :]), bias_f[...])
        s_b = biased(dot_nt(stacked(first, stretch), kb[...]), bias_b[...])
        best[:tall, :] = s_f
        top = s_b[:, :stretch]
        for k in range(1, count + 1):
            top = jnp.maximum(top, s_b[:, k * stretch : (k + 1) * stretch])
        best[tall:, :] = top
        s_a = []
        places = []
        for r in range(others):
            base = pl.multiple_of(picks[r] * stretch, stretch)
            place = pl.ds(pl.multiple_of(picks[r] * tall, tall), tall)
            s_a.append(biased(dot_nt(stacked(first, base), ka[at_a[r], :]), bias_a[:, at_a[r]]))
            best[place, :] = jnp.maximum(best[place, :], s_a[r])
            places.append(place)
        top_f = jnp.max(best[:tall, :], axis=1, keepdims=True)
        top_b = jnp.max(best[tall:, :], axis=1, keepdims=True)
        w_f = jnp.exp2((s_f - top_f) * factor).astype(BF16)
        w_b = jnp.exp2((s_b - top_b) * factor).astype(BF16)
        out_f = jnp.dot(w_f, vb[:stretch, :], preferred_element_type=F32)
        out_b = jnp.dot(w_b, vb[...], preferred_element_type=F32)
        for r in range(others):
            top = jnp.where(lower[r], top_f, top_b)
            w = jnp.exp2((s_a[r] - top) * factor).astype(BF16)
            out = jnp.dot(w, va[at_a[r], :], preferred_element_type=F32)
            out_f += jnp.where(lower[r], out, 0.0)
            out_b += jnp.where(lower[r], 0.0, out)
        for half, out in enumerate((out_f, out_b)):
            result = (out[:, :DH] / out[:, DH:]).astype(BF16)
            sl = slice(half * stretch, (half + 1) * stretch)
            for j in range(stack):
                cols = slice((first + j) * DH, (first + j + 1) * DH)
                out_ref[sl, cols] = result[j * stretch : (j + 1) * stretch]
                copy_ref[sl, cols] = result[j * stretch : (j + 1) * stretch]


def final_kernel(
    count,
    g,
    groups,
    loss_scale,
    pre_ref,
    reach_ref,
    sx_ref,
    c_ref,
    teacher_ref,
    gain_ref,
    f_ref,
    dec_ref,
    *refs,
):
    others = count - 1
    got = refs[:others]
    before = refs[others] if g else None
    out_ref, grad_ref, front, back, flow, gated_ref, sums, gain_acc, skip_acc = refs[-9:]
    rows, width = pre_ref.shape
    stretch = rows // 2
    index = lax.axis_index("ctx")
    tile = 128
    step = 16

    @pl.when(index == 0)
    def _():
        front[...] = jnp.zeros_like(front)

    @pl.when(index == count - 1)
    def _():
        back[:N, :] = jnp.zeros((N, width), BF16)
        back[N:, :] = jnp.where(
            lax.broadcasted_iota(jnp.int32, (EXTRA, width), 0) == 0, 1.0, 0.0
        ).astype(BF16)

    for r in range(1, count):

        @pl.when(index == r)
        def _():
            front[...] = got[r - 1][:N, :]

        @pl.when(index == count - 1 - r)
        def _():
            back[...] = got[r - 1][...]

    d_in = back[N : N + 1, :].astype(F32) + back[N + 1 : N + 2, :].astype(F32)
    through = dec_ref[0:1, :] * front[...].astype(F32) + f_ref[...].astype(F32)
    entering = (d_in * through + back[:N, :].astype(F32)).astype(BF16)
    flow[:stretch, :] = jnp.dot(c_ref[:stretch, :], front[...], preferred_element_type=F32)
    flow[stretch:, :] = jnp.dot(c_ref[stretch:, :], entering, preferred_element_type=F32)
    gain_acc[...] = jnp.zeros_like(gain_acc)
    skip_acc[...] = jnp.zeros_like(skip_acc)

    @pl.loop(0, rows // step, unroll=2)
    def _(k):
        sl = pl.ds(pl.multiple_of(k * step, step), step)
        totals = [jnp.zeros((step, tile), F32)] * 3
        for j in range(0, width, tile):
            cols = slice(j, j + tile)
            gated = pre_ref[sl, cols] + reach_ref[sl, cols] * flow[sl, cols]
            gated_ref[sl, cols] = gated
            scaled = gated * gain_ref[:, cols]
            totals[0] += gated * gated
            totals[1] += scaled * scaled
            totals[2] += scaled * teacher_ref[sl, cols].astype(F32)
        for k3 in range(3):
            sums[sl, k3 * tile : (k3 + 1) * tile] = totals[k3]

    square, weighted, crossed = (
        jnp.sum(sums[:, k3 * tile : (k3 + 1) * tile], axis=1, keepdims=True) * (1.0 / width)
        for k3 in range(3)
    )
    scale = lax.rsqrt(square + EPS)
    push_scale = 2.0 * loss_scale
    mean = push_scale * scale * (scale * weighted - crossed)
    sums[:, :tile] = jnp.broadcast_to(scale, (rows, tile))
    sums[:, tile : 2 * tile] = jnp.broadcast_to(mean, (rows, tile))

    @pl.loop(0, rows // step, unroll=2)
    def _(k):
        sl = pl.ds(pl.multiple_of(k * step, step), step)
        scale = sums[sl, :tile]
        mean = sums[sl, tile : 2 * tile]
        for j in range(0, width, tile):
            cols = slice(j, j + tile)
            gain = gain_ref[:, cols]
            unit = gated_ref[sl, cols] * scale
            normed = unit * gain
            out_ref[sl, cols] = normed.astype(BF16)
            push = (normed - teacher_ref[sl, cols].astype(F32)) * push_scale
            by_gain = push * unit
            by_skip = (push * gain - unit * mean) * (scale * sx_ref[sl, cols])
            gain_acc[:, cols] += by_gain[:8] + by_gain[8:]
            skip_acc[:, cols] += by_skip[:8] + by_skip[8:]

    row = lax.broadcasted_iota(jnp.int32, (tile, width), 0)
    lane = lax.broadcasted_iota(jnp.int32, (tile, width), 1)
    matrix = jnp.where(row == lane // P_SIZE + g * (width // P_SIZE), 1.0, 0.0).astype(BF16)
    hi, lo = parts(skip_acc[...])
    by_head = jnp.sum(dot_nt(hi, matrix) + dot_nt(lo, matrix), axis=0, keepdims=True)
    grad_ref[...] = jnp.zeros_like(grad_ref)
    if g:
        grad_ref[:g, :] = before[:g, :]
        by_head += before[groups : groups + 1, :tile]
    grad_ref[g : g + 1, :] = jnp.sum(gain_acc[...], axis=0, keepdims=True)
    grad_ref[groups : groups + 1, :tile] = by_head


def closing_kernel(a_ref, b_ref, gain_ref, skip_ref):
    total = a_ref[...] + b_ref[...]
    groups, width = total.shape[0] - 1, total.shape[1]
    for g in range(groups):
        gain_ref[:, g * width : (g + 1) * width] = total[g : g + 1, :]
    skip_ref[...] = total[groups : groups + 1, : skip_ref.shape[1]]


def exchange(part, axis, step):
    size = lax.axis_size(axis)
    return lax.ppermute(part, axis, [(d, d ^ step) for d in range(size)])


def body(
    queries,
    keys,
    values,
    doc_ids,
    inputs,
    gate_input,
    b_input,
    c_input,
    dt_raw,
    dt_bias,
    decay_log,
    skip,
    gain,
):
    count = lax.axis_size("ctx")
    rows, features = queries.shape[1:]
    stretch = rows // 2
    kv_dev = keys.shape[2] // DH
    per_kv = queries.shape[2] // keys.shape[2]
    groups = b_input.shape[2] // N
    heads = features // P_SIZE
    width = features // groups
    length = doc_ids.shape[1]
    others = count - 1
    loss_scale = 1.0 / (lax.axis_size("dp") * count * rows)
    x, gate, bmat, cmat = inputs[0], gate_input[0], b_input[0], c_input[0]
    struct = jax.ShapeDtypeStruct

    def whole(*shape):
        return pl.BlockSpec(shape, lambda k: (0, 0))

    def chosen(size, g):
        return pl.BlockSpec((rows, size), lambda k: (0, g))

    state = struct((N, width), BF16)
    payload = struct((N + EXTRA, width), BF16)
    outs = pl.pallas_call(
        functools.partial(opening_kernel, count, groups),
        out_shape=(
            struct((rows, 2 * kv_dev * DH), BF16),
            struct((heads, rows), F32),
            *([struct((rows, width), BF16)] * groups),
            *([struct((8, width), F32)] * groups),
            *([state] * (2 * groups)),
            *([payload] * groups),
        ),
        in_specs=[VMEM] * 8,
        out_specs=(VMEM,) * (2 + 5 * groups),
        compiler_params=params(32),
        cost_estimate=cost(4 * rows * features * N, 8 * rows * features),
        name="opening",
    )(
        *(
            pltpu.with_memory_space_constraint(array, pltpu.HBM)
            for array in (
                doc_ids,
                keys[0],
                values[0],
                x,
                bmat,
                dt_raw[0].T,
                dt_bias.reshape(1, heads),
                decay_log.reshape(1, heads),
            )
        )
    )
    kv, ec = outs[:2]
    xw, dec, f_parts, b_parts, send = (
        outs[2 + k * groups : 2 + (k + 1) * groups] for k in range(5)
    )

    send = list(send)
    got = [[] for _ in range(groups)]
    ring = ring_order(count)
    ring_pairs = [(ring[d], ring[(d + 1) % count]) for d in range(count)]
    moving = kv
    kv_got = []
    for r in range(1, count):
        for g in range(groups):
            if r > 1:
                send[g] = pl.pallas_call(
                    functools.partial(chain_kernel, count, r - 1),
                    out_shape=payload,
                    in_specs=[VMEM] * 4,
                    out_specs=VMEM,
                    cost_estimate=cost(8 * N * width, 8 * N * width),
                    name="chain",
                )(got[g][-1], f_parts[g], b_parts[g], dec[g])
            pairs = [(r - 1, r), (count - r, count - r - 1)]
            got[g].append(lax.ppermute(send[g], "ctx", pairs))
        moving = lax.ppermute(moving, "ctx", ring_pairs)
        kv_got.append(moving)

    local = []
    for g in range(groups):
        local.append(
            pl.pallas_call(
                functools.partial(local_kernel, count, g * (heads // groups)),
                out_shape=(struct((rows, width), F32),) * 3,
                grid=(1,),
                in_specs=[
                    whole(1, length),
                    chosen(width, g),
                    chosen(width, g),
                    chosen(N, g),
                    chosen(N, g),
                    whole(heads, rows),
                    whole(1, heads),
                    whole(rows, width),
                ],
                out_specs=(whole(rows, width),) * 3,
                compiler_params=params(24),
                cost_estimate=cost(2 * rows * width * N, 16 * rows * width),
                name="local",
            )(doc_ids, x, gate, bmat, cmat, ec, skip.reshape(1, heads), xw[g])
        )

    stack = 4 if per_kv % 4 == 0 and count <= 4 else 1
    teacher = None
    targets = []
    for g in range(kv_dev):
        more = [] if teacher is None else [teacher]
        teacher, target = pl.pallas_call(
            functools.partial(attention_kernel, count, per_kv, stack, g),
            out_shape=(struct((rows, features), BF16), struct((rows, per_kv * DH), BF16)),
            grid=(1,),
            in_specs=[
                whole(1, length),
                chosen(per_kv * DH, g),
                chosen(DH, g),
                chosen(DH, g),
                *[whole(rows, 2 * kv_dev * DH)] * others,
                *[pl.BlockSpec(memory_space=pl.ANY)] * len(more),
            ],
            out_specs=(chosen(per_kv * DH, g), whole(rows, per_kv * DH)),
            scratch_shapes=[
                pltpu.VMEM(((count + 1) * stretch, DH), BF16),
                pltpu.VMEM(((count + 1) * stretch, 2 * DH), BF16),
                pltpu.VMEM((others * stretch, DH), BF16),
                pltpu.VMEM((others * stretch, 2 * DH), BF16),
                pltpu.VMEM((stretch, (count + 1) * stretch), F32),
                pltpu.VMEM((stretch, stretch), F32),
                pltpu.VMEM((stretch, others * stretch), F32),
                pltpu.VMEM((2 * stack * stretch, stretch), F32),
            ],
            input_output_aliases={4 + others: 0} if more else {},
            compiler_params=params(40),
            cost_estimate=cost(
                4 * (2 * count + 1) * stretch * stretch * per_kv * DH, 8 * rows * per_kv * DH
            ),
            name="attention",
        )(doc_ids, queries[0], keys[0], values[0], *kv_got, *more)
        targets.append(target)

    student = grads = None
    for g in range(groups):
        more = [] if student is None else [grads, student]
        student, grads = pl.pallas_call(
            functools.partial(final_kernel, count, g, groups, loss_scale),
            out_shape=(struct((rows, features), BF16), struct((groups + 1, width), F32)),
            grid=(1,),
            in_specs=[
                *[whole(rows, width)] * 3,
                chosen(N, g),
                whole(rows, width),
                pl.BlockSpec((1, width), lambda k, g=g: (0, g)),
                whole(N, width),
                whole(8, width),
                *[whole(N + EXTRA, width)] * others,
                *([whole(groups + 1, width), pl.BlockSpec(memory_space=pl.ANY)] if more else []),
            ],
            out_specs=(chosen(width, g), whole(groups + 1, width)),
            scratch_shapes=[
                pltpu.VMEM((N, width), BF16),
                pltpu.VMEM((N + EXTRA, width), BF16),
                pltpu.VMEM((rows, width), F32),
                pltpu.VMEM((rows, width), F32),
                pltpu.VMEM((rows, 3 * 128), F32),
                pltpu.VMEM((8, width), F32),
                pltpu.VMEM((8, width), F32),
            ],
            input_output_aliases={9 + others: 0} if more else {},
            compiler_params=params(32),
            cost_estimate=cost(2 * rows * width * N, 20 * rows * width),
            name="final",
        )(
            *local[g],
            cmat,
            targets[g],
            gain.reshape(1, features),
            f_parts[g],
            dec[g],
            *got[g],
            *more,
        )
    steps = []
    for axis in ("ctx", "dp"):
        step = 1
        while step < lax.axis_size(axis):
            steps.append((axis, step))
            step *= 2
    for axis, step in steps[:-1]:
        grads = grads + exchange(grads, axis, step)
    grad_gain, grad_skip = pl.pallas_call(
        closing_kernel,
        out_shape=(struct((1, features), F32), struct((1, heads), F32)),
        in_specs=[VMEM] * 2,
        out_specs=(VMEM,) * 2,
        name="closing",
    )(grads, exchange(grads, *steps[-1]))
    return (teacher[None], student[None], grad_gain[0], grad_skip[0])


def solution(mesh):
    rows = P("dp", "ctx", "head")
    in_specs = (
        rows,
        rows,
        rows,
        P("dp", None),
        rows,
        rows,
        rows,
        rows,
        rows,
        P("head"),
        P("head"),
        P("head"),
        P("head"),
    )
    out_specs = (rows, rows, P("head"), P("head"))
    return jax.shard_map(body, mesh=mesh, in_specs=in_specs, out_specs=out_specs, check_vma=False)
```

```python
import functools
import math

import jax
import jax.numpy as jnp
from jax import lax
from jax.experimental import pallas as pl
from jax.experimental.pallas import tpu as pltpu
from jax.sharding import PartitionSpec as P

DH = 128
P_SIZE = 64
N = 128
EXTRA = 16
EPS = 1e-05
MASKED = -1e30
F32 = jnp.float32
BF16 = jnp.bfloat16
VMEM = pl.BlockSpec(memory_space=pltpu.VMEM)


def params(mib):
    return pltpu.CompilerParams(vmem_limit_bytes=mib << 20)


def cost(flops, size):
    return pl.CostEstimate(flops=flops, bytes_accessed=size, transcendentals=0)


def parts(v):
    hi = v.astype(BF16)
    return hi, (v - hi.astype(F32)).astype(BF16)


def spread_matrix(heads, width, first):
    row = lax.broadcasted_iota(jnp.int32, (heads, width), 0)
    lane = lax.broadcasted_iota(jnp.int32, (heads, width), 1)
    return jnp.where(row == (lane // P_SIZE) + first, 1.0, 0.0).astype(BF16)


def dot_nt(a, b):
    return lax.dot_general(a, b, (((1,), (1,)), ((), ())), preferred_element_type=F32)


def dot_tn(a, b):
    return lax.dot_general(a, b, (((0,), (0,)), ((), ())), preferred_element_type=F32)


def spread(v, matrix):
    hi, lo = parts(v)
    return dot_tn(hi, matrix) + dot_tn(lo, matrix)


def doc_row(docs_ref, block, stretch):
    return docs_ref[:, pl.ds(pl.multiple_of(block * stretch, stretch), stretch)]


def as_column(row):
    size = row.shape[1]
    r = lax.broadcasted_iota(jnp.int32, (size, size), 0)
    c = lax.broadcasted_iota(jnp.int32, (size, size), 1)
    return jnp.sum(jnp.where(r == c, row.astype(F32), 0.0), axis=1, keepdims=True)


def lower_triangle(size):
    r = lax.broadcasted_iota(jnp.int32, (size, size), 0)
    c = lax.broadcasted_iota(jnp.int32, (size, size), 1)
    return r >= c


def prior_doc(docs_ref, block, stretch):
    before = doc_row(docs_ref, jnp.maximum(block - 1, 0), stretch)[:, stretch - 1 :]
    return jnp.where(block > 0, before, -1)


def own_block(index, count, half):
    return index if half == 0 else 2 * count - 1 - index


def ring_order(count):
    return [0] + list(range(1, count, 2)) + list(range(2, count, 2))[::-1]


def ring_source(index, count, steps):
    order = ring_order(count)
    source = jnp.int32(0)
    for place, member in enumerate(order):
        source = jnp.where(index == member, order[(place - steps) % count], source)
    return source


def put_state(ref, state):
    ref[:N, :] = state.astype(BF16)
    ref[N:, :] = jnp.zeros((EXTRA, ref.shape[1]), BF16)


def put_composite(ref, state, decay):
    hi, lo = parts(decay)
    ref[:N, :] = state.astype(BF16)
    ref[N:, :] = jnp.concatenate(
        [hi, lo, jnp.zeros((EXTRA - 2, ref.shape[1]), BF16)], axis=0
    )


def opening_kernel(
    count,
    groups,
    docs_ref,
    k_ref,
    v_ref,
    x_ref,
    b_ref,
    dt_ref,
    bias_ref,
    log_ref,
    kv_ref,
    ec_ref,
    *outs,
):
    xw_refs, dec_refs, f_refs, b_refs, send_refs = (
        outs[k * groups : (k + 1) * groups] for k in range(5)
    )
    heads, rows = dt_ref.shape
    stretch = rows // 2
    width = x_ref.shape[1] // groups
    kv_width = k_ref.shape[1]
    index = lax.axis_index("ctx")
    kv_ref[:, :kv_width] = k_ref[...]
    kv_ref[:, kv_width:] = v_ref[...]
    triangle = jnp.where(lower_triangle(stretch), 1.0, 0.0)
    slope = jnp.exp(as_column(log_ref[...]))
    bias = as_column(bias_ref[...])
    lane = lax.broadcasted_iota(jnp.int32, (heads, 8), 1)
    ends = jnp.zeros((heads, 8), F32)
    loads = []
    projs = []
    for half in range(2):
        block = own_block(index, count, half)
        sl = slice(half * stretch, (half + 1) * stretch)
        raw = dt_ref[:, sl] + bias
        dt = jnp.maximum(raw, 0.0) + jnp.log1p(jnp.exp(-jnp.abs(raw)))
        cum = lax.dot_general(
            -dt * slope,
            triangle,
            (((1,), (1,)), ((), ())),
            precision=lax.Precision.HIGHEST,
            preferred_element_type=F32,
        )
        ec_ref[:, sl] = jnp.exp(cum)
        loads.append(jnp.exp(-cum) * dt)
        final = jnp.exp(cum[:, stretch - 1 :])
        row = doc_row(docs_ref, block, stretch)
        last = row[:, stretch - 1 :]
        kept = jnp.where(last == prior_doc(docs_ref, block, stretch), 1.0, 0.0)
        ends = jnp.where(lane == half, final * kept, ends)
        ends = jnp.where(lane == 2 + half, final, ends)
        same = jnp.where(as_column(row) == last.astype(F32), 1.0, 0.0)
        projs.append((b_ref[sl, :].astype(F32) * same).astype(BF16))
    for g in range(groups):
        cols = slice(g * width, (g + 1) * width)
        matrix = spread_matrix(heads, width, g * (heads // groups))
        wide = spread(ends, matrix)
        dec_refs[g][...] = wide
        sums = []
        for half in range(2):
            sl = slice(half * stretch, (half + 1) * stretch)
            xw = (x_ref[sl, cols].astype(F32) * spread(loads[half], matrix)).astype(BF16)
            xw_refs[g][sl, :] = xw
            sums.append(dot_tn(projs[half][:, g * N : (g + 1) * N], xw) * wide[2 + half : 3 + half])
        f_refs[g][...] = sums[0].astype(BF16)
        b_refs[g][...] = sums[1].astype(BF16)

        @pl.when(index == 0)
        def _():
            put_state(send_refs[g], sums[0])

        @pl.when(index != 0)
        def _():
            put_composite(send_refs[g], wide[1:2] * sums[0] + sums[1], wide[0:1] * wide[1:2])


def chain_kernel(count, stage, got_ref, f_ref, b_ref, dec_ref, send_ref):
    index = lax.axis_index("ctx")

    @pl.when(index == stage)
    def _():
        state = dec_ref[0:1, :] * got_ref[:N, :].astype(F32) + f_ref[...].astype(F32)
        put_state(send_ref, state)

    @pl.when(index == count - 1 - stage)
    def _():
        decay = got_ref[N : N + 1, :].astype(F32) + got_ref[N + 1 : N + 2, :].astype(F32)
        inner = decay * f_ref[...].astype(F32) + got_ref[:N, :].astype(F32)
        state = dec_ref[1:2, :] * inner + b_ref[...].astype(F32)
        put_composite(send_ref, state, dec_ref[1:2, :] * decay * dec_ref[0:1, :])


def local_kernel(
    count,
    first,
    docs_ref,
    x_ref,
    gate_ref,
    b_ref,
    c_ref,
    ec_ref,
    skip_ref,
    xw_ref,
    pre_ref,
    reach_ref,
    sx_ref,
):
    heads, rows = ec_ref.shape
    stretch = rows // 2
    width = x_ref.shape[1]
    index = lax.axis_index("ctx")
    matrix = spread_matrix(heads, width, first)
    wide_skip = spread(as_column(skip_ref[...]), matrix)
    triangle = lower_triangle(stretch)
    step = 16
    for half in range(2):
        block = own_block(index, count, half)
        sl = slice(half * stretch, (half + 1) * stretch)
        row = doc_row(docs_ref, block, stretch)
        column = as_column(row)
        gram = dot_nt(c_ref[sl, :], b_ref[sl, :])
        gram = jnp.where(triangle & (column == row.astype(F32)), gram, 0.0).astype(BF16)
        wide = spread(ec_ref[:, sl], matrix)
        inner = jnp.dot(gram, xw_ref[sl, :], preferred_element_type=F32)
        reached = jnp.where(column == prior_doc(docs_ref, block, stretch).astype(F32), 1.0, 0.0)
        for k in range(0, stretch, step):
            at = slice(half * stretch + k, half * stretch + k + step)
            here = slice(k, k + step)
            x = x_ref[at, :].astype(F32)
            gate = gate_ref[at, :].astype(F32)
            silu = gate / (1.0 + jnp.exp(-gate))
            fade = wide[here] * silu
            sx = silu * x
            sx_ref[at, :] = sx
            pre_ref[at, :] = inner[here] * fade + wide_skip * sx
            reach_ref[at, :] = reached[here] * fade


def attention_kernel(count, per, stack, g, docs_ref, q_ref, k_ref, v_ref, *refs):
    others = count - 1
    got = refs[:others]
    out_ref, copy_ref = refs[-11:-9]
    kb, vb, ka, va, bias_b, bias_f, bias_a, bests, accs = refs[-9:]
    rows = q_ref.shape[0]
    stretch = rows // 2
    index = lax.axis_index("ctx")
    last = 2 * count - 1
    kv_width = got[0].shape[1] // 2
    k_cols = slice(g * DH, (g + 1) * DH)
    v_cols = slice(kv_width + g * DH, kv_width + (g + 1) * DH)
    row_f = doc_row(docs_ref, index, stretch).astype(F32)
    row_b = doc_row(docs_ref, last - index, stretch).astype(F32)
    col_f = as_column(row_f)
    col_b = as_column(row_b)
    triangle = lower_triangle(stretch)
    bias_f[...] = jnp.where(triangle & (col_f == row_f), 0.0, MASKED)
    bias_b[:, :stretch] = jnp.where(col_b == row_f, 0.0, MASKED)
    bias_b[:, stretch:rows] = jnp.where(triangle & (col_b == row_b), 0.0, MASKED)
    vb[:, DH:] = jnp.ones((vb.shape[0], DH), BF16)
    va[:, DH:] = jnp.ones((va.shape[0], DH), BF16)
    kb[:rows, :] = k_ref[...]
    vb[:rows, :DH] = v_ref[...]
    lower, at_a, picks = [], [], []
    for r in range(others):
        at_b = slice(rows + r * stretch, rows + (r + 1) * stretch)
        at_a.append(slice(r * stretch, (r + 1) * stretch))
        source = ring_source(index, count, r + 1)
        lower.append(source < index)
        picks.append(jnp.where(lower[r], 0, 1))
        own = pl.ds(pl.multiple_of(picks[r] * stretch, stretch), stretch)
        kb[at_b, :] = got[r][:stretch, k_cols]
        vb[at_b, :DH] = got[r][:stretch, v_cols]
        ka[at_a[r], :] = got[r][own, k_cols]
        va[at_a[r], :DH] = got[r][own, v_cols]
        key_f = doc_row(docs_ref, source, stretch).astype(F32)
        key_a = doc_row(docs_ref, jnp.where(lower[r], source, last - source), stretch).astype(F32)
        bias_b[:, at_b] = jnp.where(col_b == key_f, 0.0, MASKED)
        bias_a[:, at_a[r]] = jnp.where(
            jnp.where(lower[r], col_f, col_b) == key_a, 0.0, MASKED
        )

    factor = math.log2(math.e) / math.sqrt(DH)
    tall = stack * stretch

    def stacked(first, base):
        return jnp.concatenate(
            [q_ref[pl.ds(base, stretch), (first + j) * DH : (first + j + 1) * DH] for j in range(stack)],
            axis=0,
        )

    def biased(score, bias):
        size = score.shape[1]
        return (score.reshape(stack, stretch, size) + bias[None]).reshape(tall, size)

    for first in range(0, per, stack):
        best = bests.at[first // stack % 2]
        acc = accs.at[first // stack % 2]
        s_f = biased(dot_nt(stacked(first, 0), kb[:stretch, :]), bias_f[...])
        s_b = biased(dot_nt(stacked(first, stretch), kb[...]), bias_b[...])
        best[:tall, :] = s_f
        top = s_b[:, :stretch]
        for k in range(1, count + 1):
            top = jnp.maximum(top, s_b[:, k * stretch : (k + 1) * stretch])
        best[tall:, :] = top
        s_a = []
        places = []
        for r in range(others):
            base = pl.multiple_of(picks[r] * stretch, stretch)
            place = pl.ds(pl.multiple_of(picks[r] * tall, tall), tall)
            s_a.append(biased(dot_nt(stacked(first, base), ka[at_a[r], :]), bias_a[:, at_a[r]]))
            best[place, :] = jnp.maximum(best[place, :], s_a[r])
            places.append(place)
        top_f = jnp.max(best[:tall, :], axis=1, keepdims=True)
        top_b = jnp.max(best[tall:, :], axis=1, keepdims=True)
        w_f = jnp.exp2((s_f - top_f) * factor).astype(BF16)
        w_b = jnp.exp2((s_b - top_b) * factor).astype(BF16)
        out_f = jnp.dot(w_f, vb[:stretch, :], preferred_element_type=F32)
        out_b = jnp.dot(w_b, vb[...], preferred_element_type=F32)
        acc[:tall, :] = out_f
        acc[tall:, :] = out_b
        for r in range(others):
            top = jnp.where(lower[r], top_f, top_b)
            w = jnp.exp2((s_a[r] - top) * factor).astype(BF16)
            acc[places[r], :] += jnp.dot(w, va[at_a[r], :], preferred_element_type=F32)
        for half in range(2):
            out = acc[half * tall : (half + 1) * tall, :]
            result = (out[:, :DH] / out[:, DH:]).astype(BF16)
            sl = slice(half * stretch, (half + 1) * stretch)
            for j in range(stack):
                cols = slice((first + j) * DH, (first + j + 1) * DH)
                out_ref[sl, cols] = result[j * stretch : (j + 1) * stretch]
                copy_ref[sl, cols] = result[j * stretch : (j + 1) * stretch]


def final_kernel(
    count,
    g,
    groups,
    loss_scale,
    pre_ref,
    reach_ref,
    sx_ref,
    c_ref,
    teacher_ref,
    gain_ref,
    f_ref,
    dec_ref,
    *refs,
):
    others = count - 1
    got = refs[:others]
    before = refs[others] if g else None
    out_ref, grad_ref, front, back, flow, gated_ref, sums, gain_acc, skip_acc = refs[-9:]
    rows, width = pre_ref.shape
    stretch = rows // 2
    index = lax.axis_index("ctx")
    tile = 128
    step = 16

    @pl.when(index == 0)
    def _():
        front[...] = jnp.zeros_like(front)

    @pl.when(index == count - 1)
    def _():
        back[:N, :] = jnp.zeros((N, width), BF16)
        back[N:, :] = jnp.where(
            lax.broadcasted_iota(jnp.int32, (EXTRA, width), 0) == 0, 1.0, 0.0
        ).astype(BF16)

    for r in range(1, count):

        @pl.when(index == r)
        def _():
            front[...] = got[r - 1][:N, :]

        @pl.when(index == count - 1 - r)
        def _():
            back[...] = got[r - 1][...]

    d_in = back[N : N + 1, :].astype(F32) + back[N + 1 : N + 2, :].astype(F32)
    through = dec_ref[0:1, :] * front[...].astype(F32) + f_ref[...].astype(F32)
    entering = (d_in * through + back[:N, :].astype(F32)).astype(BF16)
    flow[:stretch, :] = jnp.dot(c_ref[:stretch, :], front[...], preferred_element_type=F32)
    flow[stretch:, :] = jnp.dot(c_ref[stretch:, :], entering, preferred_element_type=F32)
    gain_acc[...] = jnp.zeros_like(gain_acc)
    skip_acc[...] = jnp.zeros_like(skip_acc)

    @pl.loop(0, rows // step, unroll=2)
    def _(k):
        sl = pl.ds(pl.multiple_of(k * step, step), step)
        totals = [jnp.zeros((step, tile), F32)] * 3
        for j in range(0, width, tile):
            cols = slice(j, j + tile)
            gated = pre_ref[sl, cols] + reach_ref[sl, cols] * flow[sl, cols]
            gated_ref[sl, cols] = gated
            scaled = gated * gain_ref[:, cols]
            totals[0] += gated * gated
            totals[1] += scaled * scaled
            totals[2] += scaled * teacher_ref[sl, cols].astype(F32)
        for k3 in range(3):
            sums[sl, k3 * tile : (k3 + 1) * tile] = totals[k3]

    square, weighted, crossed = (
        jnp.sum(sums[:, k3 * tile : (k3 + 1) * tile], axis=1, keepdims=True) * (1.0 / width)
        for k3 in range(3)
    )
    scale = lax.rsqrt(square + EPS)
    push_scale = 2.0 * loss_scale
    mean = push_scale * scale * (scale * weighted - crossed)
    sums[:, :tile] = jnp.broadcast_to(scale, (rows, tile))
    sums[:, tile : 2 * tile] = jnp.broadcast_to(mean, (rows, tile))

    @pl.loop(0, rows // step, unroll=2)
    def _(k):
        sl = pl.ds(pl.multiple_of(k * step, step), step)
        scale = sums[sl, :tile]
        mean = sums[sl, tile : 2 * tile]
        for j in range(0, width, tile):
            cols = slice(j, j + tile)
            gain = gain_ref[:, cols]
            unit = gated_ref[sl, cols] * scale
            normed = unit * gain
            out_ref[sl, cols] = normed.astype(BF16)
            push = (normed - teacher_ref[sl, cols].astype(F32)) * push_scale
            by_gain = push * unit
            by_skip = (push * gain - unit * mean) * (scale * sx_ref[sl, cols])
            gain_acc[:, cols] += by_gain[:8] + by_gain[8:]
            skip_acc[:, cols] += by_skip[:8] + by_skip[8:]

    row = lax.broadcasted_iota(jnp.int32, (tile, width), 0)
    lane = lax.broadcasted_iota(jnp.int32, (tile, width), 1)
    matrix = jnp.where(row == lane // P_SIZE + g * (width // P_SIZE), 1.0, 0.0).astype(BF16)
    hi, lo = parts(skip_acc[...])
    by_head = jnp.sum(dot_nt(hi, matrix) + dot_nt(lo, matrix), axis=0, keepdims=True)
    grad_ref[...] = jnp.zeros_like(grad_ref)
    if g:
        grad_ref[:g, :] = before[:g, :]
        by_head += before[groups : groups + 1, :tile]
    grad_ref[g : g + 1, :] = jnp.sum(gain_acc[...], axis=0, keepdims=True)
    grad_ref[groups : groups + 1, :tile] = by_head


def closing_kernel(a_ref, b_ref, gain_ref, skip_ref):
    total = a_ref[...] + b_ref[...]
    groups, width = total.shape[0] - 1, total.shape[1]
    for g in range(groups):
        gain_ref[:, g * width : (g + 1) * width] = total[g : g + 1, :]
    skip_ref[...] = total[groups : groups + 1, : skip_ref.shape[1]]


def exchange(part, shift):
    axes = ("dp", "ctx")
    size = lax.axis_size(axes)
    return lax.ppermute(part, axes, [(d, d ^ shift) for d in range(size)])


def body(
    queries,
    keys,
    values,
    doc_ids,
    inputs,
    gate_input,
    b_input,
    c_input,
    dt_raw,
    dt_bias,
    decay_log,
    skip,
    gain,
):
    count = lax.axis_size("ctx")
    rows, features = queries.shape[1:]
    stretch = rows // 2
    kv_dev = keys.shape[2] // DH
    per_kv = queries.shape[2] // keys.shape[2]
    groups = b_input.shape[2] // N
    heads = features // P_SIZE
    width = features // groups
    length = doc_ids.shape[1]
    others = count - 1
    loss_scale = 1.0 / (lax.axis_size("dp") * count * rows)
    x, gate, bmat, cmat = inputs[0], gate_input[0], b_input[0], c_input[0]
    struct = jax.ShapeDtypeStruct

    def whole(*shape):
        return pl.BlockSpec(shape, lambda k: (0, 0))

    def chosen(size, g):
        return pl.BlockSpec((rows, size), lambda k: (0, g))

    state = struct((N, width), BF16)
    payload = struct((N + EXTRA, width), BF16)
    outs = pl.pallas_call(
        functools.partial(opening_kernel, count, groups),
        out_shape=(
            struct((rows, 2 * kv_dev * DH), BF16),
            struct((heads, rows), F32),
            *([struct((rows, width), BF16)] * groups),
            *([struct((8, width), F32)] * groups),
            *([state] * (2 * groups)),
            *([payload] * groups),
        ),
        in_specs=[VMEM] * 8,
        out_specs=(VMEM,) * (2 + 5 * groups),
        compiler_params=params(16),
        cost_estimate=cost(4 * rows * features * N, 8 * rows * features),
        name="opening",
    )(
        *(
            pltpu.with_memory_space_constraint(array, pltpu.HBM)
            for array in (
                doc_ids,
                keys[0],
                values[0],
                x,
                bmat,
                dt_raw[0].T,
                dt_bias.reshape(1, heads),
                decay_log.reshape(1, heads),
            )
        )
    )
    kv, ec = outs[:2]
    xw, dec, f_parts, b_parts, send = (
        outs[2 + k * groups : 2 + (k + 1) * groups] for k in range(5)
    )

    local = []
    for g in range(groups):
        local.append(
            pl.pallas_call(
                functools.partial(local_kernel, count, g * (heads // groups)),
                out_shape=(struct((rows, width), F32),) * 3,
                grid=(1,),
                in_specs=[
                    whole(1, length),
                    chosen(width, g),
                    chosen(width, g),
                    chosen(N, g),
                    chosen(N, g),
                    whole(heads, rows),
                    whole(1, heads),
                    whole(rows, width),
                ],
                out_specs=(whole(rows, width),) * 3,
                compiler_params=params(16),
                cost_estimate=cost(2 * rows * width * N, 16 * rows * width),
                name="local",
            )(doc_ids, x, gate, bmat, cmat, ec, skip.reshape(1, heads), xw[g])
        )

    send = list(send)
    got = [[] for _ in range(groups)]
    ring = ring_order(count)
    ring_pairs = [(ring[d], ring[(d + 1) % count]) for d in range(count)]
    moving = kv
    kv_got = []
    for r in range(1, count):
        for g in range(groups):
            if r == 2:
                got[g][0], *local[g] = lax.optimization_barrier((got[g][0], *local[g]))
            if r > 1:
                send[g] = pl.pallas_call(
                    functools.partial(chain_kernel, count, r - 1),
                    out_shape=payload,
                    in_specs=[VMEM] * 4,
                    out_specs=VMEM,
                    compiler_params=params(4),
                    cost_estimate=cost(8 * N * width, 8 * N * width),
                    name="chain",
                )(got[g][-1], f_parts[g], b_parts[g], dec[g])
            pairs = [(r - 1, r), (count - r, count - r - 1)]
            got[g].append(lax.ppermute(send[g], "ctx", pairs))
        moving = lax.ppermute(moving, "ctx", ring_pairs)
        kv_got.append(moving)

    stack = 4 if per_kv % 4 == 0 and count <= 4 else 1
    teacher = None
    targets = []
    for g in range(kv_dev):
        more = [] if teacher is None else [teacher]
        teacher, target = pl.pallas_call(
            functools.partial(attention_kernel, count, per_kv, stack, g),
            out_shape=(struct((rows, features), BF16), struct((rows, per_kv * DH), BF16)),
            grid=(1,),
            in_specs=[
                whole(1, length),
                chosen(per_kv * DH, g),
                chosen(DH, g),
                chosen(DH, g),
                *[whole(rows, 2 * kv_dev * DH)] * others,
                *[pl.BlockSpec(memory_space=pl.ANY)] * len(more),
            ],
            out_specs=(chosen(per_kv * DH, g), whole(rows, per_kv * DH)),
            scratch_shapes=[
                pltpu.VMEM(((count + 1) * stretch, DH), BF16),
                pltpu.VMEM(((count + 1) * stretch, 2 * DH), BF16),
                pltpu.VMEM((others * stretch, DH), BF16),
                pltpu.VMEM((others * stretch, 2 * DH), BF16),
                pltpu.VMEM((stretch, (count + 1) * stretch), F32),
                pltpu.VMEM((stretch, stretch), F32),
                pltpu.VMEM((stretch, others * stretch), F32),
                pltpu.VMEM((2, 2 * stack * stretch, stretch), F32),
                pltpu.VMEM((2, 2 * stack * stretch, 2 * DH), F32),
            ],
            input_output_aliases={4 + others: 0} if more else {},
            compiler_params=params(24),
            cost_estimate=cost(
                4 * (2 * count + 1) * stretch * stretch * per_kv * DH, 8 * rows * per_kv * DH
            ),
            name="attention",
        )(doc_ids, queries[0], keys[0], values[0], *kv_got, *more)
        targets.append(target)

    student = grads = None
    for g in range(groups):
        more = [] if student is None else [grads, student]
        student, grads = pl.pallas_call(
            functools.partial(final_kernel, count, g, groups, loss_scale),
            out_shape=(struct((rows, features), BF16), struct((groups + 1, width), F32)),
            grid=(1,),
            in_specs=[
                *[whole(rows, width)] * 3,
                chosen(N, g),
                whole(rows, width),
                pl.BlockSpec((1, width), lambda k, g=g: (0, g)),
                whole(N, width),
                whole(8, width),
                *[whole(N + EXTRA, width)] * others,
                *([whole(groups + 1, width), pl.BlockSpec(memory_space=pl.ANY)] if more else []),
            ],
            out_specs=(chosen(width, g), whole(groups + 1, width)),
            scratch_shapes=[
                pltpu.VMEM((N, width), BF16),
                pltpu.VMEM((N + EXTRA, width), BF16),
                pltpu.VMEM((rows, width), F32),
                pltpu.VMEM((rows, width), F32),
                pltpu.VMEM((rows, 3 * 128), F32),
                pltpu.VMEM((8, width), F32),
                pltpu.VMEM((8, width), F32),
            ],
            input_output_aliases={9 + others: 0} if more else {},
            compiler_params=params(16),
            cost_estimate=cost(2 * rows * width * N, 20 * rows * width),
            name="final",
        )(
            *local[g],
            cmat,
            targets[g],
            gain.reshape(1, features),
            f_parts[g],
            dec[g],
            *got[g],
            *more,
        )
    partner = exchange(grads, 1)
    if lax.axis_size("dp") == 2:
        grads = (grads + partner) + (exchange(grads, count) + exchange(grads, count + 1))
    else:
        grads = grads + partner
    shifts = [1 << k for k in range(1, count.bit_length() - 1)]
    for shift in shifts[:-1]:
        grads = grads + exchange(grads, shift)
    grad_gain, grad_skip = pl.pallas_call(
        closing_kernel,
        out_shape=(struct((1, features), F32), struct((1, heads), F32)),
        in_specs=[VMEM] * 2,
        out_specs=(VMEM,) * 2,
        compiler_params=params(2),
        name="closing",
    )(grads, exchange(grads, shifts[-1]))
    return (teacher[None], student[None], grad_gain[0], grad_skip[0])


def solution(mesh):
    rows = P("dp", "ctx", "head")
    in_specs = (
        rows,
        rows,
        rows,
        P("dp", None),
        rows,
        rows,
        rows,
        rows,
        rows,
        P("head"),
        P("head"),
        P("head"),
        P("head"),
    )
    out_specs = (rows, rows, P("head"), P("head"))
    return jax.shard_map(body, mesh=mesh, in_specs=in_specs, out_specs=out_specs, check_vma=False)
```

```python
import functools
import math

import jax
import jax.numpy as jnp
from jax import lax
from jax.experimental import pallas as pl
from jax.experimental.pallas import tpu as pltpu
from jax.sharding import PartitionSpec as P

DH = 128
P_SIZE = 64
N = 128
EXTRA = 16
EPS = 1e-05
MASKED = -1e30
F32 = jnp.float32
BF16 = jnp.bfloat16
VMEM = pl.BlockSpec(memory_space=pltpu.VMEM)


def params(mib):
    return pltpu.CompilerParams(vmem_limit_bytes=mib << 20)


def cost(flops, size):
    return pl.CostEstimate(flops=flops, bytes_accessed=size, transcendentals=0)


def parts(v):
    hi = v.astype(BF16)
    return hi, (v - hi.astype(F32)).astype(BF16)


def spread_matrix(heads, width, first):
    row = lax.broadcasted_iota(jnp.int32, (heads, width), 0)
    lane = lax.broadcasted_iota(jnp.int32, (heads, width), 1)
    return jnp.where(row == (lane // P_SIZE) + first, 1.0, 0.0).astype(BF16)


def dot_nt(a, b):
    return lax.dot_general(a, b, (((1,), (1,)), ((), ())), preferred_element_type=F32)


def dot_tn(a, b):
    return lax.dot_general(a, b, (((0,), (0,)), ((), ())), preferred_element_type=F32)


def spread(v, matrix):
    hi, lo = parts(v)
    return dot_tn(hi, matrix) + dot_tn(lo, matrix)


def doc_row(docs_ref, block, stretch):
    return docs_ref[:, pl.ds(pl.multiple_of(block * stretch, stretch), stretch)]


def as_column(row):
    size = row.shape[1]
    r = lax.broadcasted_iota(jnp.int32, (size, size), 0)
    c = lax.broadcasted_iota(jnp.int32, (size, size), 1)
    return jnp.sum(jnp.where(r == c, row.astype(F32), 0.0), axis=1, keepdims=True)


def lower_triangle(size):
    r = lax.broadcasted_iota(jnp.int32, (size, size), 0)
    c = lax.broadcasted_iota(jnp.int32, (size, size), 1)
    return r >= c


def prior_doc(docs_ref, block, stretch):
    before = doc_row(docs_ref, jnp.maximum(block - 1, 0), stretch)[:, stretch - 1 :]
    return jnp.where(block > 0, before, -1)


def own_block(index, count, half):
    return index if half == 0 else 2 * count - 1 - index


def ring_order(count):
    return [0] + list(range(1, count, 2)) + list(range(2, count, 2))[::-1]


def ring_source(index, count, steps):
    order = ring_order(count)
    source = jnp.int32(0)
    for place, member in enumerate(order):
        source = jnp.where(index == member, order[(place - steps) % count], source)
    return source


def put_state(ref, state):
    ref[:N, :] = state.astype(BF16)
    ref[N:, :] = jnp.zeros((EXTRA, ref.shape[1]), BF16)


def put_composite(ref, state, decay):
    hi, lo = parts(decay)
    ref[:N, :] = state.astype(BF16)
    ref[N:, :] = jnp.concatenate(
        [hi, lo, jnp.zeros((EXTRA - 2, ref.shape[1]), BF16)], axis=0
    )


def opening_kernel(
    count,
    groups,
    docs_ref,
    k_ref,
    v_ref,
    x_ref,
    b_ref,
    dt_ref,
    bias_ref,
    log_ref,
    kv_ref,
    ec_ref,
    *outs,
):
    xw_refs, dec_refs, f_refs, b_refs, send_refs = (
        outs[k * groups : (k + 1) * groups] for k in range(5)
    )
    heads, rows = dt_ref.shape
    stretch = rows // 2
    width = x_ref.shape[1] // groups
    kv_width = k_ref.shape[1]
    index = lax.axis_index("ctx")
    kv_ref[:, :kv_width] = k_ref[...]
    kv_ref[:, kv_width:] = v_ref[...]
    triangle = jnp.where(lower_triangle(stretch), 1.0, 0.0)
    slope = jnp.exp(as_column(log_ref[...]))
    bias = as_column(bias_ref[...])
    lane = lax.broadcasted_iota(jnp.int32, (heads, 8), 1)
    ends = jnp.zeros((heads, 8), F32)
    loads = []
    projs = []
    for half in range(2):
        block = own_block(index, count, half)
        sl = slice(half * stretch, (half + 1) * stretch)
        raw = dt_ref[:, sl] + bias
        dt = jnp.maximum(raw, 0.0) + jnp.log1p(jnp.exp(-jnp.abs(raw)))
        cum = lax.dot_general(
            -dt * slope,
            triangle,
            (((1,), (1,)), ((), ())),
            precision=lax.Precision.HIGHEST,
            preferred_element_type=F32,
        )
        ec_ref[:, sl] = jnp.exp(cum)
        loads.append(jnp.exp(-cum) * dt)
        final = jnp.exp(cum[:, stretch - 1 :])
        row = doc_row(docs_ref, block, stretch)
        last = row[:, stretch - 1 :]
        kept = jnp.where(last == prior_doc(docs_ref, block, stretch), 1.0, 0.0)
        ends = jnp.where(lane == half, final * kept, ends)
        ends = jnp.where(lane == 2 + half, final, ends)
        same = jnp.where(as_column(row) == last.astype(F32), 1.0, 0.0)
        projs.append((b_ref[sl, :].astype(F32) * same).astype(BF16))
    for g in range(groups):
        cols = slice(g * width, (g + 1) * width)
        matrix = spread_matrix(heads, width, g * (heads // groups))
        wide = spread(ends, matrix)
        dec_refs[g][...] = wide
        sums = []
        for half in range(2):
            sl = slice(half * stretch, (half + 1) * stretch)
            xw = (x_ref[sl, cols].astype(F32) * spread(loads[half], matrix)).astype(BF16)
            xw_refs[g][sl, :] = xw
            sums.append(dot_tn(projs[half][:, g * N : (g + 1) * N], xw) * wide[2 + half : 3 + half])
        f_refs[g][...] = sums[0].astype(BF16)
        b_refs[g][...] = sums[1].astype(BF16)

        @pl.when(index == 0)
        def _():
            put_state(send_refs[g], sums[0])

        @pl.when(index != 0)
        def _():
            put_composite(send_refs[g], wide[1:2] * sums[0] + sums[1], wide[0:1] * wide[1:2])


def chain_kernel(count, stage, got_ref, f_ref, b_ref, dec_ref, send_ref):
    index = lax.axis_index("ctx")

    @pl.when(index == stage)
    def _():
        state = dec_ref[0:1, :] * got_ref[:N, :].astype(F32) + f_ref[...].astype(F32)
        put_state(send_ref, state)

    @pl.when(index == count - 1 - stage)
    def _():
        decay = got_ref[N : N + 1, :].astype(F32) + got_ref[N + 1 : N + 2, :].astype(F32)
        inner = decay * f_ref[...].astype(F32) + got_ref[:N, :].astype(F32)
        state = dec_ref[1:2, :] * inner + b_ref[...].astype(F32)
        put_composite(send_ref, state, dec_ref[1:2, :] * decay * dec_ref[0:1, :])


def local_kernel(
    count,
    first,
    docs_ref,
    x_ref,
    gate_ref,
    b_ref,
    c_ref,
    ec_ref,
    skip_ref,
    xw_ref,
    pre_ref,
    reach_ref,
    sx_ref,
):
    heads, rows = ec_ref.shape
    stretch = rows // 2
    width = x_ref.shape[1]
    index = lax.axis_index("ctx")
    matrix = spread_matrix(heads, width, first)
    wide_skip = spread(as_column(skip_ref[...]), matrix)
    triangle = lower_triangle(stretch)
    step = 16
    for half in range(2):
        block = own_block(index, count, half)
        sl = slice(half * stretch, (half + 1) * stretch)
        row = doc_row(docs_ref, block, stretch)
        column = as_column(row)
        gram = dot_nt(c_ref[sl, :], b_ref[sl, :])
        gram = jnp.where(triangle & (column == row.astype(F32)), gram, 0.0).astype(BF16)
        wide = spread(ec_ref[:, sl], matrix)
        inner = jnp.dot(gram, xw_ref[sl, :], preferred_element_type=F32)
        reached = jnp.where(column == prior_doc(docs_ref, block, stretch).astype(F32), 1.0, 0.0)
        for k in range(0, stretch, step):
            at = slice(half * stretch + k, half * stretch + k + step)
            here = slice(k, k + step)
            x = x_ref[at, :].astype(F32)
            gate = gate_ref[at, :].astype(F32)
            silu = gate / (1.0 + jnp.exp(-gate))
            fade = wide[here] * silu
            sx = silu * x
            sx_ref[at, :] = sx
            pre_ref[at, :] = inner[here] * fade + wide_skip * sx
            reach_ref[at, :] = reached[here] * fade


def pair_kernel(a_ref, b_ref, out_ref):
    rows = a_ref.shape[0]
    out_ref[:rows, :] = a_ref[...]
    out_ref[rows:, :] = b_ref[...]


def arrivals(index, count, rows, refs):
    if count != 4:
        return [(ring_source(index, count, r + 1), [(None, refs[r], 0)]) for r in range(count - 1)]
    near, own_of_middle, next_of_middle, far = refs
    middle = (index == 1) | (index == 2)
    low = index < 2
    return [
        (index ^ 1, [(None, near, 0)]),
        (
            jnp.where(low, 2, 1),
            [(middle, own_of_middle, 0), (jnp.logical_not(middle), far, 0)],
        ),
        (
            jnp.where(low, 3, 0),
            [(middle, next_of_middle, 0), (jnp.logical_not(middle), far, rows)],
        ),
    ]


def attention_kernel(count, per, stack, g, docs_ref, q_ref, k_ref, v_ref, *refs):
    others = count - 1
    sent = 4 if count == 4 else others
    out_ref, copy_ref, kt, vt, bias_f, bias_b, bias_a = refs[-7:]
    rows = q_ref.shape[0]
    stretch = rows // 2
    index = lax.axis_index("ctx")
    last = 2 * count - 1
    kv_width = refs[0].shape[1] // 2
    k_cols = slice(g * DH, (g + 1) * DH)
    v_cols = slice(kv_width + g * DH, kv_width + (g + 1) * DH)
    row_f = doc_row(docs_ref, index, stretch).astype(F32)
    row_b = doc_row(docs_ref, last - index, stretch).astype(F32)
    col_f = as_column(row_f)
    col_b = as_column(row_b)
    triangle = lower_triangle(stretch)

    def tile(k):
        return slice(k * stretch, (k + 1) * stretch)

    bias_f[...] = jnp.where(triangle & (col_f == row_f), 0.0, MASKED)
    bias_b[:, tile(0)] = jnp.where(col_b == row_f, 0.0, MASKED)
    bias_b[:, tile(1)] = jnp.where(triangle & (col_b == row_b), 0.0, MASKED)
    vt[:, DH:] = jnp.ones((vt.shape[0], DH), BF16)
    kt[tile(0), :] = k_ref[:stretch, :]
    vt[tile(0), :DH] = v_ref[:stretch, :]
    kt[tile(count), :] = k_ref[stretch:, :]
    vt[tile(count), :DH] = v_ref[stretch:, :]
    lower = []
    for r, (source, places) in enumerate(arrivals(index, count, rows, refs[:sent])):
        lower.append(source < index)
        for condition, ref, first in places:

            def fetch(ref=ref, first=first, r=r):
                front = slice(first, first + stretch)
                start = jnp.where(lower[r], first, first + stretch)
                own = pl.ds(pl.multiple_of(start, stretch), stretch)
                kt[tile(1 + r), :] = ref[own, k_cols]
                vt[tile(1 + r), :DH] = ref[own, v_cols]
                kt[tile(count + 1 + r), :] = ref[front, k_cols]
                vt[tile(count + 1 + r), :DH] = ref[front, v_cols]

            if condition is None:
                fetch()
            else:
                pl.when(condition)(fetch)
        key_f = doc_row(docs_ref, source, stretch).astype(F32)
        key_a = doc_row(docs_ref, jnp.where(lower[r], source, last - source), stretch).astype(F32)
        bias_b[:, tile(2 + r)] = jnp.where(col_b == key_f, 0.0, MASKED)
        bias_a[:, tile(r)] = jnp.where(jnp.where(lower[r], col_f, col_b) == key_a, 0.0, MASKED)

    factor = math.log2(math.e) / math.sqrt(DH)
    tall = stack * stretch
    half_keys = count * stretch

    def stacked(first, base):
        return jnp.concatenate(
            [
                q_ref[base : base + stretch, (first + j) * DH : (first + j + 1) * DH]
                for j in range(stack)
            ],
            axis=0,
        )

    def biased(score, bias):
        size = score.shape[1]
        return (score.reshape(stack, stretch, size) + bias[None]).reshape(tall, size)

    for first in range(0, per, stack):
        s_f = dot_nt(stacked(first, 0), kt[:half_keys, :])
        s_b = dot_nt(stacked(first, stretch), kt[...])
        t_f = biased(s_f[:, tile(0)], bias_f[...])
        t_b = [biased(s_b[:, tile(0)], bias_b[:, tile(0)])]
        for k in range(1, count + 1):
            t_b.append(biased(s_b[:, tile(count + k - 1)], bias_b[:, tile(k)]))
        t_a = []
        for r in range(others):
            score = jnp.where(lower[r], s_f[:, tile(1 + r)], s_b[:, tile(1 + r)])
            t_a.append(biased(score, bias_a[:, tile(r)]))
        best_f = t_f
        best_b = functools.reduce(jnp.maximum, t_b)
        for r in range(others):
            best_f = jnp.maximum(best_f, jnp.where(lower[r], t_a[r], MASKED))
            best_b = jnp.maximum(best_b, jnp.where(lower[r], MASKED, t_a[r]))
        top_f = jnp.max(best_f, axis=1, keepdims=True)
        top_b = jnp.max(best_b, axis=1, keepdims=True)
        w_f = [jnp.exp2((t_f - top_f) * factor).astype(BF16)]
        w_b = [jnp.exp2((t - top_b) * factor).astype(BF16) for t in t_b]
        w_x = []
        for r in range(others):
            top = jnp.where(lower[r], top_f, top_b)
            w = jnp.exp2((t_a[r] - top) * factor)
            w_f.append(jnp.where(lower[r], w, 0.0).astype(BF16))
            w_x.append(jnp.where(lower[r], 0.0, w).astype(BF16))
        w_b = w_b[:1] + w_x + w_b[1:]
        out_f = jnp.dot(
            jnp.concatenate(w_f, axis=1), vt[:half_keys, :], preferred_element_type=F32
        )
        out_b = jnp.dot(jnp.concatenate(w_b, axis=1), vt[...], preferred_element_type=F32)
        for half, out in enumerate((out_f, out_b)):
            result = (out[:, :DH] / out[:, DH:]).astype(BF16)
            for j in range(stack):
                cols = slice((first + j) * DH, (first + j + 1) * DH)
                out_ref[tile(half), cols] = result[tile(j)]
                copy_ref[tile(half), cols] = result[tile(j)]


def final_kernel(
    count,
    g,
    groups,
    loss_scale,
    pre_ref,
    reach_ref,
    sx_ref,
    c_ref,
    teacher_ref,
    gain_ref,
    f_ref,
    dec_ref,
    *refs,
):
    others = count - 1
    got = refs[:others]
    before = refs[others] if g else None
    out_ref, grad_ref, front, back, flow, gated_ref, sums, gain_acc, skip_acc = refs[-9:]
    rows, width = pre_ref.shape
    stretch = rows // 2
    index = lax.axis_index("ctx")
    tile = 128
    step = 16

    @pl.when(index == 0)
    def _():
        front[...] = jnp.zeros_like(front)

    @pl.when(index == count - 1)
    def _():
        back[:N, :] = jnp.zeros((N, width), BF16)
        back[N:, :] = jnp.where(
            lax.broadcasted_iota(jnp.int32, (EXTRA, width), 0) == 0, 1.0, 0.0
        ).astype(BF16)

    for r in range(1, count):

        @pl.when(index == r)
        def _():
            front[...] = got[r - 1][:N, :]

        @pl.when(index == count - 1 - r)
        def _():
            back[...] = got[r - 1][...]

    d_in = back[N : N + 1, :].astype(F32) + back[N + 1 : N + 2, :].astype(F32)
    through = dec_ref[0:1, :] * front[...].astype(F32) + f_ref[...].astype(F32)
    entering = (d_in * through + back[:N, :].astype(F32)).astype(BF16)
    flow[:stretch, :] = jnp.dot(c_ref[:stretch, :], front[...], preferred_element_type=F32)
    flow[stretch:, :] = jnp.dot(c_ref[stretch:, :], entering, preferred_element_type=F32)
    gain_acc[...] = jnp.zeros_like(gain_acc)
    skip_acc[...] = jnp.zeros_like(skip_acc)

    @pl.loop(0, rows // step, unroll=2)
    def _(k):
        sl = pl.ds(pl.multiple_of(k * step, step), step)
        totals = [jnp.zeros((step, tile), F32)] * 3
        for j in range(0, width, tile):
            cols = slice(j, j + tile)
            gated = pre_ref[sl, cols] + reach_ref[sl, cols] * flow[sl, cols]
            gated_ref[sl, cols] = gated
            scaled = gated * gain_ref[:, cols]
            totals[0] += gated * gated
            totals[1] += scaled * scaled
            totals[2] += scaled * teacher_ref[sl, cols].astype(F32)
        for k3 in range(3):
            sums[sl, k3 * tile : (k3 + 1) * tile] = totals[k3]

    square, weighted, crossed = (
        jnp.sum(sums[:, k3 * tile : (k3 + 1) * tile], axis=1, keepdims=True) * (1.0 / width)
        for k3 in range(3)
    )
    scale = lax.rsqrt(square + EPS)
    push_scale = 2.0 * loss_scale
    mean = push_scale * scale * (scale * weighted - crossed)
    sums[:, :tile] = jnp.broadcast_to(scale, (rows, tile))
    sums[:, tile : 2 * tile] = jnp.broadcast_to(mean, (rows, tile))

    @pl.loop(0, rows // step, unroll=2)
    def _(k):
        sl = pl.ds(pl.multiple_of(k * step, step), step)
        scale = sums[sl, :tile]
        mean = sums[sl, tile : 2 * tile]
        for j in range(0, width, tile):
            cols = slice(j, j + tile)
            gain = gain_ref[:, cols]
            unit = gated_ref[sl, cols] * scale
            normed = unit * gain
            out_ref[sl, cols] = normed.astype(BF16)
            push = (normed - teacher_ref[sl, cols].astype(F32)) * push_scale
            by_gain = push * unit
            by_skip = (push * gain - unit * mean) * (scale * sx_ref[sl, cols])
            gain_acc[:, cols] += by_gain[:8] + by_gain[8:]
            skip_acc[:, cols] += by_skip[:8] + by_skip[8:]

    row = lax.broadcasted_iota(jnp.int32, (tile, width), 0)
    lane = lax.broadcasted_iota(jnp.int32, (tile, width), 1)
    matrix = jnp.where(row == lane // P_SIZE + g * (width // P_SIZE), 1.0, 0.0).astype(BF16)
    hi, lo = parts(skip_acc[...])
    by_head = jnp.sum(dot_nt(hi, matrix) + dot_nt(lo, matrix), axis=0, keepdims=True)
    grad_ref[...] = jnp.zeros_like(grad_ref)
    if g:
        grad_ref[:g, :] = before[:g, :]
        by_head += before[groups : groups + 1, :tile]
    grad_ref[g : g + 1, :] = jnp.sum(gain_acc[...], axis=0, keepdims=True)
    grad_ref[groups : groups + 1, :tile] = by_head


def closing_kernel(a_ref, b_ref, gain_ref, skip_ref):
    total = a_ref[...] + b_ref[...]
    groups, width = total.shape[0] - 1, total.shape[1]
    for g in range(groups):
        gain_ref[:, g * width : (g + 1) * width] = total[g : g + 1, :]
    skip_ref[...] = total[groups : groups + 1, : skip_ref.shape[1]]


def exchange(part, shift):
    axes = ("dp", "ctx")
    size = lax.axis_size(axes)
    return lax.ppermute(part, axes, [(d, d ^ shift) for d in range(size)])


def body(
    queries,
    keys,
    values,
    doc_ids,
    inputs,
    gate_input,
    b_input,
    c_input,
    dt_raw,
    dt_bias,
    decay_log,
    skip,
    gain,
):
    count = lax.axis_size("ctx")
    rows, features = queries.shape[1:]
    stretch = rows // 2
    kv_dev = keys.shape[2] // DH
    per_kv = queries.shape[2] // keys.shape[2]
    groups = b_input.shape[2] // N
    heads = features // P_SIZE
    width = features // groups
    length = doc_ids.shape[1]
    others = count - 1
    loss_scale = 1.0 / (lax.axis_size("dp") * count * rows)
    x, gate, bmat, cmat = inputs[0], gate_input[0], b_input[0], c_input[0]
    struct = jax.ShapeDtypeStruct

    def whole(*shape):
        return pl.BlockSpec(shape, lambda k: (0, 0))

    def chosen(size, g):
        return pl.BlockSpec((rows, size), lambda k: (0, g))

    state = struct((N, width), BF16)
    payload = struct((N + EXTRA, width), BF16)
    outs = pl.pallas_call(
        functools.partial(opening_kernel, count, groups),
        out_shape=(
            struct((rows, 2 * kv_dev * DH), BF16),
            struct((heads, rows), F32),
            *([struct((rows, width), BF16)] * groups),
            *([struct((8, width), F32)] * groups),
            *([state] * (2 * groups)),
            *([payload] * groups),
        ),
        in_specs=[VMEM] * 8,
        out_specs=(VMEM,) * (2 + 5 * groups),
        compiler_params=params(16),
        cost_estimate=cost(4 * rows * features * N, 8 * rows * features),
        name="opening",
    )(
        *(
            pltpu.with_memory_space_constraint(array, pltpu.HBM)
            for array in (
                doc_ids,
                keys[0],
                values[0],
                x,
                bmat,
                dt_raw[0].T,
                dt_bias.reshape(1, heads),
                decay_log.reshape(1, heads),
            )
        )
    )
    kv, ec = outs[:2]
    xw, dec, f_parts, b_parts, send = (
        outs[2 + k * groups : 2 + (k + 1) * groups] for k in range(5)
    )

    local = []
    for g in range(groups):
        local.append(
            pl.pallas_call(
                functools.partial(local_kernel, count, g * (heads // groups)),
                out_shape=(struct((rows, width), F32),) * 3,
                grid=(1,),
                in_specs=[
                    whole(1, length),
                    chosen(width, g),
                    chosen(width, g),
                    chosen(N, g),
                    chosen(N, g),
                    whole(heads, rows),
                    whole(1, heads),
                    whole(rows, width),
                ],
                out_specs=(whole(rows, width),) * 3,
                compiler_params=params(16),
                cost_estimate=cost(2 * rows * width * N, 16 * rows * width),
                name="local",
            )(doc_ids, x, gate, bmat, cmat, ec, skip.reshape(1, heads), xw[g])
        )

    send = list(send)
    got = [[] for _ in range(groups)]
    if count == 4:
        across = [(1, 2), (2, 1)]
        near = lax.ppermute(kv, "ctx", [(0, 1), (1, 0), (2, 3), (3, 2)])
        middle = lax.ppermute(kv, "ctx", across)
        beyond = lax.ppermute(near, "ctx", across)
        both = pl.pallas_call(
            pair_kernel,
            out_shape=struct((2 * rows, kv.shape[1]), BF16),
            in_specs=[VMEM] * 2,
            out_specs=VMEM,
            compiler_params=params(4),
            cost_estimate=cost(0, 4 * kv.size),
            name="pair",
        )(middle, beyond)
        far = lax.ppermute(both, "ctx", [(1, 0), (2, 3)])
        kv_got = [near, middle, beyond, far]
    else:
        ring = ring_order(count)
        ring_pairs = [(ring[d], ring[(d + 1) % count]) for d in range(count)]
        kv_got = [kv]
        for _ in range(others):
            kv_got.append(lax.ppermute(kv_got[-1], "ctx", ring_pairs))
        kv_got = kv_got[1:]
    for r in range(1, count):
        for g in range(groups):
            if r == 2:
                got[g][0], *local[g] = lax.optimization_barrier((got[g][0], *local[g]))
            if r > 1:
                send[g] = pl.pallas_call(
                    functools.partial(chain_kernel, count, r - 1),
                    out_shape=payload,
                    in_specs=[VMEM] * 4,
                    out_specs=VMEM,
                    compiler_params=params(4),
                    cost_estimate=cost(8 * N * width, 8 * N * width),
                    name="chain",
                )(got[g][-1], f_parts[g], b_parts[g], dec[g])
            pairs = [(r - 1, r), (count - r, count - r - 1)]
            got[g].append(lax.ppermute(send[g], "ctx", pairs))

    stack = 4 if per_kv % 4 == 0 and count <= 4 else 1
    teacher = None
    targets = []
    for g in range(kv_dev):
        more = [] if teacher is None else [teacher]
        teacher, target = pl.pallas_call(
            functools.partial(attention_kernel, count, per_kv, stack, g),
            out_shape=(struct((rows, features), BF16), struct((rows, per_kv * DH), BF16)),
            grid=(1,),
            in_specs=[
                whole(1, length),
                chosen(per_kv * DH, g),
                chosen(DH, g),
                chosen(DH, g),
                *[whole(*part.shape) for part in kv_got],
                *[pl.BlockSpec(memory_space=pl.ANY)] * len(more),
            ],
            out_specs=(chosen(per_kv * DH, g), whole(rows, per_kv * DH)),
            scratch_shapes=[
                pltpu.VMEM((2 * count * stretch, DH), BF16),
                pltpu.VMEM((2 * count * stretch, 2 * DH), BF16),
                pltpu.VMEM((stretch, stretch), F32),
                pltpu.VMEM((stretch, (count + 1) * stretch), F32),
                pltpu.VMEM((stretch, others * stretch), F32),
            ],
            input_output_aliases={4 + len(kv_got): 0} if more else {},
            compiler_params=params(24),
            cost_estimate=cost(
                4 * (2 * count + 1) * stretch * stretch * per_kv * DH, 8 * rows * per_kv * DH
            ),
            name="attention",
        )(doc_ids, queries[0], keys[0], values[0], *kv_got, *more)
        targets.append(target)

    student = grads = None
    for g in range(groups):
        more = [] if student is None else [grads, student]
        student, grads = pl.pallas_call(
            functools.partial(final_kernel, count, g, groups, loss_scale),
            out_shape=(struct((rows, features), BF16), struct((groups + 1, width), F32)),
            grid=(1,),
            in_specs=[
                *[whole(rows, width)] * 3,
                chosen(N, g),
                whole(rows, width),
                pl.BlockSpec((1, width), lambda k, g=g: (0, g)),
                whole(N, width),
                whole(8, width),
                *[whole(N + EXTRA, width)] * others,
                *([whole(groups + 1, width), pl.BlockSpec(memory_space=pl.ANY)] if more else []),
            ],
            out_specs=(chosen(width, g), whole(groups + 1, width)),
            scratch_shapes=[
                pltpu.VMEM((N, width), BF16),
                pltpu.VMEM((N + EXTRA, width), BF16),
                pltpu.VMEM((rows, width), F32),
                pltpu.VMEM((rows, width), F32),
                pltpu.VMEM((rows, 3 * 128), F32),
                pltpu.VMEM((8, width), F32),
                pltpu.VMEM((8, width), F32),
            ],
            input_output_aliases={9 + others: 0} if more else {},
            compiler_params=params(16),
            cost_estimate=cost(2 * rows * width * N, 20 * rows * width),
            name="final",
        )(
            *local[g],
            cmat,
            targets[g],
            gain.reshape(1, features),
            f_parts[g],
            dec[g],
            *got[g],
            *more,
        )
    partner = exchange(grads, 1)
    if lax.axis_size("dp") == 2:
        grads = (grads + partner) + (exchange(grads, count) + exchange(grads, count + 1))
    else:
        grads = grads + partner
    shifts = [1 << k for k in range(1, count.bit_length() - 1)]
    for shift in shifts[:-1]:
        grads = grads + exchange(grads, shift)
    grad_gain, grad_skip = pl.pallas_call(
        closing_kernel,
        out_shape=(struct((1, features), F32), struct((1, heads), F32)),
        in_specs=[VMEM] * 2,
        out_specs=(VMEM,) * 2,
        compiler_params=params(2),
        name="closing",
    )(grads, exchange(grads, shifts[-1]))
    return (teacher[None], student[None], grad_gain[0], grad_skip[0])


def solution(mesh):
    rows = P("dp", "ctx", "head")
    in_specs = (
        rows,
        rows,
        rows,
        P("dp", None),
        rows,
        rows,
        rows,
        rows,
        rows,
        P("head"),
        P("head"),
        P("head"),
        P("head"),
    )
    out_specs = (rows, rows, P("head"), P("head"))
    return jax.shard_map(body, mesh=mesh, in_specs=in_specs, out_specs=out_specs, check_vma=False)
```

```python
import functools
import math

import jax
import jax.numpy as jnp
from jax import lax
from jax.experimental import pallas as pl
from jax.experimental.pallas import tpu as pltpu
from jax.sharding import PartitionSpec as P

DH = 128
P_SIZE = 64
N = 128
EXTRA = 16
EPS = 1e-05
MASKED = -1e30
F32 = jnp.float32
BF16 = jnp.bfloat16
VMEM = pl.BlockSpec(memory_space=pltpu.VMEM)


def params(mib):
    return pltpu.CompilerParams(vmem_limit_bytes=mib << 20)


def cost(flops, size):
    return pl.CostEstimate(flops=flops, bytes_accessed=size, transcendentals=0)


def parts(v):
    hi = v.astype(BF16)
    return hi, (v - hi.astype(F32)).astype(BF16)


def spread_matrix(heads, width, first):
    row = lax.broadcasted_iota(jnp.int32, (heads, width), 0)
    lane = lax.broadcasted_iota(jnp.int32, (heads, width), 1)
    return jnp.where(row == (lane // P_SIZE) + first, 1.0, 0.0).astype(BF16)


def dot_nt(a, b):
    return lax.dot_general(a, b, (((1,), (1,)), ((), ())), preferred_element_type=F32)


def dot_tn(a, b):
    return lax.dot_general(a, b, (((0,), (0,)), ((), ())), preferred_element_type=F32)


def spread(v, matrix):
    hi, lo = parts(v)
    return dot_tn(hi, matrix) + dot_tn(lo, matrix)


def doc_row(docs_ref, block, stretch):
    return docs_ref[:, pl.ds(pl.multiple_of(block * stretch, stretch), stretch)]


def as_column(row):
    size = row.shape[1]
    r = lax.broadcasted_iota(jnp.int32, (size, size), 0)
    c = lax.broadcasted_iota(jnp.int32, (size, size), 1)
    return jnp.sum(jnp.where(r == c, row.astype(F32), 0.0), axis=1, keepdims=True)


def lower_triangle(size):
    r = lax.broadcasted_iota(jnp.int32, (size, size), 0)
    c = lax.broadcasted_iota(jnp.int32, (size, size), 1)
    return r >= c


def prior_doc(docs_ref, block, stretch):
    before = doc_row(docs_ref, jnp.maximum(block - 1, 0), stretch)[:, stretch - 1 :]
    return jnp.where(block > 0, before, -1)


def own_block(index, count, half):
    return index if half == 0 else 2 * count - 1 - index


def ring_order(count):
    return [0] + list(range(1, count, 2)) + list(range(2, count, 2))[::-1]


def ring_source(index, count, steps):
    order = ring_order(count)
    source = jnp.int32(0)
    for place, member in enumerate(order):
        source = jnp.where(index == member, order[(place - steps) % count], source)
    return source


def put_state(ref, state):
    ref[:N, :] = state.astype(BF16)
    ref[N:, :] = jnp.zeros((EXTRA, ref.shape[1]), BF16)


def put_composite(ref, state, decay):
    hi, lo = parts(decay)
    ref[:N, :] = state.astype(BF16)
    ref[N:, :] = jnp.concatenate(
        [hi, lo, jnp.zeros((EXTRA - 2, ref.shape[1]), BF16)], axis=0
    )


def opening_kernel(
    count,
    groups,
    docs_ref,
    k_ref,
    v_ref,
    x_ref,
    b_ref,
    dt_ref,
    bias_ref,
    log_ref,
    kv_ref,
    ec_ref,
    *outs,
):
    xw_refs, dec_refs, f_refs, b_refs, send_refs = (
        outs[k * groups : (k + 1) * groups] for k in range(5)
    )
    heads, rows = dt_ref.shape
    stretch = rows // 2
    width = x_ref.shape[1] // groups
    kv_width = k_ref.shape[1]
    index = lax.axis_index("ctx")
    kv_ref[:, :kv_width] = k_ref[...]
    kv_ref[:, kv_width:] = v_ref[...]
    triangle = jnp.where(lower_triangle(stretch), 1.0, 0.0)
    slope = jnp.exp(as_column(log_ref[...]))
    bias = as_column(bias_ref[...])
    lane = lax.broadcasted_iota(jnp.int32, (heads, 8), 1)
    ends = jnp.zeros((heads, 8), F32)
    loads = []
    projs = []
    for half in range(2):
        block = own_block(index, count, half)
        sl = slice(half * stretch, (half + 1) * stretch)
        raw = dt_ref[:, sl] + bias
        dt = jnp.maximum(raw, 0.0) + jnp.log1p(jnp.exp(-jnp.abs(raw)))
        cum = lax.dot_general(
            -dt * slope,
            triangle,
            (((1,), (1,)), ((), ())),
            precision=lax.Precision.HIGHEST,
            preferred_element_type=F32,
        )
        ec_ref[:, sl] = jnp.exp(cum)
        loads.append(jnp.exp(-cum) * dt)
        final = jnp.exp(cum[:, stretch - 1 :])
        row = doc_row(docs_ref, block, stretch)
        last = row[:, stretch - 1 :]
        kept = jnp.where(last == prior_doc(docs_ref, block, stretch), 1.0, 0.0)
        ends = jnp.where(lane == half, final * kept, ends)
        ends = jnp.where(lane == 2 + half, final, ends)
        same = jnp.where(as_column(row) == last.astype(F32), 1.0, 0.0)
        projs.append((b_ref[sl, :].astype(F32) * same).astype(BF16))
    for g in range(groups):
        cols = slice(g * width, (g + 1) * width)
        matrix = spread_matrix(heads, width, g * (heads // groups))
        wide = spread(ends, matrix)
        dec_refs[g][...] = wide
        sums = []
        for half in range(2):
            sl = slice(half * stretch, (half + 1) * stretch)
            xw = (x_ref[sl, cols].astype(F32) * spread(loads[half], matrix)).astype(BF16)
            xw_refs[g][sl, :] = xw
            sums.append(dot_tn(projs[half][:, g * N : (g + 1) * N], xw) * wide[2 + half : 3 + half])
        f_refs[g][...] = sums[0].astype(BF16)
        b_refs[g][...] = sums[1].astype(BF16)

        @pl.when(index == 0)
        def _():
            put_state(send_refs[g], sums[0])

        @pl.when(index != 0)
        def _():
            put_composite(send_refs[g], wide[1:2] * sums[0] + sums[1], wide[0:1] * wide[1:2])


def chain_kernel(count, stage, got_ref, f_ref, b_ref, dec_ref, send_ref):
    index = lax.axis_index("ctx")

    @pl.when(index == stage)
    def _():
        state = dec_ref[0:1, :] * got_ref[:N, :].astype(F32) + f_ref[...].astype(F32)
        put_state(send_ref, state)

    @pl.when(index == count - 1 - stage)
    def _():
        decay = got_ref[N : N + 1, :].astype(F32) + got_ref[N + 1 : N + 2, :].astype(F32)
        inner = decay * f_ref[...].astype(F32) + got_ref[:N, :].astype(F32)
        state = dec_ref[1:2, :] * inner + b_ref[...].astype(F32)
        put_composite(send_ref, state, dec_ref[1:2, :] * decay * dec_ref[0:1, :])


def local_kernel(
    count,
    first,
    docs_ref,
    x_ref,
    gate_ref,
    b_ref,
    c_ref,
    ec_ref,
    skip_ref,
    xw_ref,
    pre_ref,
    reach_ref,
    sx_ref,
):
    heads, rows = ec_ref.shape
    stretch = rows // 2
    width = x_ref.shape[1]
    index = lax.axis_index("ctx")
    matrix = spread_matrix(heads, width, first)
    wide_skip = spread(as_column(skip_ref[...]), matrix)
    triangle = lower_triangle(stretch)
    step = 16
    for half in range(2):
        block = own_block(index, count, half)
        sl = slice(half * stretch, (half + 1) * stretch)
        row = doc_row(docs_ref, block, stretch)
        column = as_column(row)
        gram = dot_nt(c_ref[sl, :], b_ref[sl, :])
        gram = jnp.where(triangle & (column == row.astype(F32)), gram, 0.0).astype(BF16)
        wide = spread(ec_ref[:, sl], matrix)
        inner = jnp.dot(gram, xw_ref[sl, :], preferred_element_type=F32)
        reached = jnp.where(column == prior_doc(docs_ref, block, stretch).astype(F32), 1.0, 0.0)
        for k in range(0, stretch, step):
            at = slice(half * stretch + k, half * stretch + k + step)
            here = slice(k, k + step)
            x = x_ref[at, :].astype(F32)
            gate = gate_ref[at, :].astype(F32)
            silu = gate / (1.0 + jnp.exp(-gate))
            fade = wide[here] * silu
            sx = silu * x
            sx_ref[at, :] = sx
            pre_ref[at, :] = inner[here] * fade + wide_skip * sx
            reach_ref[at, :] = reached[here] * fade


def arrivals(index, count, refs):
    if count != 4:
        return [(ring_source(index, count, r + 1), [(None, refs[r])]) for r in range(count - 1)]
    near, own_of_middle, next_of_middle, far, farther = refs
    middle = (index == 1) | (index == 2)
    low = index < 2
    return [
        (index ^ 1, [(None, near)]),
        (
            jnp.where(low, 2, 1),
            [(middle, own_of_middle), (jnp.logical_not(middle), far)],
        ),
        (
            jnp.where(low, 3, 0),
            [(middle, next_of_middle), (jnp.logical_not(middle), farther)],
        ),
    ]


def attention_kernel(count, per, stack, g, docs_ref, q_ref, k_ref, v_ref, *refs):
    others = count - 1
    sent = 5 if count == 4 else others
    out_ref, copy_ref, kt, vt, bias_f, bias_b, bias_a = refs[-7:]
    rows = q_ref.shape[0]
    stretch = rows // 2
    index = lax.axis_index("ctx")
    last = 2 * count - 1
    kv_width = refs[0].shape[1] // 2
    k_cols = slice(g * DH, (g + 1) * DH)
    v_cols = slice(kv_width + g * DH, kv_width + (g + 1) * DH)
    row_f = doc_row(docs_ref, index, stretch).astype(F32)
    row_b = doc_row(docs_ref, last - index, stretch).astype(F32)
    col_f = as_column(row_f)
    col_b = as_column(row_b)
    triangle = lower_triangle(stretch)

    def tile(k):
        return slice(k * stretch, (k + 1) * stretch)

    bias_f[...] = jnp.where(triangle & (col_f == row_f), 0.0, MASKED)
    bias_b[:, tile(0)] = jnp.where(col_b == row_f, 0.0, MASKED)
    bias_b[:, tile(1)] = jnp.where(triangle & (col_b == row_b), 0.0, MASKED)
    vt[:, DH:] = jnp.ones((vt.shape[0], DH), BF16)
    kt[tile(0), :] = k_ref[:stretch, :]
    vt[tile(0), :DH] = v_ref[:stretch, :]
    kt[tile(count), :] = k_ref[stretch:, :]
    vt[tile(count), :DH] = v_ref[stretch:, :]
    lower = []
    for r, (source, places) in enumerate(arrivals(index, count, refs[:sent])):
        lower.append(source < index)
        for condition, ref in places:

            def fetch(ref=ref, r=r):
                front = slice(0, stretch)
                start = jnp.where(lower[r], 0, stretch)
                own = pl.ds(pl.multiple_of(start, stretch), stretch)
                kt[tile(1 + r), :] = ref[own, k_cols]
                vt[tile(1 + r), :DH] = ref[own, v_cols]
                kt[tile(count + 1 + r), :] = ref[front, k_cols]
                vt[tile(count + 1 + r), :DH] = ref[front, v_cols]

            if condition is None:
                fetch()
            else:
                pl.when(condition)(fetch)
        key_f = doc_row(docs_ref, source, stretch).astype(F32)
        key_a = doc_row(docs_ref, jnp.where(lower[r], source, last - source), stretch).astype(F32)
        bias_b[:, tile(2 + r)] = jnp.where(col_b == key_f, 0.0, MASKED)
        bias_a[:, tile(r)] = jnp.where(jnp.where(lower[r], col_f, col_b) == key_a, 0.0, MASKED)

    factor = math.log2(math.e) / math.sqrt(DH)
    tall = stack * stretch
    half_keys = count * stretch

    def stacked(first, base):
        return jnp.concatenate(
            [
                q_ref[base : base + stretch, (first + j) * DH : (first + j + 1) * DH]
                for j in range(stack)
            ],
            axis=0,
        )

    def biased(score, bias):
        size = score.shape[1]
        return (score.reshape(stack, stretch, size) + bias[None]).reshape(tall, size)

    for first in range(0, per, stack):
        s_f = dot_nt(stacked(first, 0), kt[:half_keys, :])
        s_b = dot_nt(stacked(first, stretch), kt[...])
        t_f = biased(s_f[:, tile(0)], bias_f[...])
        t_b = [biased(s_b[:, tile(0)], bias_b[:, tile(0)])]
        for k in range(1, count + 1):
            t_b.append(biased(s_b[:, tile(count + k - 1)], bias_b[:, tile(k)]))
        t_a = []
        for r in range(others):
            score = jnp.where(lower[r], s_f[:, tile(1 + r)], s_b[:, tile(1 + r)])
            t_a.append(biased(score, bias_a[:, tile(r)]))
        best_f = t_f
        best_b = functools.reduce(jnp.maximum, t_b)
        for r in range(others):
            best_f = jnp.maximum(best_f, jnp.where(lower[r], t_a[r], MASKED))
            best_b = jnp.maximum(best_b, jnp.where(lower[r], MASKED, t_a[r]))
        top_f = jnp.max(best_f, axis=1, keepdims=True)
        top_b = jnp.max(best_b, axis=1, keepdims=True)
        w_f = [jnp.exp2((t_f - top_f) * factor).astype(BF16)]
        w_b = [jnp.exp2((t - top_b) * factor).astype(BF16) for t in t_b]
        w_x = []
        for r in range(others):
            top = jnp.where(lower[r], top_f, top_b)
            w = jnp.exp2((t_a[r] - top) * factor)
            w_f.append(jnp.where(lower[r], w, 0.0).astype(BF16))
            w_x.append(jnp.where(lower[r], 0.0, w).astype(BF16))
        w_b = w_b[:1] + w_x + w_b[1:]
        out_f = jnp.dot(
            jnp.concatenate(w_f, axis=1), vt[:half_keys, :], preferred_element_type=F32
        )
        out_b = jnp.dot(jnp.concatenate(w_b, axis=1), vt[...], preferred_element_type=F32)
        for half, out in enumerate((out_f, out_b)):
            result = (out[:, :DH] / out[:, DH:]).astype(BF16)
            for j in range(stack):
                cols = slice((first + j) * DH, (first + j + 1) * DH)
                out_ref[tile(half), cols] = result[tile(j)]
                copy_ref[tile(half), cols] = result[tile(j)]


def final_kernel(
    count,
    g,
    groups,
    loss_scale,
    pre_ref,
    reach_ref,
    sx_ref,
    c_ref,
    teacher_ref,
    gain_ref,
    f_ref,
    dec_ref,
    *refs,
):
    others = count - 1
    got = refs[:others]
    before = refs[others] if g else None
    out_ref, grad_ref, front, back, flow, gated_ref, sums, gain_acc, skip_acc = refs[-9:]
    rows, width = pre_ref.shape
    stretch = rows // 2
    index = lax.axis_index("ctx")
    tile = 128
    step = 16

    @pl.when(index == 0)
    def _():
        front[...] = jnp.zeros_like(front)

    @pl.when(index == count - 1)
    def _():
        back[:N, :] = jnp.zeros((N, width), BF16)
        back[N:, :] = jnp.where(
            lax.broadcasted_iota(jnp.int32, (EXTRA, width), 0) == 0, 1.0, 0.0
        ).astype(BF16)

    for r in range(1, count):

        @pl.when(index == r)
        def _():
            front[...] = got[r - 1][:N, :]

        @pl.when(index == count - 1 - r)
        def _():
            back[...] = got[r - 1][...]

    d_in = back[N : N + 1, :].astype(F32) + back[N + 1 : N + 2, :].astype(F32)
    through = dec_ref[0:1, :] * front[...].astype(F32) + f_ref[...].astype(F32)
    entering = (d_in * through + back[:N, :].astype(F32)).astype(BF16)
    flow[:stretch, :] = jnp.dot(c_ref[:stretch, :], front[...], preferred_element_type=F32)
    flow[stretch:, :] = jnp.dot(c_ref[stretch:, :], entering, preferred_element_type=F32)
    gain_acc[...] = jnp.zeros_like(gain_acc)
    skip_acc[...] = jnp.zeros_like(skip_acc)

    @pl.loop(0, rows // step, unroll=2)
    def _(k):
        sl = pl.ds(pl.multiple_of(k * step, step), step)
        totals = [jnp.zeros((step, tile), F32)] * 3
        for j in range(0, width, tile):
            cols = slice(j, j + tile)
            gated = pre_ref[sl, cols] + reach_ref[sl, cols] * flow[sl, cols]
            gated_ref[sl, cols] = gated
            scaled = gated * gain_ref[:, cols]
            totals[0] += gated * gated
            totals[1] += scaled * scaled
            totals[2] += scaled * teacher_ref[sl, cols].astype(F32)
        for k3 in range(3):
            sums[sl, k3 * tile : (k3 + 1) * tile] = totals[k3]

    square, weighted, crossed = (
        jnp.sum(sums[:, k3 * tile : (k3 + 1) * tile], axis=1, keepdims=True) * (1.0 / width)
        for k3 in range(3)
    )
    scale = lax.rsqrt(square + EPS)
    push_scale = 2.0 * loss_scale
    mean = push_scale * scale * (scale * weighted - crossed)
    sums[:, :tile] = jnp.broadcast_to(scale, (rows, tile))
    sums[:, tile : 2 * tile] = jnp.broadcast_to(mean, (rows, tile))

    @pl.loop(0, rows // step, unroll=2)
    def _(k):
        sl = pl.ds(pl.multiple_of(k * step, step), step)
        scale = sums[sl, :tile]
        mean = sums[sl, tile : 2 * tile]
        for j in range(0, width, tile):
            cols = slice(j, j + tile)
            gain = gain_ref[:, cols]
            unit = gated_ref[sl, cols] * scale
            normed = unit * gain
            out_ref[sl, cols] = normed.astype(BF16)
            push = (normed - teacher_ref[sl, cols].astype(F32)) * push_scale
            by_gain = push * unit
            by_skip = (push * gain - unit * mean) * (scale * sx_ref[sl, cols])
            gain_acc[:, cols] += by_gain[:8] + by_gain[8:]
            skip_acc[:, cols] += by_skip[:8] + by_skip[8:]

    row = lax.broadcasted_iota(jnp.int32, (tile, width), 0)
    lane = lax.broadcasted_iota(jnp.int32, (tile, width), 1)
    matrix = jnp.where(row == lane // P_SIZE + g * (width // P_SIZE), 1.0, 0.0).astype(BF16)
    hi, lo = parts(skip_acc[...])
    by_head = jnp.sum(dot_nt(hi, matrix) + dot_nt(lo, matrix), axis=0, keepdims=True)
    grad_ref[...] = jnp.zeros_like(grad_ref)
    if g:
        grad_ref[:g, :] = before[:g, :]
        by_head += before[groups : groups + 1, :tile]
    grad_ref[g : g + 1, :] = jnp.sum(gain_acc[...], axis=0, keepdims=True)
    grad_ref[groups : groups + 1, :tile] = by_head


def closing_kernel(a_ref, b_ref, gain_ref, skip_ref):
    total = a_ref[...] + b_ref[...]
    groups, width = total.shape[0] - 1, total.shape[1]
    for g in range(groups):
        gain_ref[:, g * width : (g + 1) * width] = total[g : g + 1, :]
    skip_ref[...] = total[groups : groups + 1, : skip_ref.shape[1]]


def exchange(part, shift):
    axes = ("dp", "ctx")
    size = lax.axis_size(axes)
    return lax.ppermute(part, axes, [(d, d ^ shift) for d in range(size)])


def body(
    queries,
    keys,
    values,
    doc_ids,
    inputs,
    gate_input,
    b_input,
    c_input,
    dt_raw,
    dt_bias,
    decay_log,
    skip,
    gain,
):
    count = lax.axis_size("ctx")
    rows, features = queries.shape[1:]
    stretch = rows // 2
    kv_dev = keys.shape[2] // DH
    per_kv = queries.shape[2] // keys.shape[2]
    groups = b_input.shape[2] // N
    heads = features // P_SIZE
    width = features // groups
    length = doc_ids.shape[1]
    others = count - 1
    loss_scale = 1.0 / (lax.axis_size("dp") * count * rows)
    x, gate, bmat, cmat = inputs[0], gate_input[0], b_input[0], c_input[0]
    struct = jax.ShapeDtypeStruct

    def whole(*shape):
        return pl.BlockSpec(shape, lambda k: (0, 0))

    def chosen(size, g):
        return pl.BlockSpec((rows, size), lambda k: (0, g))

    state = struct((N, width), BF16)
    payload = struct((N + EXTRA, width), BF16)
    outs = pl.pallas_call(
        functools.partial(opening_kernel, count, groups),
        out_shape=(
            struct((rows, 2 * kv_dev * DH), BF16),
            struct((heads, rows), F32),
            *([struct((rows, width), BF16)] * groups),
            *([struct((8, width), F32)] * groups),
            *([state] * (2 * groups)),
            *([payload] * groups),
        ),
        in_specs=[VMEM] * 8,
        out_specs=(VMEM,) * (2 + 5 * groups),
        compiler_params=params(16),
        cost_estimate=cost(4 * rows * features * N, 8 * rows * features),
        name="opening",
    )(
        *(
            pltpu.with_memory_space_constraint(array, pltpu.HBM)
            for array in (
                doc_ids,
                keys[0],
                values[0],
                x,
                bmat,
                dt_raw[0].T,
                dt_bias.reshape(1, heads),
                decay_log.reshape(1, heads),
            )
        )
    )
    kv, ec = outs[:2]
    xw, dec, f_parts, b_parts, send = (
        outs[2 + k * groups : 2 + (k + 1) * groups] for k in range(5)
    )

    local = []
    for g in range(groups):
        local.append(
            pl.pallas_call(
                functools.partial(local_kernel, count, g * (heads // groups)),
                out_shape=(struct((rows, width), F32),) * 3,
                grid=(1,),
                in_specs=[
                    whole(1, length),
                    chosen(width, g),
                    chosen(width, g),
                    chosen(N, g),
                    chosen(N, g),
                    whole(heads, rows),
                    whole(1, heads),
                    whole(rows, width),
                ],
                out_specs=(whole(rows, width),) * 3,
                compiler_params=params(16),
                cost_estimate=cost(2 * rows * width * N, 16 * rows * width),
                name="local",
            )(doc_ids, x, gate, bmat, cmat, ec, skip.reshape(1, heads), xw[g])
        )

    send = list(send)
    got = [[] for _ in range(groups)]
    if count == 4:
        across = [(1, 2), (2, 1)]
        near = lax.ppermute(kv, "ctx", [(0, 1), (1, 0), (2, 3), (3, 2)])
        middle = lax.ppermute(kv, "ctx", across)
        near, local = lax.optimization_barrier((near, local))
        beyond = lax.ppermute(near, "ctx", across)
        outward = [(1, 0), (2, 3)]
        far = lax.ppermute(middle, "ctx", outward)
        farther = lax.ppermute(beyond, "ctx", outward)
        kv_got = [near, middle, beyond, far, farther]
    else:
        ring = ring_order(count)
        ring_pairs = [(ring[d], ring[(d + 1) % count]) for d in range(count)]
        kv_got = [kv]
        for _ in range(others):
            kv_got.append(lax.ppermute(kv_got[-1], "ctx", ring_pairs))
        kv_got = kv_got[1:]
    stack = 4 if per_kv % 4 == 0 and count <= 4 else 1
    teacher = None
    targets = []
    for g in range(kv_dev):
        more = [] if teacher is None else [teacher]
        teacher, target = pl.pallas_call(
            functools.partial(attention_kernel, count, per_kv, stack, g),
            out_shape=(struct((rows, features), BF16), struct((rows, per_kv * DH), BF16)),
            grid=(1,),
            in_specs=[
                whole(1, length),
                chosen(per_kv * DH, g),
                chosen(DH, g),
                chosen(DH, g),
                *[whole(*part.shape) for part in kv_got],
                *[pl.BlockSpec(memory_space=pl.ANY)] * len(more),
            ],
            out_specs=(chosen(per_kv * DH, g), whole(rows, per_kv * DH)),
            scratch_shapes=[
                pltpu.VMEM((2 * count * stretch, DH), BF16),
                pltpu.VMEM((2 * count * stretch, 2 * DH), BF16),
                pltpu.VMEM((stretch, stretch), F32),
                pltpu.VMEM((stretch, (count + 1) * stretch), F32),
                pltpu.VMEM((stretch, others * stretch), F32),
            ],
            input_output_aliases={4 + len(kv_got): 0} if more else {},
            compiler_params=params(24),
            cost_estimate=cost(
                4 * (2 * count + 1) * stretch * stretch * per_kv * DH, 8 * rows * per_kv * DH
            ),
            name="attention",
        )(doc_ids, queries[0], keys[0], values[0], *kv_got, *more)
        targets.append(target)

    for r in range(1, count):
        for g in range(groups):
            if r == 3 and g == groups - 1:
                got[g][-1], targets[0] = lax.optimization_barrier((got[g][-1], targets[0]))
            if r > 1:
                send[g] = pl.pallas_call(
                    functools.partial(chain_kernel, count, r - 1),
                    out_shape=payload,
                    in_specs=[VMEM] * 4,
                    out_specs=VMEM,
                    compiler_params=params(4),
                    cost_estimate=cost(8 * N * width, 8 * N * width),
                    name="chain",
                )(got[g][-1], f_parts[g], b_parts[g], dec[g])
            pairs = [(r - 1, r), (count - r, count - r - 1)]
            got[g].append(lax.ppermute(send[g], "ctx", pairs))

    student = grads = None
    for g in range(groups):
        more = [] if student is None else [grads, student]
        student, grads = pl.pallas_call(
            functools.partial(final_kernel, count, g, groups, loss_scale),
            out_shape=(struct((rows, features), BF16), struct((groups + 1, width), F32)),
            grid=(1,),
            in_specs=[
                *[whole(rows, width)] * 3,
                chosen(N, g),
                whole(rows, width),
                pl.BlockSpec((1, width), lambda k, g=g: (0, g)),
                whole(N, width),
                whole(8, width),
                *[whole(N + EXTRA, width)] * others,
                *([whole(groups + 1, width), pl.BlockSpec(memory_space=pl.ANY)] if more else []),
            ],
            out_specs=(chosen(width, g), whole(groups + 1, width)),
            scratch_shapes=[
                pltpu.VMEM((N, width), BF16),
                pltpu.VMEM((N + EXTRA, width), BF16),
                pltpu.VMEM((rows, width), F32),
                pltpu.VMEM((rows, width), F32),
                pltpu.VMEM((rows, 3 * 128), F32),
                pltpu.VMEM((8, width), F32),
                pltpu.VMEM((8, width), F32),
            ],
            input_output_aliases={9 + others: 0} if more else {},
            compiler_params=params(16),
            cost_estimate=cost(2 * rows * width * N, 20 * rows * width),
            name="final",
        )(
            *local[g],
            cmat,
            targets[g],
            gain.reshape(1, features),
            f_parts[g],
            dec[g],
            *got[g],
            *more,
        )
    partner = exchange(grads, 1)
    if lax.axis_size("dp") == 2:
        grads = (grads + partner) + (exchange(grads, count) + exchange(grads, count + 1))
    else:
        grads = grads + partner
    shifts = [1 << k for k in range(1, count.bit_length() - 1)]
    for shift in shifts[:-1]:
        grads = grads + exchange(grads, shift)
    grad_gain, grad_skip = pl.pallas_call(
        closing_kernel,
        out_shape=(struct((1, features), F32), struct((1, heads), F32)),
        in_specs=[VMEM] * 2,
        out_specs=(VMEM,) * 2,
        compiler_params=params(2),
        name="closing",
    )(grads, exchange(grads, shifts[-1]))
    return (teacher[None], student[None], grad_gain[0], grad_skip[0])


def solution(mesh):
    rows = P("dp", "ctx", "head")
    in_specs = (
        rows,
        rows,
        rows,
        P("dp", None),
        rows,
        rows,
        rows,
        rows,
        rows,
        P("head"),
        P("head"),
        P("head"),
        P("head"),
    )
    out_specs = (rows, rows, P("head"), P("head"))
    return jax.shard_map(body, mesh=mesh, in_specs=in_specs, out_specs=out_specs, check_vma=False)
```

```python
import functools
import math

import jax
import jax.numpy as jnp
from jax import lax
from jax.experimental import pallas as pl
from jax.experimental.pallas import tpu as pltpu
from jax.sharding import PartitionSpec as P

DH = 128
P_SIZE = 64
N = 128
EXTRA = 16
EPS = 1e-05
MASKED = -1e30
F32 = jnp.float32
BF16 = jnp.bfloat16
VMEM = pl.BlockSpec(memory_space=pltpu.VMEM)


def params(mib):
    return pltpu.CompilerParams(vmem_limit_bytes=mib << 20)


def cost(flops, size):
    return pl.CostEstimate(flops=flops, bytes_accessed=size, transcendentals=0)


def parts(v):
    hi = v.astype(BF16)
    return hi, (v - hi.astype(F32)).astype(BF16)


def spread_matrix(heads, width, first):
    row = lax.broadcasted_iota(jnp.int32, (heads, width), 0)
    lane = lax.broadcasted_iota(jnp.int32, (heads, width), 1)
    return jnp.where(row == (lane // P_SIZE) + first, 1.0, 0.0).astype(BF16)


def dot_nt(a, b):
    return lax.dot_general(a, b, (((1,), (1,)), ((), ())), preferred_element_type=F32)


def dot_tn(a, b):
    return lax.dot_general(a, b, (((0,), (0,)), ((), ())), preferred_element_type=F32)


def spread(v, matrix):
    hi, lo = parts(v)
    return dot_tn(hi, matrix) + dot_tn(lo, matrix)


def doc_row(docs_ref, block, stretch):
    return docs_ref[:, pl.ds(pl.multiple_of(block * stretch, stretch), stretch)]


def as_column(row):
    size = row.shape[1]
    r = lax.broadcasted_iota(jnp.int32, (size, size), 0)
    c = lax.broadcasted_iota(jnp.int32, (size, size), 1)
    return jnp.sum(jnp.where(r == c, row.astype(F32), 0.0), axis=1, keepdims=True)


def lower_triangle(size):
    r = lax.broadcasted_iota(jnp.int32, (size, size), 0)
    c = lax.broadcasted_iota(jnp.int32, (size, size), 1)
    return r >= c


def prior_doc(docs_ref, block, stretch):
    before = doc_row(docs_ref, jnp.maximum(block - 1, 0), stretch)[:, stretch - 1 :]
    return jnp.where(block > 0, before, -1)


def own_block(index, count, half):
    return index if half == 0 else 2 * count - 1 - index


def ring_order(count):
    return [0] + list(range(1, count, 2)) + list(range(2, count, 2))[::-1]


def ring_source(index, count, steps):
    order = ring_order(count)
    source = jnp.int32(0)
    for place, member in enumerate(order):
        source = jnp.where(index == member, order[(place - steps) % count], source)
    return source


def put_state(ref, state):
    ref[:N, :] = state.astype(BF16)
    ref[N:, :] = jnp.zeros((EXTRA, ref.shape[1]), BF16)


def put_composite(ref, state, decay):
    hi, lo = parts(decay)
    ref[:N, :] = state.astype(BF16)
    ref[N:, :] = jnp.concatenate(
        [hi, lo, jnp.zeros((EXTRA - 2, ref.shape[1]), BF16)], axis=0
    )


def opening_kernel(
    count,
    groups,
    docs_ref,
    k_ref,
    v_ref,
    x_ref,
    b_ref,
    dt_ref,
    bias_ref,
    log_ref,
    kv_ref,
    ec_ref,
    *outs,
):
    xw_refs, dec_refs, f_refs, b_refs, send_refs = (
        outs[k * groups : (k + 1) * groups] for k in range(5)
    )
    x_here, x_sem = outs[5 * groups :]
    heads, rows = dt_ref.shape
    stretch = rows // 2
    width = x_ref.shape[1] // groups
    kv_width = k_ref.shape[1]
    index = lax.axis_index("ctx")
    loads_x = [
        pltpu.make_async_copy(
            x_ref.at[:, pl.ds(g * width, width)], x_here.at[g], x_sem.at[g]
        )
        for g in range(groups)
    ]
    for load in loads_x:
        load.start()
    kv_ref[:, :kv_width] = k_ref[...]
    kv_ref[:, kv_width:] = v_ref[...]
    triangle = jnp.where(lower_triangle(stretch), 1.0, 0.0)
    slope = jnp.exp(as_column(log_ref[...]))
    bias = as_column(bias_ref[...])
    lane = lax.broadcasted_iota(jnp.int32, (heads, 8), 1)
    ends = jnp.zeros((heads, 8), F32)
    loads = []
    projs = []
    for half in range(2):
        block = own_block(index, count, half)
        sl = slice(half * stretch, (half + 1) * stretch)
        raw = dt_ref[:, sl] + bias
        dt = jnp.maximum(raw, 0.0) + jnp.log1p(jnp.exp(-jnp.abs(raw)))
        cum = lax.dot_general(
            -dt * slope,
            triangle,
            (((1,), (1,)), ((), ())),
            precision=lax.Precision.HIGHEST,
            preferred_element_type=F32,
        )
        ec_ref[:, sl] = jnp.exp(cum)
        loads.append(jnp.exp(-cum) * dt)
        final = jnp.exp(cum[:, stretch - 1 :])
        row = doc_row(docs_ref, block, stretch)
        last = row[:, stretch - 1 :]
        kept = jnp.where(last == prior_doc(docs_ref, block, stretch), 1.0, 0.0)
        ends = jnp.where(lane == half, final * kept, ends)
        ends = jnp.where(lane == 2 + half, final, ends)
        same = jnp.where(as_column(row) == last.astype(F32), 1.0, 0.0)
        projs.append((b_ref[sl, :].astype(F32) * same).astype(BF16))
    for g in range(groups):
        matrix = spread_matrix(heads, width, g * (heads // groups))
        wide = spread(ends, matrix)
        dec_refs[g][...] = wide
        sums = []
        loads_x[g].wait()
        for half in range(2):
            sl = slice(half * stretch, (half + 1) * stretch)
            xw = (x_here[g, sl, :].astype(F32) * spread(loads[half], matrix)).astype(BF16)
            xw_refs[g][sl, :] = xw
            sums.append(dot_tn(projs[half][:, g * N : (g + 1) * N], xw) * wide[2 + half : 3 + half])
        f_refs[g][...] = sums[0].astype(BF16)
        b_refs[g][...] = sums[1].astype(BF16)

        @pl.when(index == 0)
        def _():
            put_state(send_refs[g], sums[0])

        @pl.when(index != 0)
        def _():
            put_composite(send_refs[g], wide[1:2] * sums[0] + sums[1], wide[0:1] * wide[1:2])


def chain_kernel(count, stage, got_ref, f_ref, b_ref, dec_ref, send_ref):
    index = lax.axis_index("ctx")

    @pl.when(index == stage)
    def _():
        state = dec_ref[0:1, :] * got_ref[:N, :].astype(F32) + f_ref[...].astype(F32)
        put_state(send_ref, state)

    @pl.when(index == count - 1 - stage)
    def _():
        decay = got_ref[N : N + 1, :].astype(F32) + got_ref[N + 1 : N + 2, :].astype(F32)
        inner = decay * f_ref[...].astype(F32) + got_ref[:N, :].astype(F32)
        state = dec_ref[1:2, :] * inner + b_ref[...].astype(F32)
        put_composite(send_ref, state, dec_ref[1:2, :] * decay * dec_ref[0:1, :])


def local_kernel(
    count, groups, docs_ref, x_ref, gate_ref, b_ref, c_ref, skip_ref, ec_ref, *refs
):
    xw_refs, pre_refs, reach_refs, sx_refs = (
        refs[k * groups : (k + 1) * groups] for k in range(4)
    )
    x_here, gate_here, sems = refs[4 * groups :]
    heads, rows = ec_ref.shape
    stretch = rows // 2
    width = x_ref.shape[1] // groups
    index = lax.axis_index("ctx")
    moves = []
    for g in range(groups):
        cols = pl.ds(g * width, width)
        moves.append(
            [
                pltpu.make_async_copy(x_ref.at[:, cols], x_here.at[g], sems.at[0, g]),
                pltpu.make_async_copy(gate_ref.at[:, cols], gate_here.at[g], sems.at[1, g]),
            ]
        )
        for move in moves[g]:
            move.start()
    triangle = lower_triangle(stretch)
    skip = as_column(skip_ref[...])
    step = 16
    masks = []
    for half in range(2):
        block = own_block(index, count, half)
        row = doc_row(docs_ref, block, stretch)
        column = as_column(row)
        reached = jnp.where(column == prior_doc(docs_ref, block, stretch).astype(F32), 1.0, 0.0)
        masks.append((triangle & (column == row.astype(F32)), reached))
    for g in range(groups):
        proj = slice(g * N, (g + 1) * N)
        matrix = spread_matrix(heads, width, g * (heads // groups))
        wide_skip = spread(skip, matrix)
        for half in range(2):
            sl = slice(half * stretch, (half + 1) * stretch)
            near, reached = masks[half]
            gram = dot_nt(c_ref[sl, proj], b_ref[sl, proj])
            gram = jnp.where(near, gram, 0.0).astype(BF16)
            wide = spread(ec_ref[:, sl], matrix)
            inner = jnp.dot(gram, xw_refs[g][sl, :], preferred_element_type=F32)
            if half == 0:
                for move in moves[g]:
                    move.wait()
            for k in range(0, stretch, step):
                at = slice(half * stretch + k, half * stretch + k + step)
                here = slice(k, k + step)
                x = x_here[g, at, :].astype(F32)
                gate = gate_here[g, at, :].astype(F32)
                silu = gate / (1.0 + jnp.exp(-gate))
                fade = wide[here] * silu
                sx = silu * x
                sx_refs[g][at, :] = sx
                pre_refs[g][at, :] = inner[here] * fade + wide_skip * sx
                reach_refs[g][at, :] = reached[here] * fade


def merge_kernel(count, state_ref, kv_ref, out_ref):
    index = lax.axis_index("ctx")
    outer = (index == 0) | (index == count - 1)
    rows, wide = kv_ref.shape
    stretch = rows // 2

    @pl.when(outer)
    def _():
        out_ref[...] = state_ref[...]

    @pl.when(jnp.logical_not(outer))
    def _():
        out_ref[:stretch, :wide] = kv_ref[:stretch, :]
        out_ref[:stretch, wide:] = kv_ref[stretch:, :]
        out_ref[stretch:, :] = jnp.zeros((out_ref.shape[0] - stretch, 2 * wide), BF16)


def arrivals(index, count, refs):
    if count != 4:
        return [(ring_source(index, count, r + 1), [(None, refs[r])]) for r in range(count - 1)]
    near, own_of_middle, next_of_middle, far, farther = refs
    middle = (index == 1) | (index == 2)
    low = index < 2
    return [
        (index ^ 1, [(None, near)]),
        (
            jnp.where(low, 2, 1),
            [(middle, own_of_middle), (jnp.logical_not(middle), far)],
        ),
        (
            jnp.where(low, 3, 0),
            [(middle, next_of_middle), (jnp.logical_not(middle), farther)],
        ),
    ]


def attention_kernel(count, per, stack, g, docs_ref, q_ref, k_ref, v_ref, *refs):
    others = count - 1
    sent = 5 if count == 4 else others
    out_ref, kt, vt, bias_f, bias_b, bias_a = refs[-6:]
    rows = q_ref.shape[0]
    stretch = rows // 2
    index = lax.axis_index("ctx")
    last = 2 * count - 1
    kv_width = refs[0].shape[1] // 2
    row_f = doc_row(docs_ref, index, stretch).astype(F32)
    row_b = doc_row(docs_ref, last - index, stretch).astype(F32)
    col_f = as_column(row_f)
    col_b = as_column(row_b)
    triangle = lower_triangle(stretch)

    def tile(k):
        return slice(k * stretch, (k + 1) * stretch)

    bias_f[...] = jnp.where(triangle & (col_f == row_f), 0.0, MASKED)
    bias_b[:, tile(0)] = jnp.where(col_b == row_f, 0.0, MASKED)
    bias_b[:, tile(1)] = jnp.where(triangle & (col_b == row_b), 0.0, MASKED)
    vt[:, DH:] = jnp.ones((vt.shape[0], DH), BF16)
    here = slice(g * DH, (g + 1) * DH)
    kt[tile(0), :] = k_ref[:stretch, here]
    vt[tile(0), :DH] = v_ref[:stretch, here]
    kt[tile(count), :] = k_ref[stretch:, here]
    vt[tile(count), :DH] = v_ref[stretch:, here]
    lower = []
    for r, (source, places) in enumerate(arrivals(index, count, refs[:sent])):
        lower.append(source < index)
        for condition, ref in places:

            def fetch(ref=ref, r=r):
                folded = ref.shape[1] > 2 * kv_width
                gap = jnp.where(lower[r], 0, 2 * kv_width if folded else stretch)
                for table, first in ((kt, g * DH), (vt, kv_width + g * DH)):
                    front = ref[:stretch, first : first + DH]
                    if folded:
                        own = ref[:stretch, pl.ds(pl.multiple_of(first + gap, DH), DH)]
                    else:
                        own = ref[pl.ds(pl.multiple_of(gap, stretch), stretch), first : first + DH]
                    table[tile(1 + r), :DH] = own
                    table[tile(count + 1 + r), :DH] = front

            if condition is None:
                fetch()
            else:
                pl.when(condition)(fetch)
        key_f = doc_row(docs_ref, source, stretch).astype(F32)
        key_a = doc_row(docs_ref, jnp.where(lower[r], source, last - source), stretch).astype(F32)
        bias_b[:, tile(2 + r)] = jnp.where(col_b == key_f, 0.0, MASKED)
        bias_a[:, tile(r)] = jnp.where(jnp.where(lower[r], col_f, col_b) == key_a, 0.0, MASKED)

    factor = math.log2(math.e) / math.sqrt(DH)
    tall = stack * stretch
    half_keys = count * stretch

    def stacked(first, base):
        return jnp.concatenate(
            [
                q_ref[base : base + stretch, (g * per + first + j) * DH : (g * per + first + j + 1) * DH]
                for j in range(stack)
            ],
            axis=0,
        )

    def biased(score, bias):
        size = score.shape[1]
        return (score.reshape(stack, stretch, size) + bias[None]).reshape(tall, size)

    for first in range(0, per, stack):
        s_f = dot_nt(stacked(first, 0), kt[:half_keys, :])
        s_b = dot_nt(stacked(first, stretch), kt[...])
        t_f = biased(s_f[:, tile(0)], bias_f[...])
        t_b = [biased(s_b[:, tile(0)], bias_b[:, tile(0)])]
        for k in range(1, count + 1):
            t_b.append(biased(s_b[:, tile(count + k - 1)], bias_b[:, tile(k)]))
        t_a = []
        for r in range(others):
            score = jnp.where(lower[r], s_f[:, tile(1 + r)], s_b[:, tile(1 + r)])
            t_a.append(biased(score, bias_a[:, tile(r)]))
        best_f = t_f
        best_b = functools.reduce(jnp.maximum, t_b)
        for r in range(others):
            best_f = jnp.maximum(best_f, jnp.where(lower[r], t_a[r], MASKED))
            best_b = jnp.maximum(best_b, jnp.where(lower[r], MASKED, t_a[r]))
        top_f = jnp.max(best_f, axis=1, keepdims=True)
        top_b = jnp.max(best_b, axis=1, keepdims=True)
        w_f = [jnp.exp2((t_f - top_f) * factor).astype(BF16)]
        w_b = [jnp.exp2((t - top_b) * factor).astype(BF16) for t in t_b]
        w_x = []
        for r in range(others):
            top = jnp.where(lower[r], top_f, top_b)
            w = jnp.exp2((t_a[r] - top) * factor)
            w_f.append(jnp.where(lower[r], w, 0.0).astype(BF16))
            w_x.append(jnp.where(lower[r], 0.0, w).astype(BF16))
        w_b = w_b[:1] + w_x + w_b[1:]
        out_f = jnp.dot(
            jnp.concatenate(w_f, axis=1), vt[:half_keys, :], preferred_element_type=F32
        )
        out_b = jnp.dot(jnp.concatenate(w_b, axis=1), vt[...], preferred_element_type=F32)
        for half, out in enumerate((out_f, out_b)):
            result = (out[:, :DH] / out[:, DH:]).astype(BF16)
            for j in range(stack):
                cols = slice((first + j) * DH, (first + j + 1) * DH)
                out_ref[tile(half), cols] = result[tile(j)]


def final_kernel(
    count,
    g,
    groups,
    loss_scale,
    pre_ref,
    reach_ref,
    sx_ref,
    c_ref,
    teacher_ref,
    gain_ref,
    f_ref,
    dec_ref,
    *refs,
):
    others = count - 1
    got = refs[:others]
    before = refs[others] if g else None
    proj = slice(g * N, (g + 1) * N)
    first_lane = g * pre_ref.shape[1]
    out_ref, grad_ref, front, back, flow, gated_ref, sums, gain_acc, skip_acc = refs[-9:]
    rows, width = pre_ref.shape
    stretch = rows // 2
    index = lax.axis_index("ctx")
    tile = 128
    step = 16

    @pl.when(index == 0)
    def _():
        front[...] = jnp.zeros_like(front)

    @pl.when(index == count - 1)
    def _():
        back[:N, :] = jnp.zeros((N, width), BF16)
        back[N:, :] = jnp.where(
            lax.broadcasted_iota(jnp.int32, (EXTRA, width), 0) == 0, 1.0, 0.0
        ).astype(BF16)

    for r in range(1, count):

        @pl.when(index == r)
        def _():
            front[...] = got[r - 1][:N, :]

        @pl.when(index == count - 1 - r)
        def _():
            back[...] = got[r - 1][...]

    d_in = back[N : N + 1, :].astype(F32) + back[N + 1 : N + 2, :].astype(F32)
    through = dec_ref[0:1, :] * front[...].astype(F32) + f_ref[...].astype(F32)
    entering = (d_in * through + back[:N, :].astype(F32)).astype(BF16)
    flow[:stretch, :] = jnp.dot(c_ref[:stretch, proj], front[...], preferred_element_type=F32)
    flow[stretch:, :] = jnp.dot(c_ref[stretch:, proj], entering, preferred_element_type=F32)
    gain_acc[...] = jnp.zeros_like(gain_acc)
    skip_acc[...] = jnp.zeros_like(skip_acc)

    @pl.loop(0, rows // step, unroll=2)
    def _(k):
        sl = pl.ds(pl.multiple_of(k * step, step), step)
        totals = [jnp.zeros((step, tile), F32)] * 3
        for j in range(0, width, tile):
            cols = slice(j, j + tile)
            gated = pre_ref[sl, cols] + reach_ref[sl, cols] * flow[sl, cols]
            gated_ref[sl, cols] = gated
            scaled = gated * gain_ref[:, first_lane + j : first_lane + j + tile]
            totals[0] += gated * gated
            totals[1] += scaled * scaled
            totals[2] += scaled * teacher_ref[sl, cols].astype(F32)
        for k3 in range(3):
            sums[sl, k3 * tile : (k3 + 1) * tile] = totals[k3]

    square, weighted, crossed = (
        jnp.sum(sums[:, k3 * tile : (k3 + 1) * tile], axis=1, keepdims=True) * (1.0 / width)
        for k3 in range(3)
    )
    scale = lax.rsqrt(square + EPS)
    push_scale = 2.0 * loss_scale
    mean = push_scale * scale * (scale * weighted - crossed)
    sums[:, :tile] = jnp.broadcast_to(scale, (rows, tile))
    sums[:, tile : 2 * tile] = jnp.broadcast_to(mean, (rows, tile))

    @pl.loop(0, rows // step, unroll=2)
    def _(k):
        sl = pl.ds(pl.multiple_of(k * step, step), step)
        scale = sums[sl, :tile]
        mean = sums[sl, tile : 2 * tile]
        for j in range(0, width, tile):
            cols = slice(j, j + tile)
            gain = gain_ref[:, first_lane + j : first_lane + j + tile]
            unit = gated_ref[sl, cols] * scale
            normed = unit * gain
            out_ref[sl, cols] = normed.astype(BF16)
            push = (normed - teacher_ref[sl, cols].astype(F32)) * push_scale
            by_gain = push * unit
            by_skip = (push * gain - unit * mean) * (scale * sx_ref[sl, cols])
            gain_acc[:, cols] += by_gain[:8] + by_gain[8:]
            skip_acc[:, cols] += by_skip[:8] + by_skip[8:]

    row = lax.broadcasted_iota(jnp.int32, (tile, width), 0)
    lane = lax.broadcasted_iota(jnp.int32, (tile, width), 1)
    matrix = jnp.where(row == lane // P_SIZE + g * (width // P_SIZE), 1.0, 0.0).astype(BF16)
    hi, lo = parts(skip_acc[...])
    by_head = jnp.sum(dot_nt(hi, matrix) + dot_nt(lo, matrix), axis=0, keepdims=True)
    grad_ref[...] = jnp.zeros_like(grad_ref)
    if g:
        grad_ref[:g, :] = before[:g, :]
        by_head += before[groups : groups + 1, :tile]
    grad_ref[g : g + 1, :] = jnp.sum(gain_acc[...], axis=0, keepdims=True)
    grad_ref[groups : groups + 1, :tile] = by_head


def writing_kernel(*refs):
    parts_in, out_ref, sems = refs[:-2], refs[-2], refs[-1]
    width = parts_in[0].shape[1]
    moves = [
        pltpu.make_async_copy(part, out_ref.at[:, pl.ds(k * width, width)], sems.at[k])
        for k, part in enumerate(parts_in)
    ]
    for move in moves:
        move.start()
    for move in moves:
        move.wait()


def closing_kernel(a_ref, b_ref, gain_ref, skip_ref):
    total = a_ref[...] + b_ref[...]
    groups, width = total.shape[0] - 1, total.shape[1]
    for g in range(groups):
        gain_ref[:, g * width : (g + 1) * width] = total[g : g + 1, :]
    skip_ref[...] = total[groups : groups + 1, : skip_ref.shape[1]]


def exchange(part, shift):
    axes = ("dp", "ctx")
    size = lax.axis_size(axes)
    return lax.ppermute(part, axes, [(d, d ^ shift) for d in range(size)])


def body(
    queries,
    keys,
    values,
    doc_ids,
    inputs,
    gate_input,
    b_input,
    c_input,
    dt_raw,
    dt_bias,
    decay_log,
    skip,
    gain,
):
    count = lax.axis_size("ctx")
    rows, features = queries.shape[1:]
    stretch = rows // 2
    kv_dev = keys.shape[2] // DH
    per_kv = queries.shape[2] // keys.shape[2]
    groups = b_input.shape[2] // N
    heads = features // P_SIZE
    width = features // groups
    length = doc_ids.shape[1]
    others = count - 1
    loss_scale = 1.0 / (lax.axis_size("dp") * count * rows)
    x, gate, bmat, cmat = inputs[0], gate_input[0], b_input[0], c_input[0]
    struct = jax.ShapeDtypeStruct

    def in_hbm(*arrays):
        return [pltpu.with_memory_space_constraint(array, pltpu.HBM) for array in arrays]

    def write(*pieces):
        return pl.pallas_call(
            writing_kernel,
            out_shape=struct((rows, features), BF16),
            in_specs=[VMEM] * len(pieces),
            out_specs=pl.BlockSpec(memory_space=pl.ANY),
            scratch_shapes=[pltpu.SemaphoreType.DMA((len(pieces),))],
            compiler_params=params(2),
            cost_estimate=cost(0, 4 * rows * features),
            name="writing",
        )(*pieces)

    state = struct((N, width), BF16)
    payload = struct((N + EXTRA, width), BF16)
    outs = pl.pallas_call(
        functools.partial(opening_kernel, count, groups),
        out_shape=(
            struct((rows, 2 * kv_dev * DH), BF16),
            struct((heads, rows), F32),
            *([struct((rows, width), BF16)] * groups),
            *([struct((8, width), F32)] * groups),
            *([state] * (2 * groups)),
            *([payload] * groups),
        ),
        in_specs=[VMEM] * 3 + [pl.BlockSpec(memory_space=pl.ANY)] + [VMEM] * 4,
        out_specs=(VMEM,) * (2 + 5 * groups),
        scratch_shapes=[
            pltpu.VMEM((groups, rows, width), BF16),
            pltpu.SemaphoreType.DMA((groups,)),
        ],
        compiler_params=params(16),
        cost_estimate=cost(4 * rows * features * N, 8 * rows * features),
        name="opening",
    )(
        *in_hbm(
            doc_ids,
            keys[0],
            values[0],
            x,
            bmat,
            dt_raw[0].T,
            dt_bias.reshape(1, heads),
            decay_log.reshape(1, heads),
        )
    )
    kv, ec = outs[:2]
    xw, dec, f_parts, b_parts, send = (
        outs[2 + k * groups : 2 + (k + 1) * groups] for k in range(5)
    )

    local = pl.pallas_call(
        functools.partial(local_kernel, count, groups),
        out_shape=(struct((rows, width), F32),) * (3 * groups),
        in_specs=[
            VMEM,
            *[pl.BlockSpec(memory_space=pl.ANY)] * 2,
            *[VMEM] * (4 + groups),
        ],
        out_specs=(VMEM,) * (3 * groups),
        scratch_shapes=[
            pltpu.VMEM((groups, rows, width), BF16),
            pltpu.VMEM((groups, rows, width), BF16),
            pltpu.SemaphoreType.DMA((2, groups)),
        ],
        compiler_params=params(16),
        cost_estimate=cost(2 * rows * features * N, 16 * rows * features),
        name="local",
    )(*in_hbm(doc_ids, x, gate, bmat, cmat, skip.reshape(1, heads)), ec, *xw)

    send = list(send)
    got = [[] for _ in range(groups)]
    if count == 4:
        inward, outward, across = [(0, 1), (3, 2)], [(1, 0), (2, 3)], [(1, 2), (2, 1)]
        near = lax.ppermute(kv, "ctx", inward + outward)
        middle = lax.ppermute(kv, "ctx", across)
        middle, *local = lax.optimization_barrier((middle, *local))
        beyond = lax.ppermute(near, "ctx", across)
        send[-1] = pl.pallas_call(
            functools.partial(merge_kernel, count),
            out_shape=payload,
            in_specs=[VMEM] * 2,
            out_specs=VMEM,
            compiler_params=params(4),
            cost_estimate=cost(0, 4 * N * width),
            name="merge",
        )(send[-1], middle)
        far = lax.ppermute(send[-1], "ctx", inward + outward)
        got[-1].append(far)
        farther = lax.ppermute(beyond, "ctx", outward)
        kv_got = [near, middle, beyond, far, farther]
    else:
        ring = ring_order(count)
        ring_pairs = [(ring[d], ring[(d + 1) % count]) for d in range(count)]
        kv_got = [kv]
        for _ in range(others):
            kv_got.append(lax.ppermute(kv_got[-1], "ctx", ring_pairs))
        kv_got = kv_got[1:]
    stack = 4 if per_kv % 4 == 0 and count <= 4 else 1
    targets = [
        pl.pallas_call(
            functools.partial(attention_kernel, count, per_kv, stack, g),
            out_shape=struct((rows, per_kv * DH), BF16),
            in_specs=[VMEM] * (4 + len(kv_got)),
            out_specs=VMEM,
            scratch_shapes=[
                pltpu.VMEM((2 * count * stretch, DH), BF16),
                pltpu.VMEM((2 * count * stretch, 2 * DH), BF16),
                pltpu.VMEM((stretch, stretch), F32),
                pltpu.VMEM((stretch, (count + 1) * stretch), F32),
                pltpu.VMEM((stretch, others * stretch), F32),
            ],
            compiler_params=params(24),
            cost_estimate=cost(
                4 * (2 * count + 1) * stretch * stretch * per_kv * DH, 8 * rows * per_kv * DH
            ),
            name="attention",
        )(doc_ids, queries[0], keys[0], values[0], *kv_got)
        for g in range(kv_dev)
    ]
    for r in range(1, count):
        for g in range(groups):
            if r == 3 and g == groups - 1:
                got[g][-1], targets[0] = lax.optimization_barrier((got[g][-1], targets[0]))
            if r > 1:
                send[g] = pl.pallas_call(
                    functools.partial(chain_kernel, count, r - 1),
                    out_shape=payload,
                    in_specs=[VMEM] * 4,
                    out_specs=VMEM,
                    compiler_params=params(4),
                    cost_estimate=cost(8 * N * width, 8 * N * width),
                    name="chain",
                )(got[g][-1], f_parts[g], b_parts[g], dec[g])
            if len(got[g]) < r:
                pairs = [(r - 1, r), (count - r, count - r - 1)]
                got[g].append(lax.ppermute(send[g], "ctx", pairs))

    normed, grads = [], None
    for g in range(groups):
        more = [] if grads is None else [grads]
        made, grads = pl.pallas_call(
            functools.partial(final_kernel, count, g, groups, loss_scale),
            out_shape=(struct((rows, width), BF16), struct((groups + 1, width), F32)),
            in_specs=[VMEM] * (8 + others + len(more)),
            out_specs=(VMEM,) * 2,
            scratch_shapes=[
                pltpu.VMEM((N, width), BF16),
                pltpu.VMEM((N + EXTRA, width), BF16),
                pltpu.VMEM((rows, width), F32),
                pltpu.VMEM((rows, width), F32),
                pltpu.VMEM((rows, 3 * 128), F32),
                pltpu.VMEM((8, width), F32),
                pltpu.VMEM((8, width), F32),
            ],
            compiler_params=params(16),
            cost_estimate=cost(2 * rows * width * N, 20 * rows * width),
            name="final",
        )(
            *local[g::groups],
            cmat,
            targets[g],
            gain.reshape(1, features),
            f_parts[g],
            dec[g],
            *got[g],
            *more,
        )
        normed.append(made)
    teacher, student = write(*targets), write(*normed)
    partner = exchange(grads, 1)
    if lax.axis_size("dp") == 2:
        grads = (grads + partner) + (exchange(grads, count) + exchange(grads, count + 1))
    else:
        grads = grads + partner
    shifts = [1 << k for k in range(1, count.bit_length() - 1)]
    for shift in shifts[:-1]:
        grads = grads + exchange(grads, shift)
    grad_gain, grad_skip = pl.pallas_call(
        closing_kernel,
        out_shape=(struct((1, features), F32), struct((1, heads), F32)),
        in_specs=[VMEM] * 2,
        out_specs=(VMEM,) * 2,
        compiler_params=params(2),
        name="closing",
    )(grads, exchange(grads, shifts[-1]))
    return (teacher[None], student[None], grad_gain[0], grad_skip[0])


def solution(mesh):
    rows = P("dp", "ctx", "head")
    in_specs = (
        rows,
        rows,
        rows,
        P("dp", None),
        rows,
        rows,
        rows,
        rows,
        rows,
        P("head"),
        P("head"),
        P("head"),
        P("head"),
    )
    out_specs = (rows, rows, P("head"), P("head"))
    return jax.shard_map(body, mesh=mesh, in_specs=in_specs, out_specs=out_specs, check_vma=False)
```

```python
import functools
import math

import jax
import jax.numpy as jnp
from jax import lax
from jax.experimental import pallas as pl
from jax.experimental.pallas import tpu as pltpu
from jax.sharding import PartitionSpec as P

DH = 128
P_SIZE = 64
N = 128
EXTRA = 16
EPS = 1e-05
MASKED = -1e30
F32 = jnp.float32
BF16 = jnp.bfloat16
VMEM = pl.BlockSpec(memory_space=pltpu.VMEM)


def params(mib):
    return pltpu.CompilerParams(vmem_limit_bytes=mib << 20)


def cost(flops, size):
    return pl.CostEstimate(flops=flops, bytes_accessed=size, transcendentals=0)


def parts(v):
    hi = v.astype(BF16)
    return hi, (v - hi.astype(F32)).astype(BF16)


def spread_matrix(heads, width, first):
    row = lax.broadcasted_iota(jnp.int32, (heads, width), 0)
    lane = lax.broadcasted_iota(jnp.int32, (heads, width), 1)
    return jnp.where(row == (lane // P_SIZE) + first, 1.0, 0.0).astype(BF16)


def dot_nt(a, b):
    return lax.dot_general(a, b, (((1,), (1,)), ((), ())), preferred_element_type=F32)


def dot_tn(a, b):
    return lax.dot_general(a, b, (((0,), (0,)), ((), ())), preferred_element_type=F32)


def spread(v, matrix):
    return dot_tn(jnp.concatenate(parts(v), axis=0), jnp.concatenate([matrix, matrix], axis=0))


def doc_row(docs_ref, block, stretch):
    return docs_ref[:, pl.ds(pl.multiple_of(block * stretch, stretch), stretch)]


def as_column(row):
    size = row.shape[1]
    r = lax.broadcasted_iota(jnp.int32, (size, size), 0)
    c = lax.broadcasted_iota(jnp.int32, (size, size), 1)
    return jnp.sum(jnp.where(r == c, row.astype(F32), 0.0), axis=1, keepdims=True)


def lower_triangle(size):
    r = lax.broadcasted_iota(jnp.int32, (size, size), 0)
    c = lax.broadcasted_iota(jnp.int32, (size, size), 1)
    return r >= c


def prior_doc(docs_ref, block, stretch):
    before = doc_row(docs_ref, jnp.maximum(block - 1, 0), stretch)[:, stretch - 1 :]
    return jnp.where(block > 0, before, -1)


def own_block(index, count, half):
    return index if half == 0 else 2 * count - 1 - index


def ring_order(count):
    return [0] + list(range(1, count, 2)) + list(range(2, count, 2))[::-1]


def ring_source(index, count, steps):
    order = ring_order(count)
    source = jnp.int32(0)
    for place, member in enumerate(order):
        source = jnp.where(index == member, order[(place - steps) % count], source)
    return source


def put_state(ref, state):
    ref[:N, :] = state.astype(BF16)
    ref[N:, :] = jnp.zeros((EXTRA, ref.shape[1]), BF16)


def put_composite(ref, state, decay):
    hi, lo = parts(decay)
    ref[:N, :] = state.astype(BF16)
    ref[N:, :] = jnp.concatenate(
        [hi, lo, jnp.zeros((EXTRA - 2, ref.shape[1]), BF16)], axis=0
    )


def opening_kernel(
    count,
    groups,
    docs_ref,
    x_ref,
    b_ref,
    dt_ref,
    bias_ref,
    log_ref,
    ec_ref,
    *outs,
):
    xw_refs, dec_refs, f_refs, b_refs, send_refs = (
        outs[k * groups : (k + 1) * groups] for k in range(5)
    )
    heads, rows = dt_ref.shape
    stretch = rows // 2
    width = x_ref.shape[1] // groups
    index = lax.axis_index("ctx")
    triangle = jnp.where(lower_triangle(stretch), 1.0, 0.0)
    slope = jnp.exp(as_column(log_ref[...]))
    bias = as_column(bias_ref[...])
    lane = lax.broadcasted_iota(jnp.int32, (heads, 8), 1)
    ends = jnp.zeros((heads, 8), F32)
    loads = []
    projs = []
    for half in range(2):
        block = own_block(index, count, half)
        sl = slice(half * stretch, (half + 1) * stretch)
        raw = dt_ref[:, sl] + bias
        dt = jnp.maximum(raw, 0.0) + jnp.log1p(jnp.exp(-jnp.abs(raw)))
        cum = lax.dot_general(
            -dt * slope,
            triangle,
            (((1,), (1,)), ((), ())),
            precision=lax.Precision.HIGHEST,
            preferred_element_type=F32,
        )
        ec_ref[:, sl] = jnp.exp(cum)
        loads.append(jnp.exp(-cum) * dt)
        final = jnp.exp(cum[:, stretch - 1 :])
        row = doc_row(docs_ref, block, stretch)
        last = row[:, stretch - 1 :]
        kept = jnp.where(last == prior_doc(docs_ref, block, stretch), 1.0, 0.0)
        ends = jnp.where(lane == half, final * kept, ends)
        ends = jnp.where(lane == 2 + half, final, ends)
        same = jnp.where(as_column(row) == last.astype(F32), 1.0, 0.0)
        projs.append((b_ref[sl, :].astype(F32) * same).astype(BF16))
    for g in range(groups):
        cols = slice(g * width, (g + 1) * width)
        matrix = spread_matrix(heads, width, g * (heads // groups))
        wide = spread(ends, matrix)
        dec_refs[g][...] = wide
        sums = []
        for half in range(2):
            sl = slice(half * stretch, (half + 1) * stretch)
            xw = (x_ref[sl, cols].astype(F32) * spread(loads[half], matrix)).astype(BF16)
            xw_refs[g][sl, :] = xw
            sums.append(dot_tn(projs[half][:, g * N : (g + 1) * N], xw) * wide[2 + half : 3 + half])
        f_refs[g][...] = sums[0].astype(BF16)
        b_refs[g][...] = sums[1].astype(BF16)

        @pl.when(index == 0)
        def _():
            put_state(send_refs[g], sums[0])

        @pl.when(index != 0)
        def _():
            put_composite(send_refs[g], wide[1:2] * sums[0] + sums[1], wide[0:1] * wide[1:2])


def pack_kernel(k_ref, v_ref, kv_ref):
    width = k_ref.shape[1]
    kv_ref[:, :width] = k_ref[...]
    kv_ref[:, width:] = v_ref[...]


def chain_kernel(count, stage, got_ref, f_ref, b_ref, dec_ref, send_ref):
    index = lax.axis_index("ctx")

    @pl.when(index == stage)
    def _():
        state = dec_ref[0:1, :] * got_ref[:N, :].astype(F32) + f_ref[...].astype(F32)
        put_state(send_ref, state)

    @pl.when(index == count - 1 - stage)
    def _():
        decay = got_ref[N : N + 1, :].astype(F32) + got_ref[N + 1 : N + 2, :].astype(F32)
        inner = decay * f_ref[...].astype(F32) + got_ref[:N, :].astype(F32)
        state = dec_ref[1:2, :] * inner + b_ref[...].astype(F32)
        put_composite(send_ref, state, dec_ref[1:2, :] * decay * dec_ref[0:1, :])


def local_kernel(
    count, groups, docs_ref, x_ref, gate_ref, b_ref, c_ref, skip_ref, ec_ref, *refs
):
    xw_refs, pre_refs, reach_refs, sx_refs = (
        refs[k * groups : (k + 1) * groups] for k in range(4)
    )
    x_here, gate_here, sems = refs[4 * groups :]
    heads, rows = ec_ref.shape
    stretch = rows // 2
    width = x_ref.shape[1] // groups
    index = lax.axis_index("ctx")
    moves = []
    for g in range(groups):
        cols = pl.ds(g * width, width)
        moves.append(
            [
                pltpu.make_async_copy(x_ref.at[:, cols], x_here.at[g], sems.at[0, g]),
                pltpu.make_async_copy(gate_ref.at[:, cols], gate_here.at[g], sems.at[1, g]),
            ]
        )
        for move in moves[g]:
            move.start()
    triangle = lower_triangle(stretch)
    skip = as_column(skip_ref[...])
    step = 16
    masks = []
    for half in range(2):
        block = own_block(index, count, half)
        row = doc_row(docs_ref, block, stretch)
        column = as_column(row)
        reached = jnp.where(column == prior_doc(docs_ref, block, stretch).astype(F32), 1.0, 0.0)
        masks.append((triangle & (column == row.astype(F32)), reached))
    for g in range(groups):
        proj = slice(g * N, (g + 1) * N)
        matrix = spread_matrix(heads, width, g * (heads // groups))
        wide_skip = spread(skip, matrix)
        for half in range(2):
            sl = slice(half * stretch, (half + 1) * stretch)
            near, reached = masks[half]
            gram = dot_nt(c_ref[sl, proj], b_ref[sl, proj])
            gram = jnp.where(near, gram, 0.0).astype(BF16)
            wide = spread(ec_ref[:, sl], matrix)
            inner = jnp.dot(gram, xw_refs[g][sl, :], preferred_element_type=F32)
            if half == 0:
                for move in moves[g]:
                    move.wait()
            for k in range(0, stretch, step):
                at = slice(half * stretch + k, half * stretch + k + step)
                here = slice(k, k + step)
                x = x_here[g, at, :].astype(F32)
                gate = gate_here[g, at, :].astype(F32)
                silu = gate / (1.0 + jnp.exp(-gate))
                fade = wide[here] * silu
                sx = silu * x
                sx_refs[g][at, :] = sx
                pre_refs[g][at, :] = inner[here] * fade + wide_skip * sx
                reach_refs[g][at, :] = reached[here] * fade


def merge_kernel(count, state_ref, kv_ref, out_ref):
    index = lax.axis_index("ctx")
    outer = (index == 0) | (index == count - 1)
    rows, wide = kv_ref.shape
    stretch = rows // 2

    @pl.when(outer)
    def _():
        out_ref[...] = state_ref[...]

    @pl.when(jnp.logical_not(outer))
    def _():
        out_ref[:stretch, :wide] = kv_ref[:stretch, :]
        out_ref[:stretch, wide:] = kv_ref[stretch:, :]
        out_ref[stretch:, :] = jnp.zeros((out_ref.shape[0] - stretch, 2 * wide), BF16)


def arrivals(index, count, refs):
    if count != 4:
        return [(ring_source(index, count, r + 1), [(None, refs[r])]) for r in range(count - 1)]
    near, own_of_middle, next_of_middle, far, farther = refs
    middle = (index == 1) | (index == 2)
    low = index < 2
    return [
        (index ^ 1, [(None, near)]),
        (
            jnp.where(low, 2, 1),
            [(middle, own_of_middle), (jnp.logical_not(middle), far)],
        ),
        (
            jnp.where(low, 3, 0),
            [(middle, next_of_middle), (jnp.logical_not(middle), farther)],
        ),
    ]


def attention_kernel(count, per, stack, g, docs_ref, q_ref, k_ref, v_ref, *refs):
    others = count - 1
    sent = 5 if count == 4 else others
    out_ref, kt, vt, bias_f, bias_b, bias_a = refs[-6:]
    rows = q_ref.shape[0]
    stretch = rows // 2
    index = lax.axis_index("ctx")
    last = 2 * count - 1
    kv_width = refs[0].shape[1] // 2
    row_f = doc_row(docs_ref, index, stretch).astype(F32)
    row_b = doc_row(docs_ref, last - index, stretch).astype(F32)
    col_f = as_column(row_f)
    col_b = as_column(row_b)
    triangle = lower_triangle(stretch)

    def tile(k):
        return slice(k * stretch, (k + 1) * stretch)

    bias_f[...] = jnp.where(triangle & (col_f == row_f), 0.0, MASKED)
    bias_b[:, tile(0)] = jnp.where(col_b == row_f, 0.0, MASKED)
    bias_b[:, tile(1)] = jnp.where(triangle & (col_b == row_b), 0.0, MASKED)
    vt[:, DH:] = jnp.ones((vt.shape[0], DH), BF16)
    here = slice(g * DH, (g + 1) * DH)
    kt[tile(0), :] = k_ref[:stretch, here]
    vt[tile(0), :DH] = v_ref[:stretch, here]
    kt[tile(count), :] = k_ref[stretch:, here]
    vt[tile(count), :DH] = v_ref[stretch:, here]
    lower = []
    for r, (source, places) in enumerate(arrivals(index, count, refs[:sent])):
        lower.append(source < index)
        for condition, ref in places:

            def fetch(ref=ref, r=r):
                folded = ref.shape[1] > 2 * kv_width
                gap = jnp.where(lower[r], 0, 2 * kv_width if folded else stretch)
                for table, first in ((kt, g * DH), (vt, kv_width + g * DH)):
                    front = ref[:stretch, first : first + DH]
                    if folded:
                        own = ref[:stretch, pl.ds(pl.multiple_of(first + gap, DH), DH)]
                    else:
                        own = ref[pl.ds(pl.multiple_of(gap, stretch), stretch), first : first + DH]
                    table[tile(1 + r), :DH] = own
                    table[tile(count + 1 + r), :DH] = front

            if condition is None:
                fetch()
            else:
                pl.when(condition)(fetch)
        key_f = doc_row(docs_ref, source, stretch).astype(F32)
        key_a = doc_row(docs_ref, jnp.where(lower[r], source, last - source), stretch).astype(F32)
        bias_b[:, tile(2 + r)] = jnp.where(col_b == key_f, 0.0, MASKED)
        bias_a[:, tile(r)] = jnp.where(jnp.where(lower[r], col_f, col_b) == key_a, 0.0, MASKED)

    factor = math.log2(math.e) / math.sqrt(DH)
    tall = stack * stretch
    half_keys = count * stretch

    def stacked(first, base):
        return jnp.concatenate(
            [
                q_ref[base : base + stretch, (g * per + first + j) * DH : (g * per + first + j + 1) * DH]
                for j in range(stack)
            ],
            axis=0,
        )

    def biased(score, bias):
        size = score.shape[1]
        return (score.reshape(stack, stretch, size) + bias[None]).reshape(tall, size)

    for first in range(0, per, stack):
        s_f = dot_nt(stacked(first, 0), kt[:half_keys, :])
        s_b = dot_nt(stacked(first, stretch), kt[...])
        t_f = biased(s_f[:, tile(0)], bias_f[...])
        t_b = [biased(s_b[:, tile(0)], bias_b[:, tile(0)])]
        for k in range(1, count + 1):
            t_b.append(biased(s_b[:, tile(count + k - 1)], bias_b[:, tile(k)]))
        t_a = []
        for r in range(others):
            score = jnp.where(lower[r], s_f[:, tile(1 + r)], s_b[:, tile(1 + r)])
            t_a.append(biased(score, bias_a[:, tile(r)]))
        best_f = t_f
        best_b = functools.reduce(jnp.maximum, t_b)
        for r in range(others):
            best_f = jnp.maximum(best_f, jnp.where(lower[r], t_a[r], MASKED))
            best_b = jnp.maximum(best_b, jnp.where(lower[r], MASKED, t_a[r]))
        top_f = jnp.max(best_f, axis=1, keepdims=True)
        top_b = jnp.max(best_b, axis=1, keepdims=True)
        w_f = [jnp.exp2((t_f - top_f) * factor).astype(BF16)]
        w_b = [jnp.exp2((t - top_b) * factor).astype(BF16) for t in t_b]
        w_x = []
        for r in range(others):
            top = jnp.where(lower[r], top_f, top_b)
            w = jnp.exp2((t_a[r] - top) * factor)
            w_f.append(jnp.where(lower[r], w, 0.0).astype(BF16))
            w_x.append(jnp.where(lower[r], 0.0, w).astype(BF16))
        w_b = w_b[:1] + w_x + w_b[1:]
        out_f = jnp.dot(
            jnp.concatenate(w_f, axis=1), vt[:half_keys, :], preferred_element_type=F32
        )
        out_b = jnp.dot(jnp.concatenate(w_b, axis=1), vt[...], preferred_element_type=F32)
        for half, out in enumerate((out_f, out_b)):
            result = (out[:, :DH] / out[:, DH:]).astype(BF16)
            for j in range(stack):
                cols = slice((first + j) * DH, (first + j + 1) * DH)
                out_ref[tile(half), cols] = result[tile(j)]


def final_kernel(
    count,
    g,
    groups,
    loss_scale,
    pre_ref,
    reach_ref,
    sx_ref,
    c_ref,
    teacher_ref,
    gain_ref,
    f_ref,
    dec_ref,
    *refs,
):
    others = count - 1
    got = refs[:others]
    before = refs[others] if g else None
    proj = slice(g * N, (g + 1) * N)
    first_lane = g * pre_ref.shape[1]
    out_ref, grad_ref, front, back, flow, gated_ref, sums, gain_acc, skip_acc = refs[-9:]
    rows, width = pre_ref.shape
    stretch = rows // 2
    index = lax.axis_index("ctx")
    tile = 128
    step = 16

    @pl.when(index == 0)
    def _():
        front[...] = jnp.zeros_like(front)

    @pl.when(index == count - 1)
    def _():
        back[:N, :] = jnp.zeros((N, width), BF16)
        back[N:, :] = jnp.where(
            lax.broadcasted_iota(jnp.int32, (EXTRA, width), 0) == 0, 1.0, 0.0
        ).astype(BF16)

    for r in range(1, count):

        @pl.when(index == r)
        def _():
            front[...] = got[r - 1][:N, :]

        @pl.when(index == count - 1 - r)
        def _():
            back[...] = got[r - 1][...]

    d_in = back[N : N + 1, :].astype(F32) + back[N + 1 : N + 2, :].astype(F32)
    through = dec_ref[0:1, :] * front[...].astype(F32) + f_ref[...].astype(F32)
    entering = (d_in * through + back[:N, :].astype(F32)).astype(BF16)
    flow[:stretch, :] = jnp.dot(c_ref[:stretch, proj], front[...], preferred_element_type=F32)
    flow[stretch:, :] = jnp.dot(c_ref[stretch:, proj], entering, preferred_element_type=F32)
    gain_acc[...] = jnp.zeros_like(gain_acc)
    skip_acc[...] = jnp.zeros_like(skip_acc)

    @pl.loop(0, rows // step, unroll=2)
    def _(k):
        sl = pl.ds(pl.multiple_of(k * step, step), step)
        totals = [jnp.zeros((step, tile), F32)] * 3
        for j in range(0, width, tile):
            cols = slice(j, j + tile)
            gated = pre_ref[sl, cols] + reach_ref[sl, cols] * flow[sl, cols]
            gated_ref[sl, cols] = gated
            scaled = gated * gain_ref[:, first_lane + j : first_lane + j + tile]
            totals[0] += gated * gated
            totals[1] += scaled * scaled
            totals[2] += scaled * teacher_ref[sl, cols].astype(F32)
        for k3 in range(3):
            sums[sl, k3 * tile : (k3 + 1) * tile] = totals[k3]

    square, weighted, crossed = (
        jnp.sum(sums[:, k3 * tile : (k3 + 1) * tile], axis=1, keepdims=True) * (1.0 / width)
        for k3 in range(3)
    )
    scale = lax.rsqrt(square + EPS)
    push_scale = 2.0 * loss_scale
    mean = push_scale * scale * (scale * weighted - crossed)
    sums[:, :tile] = jnp.broadcast_to(scale, (rows, tile))
    sums[:, tile : 2 * tile] = jnp.broadcast_to(mean, (rows, tile))

    @pl.loop(0, rows // step, unroll=2)
    def _(k):
        sl = pl.ds(pl.multiple_of(k * step, step), step)
        scale = sums[sl, :tile]
        mean = sums[sl, tile : 2 * tile]
        for j in range(0, width, tile):
            cols = slice(j, j + tile)
            gain = gain_ref[:, first_lane + j : first_lane + j + tile]
            unit = gated_ref[sl, cols] * scale
            normed = unit * gain
            out_ref[sl, cols] = normed.astype(BF16)
            push = (normed - teacher_ref[sl, cols].astype(F32)) * push_scale
            by_gain = push * unit
            by_skip = (push * gain - unit * mean) * (scale * sx_ref[sl, cols])
            gain_acc[:, cols] += by_gain[:8] + by_gain[8:]
            skip_acc[:, cols] += by_skip[:8] + by_skip[8:]

    row = lax.broadcasted_iota(jnp.int32, (tile, width), 0)
    lane = lax.broadcasted_iota(jnp.int32, (tile, width), 1)
    matrix = jnp.where(row == lane // P_SIZE + g * (width // P_SIZE), 1.0, 0.0).astype(BF16)
    hi, lo = parts(skip_acc[...])
    by_head = jnp.sum(dot_nt(hi, matrix) + dot_nt(lo, matrix), axis=0, keepdims=True)
    by_lane = jnp.sum(gain_acc[...], axis=0, keepdims=True)
    if g:
        by_head += before[0, groups : groups + 1, :tile]
    for d in range(grad_ref.shape[0]):
        if g:
            grad_ref[d, :g, :] = before[0, :g, :]
        grad_ref[d, g : g + 1, :] = by_lane
        grad_ref[d, groups : groups + 1, :] = jnp.zeros((1, width), F32)
        grad_ref[d, groups : groups + 1, :tile] = by_head


def writing_kernel(*refs):
    parts_in, out_ref, sems = refs[:-2], refs[-2], refs[-1]
    width = parts_in[0].shape[1]
    moves = [
        pltpu.make_async_copy(part, out_ref.at[:, pl.ds(k * width, width)], sems.at[k])
        for k, part in enumerate(parts_in)
    ]
    for move in moves:
        move.start()
    for move in moves:
        move.wait()


def closing_kernel(all_ref, gain_ref, skip_ref):
    total = all_ref[0]
    for d in range(1, all_ref.shape[0]):
        total += all_ref[d]
    groups, width = total.shape[0] - 1, total.shape[1]
    for g in range(groups):
        gain_ref[:, g * width : (g + 1) * width] = total[g : g + 1, :]
    skip_ref[...] = total[groups : groups + 1, : skip_ref.shape[1]]


def body(
    queries,
    keys,
    values,
    doc_ids,
    inputs,
    gate_input,
    b_input,
    c_input,
    dt_raw,
    dt_bias,
    decay_log,
    skip,
    gain,
):
    count = lax.axis_size("ctx")
    rows, features = queries.shape[1:]
    stretch = rows // 2
    kv_dev = keys.shape[2] // DH
    per_kv = queries.shape[2] // keys.shape[2]
    groups = b_input.shape[2] // N
    heads = features // P_SIZE
    width = features // groups
    length = doc_ids.shape[1]
    others = count - 1
    members = lax.axis_size("dp") * count
    loss_scale = 1.0 / (lax.axis_size("dp") * count * rows)
    x, gate, bmat, cmat = inputs[0], gate_input[0], b_input[0], c_input[0]
    struct = jax.ShapeDtypeStruct

    def in_hbm(*arrays):
        return [pltpu.with_memory_space_constraint(array, pltpu.HBM) for array in arrays]

    def write(*pieces):
        return pl.pallas_call(
            writing_kernel,
            out_shape=struct((rows, features), BF16),
            in_specs=[VMEM] * len(pieces),
            out_specs=pl.BlockSpec(memory_space=pl.ANY),
            scratch_shapes=[pltpu.SemaphoreType.DMA((len(pieces),))],
            compiler_params=params(2),
            cost_estimate=cost(0, 4 * rows * features),
            name="writing",
        )(*pieces)

    state = struct((N, width), BF16)
    payload = struct((N + EXTRA, width), BF16)
    outs = pl.pallas_call(
        functools.partial(opening_kernel, count, groups),
        out_shape=(
            struct((heads, rows), F32),
            *([struct((rows, width), BF16)] * groups),
            *([struct((8, width), F32)] * groups),
            *([state] * (2 * groups)),
            *([payload] * groups),
        ),
        in_specs=[VMEM] * 6,
        out_specs=(VMEM,) * (1 + 5 * groups),
        compiler_params=params(16),
        cost_estimate=cost(4 * rows * features * N, 8 * rows * features),
        name="opening",
    )(
        *in_hbm(
            doc_ids,
            x,
            bmat,
            dt_raw[0].T,
            dt_bias.reshape(1, heads),
            decay_log.reshape(1, heads),
        )
    )
    ec = outs[0]
    xw, dec, f_parts, b_parts, send = (
        outs[1 + k * groups : 1 + (k + 1) * groups] for k in range(5)
    )
    key_part, value_part, _ = lax.optimization_barrier((keys[0], values[0], ec))
    kv = pl.pallas_call(
        pack_kernel,
        out_shape=struct((rows, 2 * kv_dev * DH), BF16),
        in_specs=[VMEM] * 2,
        out_specs=VMEM,
        compiler_params=params(4),
        cost_estimate=cost(0, 8 * keys.size),
        name="pack",
    )(key_part, value_part)

    local = pl.pallas_call(
        functools.partial(local_kernel, count, groups),
        out_shape=(struct((rows, width), F32),) * (3 * groups),
        in_specs=[
            VMEM,
            *[pl.BlockSpec(memory_space=pl.ANY)] * 2,
            *[VMEM] * (4 + groups),
        ],
        out_specs=(VMEM,) * (3 * groups),
        scratch_shapes=[
            pltpu.VMEM((groups, rows, width), BF16),
            pltpu.VMEM((groups, rows, width), BF16),
            pltpu.SemaphoreType.DMA((2, groups)),
        ],
        compiler_params=params(16),
        cost_estimate=cost(2 * rows * features * N, 16 * rows * features),
        name="local",
    )(*in_hbm(doc_ids, x, gate, bmat, cmat, skip.reshape(1, heads)), ec, *xw)

    send = list(send)
    got = [[] for _ in range(groups)]
    if count == 4:
        inward, outward, across = [(0, 1), (3, 2)], [(1, 0), (2, 3)], [(1, 2), (2, 1)]
        near = lax.ppermute(kv, "ctx", inward + outward)
        middle = lax.ppermute(kv, "ctx", across)
        middle, *local = lax.optimization_barrier((middle, *local))
        beyond = lax.ppermute(near, "ctx", across)
        send[-1] = pl.pallas_call(
            functools.partial(merge_kernel, count),
            out_shape=payload,
            in_specs=[VMEM] * 2,
            out_specs=VMEM,
            compiler_params=params(4),
            cost_estimate=cost(0, 4 * N * width),
            name="merge",
        )(send[-1], middle)
        far = lax.ppermute(send[-1], "ctx", inward + outward)
        got[-1].append(far)
        farther = lax.ppermute(beyond, "ctx", outward)
        kv_got = [near, middle, beyond, far, farther]
    else:
        ring = ring_order(count)
        ring_pairs = [(ring[d], ring[(d + 1) % count]) for d in range(count)]
        kv_got = [kv]
        for _ in range(others):
            kv_got.append(lax.ppermute(kv_got[-1], "ctx", ring_pairs))
        kv_got = kv_got[1:]
    stack = 4 if per_kv % 4 == 0 and count <= 4 else 1
    targets = [
        pl.pallas_call(
            functools.partial(attention_kernel, count, per_kv, stack, g),
            out_shape=struct((rows, per_kv * DH), BF16),
            in_specs=[VMEM] * (4 + len(kv_got)),
            out_specs=VMEM,
            scratch_shapes=[
                pltpu.VMEM((2 * count * stretch, DH), BF16),
                pltpu.VMEM((2 * count * stretch, 2 * DH), BF16),
                pltpu.VMEM((stretch, stretch), F32),
                pltpu.VMEM((stretch, (count + 1) * stretch), F32),
                pltpu.VMEM((stretch, others * stretch), F32),
            ],
            compiler_params=params(24),
            cost_estimate=cost(
                4 * (2 * count + 1) * stretch * stretch * per_kv * DH, 8 * rows * per_kv * DH
            ),
            name="attention",
        )(doc_ids, queries[0], keys[0], values[0], *kv_got)
        for g in range(kv_dev)
    ]
    for r in range(1, count):
        for g in range(groups):
            if r > 1:
                send[g] = pl.pallas_call(
                    functools.partial(chain_kernel, count, r - 1),
                    out_shape=payload,
                    in_specs=[VMEM] * 4,
                    out_specs=VMEM,
                    compiler_params=params(4),
                    cost_estimate=cost(16384 * N * width, 8 * N * width),
                    name="chain",
                )(got[g][-1], f_parts[g], b_parts[g], dec[g])
            if len(got[g]) < r:
                pairs = [(r - 1, r), (count - r, count - r - 1)]
                got[g].append(lax.ppermute(send[g], "ctx", pairs))

    normed, grads = [], None
    for g in range(groups):
        more = [] if grads is None else [grads]
        made, grads = pl.pallas_call(
            functools.partial(final_kernel, count, g, groups, loss_scale),
            out_shape=(
                struct((rows, width), BF16),
                struct((members if g == groups - 1 else 1, groups + 1, width), F32),
            ),
            in_specs=[VMEM] * (8 + others + len(more)),
            out_specs=(VMEM,) * 2,
            scratch_shapes=[
                pltpu.VMEM((N, width), BF16),
                pltpu.VMEM((N + EXTRA, width), BF16),
                pltpu.VMEM((rows, width), F32),
                pltpu.VMEM((rows, width), F32),
                pltpu.VMEM((rows, 3 * 128), F32),
                pltpu.VMEM((8, width), F32),
                pltpu.VMEM((8, width), F32),
            ],
            compiler_params=params(16),
            cost_estimate=cost(2 * rows * width * N, 20 * rows * width),
            name="final",
        )(
            *local[g::groups],
            cmat,
            targets[g],
            gain.reshape(1, features),
            f_parts[g],
            dec[g],
            *got[g],
            *more,
        )
        normed.append(made)
    teacher, student = write(*targets), write(*normed)
    gathered = lax.all_to_all(grads, ("dp", "ctx"), 0, 0)
    grad_gain, grad_skip = pl.pallas_call(
        closing_kernel,
        out_shape=(struct((1, features), F32), struct((1, heads), F32)),
        in_specs=[VMEM],
        out_specs=(VMEM,) * 2,
        compiler_params=params(4),
        name="closing",
    )(gathered)
    return (teacher[None], student[None], grad_gain[0], grad_skip[0])


def solution(mesh):
    rows = P("dp", "ctx", "head")
    in_specs = (
        rows,
        rows,
        rows,
        P("dp", None),
        rows,
        rows,
        rows,
        rows,
        rows,
        P("head"),
        P("head"),
        P("head"),
        P("head"),
    )
    out_specs = (rows, rows, P("head"), P("head"))
    return jax.shard_map(body, mesh=mesh, in_specs=in_specs, out_specs=out_specs, check_vma=False)
```

```python
import functools
import math

import jax
import jax.numpy as jnp
from jax import lax
from jax.experimental import pallas as pl
from jax.experimental.pallas import tpu as pltpu
from jax.sharding import PartitionSpec as P

DH = 128
P_SIZE = 64
N = 128
EXTRA = 16
EPS = 1e-05
MASKED = -1e30
F32 = jnp.float32
BF16 = jnp.bfloat16
VMEM = pl.BlockSpec(memory_space=pltpu.VMEM)


def params(mib):
    return pltpu.CompilerParams(vmem_limit_bytes=mib << 20)


def cost(flops, size):
    return pl.CostEstimate(flops=flops, bytes_accessed=size, transcendentals=0)


def parts(v):
    hi = v.astype(BF16)
    return hi, (v - hi.astype(F32)).astype(BF16)


def spread_matrix(heads, width, first):
    row = lax.broadcasted_iota(jnp.int32, (heads, width), 0)
    lane = lax.broadcasted_iota(jnp.int32, (heads, width), 1)
    return jnp.where(row == (lane // P_SIZE) + first, 1.0, 0.0).astype(BF16)


def dot_nt(a, b):
    return lax.dot_general(a, b, (((1,), (1,)), ((), ())), preferred_element_type=F32)


def dot_tn(a, b):
    return lax.dot_general(a, b, (((0,), (0,)), ((), ())), preferred_element_type=F32)


def spread(v, matrix):
    return dot_tn(jnp.concatenate(parts(v), axis=0), jnp.concatenate([matrix, matrix], axis=0))


def doc_row(docs_ref, block, stretch):
    return docs_ref[:, pl.ds(pl.multiple_of(block * stretch, stretch), stretch)]


def as_column(row):
    size = row.shape[1]
    r = lax.broadcasted_iota(jnp.int32, (size, size), 0)
    c = lax.broadcasted_iota(jnp.int32, (size, size), 1)
    return jnp.sum(jnp.where(r == c, row.astype(F32), 0.0), axis=1, keepdims=True)


def lower_triangle(size):
    r = lax.broadcasted_iota(jnp.int32, (size, size), 0)
    c = lax.broadcasted_iota(jnp.int32, (size, size), 1)
    return r >= c


def prior_doc(docs_ref, block, stretch):
    before = doc_row(docs_ref, jnp.maximum(block - 1, 0), stretch)[:, stretch - 1 :]
    return jnp.where(block > 0, before, -1)


def own_block(index, count, half):
    return index if half == 0 else 2 * count - 1 - index


def ring_order(count):
    return [0] + list(range(1, count, 2)) + list(range(2, count, 2))[::-1]


def ring_source(index, count, steps):
    order = ring_order(count)
    source = jnp.int32(0)
    for place, member in enumerate(order):
        source = jnp.where(index == member, order[(place - steps) % count], source)
    return source


def put_state(ref, state):
    ref[:N, :] = state.astype(BF16)
    ref[N:, :] = jnp.zeros((EXTRA, ref.shape[1]), BF16)


def put_composite(ref, state, decay):
    hi, lo = parts(decay)
    ref[:N, :] = state.astype(BF16)
    ref[N:, :] = jnp.concatenate(
        [hi, lo, jnp.zeros((EXTRA - 2, ref.shape[1]), BF16)], axis=0
    )


def opening_kernel(
    count,
    groups,
    docs_ref,
    x_ref,
    b_ref,
    dt_ref,
    bias_ref,
    log_ref,
    ec_ref,
    *outs,
):
    xw_refs, dec_refs, f_refs, b_refs, send_refs = (
        outs[k * groups : (k + 1) * groups] for k in range(5)
    )
    heads, rows = dt_ref.shape
    stretch = rows // 2
    width = x_ref.shape[1] // groups
    index = lax.axis_index("ctx")
    triangle = jnp.where(lower_triangle(stretch), 1.0, 0.0)
    slope = jnp.exp(as_column(log_ref[...]))
    bias = as_column(bias_ref[...])
    lane = lax.broadcasted_iota(jnp.int32, (heads, 8), 1)
    ends = jnp.zeros((heads, 8), F32)
    loads = []
    projs = []
    for half in range(2):
        block = own_block(index, count, half)
        sl = slice(half * stretch, (half + 1) * stretch)
        raw = dt_ref[:, sl] + bias
        dt = jnp.maximum(raw, 0.0) + jnp.log1p(jnp.exp(-jnp.abs(raw)))
        cum = lax.dot_general(
            -dt * slope,
            triangle,
            (((1,), (1,)), ((), ())),
            precision=lax.Precision.HIGHEST,
            preferred_element_type=F32,
        )
        ec_ref[:, sl] = jnp.exp(cum)
        loads.append(jnp.exp(-cum) * dt)
        final = jnp.exp(cum[:, stretch - 1 :])
        row = doc_row(docs_ref, block, stretch)
        last = row[:, stretch - 1 :]
        kept = jnp.where(last == prior_doc(docs_ref, block, stretch), 1.0, 0.0)
        ends = jnp.where(lane == half, final * kept, ends)
        ends = jnp.where(lane == 2 + half, final, ends)
        same = jnp.where(as_column(row) == last.astype(F32), 1.0, 0.0)
        projs.append((b_ref[sl, :].astype(F32) * same).astype(BF16))
    for g in range(groups):
        cols = slice(g * width, (g + 1) * width)
        matrix = spread_matrix(heads, width, g * (heads // groups))
        wide = spread(ends, matrix)
        dec_refs[g][...] = wide
        sums = []
        for half in range(2):
            sl = slice(half * stretch, (half + 1) * stretch)
            xw = (x_ref[sl, cols].astype(F32) * spread(loads[half], matrix)).astype(BF16)
            xw_refs[g][sl, :] = xw
            sums.append(dot_tn(projs[half][:, g * N : (g + 1) * N], xw) * wide[2 + half : 3 + half])
        f_refs[g][...] = sums[0].astype(BF16)
        b_refs[g][...] = sums[1].astype(BF16)

        @pl.when(index == 0)
        def _():
            put_state(send_refs[g], sums[0])

        @pl.when(index != 0)
        def _():
            put_composite(send_refs[g], wide[1:2] * sums[0] + sums[1], wide[0:1] * wide[1:2])


def pack_kernel(k_ref, v_ref, kv_ref):
    width = k_ref.shape[1]
    kv_ref[:, :width] = k_ref[...]
    kv_ref[:, width:] = v_ref[...]


def chain_kernel(count, stage, got_ref, f_ref, b_ref, dec_ref, send_ref):
    index = lax.axis_index("ctx")

    @pl.when(index == stage)
    def _():
        state = dec_ref[0:1, :] * got_ref[:N, :].astype(F32) + f_ref[...].astype(F32)
        put_state(send_ref, state)

    @pl.when(index == count - 1 - stage)
    def _():
        decay = got_ref[N : N + 1, :].astype(F32) + got_ref[N + 1 : N + 2, :].astype(F32)
        inner = decay * f_ref[...].astype(F32) + got_ref[:N, :].astype(F32)
        state = dec_ref[1:2, :] * inner + b_ref[...].astype(F32)
        put_composite(send_ref, state, dec_ref[1:2, :] * decay * dec_ref[0:1, :])


def local_kernel(
    count,
    groups,
    g,
    docs_ref,
    x_ref,
    gate_ref,
    b_ref,
    c_ref,
    skip_ref,
    ec_ref,
    xw_ref,
    pre_ref,
    reach_ref,
    sx_ref,
    x_here,
    gate_here,
    sems,
):
    heads, rows = ec_ref.shape
    stretch = rows // 2
    width = x_ref.shape[1] // groups
    index = lax.axis_index("ctx")
    cols = pl.ds(g * width, width)
    moves = [
        pltpu.make_async_copy(x_ref.at[:, cols], x_here, sems.at[0]),
        pltpu.make_async_copy(gate_ref.at[:, cols], gate_here, sems.at[1]),
    ]
    for move in moves:
        move.start()
    triangle = lower_triangle(stretch)
    proj = slice(g * N, (g + 1) * N)
    matrix = spread_matrix(heads, width, g * (heads // groups))
    wide_skip = spread(as_column(skip_ref[...]), matrix)
    step = 16
    for half in range(2):
        block = own_block(index, count, half)
        sl = slice(half * stretch, (half + 1) * stretch)
        row = doc_row(docs_ref, block, stretch)
        column = as_column(row)
        reached = jnp.where(column == prior_doc(docs_ref, block, stretch).astype(F32), 1.0, 0.0)
        gram = dot_nt(c_ref[sl, proj], b_ref[sl, proj])
        gram = jnp.where(triangle & (column == row.astype(F32)), gram, 0.0).astype(BF16)
        wide = spread(ec_ref[:, sl], matrix)
        inner = jnp.dot(gram, xw_ref[sl, :], preferred_element_type=F32)
        if half == 0:
            for move in moves:
                move.wait()
        for k in range(0, stretch, step):
            at = slice(half * stretch + k, half * stretch + k + step)
            here = slice(k, k + step)
            x = x_here[at, :].astype(F32)
            gate = gate_here[at, :].astype(F32)
            silu = gate / (1.0 + jnp.exp(-gate))
            fade = wide[here] * silu
            sx = silu * x
            sx_ref[at, :] = sx
            pre_ref[at, :] = inner[here] * fade + wide_skip * sx
            reach_ref[at, :] = reached[here] * fade


def merge_kernel(count, state_ref, kv_ref, out_ref):
    index = lax.axis_index("ctx")
    outer = (index == 0) | (index == count - 1)
    rows, wide = kv_ref.shape
    stretch = rows // 2

    @pl.when(outer)
    def _():
        out_ref[...] = state_ref[...]

    @pl.when(jnp.logical_not(outer))
    def _():
        out_ref[:stretch, :wide] = kv_ref[:stretch, :]
        out_ref[:stretch, wide:] = kv_ref[stretch:, :]
        out_ref[stretch:, :] = jnp.zeros((out_ref.shape[0] - stretch, 2 * wide), BF16)


def arrivals(index, count, refs):
    if count != 4:
        return [(ring_source(index, count, r + 1), [(None, refs[r])]) for r in range(count - 1)]
    near, own_of_middle, next_of_middle, far, farther = refs
    middle = (index == 1) | (index == 2)
    low = index < 2
    return [
        (index ^ 1, [(None, near)]),
        (
            jnp.where(low, 2, 1),
            [(middle, own_of_middle), (jnp.logical_not(middle), far)],
        ),
        (
            jnp.where(low, 3, 0),
            [(middle, next_of_middle), (jnp.logical_not(middle), farther)],
        ),
    ]


def attention_kernel(count, per, stack, g, docs_ref, q_ref, k_ref, v_ref, *refs):
    others = count - 1
    sent = 5 if count == 4 else others
    out_ref, kt, vt, bias_f, bias_b, bias_a = refs[-6:]
    rows = q_ref.shape[0]
    stretch = rows // 2
    index = lax.axis_index("ctx")
    last = 2 * count - 1
    kv_width = refs[0].shape[1] // 2
    row_f = doc_row(docs_ref, index, stretch).astype(F32)
    row_b = doc_row(docs_ref, last - index, stretch).astype(F32)
    col_f = as_column(row_f)
    col_b = as_column(row_b)
    triangle = lower_triangle(stretch)

    def tile(k):
        return slice(k * stretch, (k + 1) * stretch)

    bias_f[...] = jnp.where(triangle & (col_f == row_f), 0.0, MASKED)
    bias_b[:, tile(0)] = jnp.where(col_b == row_f, 0.0, MASKED)
    bias_b[:, tile(1)] = jnp.where(triangle & (col_b == row_b), 0.0, MASKED)
    vt[:, DH:] = jnp.ones((vt.shape[0], DH), BF16)
    here = slice(g * DH, (g + 1) * DH)
    kt[tile(0), :] = k_ref[:stretch, here]
    vt[tile(0), :DH] = v_ref[:stretch, here]
    kt[tile(count), :] = k_ref[stretch:, here]
    vt[tile(count), :DH] = v_ref[stretch:, here]
    lower = []
    for r, (source, places) in enumerate(arrivals(index, count, refs[:sent])):
        lower.append(source < index)
        for condition, ref in places:

            def fetch(ref=ref, r=r):
                folded = ref.shape[1] > 2 * kv_width
                gap = jnp.where(lower[r], 0, 2 * kv_width if folded else stretch)
                for table, first in ((kt, g * DH), (vt, kv_width + g * DH)):
                    front = ref[:stretch, first : first + DH]
                    if folded:
                        own = ref[:stretch, pl.ds(pl.multiple_of(first + gap, DH), DH)]
                    else:
                        own = ref[pl.ds(pl.multiple_of(gap, stretch), stretch), first : first + DH]
                    table[tile(1 + r), :DH] = own
                    table[tile(count + 1 + r), :DH] = front

            if condition is None:
                fetch()
            else:
                pl.when(condition)(fetch)
        key_f = doc_row(docs_ref, source, stretch).astype(F32)
        key_a = doc_row(docs_ref, jnp.where(lower[r], source, last - source), stretch).astype(F32)
        bias_b[:, tile(2 + r)] = jnp.where(col_b == key_f, 0.0, MASKED)
        bias_a[:, tile(r)] = jnp.where(jnp.where(lower[r], col_f, col_b) == key_a, 0.0, MASKED)

    factor = math.log2(math.e) / math.sqrt(DH)
    tall = stack * stretch
    half_keys = count * stretch

    def stacked(first, base):
        return jnp.concatenate(
            [
                q_ref[base : base + stretch, (g * per + first + j) * DH : (g * per + first + j + 1) * DH]
                for j in range(stack)
            ],
            axis=0,
        )

    def biased(score, bias):
        size = score.shape[1]
        return (score.reshape(stack, stretch, size) + bias[None]).reshape(tall, size)

    for first in range(0, per, stack):
        s_f = dot_nt(stacked(first, 0), kt[:half_keys, :])
        s_b = dot_nt(stacked(first, stretch), kt[...])
        t_f = biased(s_f[:, tile(0)], bias_f[...])
        t_b = [biased(s_b[:, tile(0)], bias_b[:, tile(0)])]
        for k in range(1, count + 1):
            t_b.append(biased(s_b[:, tile(count + k - 1)], bias_b[:, tile(k)]))
        t_a = []
        for r in range(others):
            score = jnp.where(lower[r], s_f[:, tile(1 + r)], s_b[:, tile(1 + r)])
            t_a.append(biased(score, bias_a[:, tile(r)]))
        best_f = t_f
        best_b = functools.reduce(jnp.maximum, t_b)
        for r in range(others):
            best_f = jnp.maximum(best_f, jnp.where(lower[r], t_a[r], MASKED))
            best_b = jnp.maximum(best_b, jnp.where(lower[r], MASKED, t_a[r]))
        top_f = jnp.max(best_f, axis=1, keepdims=True)
        top_b = jnp.max(best_b, axis=1, keepdims=True)
        w_f = [jnp.exp2((t_f - top_f) * factor).astype(BF16)]
        w_b = [jnp.exp2((t - top_b) * factor).astype(BF16) for t in t_b]
        w_x = []
        for r in range(others):
            top = jnp.where(lower[r], top_f, top_b)
            w = jnp.exp2((t_a[r] - top) * factor)
            w_f.append(jnp.where(lower[r], w, 0.0).astype(BF16))
            w_x.append(jnp.where(lower[r], 0.0, w).astype(BF16))
        w_b = w_b[:1] + w_x + w_b[1:]
        out_f = jnp.dot(
            jnp.concatenate(w_f, axis=1), vt[:half_keys, :], preferred_element_type=F32
        )
        out_b = jnp.dot(jnp.concatenate(w_b, axis=1), vt[...], preferred_element_type=F32)
        for half, out in enumerate((out_f, out_b)):
            result = (out[:, :DH] / out[:, DH:]).astype(BF16)
            for j in range(stack):
                cols = slice((first + j) * DH, (first + j + 1) * DH)
                out_ref[tile(half), cols] = result[tile(j)]


def final_kernel(
    count,
    g,
    groups,
    loss_scale,
    pre_ref,
    reach_ref,
    sx_ref,
    c_ref,
    teacher_ref,
    gain_ref,
    f_ref,
    dec_ref,
    *refs,
):
    others = count - 1
    got = refs[:others]
    before = refs[others] if g else None
    proj = slice(g * N, (g + 1) * N)
    first_lane = g * pre_ref.shape[1]
    out_ref, grad_ref, front, back, flow, gated_ref, sums, gain_acc, skip_acc = refs[-9:]
    rows, width = pre_ref.shape
    stretch = rows // 2
    index = lax.axis_index("ctx")
    tile = 128
    step = 16

    @pl.when(index == 0)
    def _():
        front[...] = jnp.zeros_like(front)

    @pl.when(index == count - 1)
    def _():
        back[:N, :] = jnp.zeros((N, width), BF16)
        back[N:, :] = jnp.where(
            lax.broadcasted_iota(jnp.int32, (EXTRA, width), 0) == 0, 1.0, 0.0
        ).astype(BF16)

    for r in range(1, count):

        @pl.when(index == r)
        def _():
            front[...] = got[r - 1][:N, :]

        @pl.when(index == count - 1 - r)
        def _():
            back[...] = got[r - 1][...]

    d_in = back[N : N + 1, :].astype(F32) + back[N + 1 : N + 2, :].astype(F32)
    through = dec_ref[0:1, :] * front[...].astype(F32) + f_ref[...].astype(F32)
    entering = (d_in * through + back[:N, :].astype(F32)).astype(BF16)
    flow[:stretch, :] = jnp.dot(c_ref[:stretch, proj], front[...], preferred_element_type=F32)
    flow[stretch:, :] = jnp.dot(c_ref[stretch:, proj], entering, preferred_element_type=F32)
    gain_acc[...] = jnp.zeros_like(gain_acc)
    skip_acc[...] = jnp.zeros_like(skip_acc)

    @pl.loop(0, rows // step, unroll=2)
    def _(k):
        sl = pl.ds(pl.multiple_of(k * step, step), step)
        totals = [jnp.zeros((step, tile), F32)] * 3
        for j in range(0, width, tile):
            cols = slice(j, j + tile)
            gated = pre_ref[sl, cols] + reach_ref[sl, cols] * flow[sl, cols]
            gated_ref[sl, cols] = gated
            scaled = gated * gain_ref[:, first_lane + j : first_lane + j + tile]
            totals[0] += gated * gated
            totals[1] += scaled * scaled
            totals[2] += scaled * teacher_ref[sl, cols].astype(F32)
        for k3 in range(3):
            sums[sl, k3 * tile : (k3 + 1) * tile] = totals[k3]

    square, weighted, crossed = (
        jnp.sum(sums[:, k3 * tile : (k3 + 1) * tile], axis=1, keepdims=True) * (1.0 / width)
        for k3 in range(3)
    )
    scale = lax.rsqrt(square + EPS)
    push_scale = 2.0 * loss_scale
    mean = push_scale * scale * (scale * weighted - crossed)
    sums[:, :tile] = jnp.broadcast_to(scale, (rows, tile))
    sums[:, tile : 2 * tile] = jnp.broadcast_to(mean, (rows, tile))

    @pl.loop(0, rows // step, unroll=2)
    def _(k):
        sl = pl.ds(pl.multiple_of(k * step, step), step)
        scale = sums[sl, :tile]
        mean = sums[sl, tile : 2 * tile]
        for j in range(0, width, tile):
            cols = slice(j, j + tile)
            gain = gain_ref[:, first_lane + j : first_lane + j + tile]
            unit = gated_ref[sl, cols] * scale
            normed = unit * gain
            out_ref[sl, cols] = normed.astype(BF16)
            push = (normed - teacher_ref[sl, cols].astype(F32)) * push_scale
            by_gain = push * unit
            by_skip = (push * gain - unit * mean) * (scale * sx_ref[sl, cols])
            gain_acc[:, cols] += by_gain[:8] + by_gain[8:]
            skip_acc[:, cols] += by_skip[:8] + by_skip[8:]

    row = lax.broadcasted_iota(jnp.int32, (tile, width), 0)
    lane = lax.broadcasted_iota(jnp.int32, (tile, width), 1)
    matrix = jnp.where(row == lane // P_SIZE + g * (width // P_SIZE), 1.0, 0.0).astype(BF16)
    hi, lo = parts(skip_acc[...])
    by_head = jnp.sum(dot_nt(hi, matrix) + dot_nt(lo, matrix), axis=0, keepdims=True)
    grad_ref[...] = jnp.zeros_like(grad_ref)
    if g:
        grad_ref[:g, :] = before[:g, :]
        by_head += before[groups : groups + 1, :tile]
    grad_ref[g : g + 1, :] = jnp.sum(gain_acc[...], axis=0, keepdims=True)
    grad_ref[groups : groups + 1, :tile] = by_head


def writing_kernel(*refs):
    parts_in, out_ref, sems = refs[:-2], refs[-2], refs[-1]
    width = parts_in[0].shape[1]
    moves = [
        pltpu.make_async_copy(part, out_ref.at[:, pl.ds(k * width, width)], sems.at[k])
        for k, part in enumerate(parts_in)
    ]
    for move in moves:
        move.start()
    for move in moves:
        move.wait()


def closing_kernel(a_ref, b_ref, gain_ref, skip_ref):
    total = a_ref[...] + b_ref[...]
    groups, width = total.shape[0] - 1, total.shape[1]
    for g in range(groups):
        gain_ref[:, g * width : (g + 1) * width] = total[g : g + 1, :]
    skip_ref[...] = total[groups : groups + 1, : skip_ref.shape[1]]


def exchange(part, shift):
    axes = ("dp", "ctx")
    size = lax.axis_size(axes)
    return lax.ppermute(part, axes, [(d, d ^ shift) for d in range(size)])


def body(
    queries,
    keys,
    values,
    doc_ids,
    inputs,
    gate_input,
    b_input,
    c_input,
    dt_raw,
    dt_bias,
    decay_log,
    skip,
    gain,
):
    count = lax.axis_size("ctx")
    rows, features = queries.shape[1:]
    stretch = rows // 2
    kv_dev = keys.shape[2] // DH
    per_kv = queries.shape[2] // keys.shape[2]
    groups = b_input.shape[2] // N
    heads = features // P_SIZE
    width = features // groups
    length = doc_ids.shape[1]
    others = count - 1
    loss_scale = 1.0 / (lax.axis_size("dp") * count * rows)
    x, gate, bmat, cmat = inputs[0], gate_input[0], b_input[0], c_input[0]
    struct = jax.ShapeDtypeStruct

    def in_hbm(*arrays):
        return [pltpu.with_memory_space_constraint(array, pltpu.HBM) for array in arrays]

    def write(*pieces):
        return pl.pallas_call(
            writing_kernel,
            out_shape=struct((rows, features), BF16),
            in_specs=[VMEM] * len(pieces),
            out_specs=pl.BlockSpec(memory_space=pl.ANY),
            scratch_shapes=[pltpu.SemaphoreType.DMA((len(pieces),))],
            compiler_params=params(2),
            cost_estimate=cost(0, 4 * rows * features),
            name="writing",
        )(*pieces)

    state = struct((N, width), BF16)
    payload = struct((N + EXTRA, width), BF16)
    outs = pl.pallas_call(
        functools.partial(opening_kernel, count, groups),
        out_shape=(
            struct((heads, rows), F32),
            *([struct((rows, width), BF16)] * groups),
            *([struct((8, width), F32)] * groups),
            *([state] * (2 * groups)),
            *([payload] * groups),
        ),
        in_specs=[VMEM] * 6,
        out_specs=(VMEM,) * (1 + 5 * groups),
        compiler_params=params(16),
        cost_estimate=cost(4 * rows * features * N, 8 * rows * features),
        name="opening",
    )(
        *in_hbm(
            doc_ids,
            x,
            bmat,
            dt_raw[0].T,
            dt_bias.reshape(1, heads),
            decay_log.reshape(1, heads),
        )
    )
    ec = outs[0]
    xw, dec, f_parts, b_parts, send = (
        outs[1 + k * groups : 1 + (k + 1) * groups] for k in range(5)
    )
    key_part, value_part, _ = lax.optimization_barrier((keys[0], values[0], ec))
    kv = pl.pallas_call(
        pack_kernel,
        out_shape=struct((rows, 2 * kv_dev * DH), BF16),
        in_specs=[VMEM] * 2,
        out_specs=VMEM,
        compiler_params=params(4),
        cost_estimate=cost(0, 8 * keys.size),
        name="pack",
    )(key_part, value_part)

    def local_terms(g, growth):
        return pl.pallas_call(
            functools.partial(local_kernel, count, groups, g),
            out_shape=(struct((rows, width), F32),) * 3,
            in_specs=[
                VMEM,
                *[pl.BlockSpec(memory_space=pl.ANY)] * 2,
                *[VMEM] * 5,
            ],
            out_specs=(VMEM,) * 3,
            scratch_shapes=[
                pltpu.VMEM((rows, width), BF16),
                pltpu.VMEM((rows, width), BF16),
                pltpu.SemaphoreType.DMA((2,)),
            ],
            compiler_params=params(12),
            cost_estimate=cost(2 * rows * width * N, 16 * rows * width),
            name="local",
        )(*in_hbm(doc_ids, x, gate, bmat, cmat, skip.reshape(1, heads)), growth, xw[g])

    send = list(send)
    got = [[] for _ in range(groups)]
    local = []
    def passed_on(g, stage):
        return pl.pallas_call(
            functools.partial(chain_kernel, count, stage),
            out_shape=payload,
            in_specs=[VMEM] * 4,
            out_specs=VMEM,
            compiler_params=params(4),
            cost_estimate=pl.CostEstimate(flops=16384 * N * width, bytes_accessed=0, transcendentals=0),
            name="chain",
        )(got[g][-1], f_parts[g], b_parts[g], dec[g])

    def stage_pairs(stage):
        return [(stage - 1, stage), (count - stage, count - stage - 1)]

    if count == 4:
        inward, outward, across = [(0, 1), (3, 2)], [(1, 0), (2, 3)], [(1, 2), (2, 1)]
        if groups > 1:
            got[0].append(lax.ppermute(send[0], "ctx", stage_pairs(1)))
        near = lax.ppermute(kv, "ctx", inward + outward)
        middle = lax.ppermute(kv, "ctx", across)
        if groups > 1:
            local = [local_terms(0, ec)]
            got[0][0], _ = lax.optimization_barrier((got[0][0], local[0][0]))
            send[0] = passed_on(0, 1)
            got[0].append(lax.ppermute(send[0], "ctx", stage_pairs(2)))
            growth, _ = lax.optimization_barrier((ec, send[0]))
            local += [local_terms(g, growth) for g in range(1, groups)]
            middle, _ = lax.optimization_barrier((middle, local[-1][0]))
        beyond = lax.ppermute(near, "ctx", across)
        send[-1] = pl.pallas_call(
            functools.partial(merge_kernel, count),
            out_shape=payload,
            in_specs=[VMEM] * 2,
            out_specs=VMEM,
            compiler_params=params(4),
            cost_estimate=cost(0, 4 * N * width),
            name="merge",
        )(send[-1], middle)
        far = lax.ppermute(send[-1], "ctx", inward + outward)
        got[-1].append(far)
        farther = lax.ppermute(beyond, "ctx", outward)
        kv_got = [near, middle, beyond, far, farther]
    else:
        ring = ring_order(count)
        ring_pairs = [(ring[d], ring[(d + 1) % count]) for d in range(count)]
        kv_got = [kv]
        for _ in range(others):
            kv_got.append(lax.ppermute(kv_got[-1], "ctx", ring_pairs))
        kv_got = kv_got[1:]
    if not local:
        local = [local_terms(g, ec) for g in range(groups)]
    ahead = None
    for r in range(1, count):
        for g in range(groups):
            if len(got[g]) >= r:
                continue
            if r == 2 and 0 < g == groups - 1 and count == 4:
                ahead = passed_on(0, 2)
                got[g][0], _, _ = lax.optimization_barrier((got[g][0], ahead, beyond))
            if r == 3 and g == 0 and ahead is not None:
                send[g] = ahead
            elif r > 1:
                send[g] = passed_on(g, r - 1)
            got[g].append(lax.ppermute(send[g], "ctx", stage_pairs(r)))
    stack = 4 if per_kv % 4 == 0 and count <= 4 else 1
    targets = [
        pl.pallas_call(
            functools.partial(attention_kernel, count, per_kv, stack, g),
            out_shape=struct((rows, per_kv * DH), BF16),
            in_specs=[VMEM] * (4 + len(kv_got)),
            out_specs=VMEM,
            scratch_shapes=[
                pltpu.VMEM((2 * count * stretch, DH), BF16),
                pltpu.VMEM((2 * count * stretch, 2 * DH), BF16),
                pltpu.VMEM((stretch, stretch), F32),
                pltpu.VMEM((stretch, (count + 1) * stretch), F32),
                pltpu.VMEM((stretch, others * stretch), F32),
            ],
            compiler_params=params(24),
            cost_estimate=cost(
                4 * (2 * count + 1) * stretch * stretch * per_kv * DH, 8 * rows * per_kv * DH
            ),
            name="attention",
        )(doc_ids, queries[0], keys[0], values[0], *kv_got)
        for g in range(kv_dev)
    ]
    normed, grads = [], None
    for g in range(groups):
        more = [] if grads is None else [grads]
        made, grads = pl.pallas_call(
            functools.partial(final_kernel, count, g, groups, loss_scale),
            out_shape=(struct((rows, width), BF16), struct((groups + 1, width), F32)),
            in_specs=[VMEM] * (8 + others + len(more)),
            out_specs=(VMEM,) * 2,
            scratch_shapes=[
                pltpu.VMEM((N, width), BF16),
                pltpu.VMEM((N + EXTRA, width), BF16),
                pltpu.VMEM((rows, width), F32),
                pltpu.VMEM((rows, width), F32),
                pltpu.VMEM((rows, 3 * 128), F32),
                pltpu.VMEM((8, width), F32),
                pltpu.VMEM((8, width), F32),
            ],
            compiler_params=params(16),
            cost_estimate=cost(2 * rows * width * N, 20 * rows * width),
            name="final",
        )(
            *local[g],
            cmat,
            targets[g],
            gain.reshape(1, features),
            f_parts[g],
            dec[g],
            *got[g],
            *more,
        )
        normed.append(made)
    teacher, student = write(*targets), write(*normed)
    partner = exchange(grads, 1)
    if lax.axis_size("dp") == 2:
        grads = (grads + partner) + (exchange(grads, count) + exchange(grads, count + 1))
    else:
        grads = grads + partner
    shifts = [1 << k for k in range(1, count.bit_length() - 1)]
    for shift in shifts[:-1]:
        grads = grads + exchange(grads, shift)
    grad_gain, grad_skip = pl.pallas_call(
        closing_kernel,
        out_shape=(struct((1, features), F32), struct((1, heads), F32)),
        in_specs=[VMEM] * 2,
        out_specs=(VMEM,) * 2,
        compiler_params=params(2),
        name="closing",
    )(grads, exchange(grads, shifts[-1]))
    return (teacher[None], student[None], grad_gain[0], grad_skip[0])


def solution(mesh):
    rows = P("dp", "ctx", "head")
    in_specs = (
        rows,
        rows,
        rows,
        P("dp", None),
        rows,
        rows,
        rows,
        rows,
        rows,
        P("head"),
        P("head"),
        P("head"),
        P("head"),
    )
    out_specs = (rows, rows, P("head"), P("head"))
    return jax.shard_map(body, mesh=mesh, in_specs=in_specs, out_specs=out_specs, check_vma=False)
```

```python
import functools
import math

import jax
import jax.numpy as jnp
from jax import lax
from jax.experimental import pallas as pl
from jax.experimental.pallas import tpu as pltpu
from jax.sharding import PartitionSpec as P

DH = 128
P_SIZE = 64
N = 128
EXTRA = 16
EPS = 1e-05
MASKED = -1e30
F32 = jnp.float32
BF16 = jnp.bfloat16
VMEM = pl.BlockSpec(memory_space=pltpu.VMEM)


def params(mib):
    return pltpu.CompilerParams(vmem_limit_bytes=mib << 20)


def cost(flops, size):
    return pl.CostEstimate(flops=flops, bytes_accessed=size, transcendentals=0)


def parts(v):
    hi = v.astype(BF16)
    return hi, (v - hi.astype(F32)).astype(BF16)


def spread_matrix(heads, width, first):
    row = lax.broadcasted_iota(jnp.int32, (heads, width), 0)
    lane = lax.broadcasted_iota(jnp.int32, (heads, width), 1)
    return jnp.where(row == (lane // P_SIZE) + first, 1.0, 0.0).astype(BF16)


def dot_nt(a, b):
    return lax.dot_general(a, b, (((1,), (1,)), ((), ())), preferred_element_type=F32)


def dot_tn(a, b):
    return lax.dot_general(a, b, (((0,), (0,)), ((), ())), preferred_element_type=F32)


def spread(v, matrix):
    return dot_tn(jnp.concatenate(parts(v), axis=0), jnp.concatenate([matrix, matrix], axis=0))


def doc_row(docs_ref, block, stretch):
    return docs_ref[:, pl.ds(pl.multiple_of(block * stretch, stretch), stretch)]


def as_column(row):
    size = row.shape[1]
    r = lax.broadcasted_iota(jnp.int32, (size, size), 0)
    c = lax.broadcasted_iota(jnp.int32, (size, size), 1)
    return jnp.sum(jnp.where(r == c, row.astype(F32), 0.0), axis=1, keepdims=True)


def lower_triangle(size):
    r = lax.broadcasted_iota(jnp.int32, (size, size), 0)
    c = lax.broadcasted_iota(jnp.int32, (size, size), 1)
    return r >= c


def prior_doc(docs_ref, block, stretch):
    before = doc_row(docs_ref, jnp.maximum(block - 1, 0), stretch)[:, stretch - 1 :]
    return jnp.where(block > 0, before, -1)


def own_block(index, count, half):
    return index if half == 0 else 2 * count - 1 - index


def ring_order(count):
    return [0] + list(range(1, count, 2)) + list(range(2, count, 2))[::-1]


def ring_source(index, count, steps):
    order = ring_order(count)
    source = jnp.int32(0)
    for place, member in enumerate(order):
        source = jnp.where(index == member, order[(place - steps) % count], source)
    return source


def put_state(ref, state):
    ref[:N, :] = state.astype(BF16)
    ref[N:, :] = jnp.zeros((EXTRA, ref.shape[1]), BF16)


def put_composite(ref, state, decay):
    hi, lo = parts(decay)
    ref[:N, :] = state.astype(BF16)
    ref[N:, :] = jnp.concatenate(
        [hi, lo, jnp.zeros((EXTRA - 2, ref.shape[1]), BF16)], axis=0
    )


def opening_kernel(
    count,
    groups,
    docs_ref,
    x_ref,
    b_ref,
    dt_ref,
    bias_ref,
    log_ref,
    ec_ref,
    *outs,
):
    xw_refs, dec_refs, f_refs, b_refs, send_refs = (
        outs[k * groups : (k + 1) * groups] for k in range(5)
    )
    heads, rows = dt_ref.shape
    stretch = rows // 2
    width = x_ref.shape[1] // groups
    index = lax.axis_index("ctx")
    triangle = jnp.where(lower_triangle(stretch), 1.0, 0.0)
    slope = jnp.exp(as_column(log_ref[...]))
    bias = as_column(bias_ref[...])
    lane = lax.broadcasted_iota(jnp.int32, (heads, 8), 1)
    ends = jnp.zeros((heads, 8), F32)
    loads = []
    projs = []
    for half in range(2):
        block = own_block(index, count, half)
        sl = slice(half * stretch, (half + 1) * stretch)
        raw = dt_ref[:, sl] + bias
        dt = jnp.maximum(raw, 0.0) + jnp.log1p(jnp.exp(-jnp.abs(raw)))
        cum = lax.dot_general(
            -dt * slope,
            triangle,
            (((1,), (1,)), ((), ())),
            precision=lax.Precision.HIGHEST,
            preferred_element_type=F32,
        )
        ec_ref[:, sl] = jnp.exp(cum)
        loads.append(jnp.exp(-cum) * dt)
        final = jnp.exp(cum[:, stretch - 1 :])
        row = doc_row(docs_ref, block, stretch)
        last = row[:, stretch - 1 :]
        kept = jnp.where(last == prior_doc(docs_ref, block, stretch), 1.0, 0.0)
        ends = jnp.where(lane == half, final * kept, ends)
        ends = jnp.where(lane == 2 + half, final, ends)
        same = jnp.where(as_column(row) == last.astype(F32), 1.0, 0.0)
        projs.append((b_ref[sl, :].astype(F32) * same).astype(BF16))
    for g in range(groups):
        cols = slice(g * width, (g + 1) * width)
        matrix = spread_matrix(heads, width, g * (heads // groups))
        wide = spread(ends, matrix)
        dec_refs[g][...] = wide
        sums = []
        for half in range(2):
            sl = slice(half * stretch, (half + 1) * stretch)
            xw = (x_ref[sl, cols].astype(F32) * spread(loads[half], matrix)).astype(BF16)
            xw_refs[g][sl, :] = xw
            sums.append(dot_tn(projs[half][:, g * N : (g + 1) * N], xw) * wide[2 + half : 3 + half])
        f_refs[g][...] = sums[0].astype(BF16)
        b_refs[g][...] = sums[1].astype(BF16)

        @pl.when(index == 0)
        def _():
            put_state(send_refs[g], sums[0])

        @pl.when(index != 0)
        def _():
            put_composite(send_refs[g], wide[1:2] * sums[0] + sums[1], wide[0:1] * wide[1:2])


def pack_kernel(k_ref, v_ref, kv_ref):
    width = k_ref.shape[1]
    kv_ref[:, :width] = k_ref[...]
    kv_ref[:, width:] = v_ref[...]


def chain_kernel(count, stage, got_ref, f_ref, b_ref, dec_ref, send_ref):
    index = lax.axis_index("ctx")

    @pl.when(index == stage)
    def _():
        state = dec_ref[0:1, :] * got_ref[:N, :].astype(F32) + f_ref[...].astype(F32)
        put_state(send_ref, state)

    @pl.when(index == count - 1 - stage)
    def _():
        decay = got_ref[N : N + 1, :].astype(F32) + got_ref[N + 1 : N + 2, :].astype(F32)
        inner = decay * f_ref[...].astype(F32) + got_ref[:N, :].astype(F32)
        state = dec_ref[1:2, :] * inner + b_ref[...].astype(F32)
        put_composite(send_ref, state, dec_ref[1:2, :] * decay * dec_ref[0:1, :])


def local_kernel(
    count, groups, docs_ref, x_ref, gate_ref, b_ref, c_ref, skip_ref, ec_ref, *refs
):
    xw_refs, pre_refs, reach_refs, sx_refs = (
        refs[k * groups : (k + 1) * groups] for k in range(4)
    )
    x_here, gate_here, sems = refs[4 * groups :]
    heads, rows = ec_ref.shape
    stretch = rows // 2
    width = x_ref.shape[1] // groups
    index = lax.axis_index("ctx")
    moves = []
    for g in range(groups):
        cols = pl.ds(g * width, width)
        moves.append(
            [
                pltpu.make_async_copy(x_ref.at[:, cols], x_here.at[g], sems.at[0, g]),
                pltpu.make_async_copy(gate_ref.at[:, cols], gate_here.at[g], sems.at[1, g]),
            ]
        )
        for move in moves[g]:
            move.start()
    triangle = lower_triangle(stretch)
    skip = as_column(skip_ref[...])
    step = 16
    masks = []
    for half in range(2):
        block = own_block(index, count, half)
        row = doc_row(docs_ref, block, stretch)
        column = as_column(row)
        reached = jnp.where(column == prior_doc(docs_ref, block, stretch).astype(F32), 1.0, 0.0)
        masks.append((triangle & (column == row.astype(F32)), reached))
    for g in range(groups):
        proj = slice(g * N, (g + 1) * N)
        matrix = spread_matrix(heads, width, g * (heads // groups))
        wide_skip = spread(skip, matrix)
        for half in range(2):
            sl = slice(half * stretch, (half + 1) * stretch)
            near, reached = masks[half]
            gram = dot_nt(c_ref[sl, proj], b_ref[sl, proj])
            gram = jnp.where(near, gram, 0.0).astype(BF16)
            wide = spread(ec_ref[:, sl], matrix)
            inner = jnp.dot(gram, xw_refs[g][sl, :], preferred_element_type=F32)
            if half == 0:
                for move in moves[g]:
                    move.wait()
            for k in range(0, stretch, step):
                at = slice(half * stretch + k, half * stretch + k + step)
                here = slice(k, k + step)
                x = x_here[g, at, :].astype(F32)
                gate = gate_here[g, at, :].astype(F32)
                silu = gate / (1.0 + jnp.exp(-gate))
                fade = wide[here] * silu
                sx = silu * x
                sx_refs[g][at, :] = sx
                pre_refs[g][at, :] = inner[here] * fade + wide_skip * sx
                reach_refs[g][at, :] = reached[here] * fade


def merge_kernel(count, state_ref, kv_ref, out_ref):
    index = lax.axis_index("ctx")
    outer = (index == 0) | (index == count - 1)
    rows, wide = kv_ref.shape
    stretch = rows // 2

    @pl.when(outer)
    def _():
        out_ref[...] = state_ref[...]

    @pl.when(jnp.logical_not(outer))
    def _():
        out_ref[:stretch, :wide] = kv_ref[:stretch, :]
        out_ref[:stretch, wide:] = kv_ref[stretch:, :]
        out_ref[stretch:, :] = jnp.zeros((out_ref.shape[0] - stretch, 2 * wide), BF16)


def arrivals(index, count, refs):
    if count != 4:
        return [(ring_source(index, count, r + 1), [(None, refs[r])]) for r in range(count - 1)]
    near, own_of_middle, next_of_middle, far, farther = refs
    middle = (index == 1) | (index == 2)
    low = index < 2
    return [
        (index ^ 1, [(None, near)]),
        (
            jnp.where(low, 2, 1),
            [(middle, own_of_middle), (jnp.logical_not(middle), far)],
        ),
        (
            jnp.where(low, 3, 0),
            [(middle, next_of_middle), (jnp.logical_not(middle), farther)],
        ),
    ]


def attention_kernel(count, per, stack, g, docs_ref, q_ref, k_ref, v_ref, *refs):
    others = count - 1
    sent = 5 if count == 4 else others
    out_ref, kt, vt, bias_f, bias_b, bias_a = refs[-6:]
    rows = q_ref.shape[0]
    stretch = rows // 2
    index = lax.axis_index("ctx")
    last = 2 * count - 1
    kv_width = refs[0].shape[1] // 2
    row_f = doc_row(docs_ref, index, stretch).astype(F32)
    row_b = doc_row(docs_ref, last - index, stretch).astype(F32)
    col_f = as_column(row_f)
    col_b = as_column(row_b)
    triangle = lower_triangle(stretch)

    def tile(k):
        return slice(k * stretch, (k + 1) * stretch)

    bias_f[...] = jnp.where(triangle & (col_f == row_f), 0.0, MASKED)
    bias_b[:, tile(0)] = jnp.where(col_b == row_f, 0.0, MASKED)
    bias_b[:, tile(1)] = jnp.where(triangle & (col_b == row_b), 0.0, MASKED)
    vt[:, DH:] = jnp.ones((vt.shape[0], DH), BF16)
    here = slice(g * DH, (g + 1) * DH)
    kt[tile(0), :] = k_ref[:stretch, here]
    vt[tile(0), :DH] = v_ref[:stretch, here]
    kt[tile(count), :] = k_ref[stretch:, here]
    vt[tile(count), :DH] = v_ref[stretch:, here]
    lower = []
    for r, (source, places) in enumerate(arrivals(index, count, refs[:sent])):
        lower.append(source < index)
        for condition, ref in places:

            def fetch(ref=ref, r=r):
                folded = ref.shape[1] > 2 * kv_width
                gap = jnp.where(lower[r], 0, 2 * kv_width if folded else stretch)
                for table, first in ((kt, g * DH), (vt, kv_width + g * DH)):
                    front = ref[:stretch, first : first + DH]
                    if folded:
                        own = ref[:stretch, pl.ds(pl.multiple_of(first + gap, DH), DH)]
                    else:
                        own = ref[pl.ds(pl.multiple_of(gap, stretch), stretch), first : first + DH]
                    table[tile(1 + r), :DH] = own
                    table[tile(count + 1 + r), :DH] = front

            if condition is None:
                fetch()
            else:
                pl.when(condition)(fetch)
        key_f = doc_row(docs_ref, source, stretch).astype(F32)
        key_a = doc_row(docs_ref, jnp.where(lower[r], source, last - source), stretch).astype(F32)
        bias_b[:, tile(2 + r)] = jnp.where(col_b == key_f, 0.0, MASKED)
        bias_a[:, tile(r)] = jnp.where(jnp.where(lower[r], col_f, col_b) == key_a, 0.0, MASKED)

    factor = math.log2(math.e) / math.sqrt(DH)
    tall = stack * stretch
    half_keys = count * stretch

    def stacked(first, base):
        return jnp.concatenate(
            [
                q_ref[base : base + stretch, (g * per + first + j) * DH : (g * per + first + j + 1) * DH]
                for j in range(stack)
            ],
            axis=0,
        )

    def biased(score, bias):
        size = score.shape[1]
        return (score.reshape(stack, stretch, size) + bias[None]).reshape(tall, size)

    for first in range(0, per, stack):
        s_f = dot_nt(stacked(first, 0), kt[:half_keys, :])
        s_b = dot_nt(stacked(first, stretch), kt[...])
        t_f = biased(s_f[:, tile(0)], bias_f[...])
        t_b = [biased(s_b[:, tile(0)], bias_b[:, tile(0)])]
        for k in range(1, count + 1):
            t_b.append(biased(s_b[:, tile(count + k - 1)], bias_b[:, tile(k)]))
        t_a = []
        for r in range(others):
            score = jnp.where(lower[r], s_f[:, tile(1 + r)], s_b[:, tile(1 + r)])
            t_a.append(biased(score, bias_a[:, tile(r)]))
        best_f = t_f
        best_b = functools.reduce(jnp.maximum, t_b)
        for r in range(others):
            best_f = jnp.maximum(best_f, jnp.where(lower[r], t_a[r], MASKED))
            best_b = jnp.maximum(best_b, jnp.where(lower[r], MASKED, t_a[r]))
        top_f = jnp.max(best_f, axis=1, keepdims=True)
        top_b = jnp.max(best_b, axis=1, keepdims=True)
        w_f = [jnp.exp2((t_f - top_f) * factor).astype(BF16)]
        w_b = [jnp.exp2((t - top_b) * factor).astype(BF16) for t in t_b]
        w_x = []
        for r in range(others):
            top = jnp.where(lower[r], top_f, top_b)
            w = jnp.exp2((t_a[r] - top) * factor)
            w_f.append(jnp.where(lower[r], w, 0.0).astype(BF16))
            w_x.append(jnp.where(lower[r], 0.0, w).astype(BF16))
        w_b = w_b[:1] + w_x + w_b[1:]
        out_f = jnp.dot(
            jnp.concatenate(w_f, axis=1), vt[:half_keys, :], preferred_element_type=F32
        )
        out_b = jnp.dot(jnp.concatenate(w_b, axis=1), vt[...], preferred_element_type=F32)
        for half, out in enumerate((out_f, out_b)):
            result = (out[:, :DH] / out[:, DH:]).astype(BF16)
            for j in range(stack):
                cols = slice((first + j) * DH, (first + j + 1) * DH)
                out_ref[tile(half), cols] = result[tile(j)]


def final_kernel(
    count,
    g,
    groups,
    loss_scale,
    pre_ref,
    reach_ref,
    sx_ref,
    c_ref,
    teacher_ref,
    gain_ref,
    f_ref,
    dec_ref,
    *refs,
):
    others = count - 1
    got = refs[:others]
    before = refs[others] if g else None
    proj = slice(g * N, (g + 1) * N)
    first_lane = g * pre_ref.shape[1]
    out_ref, grad_ref, front, back, flow, gated_ref, sums, gain_acc, skip_acc = refs[-9:]
    rows, width = pre_ref.shape
    stretch = rows // 2
    index = lax.axis_index("ctx")
    tile = 128
    step = 16

    @pl.when(index == 0)
    def _():
        front[...] = jnp.zeros_like(front)

    @pl.when(index == count - 1)
    def _():
        back[:N, :] = jnp.zeros((N, width), BF16)
        back[N:, :] = jnp.where(
            lax.broadcasted_iota(jnp.int32, (EXTRA, width), 0) == 0, 1.0, 0.0
        ).astype(BF16)

    for r in range(1, count):

        @pl.when(index == r)
        def _():
            front[...] = got[r - 1][:N, :]

        @pl.when(index == count - 1 - r)
        def _():
            back[...] = got[r - 1][...]

    d_in = back[N : N + 1, :].astype(F32) + back[N + 1 : N + 2, :].astype(F32)
    through = dec_ref[0:1, :] * front[...].astype(F32) + f_ref[...].astype(F32)
    entering = (d_in * through + back[:N, :].astype(F32)).astype(BF16)
    flow[:stretch, :] = jnp.dot(c_ref[:stretch, proj], front[...], preferred_element_type=F32)
    flow[stretch:, :] = jnp.dot(c_ref[stretch:, proj], entering, preferred_element_type=F32)
    gain_acc[...] = jnp.zeros_like(gain_acc)
    skip_acc[...] = jnp.zeros_like(skip_acc)

    @pl.loop(0, rows // step, unroll=4)
    def _(k):
        sl = pl.ds(pl.multiple_of(k * step, step), step)
        totals = [jnp.zeros((step, tile), F32)] * 3
        for j in range(0, width, tile):
            cols = slice(j, j + tile)
            gated = pre_ref[sl, cols] + reach_ref[sl, cols] * flow[sl, cols]
            gated_ref[sl, cols] = gated
            scaled = gated * gain_ref[:, first_lane + j : first_lane + j + tile]
            totals[0] += gated * gated
            totals[1] += scaled * scaled
            totals[2] += scaled * teacher_ref[sl, cols].astype(F32)
        for k3 in range(3):
            sums[sl, k3 * tile : (k3 + 1) * tile] = totals[k3]

    square, weighted, crossed = (
        jnp.sum(sums[:, k3 * tile : (k3 + 1) * tile], axis=1, keepdims=True) * (1.0 / width)
        for k3 in range(3)
    )
    scale = lax.rsqrt(square + EPS)
    push_scale = 2.0 * loss_scale
    mean = push_scale * scale * (scale * weighted - crossed)
    sums[:, :tile] = jnp.broadcast_to(scale, (rows, tile))
    sums[:, tile : 2 * tile] = jnp.broadcast_to(mean, (rows, tile))

    @pl.loop(0, rows // step, unroll=4)
    def _(k):
        sl = pl.ds(pl.multiple_of(k * step, step), step)
        scale = sums[sl, :tile]
        mean = sums[sl, tile : 2 * tile]
        for j in range(0, width, tile):
            cols = slice(j, j + tile)
            gain = gain_ref[:, first_lane + j : first_lane + j + tile]
            unit = gated_ref[sl, cols] * scale
            normed = unit * gain
            out_ref[sl, cols] = normed.astype(BF16)
            push = (normed - teacher_ref[sl, cols].astype(F32)) * push_scale
            by_gain = push * unit
            by_skip = (push * gain - unit * mean) * (scale * sx_ref[sl, cols])
            gain_acc[:, cols] += by_gain[:8] + by_gain[8:]
            skip_acc[:, cols] += by_skip[:8] + by_skip[8:]

    row = lax.broadcasted_iota(jnp.int32, (tile, width), 0)
    lane = lax.broadcasted_iota(jnp.int32, (tile, width), 1)
    matrix = jnp.where(row == lane // P_SIZE + g * (width // P_SIZE), 1.0, 0.0).astype(BF16)
    hi, lo = parts(skip_acc[...])
    by_head = jnp.sum(dot_nt(hi, matrix) + dot_nt(lo, matrix), axis=0, keepdims=True)
    grad_ref[...] = jnp.zeros_like(grad_ref)
    if g:
        grad_ref[:g, :] = before[:g, :]
        by_head += before[groups : groups + 1, :tile]
    grad_ref[g : g + 1, :] = jnp.sum(gain_acc[...], axis=0, keepdims=True)
    grad_ref[groups : groups + 1, :tile] = by_head


def writing_kernel(*refs):
    parts_in, out_ref, sems = refs[:-2], refs[-2], refs[-1]
    width = parts_in[0].shape[1]
    moves = [
        pltpu.make_async_copy(part, out_ref.at[:, pl.ds(k * width, width)], sems.at[k])
        for k, part in enumerate(parts_in)
    ]
    for move in moves:
        move.start()
    for move in moves:
        move.wait()


def closing_kernel(a_ref, b_ref, gain_ref, skip_ref):
    total = a_ref[...] + b_ref[...]
    groups, width = total.shape[0] - 1, total.shape[1]
    for g in range(groups):
        gain_ref[:, g * width : (g + 1) * width] = total[g : g + 1, :]
    skip_ref[...] = total[groups : groups + 1, : skip_ref.shape[1]]


def exchange(part, shift):
    axes = ("dp", "ctx")
    size = lax.axis_size(axes)
    return lax.ppermute(part, axes, [(d, d ^ shift) for d in range(size)])


def body(
    queries,
    keys,
    values,
    doc_ids,
    inputs,
    gate_input,
    b_input,
    c_input,
    dt_raw,
    dt_bias,
    decay_log,
    skip,
    gain,
):
    count = lax.axis_size("ctx")
    rows, features = queries.shape[1:]
    stretch = rows // 2
    kv_dev = keys.shape[2] // DH
    per_kv = queries.shape[2] // keys.shape[2]
    groups = b_input.shape[2] // N
    heads = features // P_SIZE
    width = features // groups
    length = doc_ids.shape[1]
    others = count - 1
    loss_scale = 1.0 / (lax.axis_size("dp") * count * rows)
    x, gate, bmat, cmat = inputs[0], gate_input[0], b_input[0], c_input[0]
    struct = jax.ShapeDtypeStruct

    def in_hbm(*arrays):
        return [pltpu.with_memory_space_constraint(array, pltpu.HBM) for array in arrays]

    def write(*pieces):
        return pl.pallas_call(
            writing_kernel,
            out_shape=struct((rows, features), BF16),
            in_specs=[VMEM] * len(pieces),
            out_specs=pl.BlockSpec(memory_space=pl.ANY),
            scratch_shapes=[pltpu.SemaphoreType.DMA((len(pieces),))],
            compiler_params=params(2),
            cost_estimate=cost(0, 4 * rows * features),
            name="writing",
        )(*pieces)

    state = struct((N, width), BF16)
    payload = struct((N + EXTRA, width), BF16)
    outs = pl.pallas_call(
        functools.partial(opening_kernel, count, groups),
        out_shape=(
            struct((heads, rows), F32),
            *([struct((rows, width), BF16)] * groups),
            *([struct((8, width), F32)] * groups),
            *([state] * (2 * groups)),
            *([payload] * groups),
        ),
        in_specs=[VMEM] * 6,
        out_specs=(VMEM,) * (1 + 5 * groups),
        compiler_params=params(16),
        cost_estimate=cost(4 * rows * features * N, 8 * rows * features),
        name="opening",
    )(
        *in_hbm(
            doc_ids,
            x,
            bmat,
            dt_raw[0].T,
            dt_bias.reshape(1, heads),
            decay_log.reshape(1, heads),
        )
    )
    ec = outs[0]
    xw, dec, f_parts, b_parts, send = (
        outs[1 + k * groups : 1 + (k + 1) * groups] for k in range(5)
    )
    key_part, value_part, _ = lax.optimization_barrier((keys[0], values[0], ec))
    kv = pl.pallas_call(
        pack_kernel,
        out_shape=struct((rows, 2 * kv_dev * DH), BF16),
        in_specs=[VMEM] * 2,
        out_specs=VMEM,
        compiler_params=params(4),
        cost_estimate=cost(0, 8 * keys.size),
        name="pack",
    )(key_part, value_part)

    local = pl.pallas_call(
        functools.partial(local_kernel, count, groups),
        out_shape=(struct((rows, width), F32),) * (3 * groups),
        in_specs=[
            VMEM,
            *[pl.BlockSpec(memory_space=pl.ANY)] * 2,
            *[VMEM] * (4 + groups),
        ],
        out_specs=(VMEM,) * (3 * groups),
        scratch_shapes=[
            pltpu.VMEM((groups, rows, width), BF16),
            pltpu.VMEM((groups, rows, width), BF16),
            pltpu.SemaphoreType.DMA((2, groups)),
        ],
        compiler_params=params(16),
        cost_estimate=cost(2 * rows * features * N, 16 * rows * features),
        name="local",
    )(*in_hbm(doc_ids, x, gate, bmat, cmat, skip.reshape(1, heads)), ec, *xw)

    send = list(send)
    got = [[] for _ in range(groups)]
    def passed_on(g, stage):
        return pl.pallas_call(
            functools.partial(chain_kernel, count, stage),
            out_shape=payload,
            in_specs=[VMEM] * 4,
            out_specs=VMEM,
            compiler_params=params(4),
            cost_estimate=pl.CostEstimate(flops=16384 * N * width, bytes_accessed=0, transcendentals=0),
            name="chain",
        )(got[g][-1], f_parts[g], b_parts[g], dec[g])

    def stage_pairs(stage):
        return [(stage - 1, stage), (count - stage, count - stage - 1)]

    if count == 4:
        inward, outward, across = [(0, 1), (3, 2)], [(1, 0), (2, 3)], [(1, 2), (2, 1)]
        near = lax.ppermute(kv, "ctx", inward + outward)
        middle = lax.ppermute(kv, "ctx", across)
        middle, *local = lax.optimization_barrier((middle, *local))
        beyond = lax.ppermute(near, "ctx", across)
        send[-1] = pl.pallas_call(
            functools.partial(merge_kernel, count),
            out_shape=payload,
            in_specs=[VMEM] * 2,
            out_specs=VMEM,
            compiler_params=params(4),
            cost_estimate=cost(0, 4 * N * width),
            name="merge",
        )(send[-1], middle)
        far = lax.ppermute(send[-1], "ctx", inward + outward)
        got[-1].append(far)
        farther = lax.ppermute(beyond, "ctx", outward)
        kv_got = [near, middle, beyond, far, farther]
    else:
        ring = ring_order(count)
        ring_pairs = [(ring[d], ring[(d + 1) % count]) for d in range(count)]
        kv_got = [kv]
        for _ in range(others):
            kv_got.append(lax.ppermute(kv_got[-1], "ctx", ring_pairs))
        kv_got = kv_got[1:]
    stack = 2 if per_kv % 2 == 0 and count <= 4 else 1
    targets = [
        pl.pallas_call(
            functools.partial(attention_kernel, count, per_kv, stack, g),
            out_shape=struct((rows, per_kv * DH), BF16),
            in_specs=[VMEM] * (4 + len(kv_got)),
            out_specs=VMEM,
            scratch_shapes=[
                pltpu.VMEM((2 * count * stretch, DH), BF16),
                pltpu.VMEM((2 * count * stretch, 2 * DH), BF16),
                pltpu.VMEM((stretch, stretch), F32),
                pltpu.VMEM((stretch, (count + 1) * stretch), F32),
                pltpu.VMEM((stretch, others * stretch), F32),
            ],
            compiler_params=params(24),
            cost_estimate=cost(
                32 * (2 * count + 1) * stretch * stretch * per_kv * DH, 8 * rows * per_kv * DH
            ),
            name="attention",
        )(doc_ids, queries[0], keys[0], values[0], *kv_got)
        for g in range(kv_dev)
    ]
    for r in range(1, count):
        for g in range(groups):
            if len(got[g]) >= r:
                continue
            if r == 3 and g == groups - 1:
                got[g][-1], targets[0] = lax.optimization_barrier((got[g][-1], targets[0]))
            if r > 1:
                send[g] = passed_on(g, r - 1)
            got[g].append(lax.ppermute(send[g], "ctx", stage_pairs(r)))
    normed, grads = [], None
    for g in range(groups):
        more = [] if grads is None else [grads]
        made, grads = pl.pallas_call(
            functools.partial(final_kernel, count, g, groups, loss_scale),
            out_shape=(struct((rows, width), BF16), struct((groups + 1, width), F32)),
            in_specs=[VMEM] * (8 + others + len(more)),
            out_specs=(VMEM,) * 2,
            scratch_shapes=[
                pltpu.VMEM((N, width), BF16),
                pltpu.VMEM((N + EXTRA, width), BF16),
                pltpu.VMEM((rows, width), F32),
                pltpu.VMEM((rows, width), F32),
                pltpu.VMEM((rows, 3 * 128), F32),
                pltpu.VMEM((8, width), F32),
                pltpu.VMEM((8, width), F32),
            ],
            compiler_params=params(16),
            cost_estimate=cost(2 * rows * width * N, 20 * rows * width),
            name="final",
        )(
            *local[g::groups],
            cmat,
            targets[g],
            gain.reshape(1, features),
            f_parts[g],
            dec[g],
            *got[g],
            *more,
        )
        normed.append(made)
    teacher, student = write(*targets), write(*normed)
    partner = exchange(grads, 1)
    if lax.axis_size("dp") == 2:
        grads = (grads + partner) + (exchange(grads, count) + exchange(grads, count + 1))
    else:
        grads = grads + partner
    shifts = [1 << k for k in range(1, count.bit_length() - 1)]
    for shift in shifts[:-1]:
        grads = grads + exchange(grads, shift)
    grad_gain, grad_skip = pl.pallas_call(
        closing_kernel,
        out_shape=(struct((1, features), F32), struct((1, heads), F32)),
        in_specs=[VMEM] * 2,
        out_specs=(VMEM,) * 2,
        compiler_params=params(2),
        name="closing",
    )(grads, exchange(grads, shifts[-1]))
    return (teacher[None], student[None], grad_gain[0], grad_skip[0])


def solution(mesh):
    rows = P("dp", "ctx", "head")
    in_specs = (
        rows,
        rows,
        rows,
        P("dp", None),
        rows,
        rows,
        rows,
        rows,
        rows,
        P("head"),
        P("head"),
        P("head"),
        P("head"),
    )
    out_specs = (rows, rows, P("head"), P("head"))
    return jax.shard_map(body, mesh=mesh, in_specs=in_specs, out_specs=out_specs, check_vma=False)
```

```python
import functools
import math

import jax
import jax.numpy as jnp
from jax import lax
from jax.experimental import pallas as pl
from jax.experimental.pallas import tpu as pltpu
from jax.sharding import PartitionSpec as P

DH = 128
P_SIZE = 64
N = 128
EXTRA = 16
EPS = 1e-05
MASKED = -1e30
F32 = jnp.float32
BF16 = jnp.bfloat16
VMEM = pl.BlockSpec(memory_space=pltpu.VMEM)


def params(mib):
    return pltpu.CompilerParams(vmem_limit_bytes=mib << 20)


def cost(flops, size):
    return pl.CostEstimate(flops=flops, bytes_accessed=size, transcendentals=0)


def parts(v):
    hi = v.astype(BF16)
    return hi, (v - hi.astype(F32)).astype(BF16)


def spread_matrix(heads, width, first):
    row = lax.broadcasted_iota(jnp.int32, (heads, width), 0)
    lane = lax.broadcasted_iota(jnp.int32, (heads, width), 1)
    return jnp.where(row == (lane // P_SIZE) + first, 1.0, 0.0).astype(BF16)


def dot_nt(a, b):
    return lax.dot_general(a, b, (((1,), (1,)), ((), ())), preferred_element_type=F32)


def dot_tn(a, b):
    return lax.dot_general(a, b, (((0,), (0,)), ((), ())), preferred_element_type=F32)


def spread(v, matrix):
    return dot_tn(jnp.concatenate(parts(v), axis=0), jnp.concatenate([matrix, matrix], axis=0))


def doc_row(docs_ref, block, stretch):
    return docs_ref[:, pl.ds(pl.multiple_of(block * stretch, stretch), stretch)]


def as_column(row):
    size = row.shape[1]
    r = lax.broadcasted_iota(jnp.int32, (size, size), 0)
    c = lax.broadcasted_iota(jnp.int32, (size, size), 1)
    return jnp.sum(jnp.where(r == c, row.astype(F32), 0.0), axis=1, keepdims=True)


def lower_triangle(size):
    r = lax.broadcasted_iota(jnp.int32, (size, size), 0)
    c = lax.broadcasted_iota(jnp.int32, (size, size), 1)
    return r >= c


def prior_doc(docs_ref, block, stretch):
    before = doc_row(docs_ref, jnp.maximum(block - 1, 0), stretch)[:, stretch - 1 :]
    return jnp.where(block > 0, before, -1)


def own_block(index, count, half):
    return index if half == 0 else 2 * count - 1 - index


def ring_order(count):
    return [0] + list(range(1, count, 2)) + list(range(2, count, 2))[::-1]


def ring_source(index, count, steps):
    order = ring_order(count)
    source = jnp.int32(0)
    for place, member in enumerate(order):
        source = jnp.where(index == member, order[(place - steps) % count], source)
    return source


def put_state(ref, state):
    ref[:N, :] = state.astype(BF16)
    ref[N:, :] = jnp.zeros((EXTRA, ref.shape[1]), BF16)


def put_composite(ref, state, decay):
    hi, lo = parts(decay)
    ref[:N, :] = state.astype(BF16)
    ref[N:, :] = jnp.concatenate(
        [hi, lo, jnp.zeros((EXTRA - 2, ref.shape[1]), BF16)], axis=0
    )


def opening_kernel(
    count,
    groups,
    docs_ref,
    k_ref,
    v_ref,
    x_ref,
    b_ref,
    dt_ref,
    bias_ref,
    log_ref,
    kv_ref,
    ec_ref,
    *outs,
):
    xw_refs, dec_refs, f_refs, b_refs, send_refs = (
        outs[k * groups : (k + 1) * groups] for k in range(5)
    )
    heads, rows = dt_ref.shape
    stretch = rows // 2
    width = x_ref.shape[1] // groups
    kv_width = k_ref.shape[1]
    index = lax.axis_index("ctx")
    kv_ref[:, :kv_width] = k_ref[...]
    kv_ref[:, kv_width:] = v_ref[...]
    triangle = jnp.where(lower_triangle(stretch), 1.0, 0.0)
    slope = jnp.exp(as_column(log_ref[...]))
    bias = as_column(bias_ref[...])
    lane = lax.broadcasted_iota(jnp.int32, (heads, 8), 1)
    ends = jnp.zeros((heads, 8), F32)
    loads = []
    projs = []
    for half in range(2):
        block = own_block(index, count, half)
        sl = slice(half * stretch, (half + 1) * stretch)
        raw = dt_ref[:, sl] + bias
        dt = jnp.maximum(raw, 0.0) + jnp.log1p(jnp.exp(-jnp.abs(raw)))
        cum = lax.dot_general(
            -dt * slope,
            triangle,
            (((1,), (1,)), ((), ())),
            precision=lax.Precision.HIGHEST,
            preferred_element_type=F32,
        )
        ec_ref[:, sl] = jnp.exp(cum)
        loads.append(jnp.exp(-cum) * dt)
        final = jnp.exp(cum[:, stretch - 1 :])
        row = doc_row(docs_ref, block, stretch)
        last = row[:, stretch - 1 :]
        kept = jnp.where(last == prior_doc(docs_ref, block, stretch), 1.0, 0.0)
        ends = jnp.where(lane == half, final * kept, ends)
        ends = jnp.where(lane == 2 + half, final, ends)
        same = jnp.where(as_column(row) == last.astype(F32), 1.0, 0.0)
        projs.append((b_ref[sl, :].astype(F32) * same).astype(BF16))
    for g in range(groups):
        cols = slice(g * width, (g + 1) * width)
        matrix = spread_matrix(heads, width, g * (heads // groups))
        wide = spread(ends, matrix)
        dec_refs[g][...] = wide
        sums = []
        for half in range(2):
            sl = slice(half * stretch, (half + 1) * stretch)
            xw = (x_ref[sl, cols].astype(F32) * spread(loads[half], matrix)).astype(BF16)
            xw_refs[g][sl, :] = xw
            sums.append(dot_tn(projs[half][:, g * N : (g + 1) * N], xw) * wide[2 + half : 3 + half])
        f_refs[g][...] = sums[0].astype(BF16)
        b_refs[g][...] = sums[1].astype(BF16)

        @pl.when(index == 0)
        def _():
            put_state(send_refs[g], sums[0])

        @pl.when(index != 0)
        def _():
            put_composite(send_refs[g], wide[1:2] * sums[0] + sums[1], wide[0:1] * wide[1:2])


def chain_kernel(count, stage, got_ref, f_ref, b_ref, dec_ref, send_ref):
    index = lax.axis_index("ctx")

    @pl.when(index == stage)
    def _():
        state = dec_ref[0:1, :] * got_ref[:N, :].astype(F32) + f_ref[...].astype(F32)
        put_state(send_ref, state)

    @pl.when(index == count - 1 - stage)
    def _():
        decay = got_ref[N : N + 1, :].astype(F32) + got_ref[N + 1 : N + 2, :].astype(F32)
        inner = decay * f_ref[...].astype(F32) + got_ref[:N, :].astype(F32)
        state = dec_ref[1:2, :] * inner + b_ref[...].astype(F32)
        put_composite(send_ref, state, dec_ref[1:2, :] * decay * dec_ref[0:1, :])


def local_kernel(
    count, groups, docs_ref, x_ref, gate_ref, b_ref, c_ref, skip_ref, ec_ref, *refs
):
    xw_refs, pre_refs, reach_refs, sx_refs = (
        refs[k * groups : (k + 1) * groups] for k in range(4)
    )
    x_here, gate_here, sems = refs[4 * groups :]
    heads, rows = ec_ref.shape
    stretch = rows // 2
    width = x_ref.shape[1] // groups
    index = lax.axis_index("ctx")
    moves = []
    for g in range(groups):
        cols = pl.ds(g * width, width)
        moves.append(
            [
                pltpu.make_async_copy(x_ref.at[:, cols], x_here.at[g], sems.at[0, g]),
                pltpu.make_async_copy(gate_ref.at[:, cols], gate_here.at[g], sems.at[1, g]),
            ]
        )
        for move in moves[g]:
            move.start()
    triangle = lower_triangle(stretch)
    skip = as_column(skip_ref[...])
    step = 16
    masks = []
    for half in range(2):
        block = own_block(index, count, half)
        row = doc_row(docs_ref, block, stretch)
        column = as_column(row)
        reached = jnp.where(column == prior_doc(docs_ref, block, stretch).astype(F32), 1.0, 0.0)
        masks.append((triangle & (column == row.astype(F32)), reached))
    for g in range(groups):
        proj = slice(g * N, (g + 1) * N)
        matrix = spread_matrix(heads, width, g * (heads // groups))
        wide_skip = spread(skip, matrix)
        for half in range(2):
            sl = slice(half * stretch, (half + 1) * stretch)
            near, reached = masks[half]
            gram = dot_nt(c_ref[sl, proj], b_ref[sl, proj])
            gram = jnp.where(near, gram, 0.0).astype(BF16)
            wide = spread(ec_ref[:, sl], matrix)
            inner = jnp.dot(gram, xw_refs[g][sl, :], preferred_element_type=F32)
            if half == 0:
                for move in moves[g]:
                    move.wait()
            for k in range(0, stretch, step):
                at = slice(half * stretch + k, half * stretch + k + step)
                here = slice(k, k + step)
                x = x_here[g, at, :].astype(F32)
                gate = gate_here[g, at, :].astype(F32)
                silu = gate / (1.0 + jnp.exp(-gate))
                fade = wide[here] * silu
                sx = silu * x
                sx_refs[g][at, :] = sx
                pre_refs[g][at, :] = inner[here] * fade + wide_skip * sx
                reach_refs[g][at, :] = reached[here] * fade


def merge_kernel(count, state_ref, kv_ref, out_ref):
    index = lax.axis_index("ctx")
    outer = (index == 0) | (index == count - 1)
    rows, wide = kv_ref.shape
    stretch = rows // 2

    @pl.when(outer)
    def _():
        out_ref[...] = state_ref[...]

    @pl.when(jnp.logical_not(outer))
    def _():
        out_ref[:stretch, :wide] = kv_ref[:stretch, :]
        out_ref[:stretch, wide:] = kv_ref[stretch:, :]
        out_ref[stretch:, :] = jnp.zeros((out_ref.shape[0] - stretch, 2 * wide), BF16)


def arrivals(index, count, refs):
    if count != 4:
        return [(ring_source(index, count, r + 1), [(None, refs[r])]) for r in range(count - 1)]
    near, own_of_middle, next_of_middle, far, farther = refs
    middle = (index == 1) | (index == 2)
    low = index < 2
    return [
        (index ^ 1, [(None, near)]),
        (
            jnp.where(low, 2, 1),
            [(middle, own_of_middle), (jnp.logical_not(middle), far)],
        ),
        (
            jnp.where(low, 3, 0),
            [(middle, next_of_middle), (jnp.logical_not(middle), farther)],
        ),
    ]


def attention_kernel(count, per, stack, g, docs_ref, q_ref, k_ref, v_ref, *refs):
    others = count - 1
    sent = 5 if count == 4 else others
    out_ref, kt, vt, bias_f, bias_b, bias_a = refs[-6:]
    rows = q_ref.shape[0]
    stretch = rows // 2
    index = lax.axis_index("ctx")
    last = 2 * count - 1
    kv_width = refs[0].shape[1] // 2
    row_f = doc_row(docs_ref, index, stretch).astype(F32)
    row_b = doc_row(docs_ref, last - index, stretch).astype(F32)
    col_f = as_column(row_f)
    col_b = as_column(row_b)
    triangle = lower_triangle(stretch)

    def tile(k):
        return slice(k * stretch, (k + 1) * stretch)

    bias_f[...] = jnp.where(triangle & (col_f == row_f), 0.0, MASKED)
    bias_b[:, tile(0)] = jnp.where(col_b == row_f, 0.0, MASKED)
    bias_b[:, tile(1)] = jnp.where(triangle & (col_b == row_b), 0.0, MASKED)
    vt[:, DH:] = jnp.ones((vt.shape[0], DH), BF16)
    here = slice(g * DH, (g + 1) * DH)
    kt[tile(0), :] = k_ref[:stretch, here]
    vt[tile(0), :DH] = v_ref[:stretch, here]
    kt[tile(count), :] = k_ref[stretch:, here]
    vt[tile(count), :DH] = v_ref[stretch:, here]
    lower = []
    for r, (source, places) in enumerate(arrivals(index, count, refs[:sent])):
        lower.append(source < index)
        for condition, ref in places:

            def fetch(ref=ref, r=r):
                folded = ref.shape[1] > 2 * kv_width
                gap = jnp.where(lower[r], 0, 2 * kv_width if folded else stretch)
                for table, first in ((kt, g * DH), (vt, kv_width + g * DH)):
                    front = ref[:stretch, first : first + DH]
                    if folded:
                        own = ref[:stretch, pl.ds(pl.multiple_of(first + gap, DH), DH)]
                    else:
                        own = ref[pl.ds(pl.multiple_of(gap, stretch), stretch), first : first + DH]
                    table[tile(1 + r), :DH] = own
                    table[tile(count + 1 + r), :DH] = front

            if condition is None:
                fetch()
            else:
                pl.when(condition)(fetch)
        key_f = doc_row(docs_ref, source, stretch).astype(F32)
        key_a = doc_row(docs_ref, jnp.where(lower[r], source, last - source), stretch).astype(F32)
        bias_b[:, tile(2 + r)] = jnp.where(col_b == key_f, 0.0, MASKED)
        bias_a[:, tile(r)] = jnp.where(jnp.where(lower[r], col_f, col_b) == key_a, 0.0, MASKED)

    factor = math.log2(math.e) / math.sqrt(DH)
    tall = stack * stretch
    half_keys = count * stretch

    def stacked(first, base):
        return jnp.concatenate(
            [
                q_ref[base : base + stretch, (g * per + first + j) * DH : (g * per + first + j + 1) * DH]
                for j in range(stack)
            ],
            axis=0,
        )

    def biased(score, bias):
        size = score.shape[1]
        return (score.reshape(stack, stretch, size) + bias[None]).reshape(tall, size)

    for first in range(0, per, stack):
        s_f = dot_nt(stacked(first, 0), kt[:half_keys, :])
        s_b = dot_nt(stacked(first, stretch), kt[...])
        t_f = biased(s_f[:, tile(0)], bias_f[...])
        t_b = [biased(s_b[:, tile(0)], bias_b[:, tile(0)])]
        for k in range(1, count + 1):
            t_b.append(biased(s_b[:, tile(count + k - 1)], bias_b[:, tile(k)]))
        t_a = []
        for r in range(others):
            score = jnp.where(lower[r], s_f[:, tile(1 + r)], s_b[:, tile(1 + r)])
            t_a.append(biased(score, bias_a[:, tile(r)]))
        best_f = t_f
        best_b = functools.reduce(jnp.maximum, t_b)
        for r in range(others):
            best_f = jnp.maximum(best_f, jnp.where(lower[r], t_a[r], MASKED))
            best_b = jnp.maximum(best_b, jnp.where(lower[r], MASKED, t_a[r]))
        top_f = jnp.max(best_f, axis=1, keepdims=True)
        top_b = jnp.max(best_b, axis=1, keepdims=True)
        w_f = [jnp.exp2((t_f - top_f) * factor).astype(BF16)]
        w_b = [jnp.exp2((t - top_b) * factor).astype(BF16) for t in t_b]
        w_x = []
        for r in range(others):
            top = jnp.where(lower[r], top_f, top_b)
            w = jnp.exp2((t_a[r] - top) * factor)
            w_f.append(jnp.where(lower[r], w, 0.0).astype(BF16))
            w_x.append(jnp.where(lower[r], 0.0, w).astype(BF16))
        w_b = w_b[:1] + w_x + w_b[1:]
        out_f = jnp.dot(
            jnp.concatenate(w_f, axis=1), vt[:half_keys, :], preferred_element_type=F32
        )
        out_b = jnp.dot(jnp.concatenate(w_b, axis=1), vt[...], preferred_element_type=F32)
        for half, out in enumerate((out_f, out_b)):
            result = (out[:, :DH] / out[:, DH:]).astype(BF16)
            for j in range(stack):
                cols = slice((first + j) * DH, (first + j + 1) * DH)
                out_ref[tile(half), cols] = result[tile(j)]


def final_kernel(
    count,
    g,
    groups,
    loss_scale,
    pre_ref,
    reach_ref,
    sx_ref,
    c_ref,
    teacher_ref,
    gain_ref,
    f_ref,
    dec_ref,
    *refs,
):
    others = count - 1
    got = refs[:others]
    before = refs[others] if g else None
    proj = slice(g * N, (g + 1) * N)
    first_lane = g * pre_ref.shape[1]
    out_ref, grad_ref, front, back, flow, gated_ref, sums, gain_acc, skip_acc = refs[-9:]
    rows, width = pre_ref.shape
    stretch = rows // 2
    index = lax.axis_index("ctx")
    tile = 128
    step = 16

    @pl.when(index == 0)
    def _():
        front[...] = jnp.zeros_like(front)

    @pl.when(index == count - 1)
    def _():
        back[:N, :] = jnp.zeros((N, width), BF16)
        back[N:, :] = jnp.where(
            lax.broadcasted_iota(jnp.int32, (EXTRA, width), 0) == 0, 1.0, 0.0
        ).astype(BF16)

    for r in range(1, count):

        @pl.when(index == r)
        def _():
            front[...] = got[r - 1][:N, :]

        @pl.when(index == count - 1 - r)
        def _():
            back[...] = got[r - 1][...]

    d_in = back[N : N + 1, :].astype(F32) + back[N + 1 : N + 2, :].astype(F32)
    through = dec_ref[0:1, :] * front[...].astype(F32) + f_ref[...].astype(F32)
    entering = (d_in * through + back[:N, :].astype(F32)).astype(BF16)
    flow[:stretch, :] = jnp.dot(c_ref[:stretch, proj], front[...], preferred_element_type=F32)
    flow[stretch:, :] = jnp.dot(c_ref[stretch:, proj], entering, preferred_element_type=F32)
    gain_acc[...] = jnp.zeros_like(gain_acc)
    skip_acc[...] = jnp.zeros_like(skip_acc)

    @pl.loop(0, rows // step, unroll=2)
    def _(k):
        sl = pl.ds(pl.multiple_of(k * step, step), step)
        totals = [jnp.zeros((step, tile), F32)] * 3
        for j in range(0, width, tile):
            cols = slice(j, j + tile)
            gated = pre_ref[sl, cols] + reach_ref[sl, cols] * flow[sl, cols]
            gated_ref[sl, cols] = gated
            scaled = gated * gain_ref[:, first_lane + j : first_lane + j + tile]
            totals[0] += gated * gated
            totals[1] += scaled * scaled
            totals[2] += scaled * teacher_ref[sl, cols].astype(F32)
        for k3 in range(3):
            sums[sl, k3 * tile : (k3 + 1) * tile] = totals[k3]

    square, weighted, crossed = (
        jnp.sum(sums[:, k3 * tile : (k3 + 1) * tile], axis=1, keepdims=True) * (1.0 / width)
        for k3 in range(3)
    )
    scale = lax.rsqrt(square + EPS)
    push_scale = 2.0 * loss_scale
    mean = push_scale * scale * (scale * weighted - crossed)
    sums[:, :tile] = jnp.broadcast_to(scale, (rows, tile))
    sums[:, tile : 2 * tile] = jnp.broadcast_to(mean, (rows, tile))

    @pl.loop(0, rows // step, unroll=2)
    def _(k):
        sl = pl.ds(pl.multiple_of(k * step, step), step)
        scale = sums[sl, :tile]
        mean = sums[sl, tile : 2 * tile]
        for j in range(0, width, tile):
            cols = slice(j, j + tile)
            gain = gain_ref[:, first_lane + j : first_lane + j + tile]
            unit = gated_ref[sl, cols] * scale
            normed = unit * gain
            out_ref[sl, cols] = normed.astype(BF16)
            push = (normed - teacher_ref[sl, cols].astype(F32)) * push_scale
            by_gain = push * unit
            by_skip = (push * gain - unit * mean) * (scale * sx_ref[sl, cols])
            gain_acc[:, cols] += by_gain[:8] + by_gain[8:]
            skip_acc[:, cols] += by_skip[:8] + by_skip[8:]

    row = lax.broadcasted_iota(jnp.int32, (tile, width), 0)
    lane = lax.broadcasted_iota(jnp.int32, (tile, width), 1)
    matrix = jnp.where(row == lane // P_SIZE + g * (width // P_SIZE), 1.0, 0.0).astype(BF16)
    hi, lo = parts(skip_acc[...])
    by_head = jnp.sum(dot_nt(hi, matrix) + dot_nt(lo, matrix), axis=0, keepdims=True)
    grad_ref[...] = jnp.zeros_like(grad_ref)
    if g:
        grad_ref[:g, :] = before[:g, :]
        by_head += before[groups : groups + 1, :tile]
    grad_ref[g : g + 1, :] = jnp.sum(gain_acc[...], axis=0, keepdims=True)
    grad_ref[groups : groups + 1, :tile] = by_head


def writing_kernel(*refs):
    parts_in, out_ref, sems = refs[:-2], refs[-2], refs[-1]
    width = parts_in[0].shape[1]
    moves = [
        pltpu.make_async_copy(part, out_ref.at[:, pl.ds(k * width, width)], sems.at[k])
        for k, part in enumerate(parts_in)
    ]
    for move in moves:
        move.start()
    for move in moves:
        move.wait()


def closing_kernel(a_ref, b_ref, gain_ref, skip_ref):
    total = a_ref[...] + b_ref[...]
    groups, width = total.shape[0] - 1, total.shape[1]
    for g in range(groups):
        gain_ref[:, g * width : (g + 1) * width] = total[g : g + 1, :]
    skip_ref[...] = total[groups : groups + 1, : skip_ref.shape[1]]


def exchange(part, shift):
    axes = ("dp", "ctx")
    size = lax.axis_size(axes)
    return lax.ppermute(part, axes, [(d, d ^ shift) for d in range(size)])


def body(
    queries,
    keys,
    values,
    doc_ids,
    inputs,
    gate_input,
    b_input,
    c_input,
    dt_raw,
    dt_bias,
    decay_log,
    skip,
    gain,
):
    count = lax.axis_size("ctx")
    rows, features = queries.shape[1:]
    stretch = rows // 2
    kv_dev = keys.shape[2] // DH
    per_kv = queries.shape[2] // keys.shape[2]
    groups = b_input.shape[2] // N
    heads = features // P_SIZE
    width = features // groups
    length = doc_ids.shape[1]
    others = count - 1
    loss_scale = 1.0 / (lax.axis_size("dp") * count * rows)
    x, gate, bmat, cmat = inputs[0], gate_input[0], b_input[0], c_input[0]
    struct = jax.ShapeDtypeStruct

    def in_hbm(*arrays):
        return [pltpu.with_memory_space_constraint(array, pltpu.HBM) for array in arrays]

    def write(*pieces):
        return pl.pallas_call(
            writing_kernel,
            out_shape=struct((rows, features), BF16),
            in_specs=[VMEM] * len(pieces),
            out_specs=pl.BlockSpec(memory_space=pl.ANY),
            scratch_shapes=[pltpu.SemaphoreType.DMA((len(pieces),))],
            compiler_params=params(2),
            cost_estimate=cost(0, 4 * rows * features),
            name="writing",
        )(*pieces)

    state = struct((N, width), BF16)
    payload = struct((N + EXTRA, width), BF16)
    outs = pl.pallas_call(
        functools.partial(opening_kernel, count, groups),
        out_shape=(
            struct((rows, 2 * kv_dev * DH), BF16),
            struct((heads, rows), F32),
            *([struct((rows, width), BF16)] * groups),
            *([struct((8, width), F32)] * groups),
            *([state] * (2 * groups)),
            *([payload] * groups),
        ),
        in_specs=[VMEM] * 8,
        out_specs=(VMEM,) * (2 + 5 * groups),
        compiler_params=params(16),
        cost_estimate=cost(4 * rows * features * N, 8 * rows * features),
        name="opening",
    )(
        *in_hbm(
            doc_ids,
            keys[0],
            values[0],
            x,
            bmat,
            dt_raw[0].T,
            dt_bias.reshape(1, heads),
            decay_log.reshape(1, heads),
        )
    )
    kv, ec = outs[:2]
    xw, dec, f_parts, b_parts, send = (
        outs[2 + k * groups : 2 + (k + 1) * groups] for k in range(5)
    )

    local = pl.pallas_call(
        functools.partial(local_kernel, count, groups),
        out_shape=(struct((rows, width), F32),) * (3 * groups),
        in_specs=[
            VMEM,
            *[pl.BlockSpec(memory_space=pl.ANY)] * 2,
            *[VMEM] * (4 + groups),
        ],
        out_specs=(VMEM,) * (3 * groups),
        scratch_shapes=[
            pltpu.VMEM((groups, rows, width), BF16),
            pltpu.VMEM((groups, rows, width), BF16),
            pltpu.SemaphoreType.DMA((2, groups)),
        ],
        compiler_params=params(16),
        cost_estimate=cost(2 * rows * features * N, 16 * rows * features),
        name="local",
    )(*in_hbm(doc_ids, x, gate, bmat, cmat, skip.reshape(1, heads)), ec, *xw)

    send = list(send)
    got = [[] for _ in range(groups)]
    if count == 4:
        inward, outward, across = [(0, 1), (3, 2)], [(1, 0), (2, 3)], [(1, 2), (2, 1)]
        near = lax.ppermute(kv, "ctx", inward + outward)
        middle = lax.ppermute(kv, "ctx", across)
        middle, near, *local = lax.optimization_barrier((middle, near, *local))
        beyond = lax.ppermute(near, "ctx", across)
        send[-1] = pl.pallas_call(
            functools.partial(merge_kernel, count),
            out_shape=payload,
            in_specs=[VMEM] * 2,
            out_specs=VMEM,
            compiler_params=params(4),
            cost_estimate=cost(0, 4 * N * width),
            name="merge",
        )(send[-1], middle)
        far = lax.ppermute(send[-1], "ctx", inward + outward)
        got[-1].append(far)
        farther = lax.ppermute(beyond, "ctx", outward)
        kv_got = [near, middle, beyond, far, farther]
    else:
        ring = ring_order(count)
        ring_pairs = [(ring[d], ring[(d + 1) % count]) for d in range(count)]
        kv_got = [kv]
        for _ in range(others):
            kv_got.append(lax.ppermute(kv_got[-1], "ctx", ring_pairs))
        kv_got = kv_got[1:]
    stack = 4 if per_kv % 4 == 0 and count <= 4 else 1
    targets = [
        pl.pallas_call(
            functools.partial(attention_kernel, count, per_kv, stack, g),
            out_shape=struct((rows, per_kv * DH), BF16),
            in_specs=[VMEM] * (4 + len(kv_got)),
            out_specs=VMEM,
            scratch_shapes=[
                pltpu.VMEM((2 * count * stretch, DH), BF16),
                pltpu.VMEM((2 * count * stretch, 2 * DH), BF16),
                pltpu.VMEM((stretch, stretch), F32),
                pltpu.VMEM((stretch, (count + 1) * stretch), F32),
                pltpu.VMEM((stretch, others * stretch), F32),
            ],
            compiler_params=params(24),
            cost_estimate=cost(
                4 * (2 * count + 1) * stretch * stretch * per_kv * DH, 8 * rows * per_kv * DH
            ),
            name="attention",
        )(doc_ids, queries[0], keys[0], values[0], *kv_got)
        for g in range(kv_dev)
    ]
    for r in range(1, count):
        for g in range(groups):
            if r == 3 and g == groups - 1:
                got[g][-1], targets[0] = lax.optimization_barrier((got[g][-1], targets[0]))
            if r > 1:
                send[g] = pl.pallas_call(
                    functools.partial(chain_kernel, count, r - 1),
                    out_shape=payload,
                    in_specs=[VMEM] * 4,
                    out_specs=VMEM,
                    compiler_params=params(4),
                    cost_estimate=cost(8 * N * width, 8 * N * width),
                    name="chain",
                )(got[g][-1], f_parts[g], b_parts[g], dec[g])
            if len(got[g]) < r:
                pairs = [(r - 1, r), (count - r, count - r - 1)]
                got[g].append(lax.ppermute(send[g], "ctx", pairs))

    normed, grads = [], None
    for g in range(groups):
        more = [] if grads is None else [grads]
        made, grads = pl.pallas_call(
            functools.partial(final_kernel, count, g, groups, loss_scale),
            out_shape=(struct((rows, width), BF16), struct((groups + 1, width), F32)),
            in_specs=[VMEM] * (8 + others + len(more)),
            out_specs=(VMEM,) * 2,
            scratch_shapes=[
                pltpu.VMEM((N, width), BF16),
                pltpu.VMEM((N + EXTRA, width), BF16),
                pltpu.VMEM((rows, width), F32),
                pltpu.VMEM((rows, width), F32),
                pltpu.VMEM((rows, 3 * 128), F32),
                pltpu.VMEM((8, width), F32),
                pltpu.VMEM((8, width), F32),
            ],
            compiler_params=params(16),
            cost_estimate=cost(2 * rows * width * N, 20 * rows * width),
            name="final",
        )(
            *local[g::groups],
            cmat,
            targets[g],
            gain.reshape(1, features),
            f_parts[g],
            dec[g],
            *got[g],
            *more,
        )
        normed.append(made)
    teacher, student = write(*targets), write(*normed)
    partner = exchange(grads, 1)
    if lax.axis_size("dp") == 2:
        grads = (grads + partner) + (exchange(grads, count) + exchange(grads, count + 1))
    else:
        grads = grads + partner
    shifts = [1 << k for k in range(1, count.bit_length() - 1)]
    for shift in shifts[:-1]:
        grads = grads + exchange(grads, shift)
    grad_gain, grad_skip = pl.pallas_call(
        closing_kernel,
        out_shape=(struct((1, features), F32), struct((1, heads), F32)),
        in_specs=[VMEM] * 2,
        out_specs=(VMEM,) * 2,
        compiler_params=params(2),
        name="closing",
    )(grads, exchange(grads, shifts[-1]))
    return (teacher[None], student[None], grad_gain[0], grad_skip[0])


def solution(mesh):
    rows = P("dp", "ctx", "head")
    in_specs = (
        rows,
        rows,
        rows,
        P("dp", None),
        rows,
        rows,
        rows,
        rows,
        rows,
        P("head"),
        P("head"),
        P("head"),
        P("head"),
    )
    out_specs = (rows, rows, P("head"), P("head"))
    return jax.shard_map(body, mesh=mesh, in_specs=in_specs, out_specs=out_specs, check_vma=False)
```

```python
import functools
import math

import jax
import jax.numpy as jnp
from jax import lax
from jax.experimental import pallas as pl
from jax.experimental.pallas import tpu as pltpu
from jax.sharding import PartitionSpec as P

DH = 128
P_SIZE = 64
N = 128
EXTRA = 16
EPS = 1e-05
MASKED = -1e30
F32 = jnp.float32
BF16 = jnp.bfloat16
VMEM = pl.BlockSpec(memory_space=pltpu.VMEM)


def params(mib):
    return pltpu.CompilerParams(vmem_limit_bytes=mib << 20)


def cost(flops, size):
    return pl.CostEstimate(flops=flops, bytes_accessed=size, transcendentals=0)


def parts(v):
    hi = v.astype(BF16)
    return hi, (v - hi.astype(F32)).astype(BF16)


def spread_matrix(heads, width, first):
    row = lax.broadcasted_iota(jnp.int32, (heads, width), 0)
    lane = lax.broadcasted_iota(jnp.int32, (heads, width), 1)
    return jnp.where(row == (lane // P_SIZE) + first, 1.0, 0.0).astype(BF16)


def dot_nt(a, b):
    return lax.dot_general(a, b, (((1,), (1,)), ((), ())), preferred_element_type=F32)


def dot_tn(a, b):
    return lax.dot_general(a, b, (((0,), (0,)), ((), ())), preferred_element_type=F32)


def spread(v, matrix):
    return dot_tn(jnp.concatenate(parts(v), axis=0), jnp.concatenate([matrix, matrix], axis=0))


def doc_row(docs_ref, block, stretch):
    return docs_ref[:, pl.ds(pl.multiple_of(block * stretch, stretch), stretch)]


def as_column(row):
    size = row.shape[1]
    r = lax.broadcasted_iota(jnp.int32, (size, size), 0)
    c = lax.broadcasted_iota(jnp.int32, (size, size), 1)
    return jnp.sum(jnp.where(r == c, row.astype(F32), 0.0), axis=1, keepdims=True)


def lower_triangle(size):
    r = lax.broadcasted_iota(jnp.int32, (size, size), 0)
    c = lax.broadcasted_iota(jnp.int32, (size, size), 1)
    return r >= c


def prior_doc(docs_ref, block, stretch):
    before = doc_row(docs_ref, jnp.maximum(block - 1, 0), stretch)[:, stretch - 1 :]
    return jnp.where(block > 0, before, -1)


def own_block(index, count, half):
    return index if half == 0 else 2 * count - 1 - index


def ring_order(count):
    return [0] + list(range(1, count, 2)) + list(range(2, count, 2))[::-1]


def ring_source(index, count, steps):
    order = ring_order(count)
    source = jnp.int32(0)
    for place, member in enumerate(order):
        source = jnp.where(index == member, order[(place - steps) % count], source)
    return source


def put_state(ref, state):
    ref[:N, :] = state.astype(BF16)
    ref[N:, :] = jnp.zeros((EXTRA, ref.shape[1]), BF16)


def put_composite(ref, state, decay):
    hi, lo = parts(decay)
    ref[:N, :] = state.astype(BF16)
    ref[N:, :] = jnp.concatenate(
        [hi, lo, jnp.zeros((EXTRA - 2, ref.shape[1]), BF16)], axis=0
    )


def opening_kernel(
    count,
    groups,
    docs_ref,
    k_ref,
    v_ref,
    x_ref,
    b_ref,
    dt_ref,
    bias_ref,
    log_ref,
    kv_ref,
    ec_ref,
    *outs,
):
    xw_refs, dec_refs, f_refs, b_refs, send_refs = (
        outs[k * groups : (k + 1) * groups] for k in range(5)
    )
    heads, rows = dt_ref.shape
    stretch = rows // 2
    width = x_ref.shape[1] // groups
    kv_width = k_ref.shape[1]
    index = lax.axis_index("ctx")
    kv_ref[:, :kv_width] = k_ref[...]
    kv_ref[:, kv_width:] = v_ref[...]
    triangle = jnp.where(lower_triangle(stretch), 1.0, 0.0)
    slope = jnp.exp(as_column(log_ref[...]))
    bias = as_column(bias_ref[...])
    lane = lax.broadcasted_iota(jnp.int32, (heads, 8), 1)
    ends = jnp.zeros((heads, 8), F32)
    loads = []
    projs = []
    for half in range(2):
        block = own_block(index, count, half)
        sl = slice(half * stretch, (half + 1) * stretch)
        raw = dt_ref[:, sl] + bias
        dt = jnp.maximum(raw, 0.0) + jnp.log1p(jnp.exp(-jnp.abs(raw)))
        cum = lax.dot_general(
            -dt * slope,
            triangle,
            (((1,), (1,)), ((), ())),
            precision=lax.Precision.HIGHEST,
            preferred_element_type=F32,
        )
        ec_ref[:, sl] = jnp.exp(cum)
        loads.append(jnp.exp(-cum) * dt)
        final = jnp.exp(cum[:, stretch - 1 :])
        row = doc_row(docs_ref, block, stretch)
        last = row[:, stretch - 1 :]
        kept = jnp.where(last == prior_doc(docs_ref, block, stretch), 1.0, 0.0)
        ends = jnp.where(lane == half, final * kept, ends)
        ends = jnp.where(lane == 2 + half, final, ends)
        same = jnp.where(as_column(row) == last.astype(F32), 1.0, 0.0)
        projs.append((b_ref[sl, :].astype(F32) * same).astype(BF16))
    for g in range(groups):
        cols = slice(g * width, (g + 1) * width)
        matrix = spread_matrix(heads, width, g * (heads // groups))
        wide = spread(ends, matrix)
        dec_refs[g][...] = wide
        sums = []
        for half in range(2):
            sl = slice(half * stretch, (half + 1) * stretch)
            xw = (x_ref[sl, cols].astype(F32) * spread(loads[half], matrix)).astype(BF16)
            xw_refs[g][sl, :] = xw
            sums.append(dot_tn(projs[half][:, g * N : (g + 1) * N], xw) * wide[2 + half : 3 + half])
        f_refs[g][...] = sums[0].astype(BF16)
        b_refs[g][...] = sums[1].astype(BF16)

        @pl.when(index == 0)
        def _():
            put_state(send_refs[g], sums[0])

        @pl.when(index != 0)
        def _():
            put_composite(send_refs[g], wide[1:2] * sums[0] + sums[1], wide[0:1] * wide[1:2])


def chain_kernel(count, stage, got_ref, f_ref, b_ref, dec_ref, send_ref):
    index = lax.axis_index("ctx")

    @pl.when(index == stage)
    def _():
        state = dec_ref[0:1, :] * got_ref[:N, :].astype(F32) + f_ref[...].astype(F32)
        put_state(send_ref, state)

    @pl.when(index == count - 1 - stage)
    def _():
        decay = got_ref[N : N + 1, :].astype(F32) + got_ref[N + 1 : N + 2, :].astype(F32)
        inner = decay * f_ref[...].astype(F32) + got_ref[:N, :].astype(F32)
        state = dec_ref[1:2, :] * inner + b_ref[...].astype(F32)
        put_composite(send_ref, state, dec_ref[1:2, :] * decay * dec_ref[0:1, :])


def local_kernel(
    count, groups, docs_ref, x_ref, gate_ref, b_ref, c_ref, skip_ref, ec_ref, *refs
):
    xw_refs, pre_refs, reach_refs, sx_refs = (
        refs[k * groups : (k + 1) * groups] for k in range(4)
    )
    x_here, gate_here, sems = refs[4 * groups :]
    heads, rows = ec_ref.shape
    stretch = rows // 2
    width = x_ref.shape[1] // groups
    index = lax.axis_index("ctx")
    moves = []
    for g in range(groups):
        cols = pl.ds(g * width, width)
        moves.append(
            [
                pltpu.make_async_copy(x_ref.at[:, cols], x_here.at[g], sems.at[0, g]),
                pltpu.make_async_copy(gate_ref.at[:, cols], gate_here.at[g], sems.at[1, g]),
            ]
        )
        for move in moves[g]:
            move.start()
    triangle = lower_triangle(stretch)
    skip = as_column(skip_ref[...])
    step = 16
    masks = []
    for half in range(2):
        block = own_block(index, count, half)
        row = doc_row(docs_ref, block, stretch)
        column = as_column(row)
        reached = jnp.where(column == prior_doc(docs_ref, block, stretch).astype(F32), 1.0, 0.0)
        masks.append((triangle & (column == row.astype(F32)), reached))
    for g in range(groups):
        proj = slice(g * N, (g + 1) * N)
        matrix = spread_matrix(heads, width, g * (heads // groups))
        wide_skip = spread(skip, matrix)
        for half in range(2):
            sl = slice(half * stretch, (half + 1) * stretch)
            near, reached = masks[half]
            gram = dot_nt(c_ref[sl, proj], b_ref[sl, proj])
            gram = jnp.where(near, gram, 0.0).astype(BF16)
            wide = spread(ec_ref[:, sl], matrix)
            inner = jnp.dot(gram, xw_refs[g][sl, :], preferred_element_type=F32)
            if half == 0:
                for move in moves[g]:
                    move.wait()
            for k in range(0, stretch, step):
                at = slice(half * stretch + k, half * stretch + k + step)
                here = slice(k, k + step)
                x = x_here[g, at, :].astype(F32)
                gate = gate_here[g, at, :].astype(F32)
                silu = gate / (1.0 + jnp.exp(-gate))
                fade = wide[here] * silu
                sx = silu * x
                sx_refs[g][at, :] = sx
                pre_refs[g][at, :] = inner[here] * fade + wide_skip * sx
                reach_refs[g][at, :] = reached[here] * fade


def merge_kernel(count, state_ref, kv_ref, out_ref):
    index = lax.axis_index("ctx")
    outer = (index == 0) | (index == count - 1)
    rows, wide = kv_ref.shape
    stretch = rows // 2

    @pl.when(outer)
    def _():
        out_ref[...] = state_ref[...]

    @pl.when(jnp.logical_not(outer))
    def _():
        out_ref[:stretch, :wide] = kv_ref[:stretch, :]
        out_ref[:stretch, wide:] = kv_ref[stretch:, :]
        out_ref[stretch:, :] = jnp.zeros((out_ref.shape[0] - stretch, 2 * wide), BF16)


def arrivals(index, count, refs):
    if count != 4:
        return [(ring_source(index, count, r + 1), [(None, refs[r])]) for r in range(count - 1)]
    near, own_of_middle, next_of_middle, far, farther = refs
    middle = (index == 1) | (index == 2)
    low = index < 2
    return [
        (index ^ 1, [(None, near)]),
        (
            jnp.where(low, 2, 1),
            [(middle, own_of_middle), (jnp.logical_not(middle), far)],
        ),
        (
            jnp.where(low, 3, 0),
            [(middle, next_of_middle), (jnp.logical_not(middle), farther)],
        ),
    ]


def attention_kernel(count, per, stack, g, docs_ref, q_ref, k_ref, v_ref, *refs):
    others = count - 1
    sent = 5 if count == 4 else others
    out_ref, kt, vt, bias_f, bias_b, bias_a = refs[-6:]
    rows = q_ref.shape[0]
    stretch = rows // 2
    index = lax.axis_index("ctx")
    last = 2 * count - 1
    kv_width = refs[0].shape[1] // 2
    row_f = doc_row(docs_ref, index, stretch).astype(F32)
    row_b = doc_row(docs_ref, last - index, stretch).astype(F32)
    col_f = as_column(row_f)
    col_b = as_column(row_b)
    triangle = lower_triangle(stretch)

    def tile(k):
        return slice(k * stretch, (k + 1) * stretch)

    bias_f[...] = jnp.where(triangle & (col_f == row_f), 0.0, MASKED)
    bias_b[:, tile(0)] = jnp.where(col_b == row_f, 0.0, MASKED)
    bias_b[:, tile(1)] = jnp.where(triangle & (col_b == row_b), 0.0, MASKED)
    vt[:, DH:] = jnp.ones((vt.shape[0], DH), BF16)
    here = slice(g * DH, (g + 1) * DH)
    kt[tile(0), :] = k_ref[:stretch, here]
    vt[tile(0), :DH] = v_ref[:stretch, here]
    kt[tile(count), :] = k_ref[stretch:, here]
    vt[tile(count), :DH] = v_ref[stretch:, here]
    lower = []
    for r, (source, places) in enumerate(arrivals(index, count, refs[:sent])):
        lower.append(source < index)
        for condition, ref in places:

            def fetch(ref=ref, r=r):
                folded = ref.shape[1] > 2 * kv_width
                gap = jnp.where(lower[r], 0, 2 * kv_width if folded else stretch)
                for table, first in ((kt, g * DH), (vt, kv_width + g * DH)):
                    front = ref[:stretch, first : first + DH]
                    if folded:
                        own = ref[:stretch, pl.ds(pl.multiple_of(first + gap, DH), DH)]
                    else:
                        own = ref[pl.ds(pl.multiple_of(gap, stretch), stretch), first : first + DH]
                    table[tile(1 + r), :DH] = own
                    table[tile(count + 1 + r), :DH] = front

            if condition is None:
                fetch()
            else:
                pl.when(condition)(fetch)
        key_f = doc_row(docs_ref, source, stretch).astype(F32)
        key_a = doc_row(docs_ref, jnp.where(lower[r], source, last - source), stretch).astype(F32)
        bias_b[:, tile(2 + r)] = jnp.where(col_b == key_f, 0.0, MASKED)
        bias_a[:, tile(r)] = jnp.where(jnp.where(lower[r], col_f, col_b) == key_a, 0.0, MASKED)

    factor = math.log2(math.e) / math.sqrt(DH)
    tall = stack * stretch
    half_keys = count * stretch

    def stacked(first, base):
        return jnp.concatenate(
            [
                q_ref[base : base + stretch, (g * per + first + j) * DH : (g * per + first + j + 1) * DH]
                for j in range(stack)
            ],
            axis=0,
        )

    def biased(score, bias):
        size = score.shape[1]
        return (score.reshape(stack, stretch, size) + bias[None]).reshape(tall, size)

    for first in range(0, per, stack):
        s_f = dot_nt(stacked(first, 0), kt[:half_keys, :])
        s_b = dot_nt(stacked(first, stretch), kt[...])
        t_f = biased(s_f[:, tile(0)], bias_f[...])
        t_b = [biased(s_b[:, tile(0)], bias_b[:, tile(0)])]
        for k in range(1, count + 1):
            t_b.append(biased(s_b[:, tile(count + k - 1)], bias_b[:, tile(k)]))
        t_a = []
        for r in range(others):
            score = jnp.where(lower[r], s_f[:, tile(1 + r)], s_b[:, tile(1 + r)])
            t_a.append(biased(score, bias_a[:, tile(r)]))
        best_f = t_f
        best_b = functools.reduce(jnp.maximum, t_b)
        for r in range(others):
            best_f = jnp.maximum(best_f, jnp.where(lower[r], t_a[r], MASKED))
            best_b = jnp.maximum(best_b, jnp.where(lower[r], MASKED, t_a[r]))
        top_f = jnp.max(best_f, axis=1, keepdims=True)
        top_b = jnp.max(best_b, axis=1, keepdims=True)
        w_f = [jnp.exp2((t_f - top_f) * factor).astype(BF16)]
        w_b = [jnp.exp2((t - top_b) * factor).astype(BF16) for t in t_b]
        w_x = []
        for r in range(others):
            top = jnp.where(lower[r], top_f, top_b)
            w = jnp.exp2((t_a[r] - top) * factor)
            w_f.append(jnp.where(lower[r], w, 0.0).astype(BF16))
            w_x.append(jnp.where(lower[r], 0.0, w).astype(BF16))
        w_b = w_b[:1] + w_x + w_b[1:]
        out_f = jnp.dot(
            jnp.concatenate(w_f, axis=1), vt[:half_keys, :], preferred_element_type=F32
        )
        out_b = jnp.dot(jnp.concatenate(w_b, axis=1), vt[...], preferred_element_type=F32)
        for half, out in enumerate((out_f, out_b)):
            result = (out[:, :DH] / out[:, DH:]).astype(BF16)
            for j in range(stack):
                cols = slice((first + j) * DH, (first + j + 1) * DH)
                out_ref[tile(half), cols] = result[tile(j)]


def final_kernel(
    count,
    g,
    groups,
    loss_scale,
    pre_ref,
    reach_ref,
    sx_ref,
    c_ref,
    teacher_ref,
    gain_ref,
    f_ref,
    dec_ref,
    *refs,
):
    others = count - 1
    got = refs[:others]
    before = refs[others] if g else None
    proj = slice(g * N, (g + 1) * N)
    first_lane = g * pre_ref.shape[1]
    out_ref, grad_ref, front, back, flow, gated_ref, sums, gain_acc, skip_acc = refs[-9:]
    rows, width = pre_ref.shape
    stretch = rows // 2
    index = lax.axis_index("ctx")
    tile = 128
    step = 16

    @pl.when(index == 0)
    def _():
        front[...] = jnp.zeros_like(front)

    @pl.when(index == count - 1)
    def _():
        back[:N, :] = jnp.zeros((N, width), BF16)
        back[N:, :] = jnp.where(
            lax.broadcasted_iota(jnp.int32, (EXTRA, width), 0) == 0, 1.0, 0.0
        ).astype(BF16)

    for r in range(1, count):

        @pl.when(index == r)
        def _():
            front[...] = got[r - 1][:N, :]

        @pl.when(index == count - 1 - r)
        def _():
            back[...] = got[r - 1][...]

    d_in = back[N : N + 1, :].astype(F32) + back[N + 1 : N + 2, :].astype(F32)
    through = dec_ref[0:1, :] * front[...].astype(F32) + f_ref[...].astype(F32)
    entering = (d_in * through + back[:N, :].astype(F32)).astype(BF16)
    flow[:stretch, :] = jnp.dot(c_ref[:stretch, proj], front[...], preferred_element_type=F32)
    flow[stretch:, :] = jnp.dot(c_ref[stretch:, proj], entering, preferred_element_type=F32)
    gain_acc[...] = jnp.zeros_like(gain_acc)
    skip_acc[...] = jnp.zeros_like(skip_acc)

    @pl.loop(0, rows // step, unroll=2)
    def _(k):
        sl = pl.ds(pl.multiple_of(k * step, step), step)
        totals = [jnp.zeros((step, tile), F32)] * 3
        for j in range(0, width, tile):
            cols = slice(j, j + tile)
            gated = pre_ref[sl, cols] + reach_ref[sl, cols] * flow[sl, cols]
            gated_ref[sl, cols] = gated
            scaled = gated * gain_ref[:, first_lane + j : first_lane + j + tile]
            totals[0] += gated * gated
            totals[1] += scaled * scaled
            totals[2] += scaled * teacher_ref[sl, cols].astype(F32)
        for k3 in range(3):
            sums[sl, k3 * tile : (k3 + 1) * tile] = totals[k3]

    square, weighted, crossed = (
        jnp.sum(sums[:, k3 * tile : (k3 + 1) * tile], axis=1, keepdims=True) * (1.0 / width)
        for k3 in range(3)
    )
    scale = lax.rsqrt(square + EPS)
    push_scale = 2.0 * loss_scale
    mean = push_scale * scale * (scale * weighted - crossed)
    sums[:, :tile] = jnp.broadcast_to(scale, (rows, tile))
    sums[:, tile : 2 * tile] = jnp.broadcast_to(mean, (rows, tile))

    @pl.loop(0, rows // step, unroll=2)
    def _(k):
        sl = pl.ds(pl.multiple_of(k * step, step), step)
        scale = sums[sl, :tile]
        mean = sums[sl, tile : 2 * tile]
        for j in range(0, width, tile):
            cols = slice(j, j + tile)
            gain = gain_ref[:, first_lane + j : first_lane + j + tile]
            unit = gated_ref[sl, cols] * scale
            normed = unit * gain
            out_ref[sl, cols] = normed.astype(BF16)
            push = (normed - teacher_ref[sl, cols].astype(F32)) * push_scale
            by_gain = push * unit
            by_skip = (push * gain - unit * mean) * (scale * sx_ref[sl, cols])
            gain_acc[:, cols] += by_gain[:8] + by_gain[8:]
            skip_acc[:, cols] += by_skip[:8] + by_skip[8:]

    row = lax.broadcasted_iota(jnp.int32, (tile, width), 0)
    lane = lax.broadcasted_iota(jnp.int32, (tile, width), 1)
    matrix = jnp.where(row == lane // P_SIZE + g * (width // P_SIZE), 1.0, 0.0).astype(BF16)
    hi, lo = parts(skip_acc[...])
    by_head = jnp.sum(dot_nt(hi, matrix) + dot_nt(lo, matrix), axis=0, keepdims=True)
    grad_ref[...] = jnp.zeros_like(grad_ref)
    if g:
        grad_ref[:g, :] = before[:g, :]
        by_head += before[groups : groups + 1, :tile]
    grad_ref[g : g + 1, :] = jnp.sum(gain_acc[...], axis=0, keepdims=True)
    grad_ref[groups : groups + 1, :tile] = by_head


def writing_kernel(*refs):
    parts_in, out_ref, sems = refs[:-2], refs[-2], refs[-1]
    width = parts_in[0].shape[1]
    moves = [
        pltpu.make_async_copy(part, out_ref.at[:, pl.ds(k * width, width)], sems.at[k])
        for k, part in enumerate(parts_in)
    ]
    for move in moves:
        move.start()
    for move in moves:
        move.wait()


def closing_kernel(a_ref, b_ref, gain_ref, skip_ref):
    total = a_ref[...] + b_ref[...]
    groups, width = total.shape[0] - 1, total.shape[1]
    for g in range(groups):
        gain_ref[:, g * width : (g + 1) * width] = total[g : g + 1, :]
    skip_ref[...] = total[groups : groups + 1, : skip_ref.shape[1]]


def exchange(part, shift):
    axes = ("dp", "ctx")
    size = lax.axis_size(axes)
    return lax.ppermute(part, axes, [(d, d ^ shift) for d in range(size)])


def body(
    queries,
    keys,
    values,
    doc_ids,
    inputs,
    gate_input,
    b_input,
    c_input,
    dt_raw,
    dt_bias,
    decay_log,
    skip,
    gain,
):
    count = lax.axis_size("ctx")
    rows, features = queries.shape[1:]
    stretch = rows // 2
    kv_dev = keys.shape[2] // DH
    per_kv = queries.shape[2] // keys.shape[2]
    groups = b_input.shape[2] // N
    heads = features // P_SIZE
    width = features // groups
    length = doc_ids.shape[1]
    others = count - 1
    loss_scale = 1.0 / (lax.axis_size("dp") * count * rows)
    x, gate, bmat, cmat = inputs[0], gate_input[0], b_input[0], c_input[0]
    struct = jax.ShapeDtypeStruct

    def in_hbm(*arrays):
        return [pltpu.with_memory_space_constraint(array, pltpu.HBM) for array in arrays]

    def write(*pieces):
        return pl.pallas_call(
            writing_kernel,
            out_shape=struct((rows, features), BF16),
            in_specs=[VMEM] * len(pieces),
            out_specs=pl.BlockSpec(memory_space=pl.ANY),
            scratch_shapes=[pltpu.SemaphoreType.DMA((len(pieces),))],
            compiler_params=params(2),
            cost_estimate=cost(0, 4 * rows * features),
            name="writing",
        )(*pieces)

    state = struct((N, width), BF16)
    payload = struct((N + EXTRA, width), BF16)
    outs = pl.pallas_call(
        functools.partial(opening_kernel, count, groups),
        out_shape=(
            struct((rows, 2 * kv_dev * DH), BF16),
            struct((heads, rows), F32),
            *([struct((rows, width), BF16)] * groups),
            *([struct((8, width), F32)] * groups),
            *([state] * (2 * groups)),
            *([payload] * groups),
        ),
        in_specs=[VMEM] * 8,
        out_specs=(VMEM,) * (2 + 5 * groups),
        compiler_params=params(16),
        cost_estimate=cost(4 * rows * features * N, 8 * rows * features),
        name="opening",
    )(
        *in_hbm(
            doc_ids,
            keys[0],
            values[0],
            x,
            bmat,
            dt_raw[0].T,
            dt_bias.reshape(1, heads),
            decay_log.reshape(1, heads),
        )
    )
    kv, ec = outs[:2]
    xw, dec, f_parts, b_parts, send = (
        outs[2 + k * groups : 2 + (k + 1) * groups] for k in range(5)
    )

    local = pl.pallas_call(
        functools.partial(local_kernel, count, groups),
        out_shape=(struct((rows, width), F32),) * (3 * groups),
        in_specs=[
            VMEM,
            *[pl.BlockSpec(memory_space=pl.ANY)] * 2,
            *[VMEM] * (4 + groups),
        ],
        out_specs=(VMEM,) * (3 * groups),
        scratch_shapes=[
            pltpu.VMEM((groups, rows, width), BF16),
            pltpu.VMEM((groups, rows, width), BF16),
            pltpu.SemaphoreType.DMA((2, groups)),
        ],
        compiler_params=params(16),
        cost_estimate=cost(2 * rows * features * N, 16 * rows * features),
        name="local",
    )(*in_hbm(doc_ids, x, gate, bmat, cmat, skip.reshape(1, heads)), ec, *xw)

    send = list(send)
    got = [[] for _ in range(groups)]
    def passed_on(g, stage):
        return pl.pallas_call(
            functools.partial(chain_kernel, count, stage),
            out_shape=payload,
            in_specs=[VMEM] * 4,
            out_specs=VMEM,
            compiler_params=params(4),
            cost_estimate=pl.CostEstimate(flops=16384 * N * width, bytes_accessed=0, transcendentals=0),
            name="chain",
        )(got[g][-1], f_parts[g], b_parts[g], dec[g])

    def stage_pairs(stage):
        return [(stage - 1, stage), (count - stage, count - stage - 1)]

    if count == 4:
        inward, outward, across = [(0, 1), (3, 2)], [(1, 0), (2, 3)], [(1, 2), (2, 1)]
        near = lax.ppermute(kv, "ctx", inward + outward)
        middle = lax.ppermute(kv, "ctx", across)
        middle, near, *local = lax.optimization_barrier((middle, near, *local))
        beyond = lax.ppermute(near, "ctx", across)
        send[-1] = pl.pallas_call(
            functools.partial(merge_kernel, count),
            out_shape=payload,
            in_specs=[VMEM] * 2,
            out_specs=VMEM,
            compiler_params=params(4),
            cost_estimate=cost(0, 4 * N * width),
            name="merge",
        )(send[-1], middle)
        far = lax.ppermute(send[-1], "ctx", inward + outward)
        got[-1].append(far)
        send[-1] = passed_on(groups - 1, 1)
        got[-1].append(lax.ppermute(send[-1], "ctx", stage_pairs(2)))
        beyond, _ = lax.optimization_barrier((beyond, send[-1]))
        farther = lax.ppermute(beyond, "ctx", outward)
        kv_got = [near, middle, beyond, far, farther]
    else:
        ring = ring_order(count)
        ring_pairs = [(ring[d], ring[(d + 1) % count]) for d in range(count)]
        kv_got = [kv]
        for _ in range(others):
            kv_got.append(lax.ppermute(kv_got[-1], "ctx", ring_pairs))
        kv_got = kv_got[1:]
    stack = 4 if per_kv % 4 == 0 and count <= 4 else 1
    targets = [
        pl.pallas_call(
            functools.partial(attention_kernel, count, per_kv, stack, g),
            out_shape=struct((rows, per_kv * DH), BF16),
            in_specs=[VMEM] * (4 + len(kv_got)),
            out_specs=VMEM,
            scratch_shapes=[
                pltpu.VMEM((2 * count * stretch, DH), BF16),
                pltpu.VMEM((2 * count * stretch, 2 * DH), BF16),
                pltpu.VMEM((stretch, stretch), F32),
                pltpu.VMEM((stretch, (count + 1) * stretch), F32),
                pltpu.VMEM((stretch, others * stretch), F32),
            ],
            compiler_params=params(24),
            cost_estimate=cost(
                4 * (2 * count + 1) * stretch * stretch * per_kv * DH, 8 * rows * per_kv * DH
            ),
            name="attention",
        )(doc_ids, queries[0], keys[0], values[0], *kv_got)
        for g in range(kv_dev)
    ]
    for r in range(1, count):
        for g in range(groups):
            if len(got[g]) >= r:
                continue
            if r > 1:
                send[g] = passed_on(g, r - 1)
            got[g].append(lax.ppermute(send[g], "ctx", stage_pairs(r)))
    normed, grads = [], None
    for g in range(groups):
        more = [] if grads is None else [grads]
        made, grads = pl.pallas_call(
            functools.partial(final_kernel, count, g, groups, loss_scale),
            out_shape=(struct((rows, width), BF16), struct((groups + 1, width), F32)),
            in_specs=[VMEM] * (8 + others + len(more)),
            out_specs=(VMEM,) * 2,
            scratch_shapes=[
                pltpu.VMEM((N, width), BF16),
                pltpu.VMEM((N + EXTRA, width), BF16),
                pltpu.VMEM((rows, width), F32),
                pltpu.VMEM((rows, width), F32),
                pltpu.VMEM((rows, 3 * 128), F32),
                pltpu.VMEM((8, width), F32),
                pltpu.VMEM((8, width), F32),
            ],
            compiler_params=params(16),
            cost_estimate=cost(2 * rows * width * N, 20 * rows * width),
            name="final",
        )(
            *local[g::groups],
            cmat,
            targets[g],
            gain.reshape(1, features),
            f_parts[g],
            dec[g],
            *got[g],
            *more,
        )
        normed.append(made)
    teacher, student = write(*targets), write(*normed)
    partner = exchange(grads, 1)
    if lax.axis_size("dp") == 2:
        grads = (grads + partner) + (exchange(grads, count) + exchange(grads, count + 1))
    else:
        grads = grads + partner
    shifts = [1 << k for k in range(1, count.bit_length() - 1)]
    for shift in shifts[:-1]:
        grads = grads + exchange(grads, shift)
    grad_gain, grad_skip = pl.pallas_call(
        closing_kernel,
        out_shape=(struct((1, features), F32), struct((1, heads), F32)),
        in_specs=[VMEM] * 2,
        out_specs=(VMEM,) * 2,
        compiler_params=params(2),
        name="closing",
    )(grads, exchange(grads, shifts[-1]))
    return (teacher[None], student[None], grad_gain[0], grad_skip[0])


def solution(mesh):
    rows = P("dp", "ctx", "head")
    in_specs = (
        rows,
        rows,
        rows,
        P("dp", None),
        rows,
        rows,
        rows,
        rows,
        rows,
        P("head"),
        P("head"),
        P("head"),
        P("head"),
    )
    out_specs = (rows, rows, P("head"), P("head"))
    return jax.shard_map(body, mesh=mesh, in_specs=in_specs, out_specs=out_specs, check_vma=False)
```

```python
import functools
import math

import jax
import jax.numpy as jnp
from jax import lax
from jax.experimental import pallas as pl
from jax.experimental.pallas import tpu as pltpu
from jax.sharding import PartitionSpec as P

DH = 128
P_SIZE = 64
N = 128
EXTRA = 16
EPS = 1e-05
MASKED = -1e30
F32 = jnp.float32
BF16 = jnp.bfloat16
VMEM = pl.BlockSpec(memory_space=pltpu.VMEM)


def params(mib):
    return pltpu.CompilerParams(vmem_limit_bytes=mib << 20)


def cost(flops, size):
    return pl.CostEstimate(flops=flops, bytes_accessed=size, transcendentals=0)


def parts(v):
    hi = v.astype(BF16)
    return hi, (v - hi.astype(F32)).astype(BF16)


def spread_matrix(heads, width, first):
    row = lax.broadcasted_iota(jnp.int32, (heads, width), 0)
    lane = lax.broadcasted_iota(jnp.int32, (heads, width), 1)
    return jnp.where(row == (lane // P_SIZE) + first, 1.0, 0.0).astype(BF16)


def dot_nt(a, b):
    return lax.dot_general(a, b, (((1,), (1,)), ((), ())), preferred_element_type=F32)


def dot_tn(a, b):
    return lax.dot_general(a, b, (((0,), (0,)), ((), ())), preferred_element_type=F32)


def spread(v, matrix):
    return dot_tn(jnp.concatenate(parts(v), axis=0), jnp.concatenate([matrix, matrix], axis=0))


def doc_row(docs_ref, block, stretch):
    return docs_ref[:, pl.ds(pl.multiple_of(block * stretch, stretch), stretch)]


def as_column(row):
    size = row.shape[1]
    r = lax.broadcasted_iota(jnp.int32, (size, size), 0)
    c = lax.broadcasted_iota(jnp.int32, (size, size), 1)
    return jnp.sum(jnp.where(r == c, row.astype(F32), 0.0), axis=1, keepdims=True)


def lower_triangle(size):
    r = lax.broadcasted_iota(jnp.int32, (size, size), 0)
    c = lax.broadcasted_iota(jnp.int32, (size, size), 1)
    return r >= c


def prior_doc(docs_ref, block, stretch):
    before = doc_row(docs_ref, jnp.maximum(block - 1, 0), stretch)[:, stretch - 1 :]
    return jnp.where(block > 0, before, -1)


def own_block(index, count, half):
    return index if half == 0 else 2 * count - 1 - index


def ring_order(count):
    return [0] + list(range(1, count, 2)) + list(range(2, count, 2))[::-1]


def ring_source(index, count, steps):
    order = ring_order(count)
    source = jnp.int32(0)
    for place, member in enumerate(order):
        source = jnp.where(index == member, order[(place - steps) % count], source)
    return source


def put_state(ref, state):
    ref[:N, :] = state.astype(BF16)
    ref[N:, :] = jnp.zeros((EXTRA, ref.shape[1]), BF16)


def put_composite(ref, state, decay):
    hi, lo = parts(decay)
    ref[:N, :] = state.astype(BF16)
    ref[N:, :] = jnp.concatenate(
        [hi, lo, jnp.zeros((EXTRA - 2, ref.shape[1]), BF16)], axis=0
    )


def opening_kernel(
    count,
    groups,
    docs_ref,
    k_ref,
    v_ref,
    x_ref,
    b_ref,
    dt_ref,
    bias_ref,
    log_ref,
    kv_ref,
    ec_ref,
    *outs,
):
    xw_refs, dec_refs, f_refs, b_refs, send_refs = (
        outs[k * groups : (k + 1) * groups] for k in range(5)
    )
    heads, rows = dt_ref.shape
    stretch = rows // 2
    width = x_ref.shape[1] // groups
    kv_width = k_ref.shape[1]
    index = lax.axis_index("ctx")
    kv_ref[:, :kv_width] = k_ref[...]
    kv_ref[:, kv_width:] = v_ref[...]
    triangle = jnp.where(lower_triangle(stretch), 1.0, 0.0)
    slope = jnp.exp(as_column(log_ref[...]))
    bias = as_column(bias_ref[...])
    lane = lax.broadcasted_iota(jnp.int32, (heads, 8), 1)
    ends = jnp.zeros((heads, 8), F32)
    loads = []
    projs = []
    for half in range(2):
        block = own_block(index, count, half)
        sl = slice(half * stretch, (half + 1) * stretch)
        raw = dt_ref[:, sl] + bias
        dt = jnp.maximum(raw, 0.0) + jnp.log1p(jnp.exp(-jnp.abs(raw)))
        cum = lax.dot_general(
            -dt * slope,
            triangle,
            (((1,), (1,)), ((), ())),
            precision=lax.Precision.HIGHEST,
            preferred_element_type=F32,
        )
        ec_ref[:, sl] = jnp.exp(cum)
        loads.append(jnp.exp(-cum) * dt)
        final = jnp.exp(cum[:, stretch - 1 :])
        row = doc_row(docs_ref, block, stretch)
        last = row[:, stretch - 1 :]
        kept = jnp.where(last == prior_doc(docs_ref, block, stretch), 1.0, 0.0)
        ends = jnp.where(lane == half, final * kept, ends)
        ends = jnp.where(lane == 2 + half, final, ends)
        same = jnp.where(as_column(row) == last.astype(F32), 1.0, 0.0)
        projs.append((b_ref[sl, :].astype(F32) * same).astype(BF16))
    for g in range(groups):
        cols = slice(g * width, (g + 1) * width)
        matrix = spread_matrix(heads, width, g * (heads // groups))
        wide = spread(ends, matrix)
        dec_refs[g][...] = wide
        sums = []
        for half in range(2):
            sl = slice(half * stretch, (half + 1) * stretch)
            xw = (x_ref[sl, cols].astype(F32) * spread(loads[half], matrix)).astype(BF16)
            xw_refs[g][sl, :] = xw
            sums.append(dot_tn(projs[half][:, g * N : (g + 1) * N], xw) * wide[2 + half : 3 + half])
        f_refs[g][...] = sums[0].astype(BF16)
        b_refs[g][...] = sums[1].astype(BF16)

        @pl.when(index == 0)
        def _():
            put_state(send_refs[g], sums[0])

        @pl.when(index != 0)
        def _():
            put_composite(send_refs[g], wide[1:2] * sums[0] + sums[1], wide[0:1] * wide[1:2])


def chain_kernel(count, stage, got_ref, f_ref, b_ref, dec_ref, send_ref):
    index = lax.axis_index("ctx")

    @pl.when(index == stage)
    def _():
        state = dec_ref[0:1, :] * got_ref[:N, :].astype(F32) + f_ref[...].astype(F32)
        put_state(send_ref, state)

    @pl.when(index == count - 1 - stage)
    def _():
        decay = got_ref[N : N + 1, :].astype(F32) + got_ref[N + 1 : N + 2, :].astype(F32)
        inner = decay * f_ref[...].astype(F32) + got_ref[:N, :].astype(F32)
        state = dec_ref[1:2, :] * inner + b_ref[...].astype(F32)
        put_composite(send_ref, state, dec_ref[1:2, :] * decay * dec_ref[0:1, :])


def local_kernel(
    count, groups, docs_ref, x_ref, gate_ref, b_ref, c_ref, skip_ref, ec_ref, *refs
):
    xw_refs, pre_refs, reach_refs, sx_refs = (
        refs[k * groups : (k + 1) * groups] for k in range(4)
    )
    x_here, gate_here, sems = refs[4 * groups :]
    heads, rows = ec_ref.shape
    stretch = rows // 2
    width = x_ref.shape[1] // groups
    index = lax.axis_index("ctx")
    moves = []
    for g in range(groups):
        cols = pl.ds(g * width, width)
        moves.append(
            [
                pltpu.make_async_copy(x_ref.at[:, cols], x_here.at[g], sems.at[0, g]),
                pltpu.make_async_copy(gate_ref.at[:, cols], gate_here.at[g], sems.at[1, g]),
            ]
        )
        for move in moves[g]:
            move.start()
    triangle = lower_triangle(stretch)
    skip = as_column(skip_ref[...])
    step = 16
    masks = []
    for half in range(2):
        block = own_block(index, count, half)
        row = doc_row(docs_ref, block, stretch)
        column = as_column(row)
        reached = jnp.where(column == prior_doc(docs_ref, block, stretch).astype(F32), 1.0, 0.0)
        masks.append((triangle & (column == row.astype(F32)), reached))
    for g in range(groups):
        proj = slice(g * N, (g + 1) * N)
        matrix = spread_matrix(heads, width, g * (heads // groups))
        wide_skip = spread(skip, matrix)
        for half in range(2):
            sl = slice(half * stretch, (half + 1) * stretch)
            near, reached = masks[half]
            gram = dot_nt(c_ref[sl, proj], b_ref[sl, proj])
            gram = jnp.where(near, gram, 0.0).astype(BF16)
            wide = spread(ec_ref[:, sl], matrix)
            inner = jnp.dot(gram, xw_refs[g][sl, :], preferred_element_type=F32)
            if half == 0:
                for move in moves[g]:
                    move.wait()
            for k in range(0, stretch, step):
                at = slice(half * stretch + k, half * stretch + k + step)
                here = slice(k, k + step)
                x = x_here[g, at, :].astype(F32)
                gate = gate_here[g, at, :].astype(F32)
                silu = gate / (1.0 + jnp.exp(-gate))
                fade = wide[here] * silu
                sx = silu * x
                sx_refs[g][at, :] = sx
                pre_refs[g][at, :] = inner[here] * fade + wide_skip * sx
                reach_refs[g][at, :] = reached[here] * fade


def merge_kernel(count, state_ref, kv_ref, out_ref):
    index = lax.axis_index("ctx")
    outer = (index == 0) | (index == count - 1)
    rows, wide = kv_ref.shape
    stretch = rows // 2

    @pl.when(outer)
    def _():
        out_ref[...] = state_ref[...]

    @pl.when(jnp.logical_not(outer))
    def _():
        out_ref[:stretch, :wide] = kv_ref[:stretch, :]
        out_ref[:stretch, wide:] = kv_ref[stretch:, :]
        out_ref[stretch:, :] = jnp.zeros((out_ref.shape[0] - stretch, 2 * wide), BF16)


def arrivals(index, count, refs):
    if count != 4:
        return [(ring_source(index, count, r + 1), [(None, refs[r])]) for r in range(count - 1)]
    near, own_of_middle, next_of_middle, far, farther = refs
    middle = (index == 1) | (index == 2)
    low = index < 2
    return [
        (index ^ 1, [(None, near)]),
        (
            jnp.where(low, 2, 1),
            [(middle, own_of_middle), (jnp.logical_not(middle), far)],
        ),
        (
            jnp.where(low, 3, 0),
            [(middle, next_of_middle), (jnp.logical_not(middle), farther)],
        ),
    ]


def attention_kernel(count, per, stack, g, docs_ref, q_ref, k_ref, v_ref, *refs):
    others = count - 1
    sent = 5 if count == 4 else others
    out_ref, kt, vt, bias_f, bias_b, bias_a = refs[-6:]
    rows = q_ref.shape[0]
    stretch = rows // 2
    index = lax.axis_index("ctx")
    last = 2 * count - 1
    kv_width = refs[0].shape[1] // 2
    row_f = doc_row(docs_ref, index, stretch).astype(F32)
    row_b = doc_row(docs_ref, last - index, stretch).astype(F32)
    col_f = as_column(row_f)
    col_b = as_column(row_b)
    triangle = lower_triangle(stretch)

    def tile(k):
        return slice(k * stretch, (k + 1) * stretch)

    bias_f[...] = jnp.where(triangle & (col_f == row_f), 0.0, MASKED)
    bias_b[:, tile(0)] = jnp.where(col_b == row_f, 0.0, MASKED)
    bias_b[:, tile(1)] = jnp.where(triangle & (col_b == row_b), 0.0, MASKED)
    vt[:, DH:] = jnp.ones((vt.shape[0], DH), BF16)
    here = slice(g * DH, (g + 1) * DH)
    kt[tile(0), :] = k_ref[:stretch, here]
    vt[tile(0), :DH] = v_ref[:stretch, here]
    kt[tile(count), :] = k_ref[stretch:, here]
    vt[tile(count), :DH] = v_ref[stretch:, here]
    lower = []
    for r, (source, places) in enumerate(arrivals(index, count, refs[:sent])):
        lower.append(source < index)
        for condition, ref in places:

            def fetch(ref=ref, r=r):
                folded = ref.shape[1] > 2 * kv_width
                gap = jnp.where(lower[r], 0, 2 * kv_width if folded else stretch)
                for table, first in ((kt, g * DH), (vt, kv_width + g * DH)):
                    front = ref[:stretch, first : first + DH]
                    if folded:
                        own = ref[:stretch, pl.ds(pl.multiple_of(first + gap, DH), DH)]
                    else:
                        own = ref[pl.ds(pl.multiple_of(gap, stretch), stretch), first : first + DH]
                    table[tile(1 + r), :DH] = own
                    table[tile(count + 1 + r), :DH] = front

            if condition is None:
                fetch()
            else:
                pl.when(condition)(fetch)
        key_f = doc_row(docs_ref, source, stretch).astype(F32)
        key_a = doc_row(docs_ref, jnp.where(lower[r], source, last - source), stretch).astype(F32)
        bias_b[:, tile(2 + r)] = jnp.where(col_b == key_f, 0.0, MASKED)
        bias_a[:, tile(r)] = jnp.where(jnp.where(lower[r], col_f, col_b) == key_a, 0.0, MASKED)

    factor = math.log2(math.e) / math.sqrt(DH)
    tall = stack * stretch
    half_keys = count * stretch

    def stacked(first, base):
        return jnp.concatenate(
            [
                q_ref[base : base + stretch, (g * per + first + j) * DH : (g * per + first + j + 1) * DH]
                for j in range(stack)
            ],
            axis=0,
        )

    def biased(score, bias):
        size = score.shape[1]
        return (score.reshape(stack, stretch, size) + bias[None]).reshape(tall, size)

    for first in range(0, per, stack):
        s_f = dot_nt(stacked(first, 0), kt[:half_keys, :])
        s_b = dot_nt(stacked(first, stretch), kt[...])
        t_f = biased(s_f[:, tile(0)], bias_f[...])
        t_b = [biased(s_b[:, tile(0)], bias_b[:, tile(0)])]
        for k in range(1, count + 1):
            t_b.append(biased(s_b[:, tile(count + k - 1)], bias_b[:, tile(k)]))
        t_a = []
        for r in range(others):
            score = jnp.where(lower[r], s_f[:, tile(1 + r)], s_b[:, tile(1 + r)])
            t_a.append(biased(score, bias_a[:, tile(r)]))
        best_f = t_f
        best_b = functools.reduce(jnp.maximum, t_b)
        for r in range(others):
            best_f = jnp.maximum(best_f, jnp.where(lower[r], t_a[r], MASKED))
            best_b = jnp.maximum(best_b, jnp.where(lower[r], MASKED, t_a[r]))
        top_f = jnp.max(best_f, axis=1, keepdims=True)
        top_b = jnp.max(best_b, axis=1, keepdims=True)
        w_f = [jnp.exp2((t_f - top_f) * factor).astype(BF16)]
        w_b = [jnp.exp2((t - top_b) * factor).astype(BF16) for t in t_b]
        w_x = []
        for r in range(others):
            top = jnp.where(lower[r], top_f, top_b)
            w = jnp.exp2((t_a[r] - top) * factor)
            w_f.append(jnp.where(lower[r], w, 0.0).astype(BF16))
            w_x.append(jnp.where(lower[r], 0.0, w).astype(BF16))
        w_b = w_b[:1] + w_x + w_b[1:]
        out_f = jnp.dot(
            jnp.concatenate(w_f, axis=1), vt[:half_keys, :], preferred_element_type=F32
        )
        out_b = jnp.dot(jnp.concatenate(w_b, axis=1), vt[...], preferred_element_type=F32)
        for half, out in enumerate((out_f, out_b)):
            result = (out[:, :DH] / out[:, DH:]).astype(BF16)
            for j in range(stack):
                cols = slice((first + j) * DH, (first + j + 1) * DH)
                out_ref[tile(half), cols] = result[tile(j)]


def final_kernel(
    count,
    g,
    groups,
    loss_scale,
    pre_ref,
    reach_ref,
    sx_ref,
    c_ref,
    teacher_ref,
    gain_ref,
    f_ref,
    dec_ref,
    *refs,
):
    others = count - 1
    got = refs[:others]
    before = refs[others] if g else None
    proj = slice(g * N, (g + 1) * N)
    first_lane = g * pre_ref.shape[1]
    out_ref, grad_ref, front, back, flow, gated_ref, sums, gain_acc, skip_acc = refs[-9:]
    rows, width = pre_ref.shape
    stretch = rows // 2
    index = lax.axis_index("ctx")
    tile = 128
    step = 16

    @pl.when(index == 0)
    def _():
        front[...] = jnp.zeros_like(front)

    @pl.when(index == count - 1)
    def _():
        back[:N, :] = jnp.zeros((N, width), BF16)
        back[N:, :] = jnp.where(
            lax.broadcasted_iota(jnp.int32, (EXTRA, width), 0) == 0, 1.0, 0.0
        ).astype(BF16)

    for r in range(1, count):

        @pl.when(index == r)
        def _():
            front[...] = got[r - 1][:N, :]

        @pl.when(index == count - 1 - r)
        def _():
            back[...] = got[r - 1][...]

    d_in = back[N : N + 1, :].astype(F32) + back[N + 1 : N + 2, :].astype(F32)
    through = dec_ref[0:1, :] * front[...].astype(F32) + f_ref[...].astype(F32)
    entering = (d_in * through + back[:N, :].astype(F32)).astype(BF16)
    flow[:stretch, :] = jnp.dot(c_ref[:stretch, proj], front[...], preferred_element_type=F32)
    flow[stretch:, :] = jnp.dot(c_ref[stretch:, proj], entering, preferred_element_type=F32)
    gain_acc[...] = jnp.zeros_like(gain_acc)
    skip_acc[...] = jnp.zeros_like(skip_acc)

    @pl.loop(0, rows // step, unroll=2)
    def _(k):
        sl = pl.ds(pl.multiple_of(k * step, step), step)
        totals = [jnp.zeros((step, tile), F32)] * 3
        for j in range(0, width, tile):
            cols = slice(j, j + tile)
            gated = pre_ref[sl, cols] + reach_ref[sl, cols] * flow[sl, cols]
            gated_ref[sl, cols] = gated
            scaled = gated * gain_ref[:, first_lane + j : first_lane + j + tile]
            totals[0] += gated * gated
            totals[1] += scaled * scaled
            totals[2] += scaled * teacher_ref[sl, cols].astype(F32)
        for k3 in range(3):
            sums[sl, k3 * tile : (k3 + 1) * tile] = totals[k3]

    square, weighted, crossed = (
        jnp.sum(sums[:, k3 * tile : (k3 + 1) * tile], axis=1, keepdims=True) * (1.0 / width)
        for k3 in range(3)
    )
    scale = lax.rsqrt(square + EPS)
    push_scale = 2.0 * loss_scale
    mean = push_scale * scale * (scale * weighted - crossed)
    sums[:, :tile] = jnp.broadcast_to(scale, (rows, tile))
    sums[:, tile : 2 * tile] = jnp.broadcast_to(mean, (rows, tile))

    @pl.loop(0, rows // step, unroll=2)
    def _(k):
        sl = pl.ds(pl.multiple_of(k * step, step), step)
        scale = sums[sl, :tile]
        mean = sums[sl, tile : 2 * tile]
        for j in range(0, width, tile):
            cols = slice(j, j + tile)
            gain = gain_ref[:, first_lane + j : first_lane + j + tile]
            unit = gated_ref[sl, cols] * scale
            normed = unit * gain
            out_ref[sl, cols] = normed.astype(BF16)
            push = (normed - teacher_ref[sl, cols].astype(F32)) * push_scale
            by_gain = push * unit
            by_skip = (push * gain - unit * mean) * (scale * sx_ref[sl, cols])
            gain_acc[:, cols] += by_gain[:8] + by_gain[8:]
            skip_acc[:, cols] += by_skip[:8] + by_skip[8:]

    row = lax.broadcasted_iota(jnp.int32, (tile, width), 0)
    lane = lax.broadcasted_iota(jnp.int32, (tile, width), 1)
    matrix = jnp.where(row == lane // P_SIZE + g * (width // P_SIZE), 1.0, 0.0).astype(BF16)
    hi, lo = parts(skip_acc[...])
    by_head = jnp.sum(dot_nt(hi, matrix) + dot_nt(lo, matrix), axis=0, keepdims=True)
    grad_ref[...] = jnp.zeros_like(grad_ref)
    if g:
        grad_ref[:g, :] = before[:g, :]
        by_head += before[groups : groups + 1, :tile]
    grad_ref[g : g + 1, :] = jnp.sum(gain_acc[...], axis=0, keepdims=True)
    grad_ref[groups : groups + 1, :tile] = by_head


def writing_kernel(*refs):
    parts_in, out_ref, sems = refs[:-2], refs[-2], refs[-1]
    width = parts_in[0].shape[1]
    moves = [
        pltpu.make_async_copy(part, out_ref.at[:, pl.ds(k * width, width)], sems.at[k])
        for k, part in enumerate(parts_in)
    ]
    for move in moves:
        move.start()
    for move in moves:
        move.wait()


def closing_kernel(a_ref, b_ref, gain_ref, skip_ref):
    total = a_ref[...] + b_ref[...]
    groups, width = total.shape[0] - 1, total.shape[1]
    for g in range(groups):
        gain_ref[:, g * width : (g + 1) * width] = total[g : g + 1, :]
    skip_ref[...] = total[groups : groups + 1, : skip_ref.shape[1]]


def exchange(part, shift):
    axes = ("dp", "ctx")
    size = lax.axis_size(axes)
    return lax.ppermute(part, axes, [(d, d ^ shift) for d in range(size)])


def body(
    queries,
    keys,
    values,
    doc_ids,
    inputs,
    gate_input,
    b_input,
    c_input,
    dt_raw,
    dt_bias,
    decay_log,
    skip,
    gain,
):
    count = lax.axis_size("ctx")
    rows, features = queries.shape[1:]
    stretch = rows // 2
    kv_dev = keys.shape[2] // DH
    per_kv = queries.shape[2] // keys.shape[2]
    groups = b_input.shape[2] // N
    heads = features // P_SIZE
    width = features // groups
    length = doc_ids.shape[1]
    others = count - 1
    loss_scale = 1.0 / (lax.axis_size("dp") * count * rows)
    x, gate, bmat, cmat = inputs[0], gate_input[0], b_input[0], c_input[0]
    struct = jax.ShapeDtypeStruct

    def in_hbm(*arrays):
        return [pltpu.with_memory_space_constraint(array, pltpu.HBM) for array in arrays]

    def write(*pieces):
        return pl.pallas_call(
            writing_kernel,
            out_shape=struct((rows, features), BF16),
            in_specs=[VMEM] * len(pieces),
            out_specs=pl.BlockSpec(memory_space=pl.ANY),
            scratch_shapes=[pltpu.SemaphoreType.DMA((len(pieces),))],
            compiler_params=params(2),
            cost_estimate=cost(0, 4 * rows * features),
            name="writing",
        )(*pieces)

    state = struct((N, width), BF16)
    payload = struct((N + EXTRA, width), BF16)
    outs = pl.pallas_call(
        functools.partial(opening_kernel, count, groups),
        out_shape=(
            struct((rows, 2 * kv_dev * DH), BF16),
            struct((heads, rows), F32),
            *([struct((rows, width), BF16)] * groups),
            *([struct((8, width), F32)] * groups),
            *([state] * (2 * groups)),
            *([payload] * groups),
        ),
        in_specs=[VMEM] * 8,
        out_specs=(VMEM,) * (2 + 5 * groups),
        compiler_params=params(16),
        cost_estimate=cost(4 * rows * features * N, 8 * rows * features),
        name="opening",
    )(
        *in_hbm(
            doc_ids,
            keys[0],
            values[0],
            x,
            bmat,
            dt_raw[0].T,
            dt_bias.reshape(1, heads),
            decay_log.reshape(1, heads),
        )
    )
    kv, ec = outs[:2]
    xw, dec, f_parts, b_parts, send = (
        outs[2 + k * groups : 2 + (k + 1) * groups] for k in range(5)
    )

    local = pl.pallas_call(
        functools.partial(local_kernel, count, groups),
        out_shape=(struct((rows, width), F32),) * (3 * groups),
        in_specs=[
            VMEM,
            *[pl.BlockSpec(memory_space=pl.ANY)] * 2,
            *[VMEM] * (4 + groups),
        ],
        out_specs=(VMEM,) * (3 * groups),
        scratch_shapes=[
            pltpu.VMEM((groups, rows, width), BF16),
            pltpu.VMEM((groups, rows, width), BF16),
            pltpu.SemaphoreType.DMA((2, groups)),
        ],
        compiler_params=params(16),
        cost_estimate=cost(2 * rows * features * N, 16 * rows * features),
        name="local",
    )(*in_hbm(doc_ids, x, gate, bmat, cmat, skip.reshape(1, heads)), ec, *xw)

    send = list(send)
    got = [[] for _ in range(groups)]
    def passed_on(g, stage):
        return pl.pallas_call(
            functools.partial(chain_kernel, count, stage),
            out_shape=payload,
            in_specs=[VMEM] * 4,
            out_specs=VMEM,
            compiler_params=params(4),
            cost_estimate=pl.CostEstimate(flops=16384 * N * width, bytes_accessed=0, transcendentals=0),
            name="chain",
        )(got[g][-1], f_parts[g], b_parts[g], dec[g])

    def stage_pairs(stage):
        return [(stage - 1, stage), (count - stage, count - stage - 1)]

    if count == 4:
        inward, outward, across = [(0, 1), (3, 2)], [(1, 0), (2, 3)], [(1, 2), (2, 1)]
        near = lax.ppermute(kv, "ctx", inward + outward)
        middle = lax.ppermute(kv, "ctx", across)
        near, *local = lax.optimization_barrier((near, *local))
        middle, _ = lax.optimization_barrier((middle, near))
        beyond = lax.ppermute(near, "ctx", across)
        send[-1] = pl.pallas_call(
            functools.partial(merge_kernel, count),
            out_shape=payload,
            in_specs=[VMEM] * 2,
            out_specs=VMEM,
            compiler_params=params(4),
            cost_estimate=cost(0, 4 * N * width),
            name="merge",
        )(send[-1], middle)
        far = lax.ppermute(send[-1], "ctx", inward + outward)
        got[-1].append(far)
        farther = lax.ppermute(beyond, "ctx", outward)
        if groups > 1:
            got[0].append(lax.ppermute(send[0], "ctx", stage_pairs(1)))
            got[0][0], _ = lax.optimization_barrier((got[0][0], beyond))
            send[0] = passed_on(0, 1)
            got[0].append(lax.ppermute(send[0], "ctx", stage_pairs(2)))
            send[0] = passed_on(0, 2)
            got[0].append(lax.ppermute(send[0], "ctx", stage_pairs(3)))
            farther, _ = lax.optimization_barrier((farther, send[0]))
        kv_got = [near, middle, beyond, far, farther]
    else:
        ring = ring_order(count)
        ring_pairs = [(ring[d], ring[(d + 1) % count]) for d in range(count)]
        kv_got = [kv]
        for _ in range(others):
            kv_got.append(lax.ppermute(kv_got[-1], "ctx", ring_pairs))
        kv_got = kv_got[1:]
    stack = 4 if per_kv % 4 == 0 and count <= 4 else 1
    targets = [
        pl.pallas_call(
            functools.partial(attention_kernel, count, per_kv, stack, g),
            out_shape=struct((rows, per_kv * DH), BF16),
            in_specs=[VMEM] * (4 + len(kv_got)),
            out_specs=VMEM,
            scratch_shapes=[
                pltpu.VMEM((2 * count * stretch, DH), BF16),
                pltpu.VMEM((2 * count * stretch, 2 * DH), BF16),
                pltpu.VMEM((stretch, stretch), F32),
                pltpu.VMEM((stretch, (count + 1) * stretch), F32),
                pltpu.VMEM((stretch, others * stretch), F32),
            ],
            compiler_params=params(24),
            cost_estimate=cost(
                4 * (2 * count + 1) * stretch * stretch * per_kv * DH, 8 * rows * per_kv * DH
            ),
            name="attention",
        )(doc_ids, queries[0], keys[0], values[0], *kv_got)
        for g in range(kv_dev)
    ]
    for r in range(1, count):
        for g in range(groups):
            if len(got[g]) >= r:
                continue
            if r == 3 and g == groups - 1:
                got[g][-1], targets[0] = lax.optimization_barrier((got[g][-1], targets[0]))
            if r > 1:
                send[g] = passed_on(g, r - 1)
            got[g].append(lax.ppermute(send[g], "ctx", stage_pairs(r)))
    normed, grads = [], None
    for g in range(groups):
        more = [] if grads is None else [grads]
        made, grads = pl.pallas_call(
            functools.partial(final_kernel, count, g, groups, loss_scale),
            out_shape=(struct((rows, width), BF16), struct((groups + 1, width), F32)),
            in_specs=[VMEM] * (8 + others + len(more)),
            out_specs=(VMEM,) * 2,
            scratch_shapes=[
                pltpu.VMEM((N, width), BF16),
                pltpu.VMEM((N + EXTRA, width), BF16),
                pltpu.VMEM((rows, width), F32),
                pltpu.VMEM((rows, width), F32),
                pltpu.VMEM((rows, 3 * 128), F32),
                pltpu.VMEM((8, width), F32),
                pltpu.VMEM((8, width), F32),
            ],
            compiler_params=params(16),
            cost_estimate=cost(2 * rows * width * N, 20 * rows * width),
            name="final",
        )(
            *local[g::groups],
            cmat,
            targets[g],
            gain.reshape(1, features),
            f_parts[g],
            dec[g],
            *got[g],
            *more,
        )
        normed.append(made)
    teacher, student = write(*targets), write(*normed)
    partner = exchange(grads, 1)
    if lax.axis_size("dp") == 2:
        grads = (grads + partner) + (exchange(grads, count) + exchange(grads, count + 1))
    else:
        grads = grads + partner
    shifts = [1 << k for k in range(1, count.bit_length() - 1)]
    for shift in shifts[:-1]:
        grads = grads + exchange(grads, shift)
    grad_gain, grad_skip = pl.pallas_call(
        closing_kernel,
        out_shape=(struct((1, features), F32), struct((1, heads), F32)),
        in_specs=[VMEM] * 2,
        out_specs=(VMEM,) * 2,
        compiler_params=params(2),
        name="closing",
    )(grads, exchange(grads, shifts[-1]))
    return (teacher[None], student[None], grad_gain[0], grad_skip[0])


def solution(mesh):
    rows = P("dp", "ctx", "head")
    in_specs = (
        rows,
        rows,
        rows,
        P("dp", None),
        rows,
        rows,
        rows,
        rows,
        rows,
        P("head"),
        P("head"),
        P("head"),
        P("head"),
    )
    out_specs = (rows, rows, P("head"), P("head"))
    return jax.shard_map(body, mesh=mesh, in_specs=in_specs, out_specs=out_specs, check_vma=False)
```

```python
import functools
import math

import jax
import jax.numpy as jnp
from jax import lax
from jax.experimental import pallas as pl
from jax.experimental.pallas import tpu as pltpu
from jax.sharding import PartitionSpec as P

DH = 128
P_SIZE = 64
N = 128
EXTRA = 16
EPS = 1e-05
MASKED = -1e30
F32 = jnp.float32
BF16 = jnp.bfloat16
VMEM = pl.BlockSpec(memory_space=pltpu.VMEM)


def params(mib):
    return pltpu.CompilerParams(vmem_limit_bytes=mib << 20)


def cost(flops, size):
    return pl.CostEstimate(flops=flops, bytes_accessed=size, transcendentals=0)


def parts(v):
    hi = v.astype(BF16)
    return hi, (v - hi.astype(F32)).astype(BF16)


def spread_matrix(heads, width, first):
    row = lax.broadcasted_iota(jnp.int32, (heads, width), 0)
    lane = lax.broadcasted_iota(jnp.int32, (heads, width), 1)
    return jnp.where(row == (lane // P_SIZE) + first, 1.0, 0.0).astype(BF16)


def dot_nt(a, b):
    return lax.dot_general(a, b, (((1,), (1,)), ((), ())), preferred_element_type=F32)


def dot_tn(a, b):
    return lax.dot_general(a, b, (((0,), (0,)), ((), ())), preferred_element_type=F32)


def spread(v, matrix):
    return dot_tn(jnp.concatenate(parts(v), axis=0), jnp.concatenate([matrix, matrix], axis=0))


def doc_row(docs_ref, block, stretch):
    return docs_ref[:, pl.ds(pl.multiple_of(block * stretch, stretch), stretch)]


def as_column(row):
    size = row.shape[1]
    r = lax.broadcasted_iota(jnp.int32, (size, size), 0)
    c = lax.broadcasted_iota(jnp.int32, (size, size), 1)
    return jnp.sum(jnp.where(r == c, row.astype(F32), 0.0), axis=1, keepdims=True)


def lower_triangle(size):
    r = lax.broadcasted_iota(jnp.int32, (size, size), 0)
    c = lax.broadcasted_iota(jnp.int32, (size, size), 1)
    return r >= c


def prior_doc(docs_ref, block, stretch):
    before = doc_row(docs_ref, jnp.maximum(block - 1, 0), stretch)[:, stretch - 1 :]
    return jnp.where(block > 0, before, -1)


def own_block(index, count, half):
    return index if half == 0 else 2 * count - 1 - index


def ring_order(count):
    return [0] + list(range(1, count, 2)) + list(range(2, count, 2))[::-1]


def ring_source(index, count, steps):
    order = ring_order(count)
    source = jnp.int32(0)
    for place, member in enumerate(order):
        source = jnp.where(index == member, order[(place - steps) % count], source)
    return source


def put_state(ref, state):
    ref[:N, :] = state.astype(BF16)
    ref[N:, :] = jnp.zeros((EXTRA, ref.shape[1]), BF16)


def put_composite(ref, state, decay):
    hi, lo = parts(decay)
    ref[:N, :] = state.astype(BF16)
    ref[N:, :] = jnp.concatenate(
        [hi, lo, jnp.zeros((EXTRA - 2, ref.shape[1]), BF16)], axis=0
    )


def opening_kernel(
    count,
    groups,
    docs_ref,
    k_ref,
    v_ref,
    x_ref,
    b_ref,
    dt_ref,
    bias_ref,
    log_ref,
    kv_ref,
    ec_ref,
    *outs,
):
    xw_refs, dec_refs, f_refs, b_refs, send_refs = (
        outs[k * groups : (k + 1) * groups] for k in range(5)
    )
    heads, rows = dt_ref.shape
    stretch = rows // 2
    width = x_ref.shape[1] // groups
    kv_width = k_ref.shape[1]
    index = lax.axis_index("ctx")
    kv_ref[:, :kv_width] = k_ref[...]
    kv_ref[:, kv_width:] = v_ref[...]
    triangle = jnp.where(lower_triangle(stretch), 1.0, 0.0)
    slope = jnp.exp(as_column(log_ref[...]))
    bias = as_column(bias_ref[...])
    lane = lax.broadcasted_iota(jnp.int32, (heads, 8), 1)
    ends = jnp.zeros((heads, 8), F32)
    loads = []
    projs = []
    for half in range(2):
        block = own_block(index, count, half)
        sl = slice(half * stretch, (half + 1) * stretch)
        raw = dt_ref[:, sl] + bias
        dt = jnp.maximum(raw, 0.0) + jnp.log1p(jnp.exp(-jnp.abs(raw)))
        cum = lax.dot_general(
            -dt * slope,
            triangle,
            (((1,), (1,)), ((), ())),
            precision=lax.Precision.HIGHEST,
            preferred_element_type=F32,
        )
        ec_ref[:, sl] = jnp.exp(cum)
        loads.append(jnp.exp(-cum) * dt)
        final = jnp.exp(cum[:, stretch - 1 :])
        row = doc_row(docs_ref, block, stretch)
        last = row[:, stretch - 1 :]
        kept = jnp.where(last == prior_doc(docs_ref, block, stretch), 1.0, 0.0)
        ends = jnp.where(lane == half, final * kept, ends)
        ends = jnp.where(lane == 2 + half, final, ends)
        same = jnp.where(as_column(row) == last.astype(F32), 1.0, 0.0)
        projs.append((b_ref[sl, :].astype(F32) * same).astype(BF16))
    for g in range(groups):
        cols = slice(g * width, (g + 1) * width)
        matrix = spread_matrix(heads, width, g * (heads // groups))
        wide = spread(ends, matrix)
        dec_refs[g][...] = wide
        sums = []
        for half in range(2):
            sl = slice(half * stretch, (half + 1) * stretch)
            xw = (x_ref[sl, cols].astype(F32) * spread(loads[half], matrix)).astype(BF16)
            xw_refs[g][sl, :] = xw
            sums.append(dot_tn(projs[half][:, g * N : (g + 1) * N], xw) * wide[2 + half : 3 + half])
        f_refs[g][...] = sums[0].astype(BF16)
        b_refs[g][...] = sums[1].astype(BF16)

        @pl.when(index == 0)
        def _():
            put_state(send_refs[g], sums[0])

        @pl.when(index != 0)
        def _():
            put_composite(send_refs[g], wide[1:2] * sums[0] + sums[1], wide[0:1] * wide[1:2])


def chain_kernel(count, stage, got_ref, f_ref, b_ref, dec_ref, send_ref):
    index = lax.axis_index("ctx")

    @pl.when(index == stage)
    def _():
        state = dec_ref[0:1, :] * got_ref[:N, :].astype(F32) + f_ref[...].astype(F32)
        put_state(send_ref, state)

    @pl.when(index == count - 1 - stage)
    def _():
        decay = got_ref[N : N + 1, :].astype(F32) + got_ref[N + 1 : N + 2, :].astype(F32)
        inner = decay * f_ref[...].astype(F32) + got_ref[:N, :].astype(F32)
        state = dec_ref[1:2, :] * inner + b_ref[...].astype(F32)
        put_composite(send_ref, state, dec_ref[1:2, :] * decay * dec_ref[0:1, :])


def local_kernel(
    count, groups, docs_ref, x_ref, gate_ref, b_ref, c_ref, skip_ref, ec_ref, *refs
):
    xw_refs, pre_refs, reach_refs, sx_refs = (
        refs[k * groups : (k + 1) * groups] for k in range(4)
    )
    x_here, gate_here, sems = refs[4 * groups :]
    heads, rows = ec_ref.shape
    stretch = rows // 2
    width = x_ref.shape[1] // groups
    index = lax.axis_index("ctx")
    moves = []
    for g in range(groups):
        cols = pl.ds(g * width, width)
        moves.append(
            [
                pltpu.make_async_copy(x_ref.at[:, cols], x_here.at[g], sems.at[0, g]),
                pltpu.make_async_copy(gate_ref.at[:, cols], gate_here.at[g], sems.at[1, g]),
            ]
        )
        for move in moves[g]:
            move.start()
    triangle = lower_triangle(stretch)
    skip = as_column(skip_ref[...])
    step = 16
    masks = []
    for half in range(2):
        block = own_block(index, count, half)
        row = doc_row(docs_ref, block, stretch)
        column = as_column(row)
        reached = jnp.where(column == prior_doc(docs_ref, block, stretch).astype(F32), 1.0, 0.0)
        masks.append((triangle & (column == row.astype(F32)), reached))
    for g in range(groups):
        proj = slice(g * N, (g + 1) * N)
        matrix = spread_matrix(heads, width, g * (heads // groups))
        wide_skip = spread(skip, matrix)
        for half in range(2):
            sl = slice(half * stretch, (half + 1) * stretch)
            near, reached = masks[half]
            gram = dot_nt(c_ref[sl, proj], b_ref[sl, proj])
            gram = jnp.where(near, gram, 0.0).astype(BF16)
            wide = spread(ec_ref[:, sl], matrix)
            inner = jnp.dot(gram, xw_refs[g][sl, :], preferred_element_type=F32)
            if half == 0:
                for move in moves[g]:
                    move.wait()
            for k in range(0, stretch, step):
                at = slice(half * stretch + k, half * stretch + k + step)
                here = slice(k, k + step)
                x = x_here[g, at, :].astype(F32)
                gate = gate_here[g, at, :].astype(F32)
                silu = gate / (1.0 + jnp.exp(-gate))
                fade = wide[here] * silu
                sx = silu * x
                sx_refs[g][at, :] = sx
                pre_refs[g][at, :] = inner[here] * fade + wide_skip * sx
                reach_refs[g][at, :] = reached[here] * fade


def merge_kernel(count, state_ref, kv_ref, out_ref):
    index = lax.axis_index("ctx")
    outer = (index == 0) | (index == count - 1)
    rows, wide = kv_ref.shape
    stretch = rows // 2

    @pl.when(outer)
    def _():
        out_ref[...] = state_ref[...]

    @pl.when(jnp.logical_not(outer))
    def _():
        out_ref[:stretch, :wide] = kv_ref[:stretch, :]
        out_ref[:stretch, wide:] = kv_ref[stretch:, :]
        out_ref[stretch:, :] = jnp.zeros((out_ref.shape[0] - stretch, 2 * wide), BF16)


def arrivals(index, count, refs):
    if count != 4:
        return [(ring_source(index, count, r + 1), [(None, refs[r])]) for r in range(count - 1)]
    near, own_of_middle, next_of_middle, far, farther = refs
    middle = (index == 1) | (index == 2)
    low = index < 2
    return [
        (index ^ 1, [(None, near)]),
        (
            jnp.where(low, 2, 1),
            [(middle, own_of_middle), (jnp.logical_not(middle), far)],
        ),
        (
            jnp.where(low, 3, 0),
            [(middle, next_of_middle), (jnp.logical_not(middle), farther)],
        ),
    ]


def attention_kernel(count, per, stack, g, docs_ref, q_ref, k_ref, v_ref, *refs):
    others = count - 1
    sent = 5 if count == 4 else others
    out_ref, kt, vt, bias_f, bias_b, bias_a = refs[-6:]
    rows = q_ref.shape[0]
    stretch = rows // 2
    index = lax.axis_index("ctx")
    last = 2 * count - 1
    kv_width = refs[0].shape[1] // 2
    row_f = doc_row(docs_ref, index, stretch).astype(F32)
    row_b = doc_row(docs_ref, last - index, stretch).astype(F32)
    col_f = as_column(row_f)
    col_b = as_column(row_b)
    triangle = lower_triangle(stretch)

    def tile(k):
        return slice(k * stretch, (k + 1) * stretch)

    bias_f[...] = jnp.where(triangle & (col_f == row_f), 0.0, MASKED)
    bias_b[:, tile(0)] = jnp.where(col_b == row_f, 0.0, MASKED)
    bias_b[:, tile(1)] = jnp.where(triangle & (col_b == row_b), 0.0, MASKED)
    vt[:, DH:] = jnp.ones((vt.shape[0], DH), BF16)
    here = slice(g * DH, (g + 1) * DH)
    kt[tile(0), :] = k_ref[:stretch, here]
    vt[tile(0), :DH] = v_ref[:stretch, here]
    kt[tile(count), :] = k_ref[stretch:, here]
    vt[tile(count), :DH] = v_ref[stretch:, here]
    lower = []
    for r, (source, places) in enumerate(arrivals(index, count, refs[:sent])):
        lower.append(source < index)
        for condition, ref in places:

            def fetch(ref=ref, r=r):
                folded = ref.shape[1] > 2 * kv_width
                gap = jnp.where(lower[r], 0, 2 * kv_width if folded else stretch)
                for table, first in ((kt, g * DH), (vt, kv_width + g * DH)):
                    front = ref[:stretch, first : first + DH]
                    if folded:
                        own = ref[:stretch, pl.ds(pl.multiple_of(first + gap, DH), DH)]
                    else:
                        own = ref[pl.ds(pl.multiple_of(gap, stretch), stretch), first : first + DH]
                    table[tile(1 + r), :DH] = own
                    table[tile(count + 1 + r), :DH] = front

            if condition is None:
                fetch()
            else:
                pl.when(condition)(fetch)
        key_f = doc_row(docs_ref, source, stretch).astype(F32)
        key_a = doc_row(docs_ref, jnp.where(lower[r], source, last - source), stretch).astype(F32)
        bias_b[:, tile(2 + r)] = jnp.where(col_b == key_f, 0.0, MASKED)
        bias_a[:, tile(r)] = jnp.where(jnp.where(lower[r], col_f, col_b) == key_a, 0.0, MASKED)

    factor = math.log2(math.e) / math.sqrt(DH)
    tall = stack * stretch
    half_keys = count * stretch

    def stacked(first, base):
        return jnp.concatenate(
            [
                q_ref[base : base + stretch, (g * per + first + j) * DH : (g * per + first + j + 1) * DH]
                for j in range(stack)
            ],
            axis=0,
        )

    def biased(score, bias):
        size = score.shape[1]
        return (score.reshape(stack, stretch, size) + bias[None]).reshape(tall, size)

    for first in range(0, per, stack):
        s_f = dot_nt(stacked(first, 0), kt[:half_keys, :])
        s_b = dot_nt(stacked(first, stretch), kt[...])
        t_f = biased(s_f[:, tile(0)], bias_f[...])
        t_b = [biased(s_b[:, tile(0)], bias_b[:, tile(0)])]
        for k in range(1, count + 1):
            t_b.append(biased(s_b[:, tile(count + k - 1)], bias_b[:, tile(k)]))
        t_a = []
        for r in range(others):
            score = jnp.where(lower[r], s_f[:, tile(1 + r)], s_b[:, tile(1 + r)])
            t_a.append(biased(score, bias_a[:, tile(r)]))
        best_f = t_f
        best_b = functools.reduce(jnp.maximum, t_b)
        for r in range(others):
            best_f = jnp.maximum(best_f, jnp.where(lower[r], t_a[r], MASKED))
            best_b = jnp.maximum(best_b, jnp.where(lower[r], MASKED, t_a[r]))
        top_f = jnp.max(best_f, axis=1, keepdims=True)
        top_b = jnp.max(best_b, axis=1, keepdims=True)
        w_f = [jnp.exp2((t_f - top_f) * factor).astype(BF16)]
        w_b = [jnp.exp2((t - top_b) * factor).astype(BF16) for t in t_b]
        w_x = []
        for r in range(others):
            top = jnp.where(lower[r], top_f, top_b)
            w = jnp.exp2((t_a[r] - top) * factor)
            w_f.append(jnp.where(lower[r], w, 0.0).astype(BF16))
            w_x.append(jnp.where(lower[r], 0.0, w).astype(BF16))
        w_b = w_b[:1] + w_x + w_b[1:]
        out_f = jnp.dot(
            jnp.concatenate(w_f, axis=1), vt[:half_keys, :], preferred_element_type=F32
        )
        out_b = jnp.dot(jnp.concatenate(w_b, axis=1), vt[...], preferred_element_type=F32)
        for half, out in enumerate((out_f, out_b)):
            result = (out[:, :DH] / out[:, DH:]).astype(BF16)
            for j in range(stack):
                cols = slice((first + j) * DH, (first + j + 1) * DH)
                out_ref[tile(half), cols] = result[tile(j)]


def final_kernel(
    count,
    g,
    groups,
    loss_scale,
    pre_ref,
    reach_ref,
    sx_ref,
    c_ref,
    teacher_ref,
    gain_ref,
    f_ref,
    dec_ref,
    *refs,
):
    others = count - 1
    got = refs[:others]
    before = refs[others] if g else None
    proj = slice(g * N, (g + 1) * N)
    first_lane = g * pre_ref.shape[1]
    out_ref, grad_ref, front, back, flow, gated_ref, sums, gain_acc, skip_acc = refs[-9:]
    rows, width = pre_ref.shape
    stretch = rows // 2
    index = lax.axis_index("ctx")
    tile = 128
    step = 16

    @pl.when(index == 0)
    def _():
        front[...] = jnp.zeros_like(front)

    @pl.when(index == count - 1)
    def _():
        back[:N, :] = jnp.zeros((N, width), BF16)
        back[N:, :] = jnp.where(
            lax.broadcasted_iota(jnp.int32, (EXTRA, width), 0) == 0, 1.0, 0.0
        ).astype(BF16)

    for r in range(1, count):

        @pl.when(index == r)
        def _():
            front[...] = got[r - 1][:N, :]

        @pl.when(index == count - 1 - r)
        def _():
            back[...] = got[r - 1][...]

    d_in = back[N : N + 1, :].astype(F32) + back[N + 1 : N + 2, :].astype(F32)
    through = dec_ref[0:1, :] * front[...].astype(F32) + f_ref[...].astype(F32)
    entering = (d_in * through + back[:N, :].astype(F32)).astype(BF16)
    flow[:stretch, :] = jnp.dot(c_ref[:stretch, proj], front[...], preferred_element_type=F32)
    flow[stretch:, :] = jnp.dot(c_ref[stretch:, proj], entering, preferred_element_type=F32)
    gain_acc[...] = jnp.zeros_like(gain_acc)
    skip_acc[...] = jnp.zeros_like(skip_acc)

    @pl.loop(0, rows // step, unroll=2)
    def _(k):
        sl = pl.ds(pl.multiple_of(k * step, step), step)
        totals = [jnp.zeros((step, tile), F32)] * 3
        for j in range(0, width, tile):
            cols = slice(j, j + tile)
            gated = pre_ref[sl, cols] + reach_ref[sl, cols] * flow[sl, cols]
            gated_ref[sl, cols] = gated
            scaled = gated * gain_ref[:, first_lane + j : first_lane + j + tile]
            totals[0] += gated * gated
            totals[1] += scaled * scaled
            totals[2] += scaled * teacher_ref[sl, cols].astype(F32)
        for k3 in range(3):
            sums[sl, k3 * tile : (k3 + 1) * tile] = totals[k3]

    square, weighted, crossed = (
        jnp.sum(sums[:, k3 * tile : (k3 + 1) * tile], axis=1, keepdims=True) * (1.0 / width)
        for k3 in range(3)
    )
    scale = lax.rsqrt(square + EPS)
    push_scale = 2.0 * loss_scale
    mean = push_scale * scale * (scale * weighted - crossed)
    sums[:, :tile] = jnp.broadcast_to(scale, (rows, tile))
    sums[:, tile : 2 * tile] = jnp.broadcast_to(mean, (rows, tile))

    @pl.loop(0, rows // step, unroll=2)
    def _(k):
        sl = pl.ds(pl.multiple_of(k * step, step), step)
        scale = sums[sl, :tile]
        mean = sums[sl, tile : 2 * tile]
        for j in range(0, width, tile):
            cols = slice(j, j + tile)
            gain = gain_ref[:, first_lane + j : first_lane + j + tile]
            unit = gated_ref[sl, cols] * scale
            normed = unit * gain
            out_ref[sl, cols] = normed.astype(BF16)
            push = (normed - teacher_ref[sl, cols].astype(F32)) * push_scale
            by_gain = push * unit
            by_skip = (push * gain - unit * mean) * (scale * sx_ref[sl, cols])
            gain_acc[:, cols] += by_gain[:8] + by_gain[8:]
            skip_acc[:, cols] += by_skip[:8] + by_skip[8:]

    row = lax.broadcasted_iota(jnp.int32, (tile, width), 0)
    lane = lax.broadcasted_iota(jnp.int32, (tile, width), 1)
    matrix = jnp.where(row == lane // P_SIZE + g * (width // P_SIZE), 1.0, 0.0).astype(BF16)
    hi, lo = parts(skip_acc[...])
    by_head = jnp.sum(dot_nt(hi, matrix) + dot_nt(lo, matrix), axis=0, keepdims=True)
    grad_ref[...] = jnp.zeros_like(grad_ref)
    if g:
        grad_ref[:g, :] = before[:g, :]
        by_head += before[groups : groups + 1, :tile]
    grad_ref[g : g + 1, :] = jnp.sum(gain_acc[...], axis=0, keepdims=True)
    grad_ref[groups : groups + 1, :tile] = by_head


def writing_kernel(count, first, *refs):
    out_ref, sems = refs[-2:]
    width = refs[0].shape[1]
    moves = [
        pltpu.make_async_copy(
            refs[k], out_ref.at[:, pl.ds((first + k) * width, width)], sems.at[k]
        )
        for k in range(count)
    ]
    for move in moves:
        move.start()
    for move in moves:
        move.wait()


def closing_kernel(a_ref, b_ref, gain_ref, skip_ref):
    total = a_ref[...] + b_ref[...]
    groups, width = total.shape[0] - 1, total.shape[1]
    for g in range(groups):
        gain_ref[:, g * width : (g + 1) * width] = total[g : g + 1, :]
    skip_ref[...] = total[groups : groups + 1, : skip_ref.shape[1]]


def exchange(part, shift):
    axes = ("dp", "ctx")
    size = lax.axis_size(axes)
    return lax.ppermute(part, axes, [(d, d ^ shift) for d in range(size)])


def body(
    queries,
    keys,
    values,
    doc_ids,
    inputs,
    gate_input,
    b_input,
    c_input,
    dt_raw,
    dt_bias,
    decay_log,
    skip,
    gain,
):
    count = lax.axis_size("ctx")
    rows, features = queries.shape[1:]
    stretch = rows // 2
    kv_dev = keys.shape[2] // DH
    per_kv = queries.shape[2] // keys.shape[2]
    groups = b_input.shape[2] // N
    heads = features // P_SIZE
    width = features // groups
    length = doc_ids.shape[1]
    others = count - 1
    loss_scale = 1.0 / (lax.axis_size("dp") * count * rows)
    x, gate, bmat, cmat = inputs[0], gate_input[0], b_input[0], c_input[0]
    struct = jax.ShapeDtypeStruct

    def in_hbm(*arrays):
        return [pltpu.with_memory_space_constraint(array, pltpu.HBM) for array in arrays]

    def write(pieces, first=0, into=()):
        anywhere = pl.BlockSpec(memory_space=pl.ANY)
        return pl.pallas_call(
            functools.partial(writing_kernel, len(pieces), first),
            out_shape=struct((rows, features), BF16),
            in_specs=[VMEM] * len(pieces) + [anywhere] * len(into),
            out_specs=anywhere,
            scratch_shapes=[pltpu.SemaphoreType.DMA((len(pieces),))],
            input_output_aliases={len(pieces): 0} if into else {},
            compiler_params=params(2),
            cost_estimate=cost(0, 4 * rows * features),
            name="writing",
        )(*pieces, *into)

    state = struct((N, width), BF16)
    payload = struct((N + EXTRA, width), BF16)
    outs = pl.pallas_call(
        functools.partial(opening_kernel, count, groups),
        out_shape=(
            struct((rows, 2 * kv_dev * DH), BF16),
            struct((heads, rows), F32),
            *([struct((rows, width), BF16)] * groups),
            *([struct((8, width), F32)] * groups),
            *([state] * (2 * groups)),
            *([payload] * groups),
        ),
        in_specs=[VMEM] * 8,
        out_specs=(VMEM,) * (2 + 5 * groups),
        compiler_params=params(16),
        cost_estimate=cost(4 * rows * features * N, 8 * rows * features),
        name="opening",
    )(
        *in_hbm(
            doc_ids,
            keys[0],
            values[0],
            x,
            bmat,
            dt_raw[0].T,
            dt_bias.reshape(1, heads),
            decay_log.reshape(1, heads),
        )
    )
    kv, ec = outs[:2]
    xw, dec, f_parts, b_parts, send = (
        outs[2 + k * groups : 2 + (k + 1) * groups] for k in range(5)
    )

    local = pl.pallas_call(
        functools.partial(local_kernel, count, groups),
        out_shape=(struct((rows, width), F32),) * (3 * groups),
        in_specs=[
            VMEM,
            *[pl.BlockSpec(memory_space=pl.ANY)] * 2,
            *[VMEM] * (4 + groups),
        ],
        out_specs=(VMEM,) * (3 * groups),
        scratch_shapes=[
            pltpu.VMEM((groups, rows, width), BF16),
            pltpu.VMEM((groups, rows, width), BF16),
            pltpu.SemaphoreType.DMA((2, groups)),
        ],
        compiler_params=params(16),
        cost_estimate=cost(2 * rows * features * N, 16 * rows * features),
        name="local",
    )(*in_hbm(doc_ids, x, gate, bmat, cmat, skip.reshape(1, heads)), ec, *xw)

    send = list(send)
    got = [[] for _ in range(groups)]
    if count == 4:
        inward, outward, across = [(0, 1), (3, 2)], [(1, 0), (2, 3)], [(1, 2), (2, 1)]
        near = lax.ppermute(kv, "ctx", inward + outward)
        middle = lax.ppermute(kv, "ctx", across)
        middle, *local = lax.optimization_barrier((middle, *local))
        beyond = lax.ppermute(near, "ctx", across)
        send[-1] = pl.pallas_call(
            functools.partial(merge_kernel, count),
            out_shape=payload,
            in_specs=[VMEM] * 2,
            out_specs=VMEM,
            compiler_params=params(4),
            cost_estimate=cost(0, 4 * N * width),
            name="merge",
        )(send[-1], middle)
        far = lax.ppermute(send[-1], "ctx", inward + outward)
        got[-1].append(far)
        farther = lax.ppermute(beyond, "ctx", outward)
        kv_got = [near, middle, beyond, far, farther]
    else:
        ring = ring_order(count)
        ring_pairs = [(ring[d], ring[(d + 1) % count]) for d in range(count)]
        kv_got = [kv]
        for _ in range(others):
            kv_got.append(lax.ppermute(kv_got[-1], "ctx", ring_pairs))
        kv_got = kv_got[1:]
    stack = 4 if per_kv % 4 == 0 and count <= 4 else 1
    targets = [
        pl.pallas_call(
            functools.partial(attention_kernel, count, per_kv, stack, g),
            out_shape=struct((rows, per_kv * DH), BF16),
            in_specs=[VMEM] * (4 + len(kv_got)),
            out_specs=VMEM,
            scratch_shapes=[
                pltpu.VMEM((2 * count * stretch, DH), BF16),
                pltpu.VMEM((2 * count * stretch, 2 * DH), BF16),
                pltpu.VMEM((stretch, stretch), F32),
                pltpu.VMEM((stretch, (count + 1) * stretch), F32),
                pltpu.VMEM((stretch, others * stretch), F32),
            ],
            compiler_params=params(24),
            cost_estimate=cost(
                4 * (2 * count + 1) * stretch * stretch * per_kv * DH, 8 * rows * per_kv * DH
            ),
            name="attention",
        )(doc_ids, queries[0], keys[0], values[0], *kv_got)
        for g in range(kv_dev)
    ]
    for r in range(1, count):
        for g in range(groups):
            if r == 3 and g == groups - 1:
                got[g][-1], targets[0] = lax.optimization_barrier((got[g][-1], targets[0]))
            if r > 1:
                send[g] = pl.pallas_call(
                    functools.partial(chain_kernel, count, r - 1),
                    out_shape=payload,
                    in_specs=[VMEM] * 4,
                    out_specs=VMEM,
                    compiler_params=params(4),
                    cost_estimate=cost(8 * N * width, 8 * N * width),
                    name="chain",
                )(got[g][-1], f_parts[g], b_parts[g], dec[g])
            if len(got[g]) < r:
                pairs = [(r - 1, r), (count - r, count - r - 1)]
                got[g].append(lax.ppermute(send[g], "ctx", pairs))

    teacher = write(targets)
    student, grads = (), None
    for g in range(groups):
        more = [] if grads is None else [grads]
        if g == groups - 1:
            got[g][-1], teacher, *student = lax.optimization_barrier(
                (got[g][-1], teacher, *student)
            )
        made, grads = pl.pallas_call(
            functools.partial(final_kernel, count, g, groups, loss_scale),
            out_shape=(struct((rows, width), BF16), struct((groups + 1, width), F32)),
            in_specs=[VMEM] * (8 + others + len(more)),
            out_specs=(VMEM,) * 2,
            scratch_shapes=[
                pltpu.VMEM((N, width), BF16),
                pltpu.VMEM((N + EXTRA, width), BF16),
                pltpu.VMEM((rows, width), F32),
                pltpu.VMEM((rows, width), F32),
                pltpu.VMEM((rows, 3 * 128), F32),
                pltpu.VMEM((8, width), F32),
                pltpu.VMEM((8, width), F32),
            ],
            compiler_params=params(16),
            cost_estimate=cost(2 * rows * width * N, 20 * rows * width),
            name="final",
        )(
            *local[g::groups],
            cmat,
            targets[g],
            gain.reshape(1, features),
            f_parts[g],
            dec[g],
            *got[g],
            *more,
        )
        student = [write([made], g, student)]
    student = student[0]
    shifts = [1 << k for k in reversed(range(count.bit_length() - 1))]
    partner = exchange(grads, shifts[0])
    if lax.axis_size("dp") == 2:
        grads = (grads + partner) + (exchange(grads, count) + exchange(grads, count + shifts[0]))
    else:
        grads = grads + partner
    for shift in shifts[1:-1]:
        grads = grads + exchange(grads, shift)
    grad_gain, grad_skip = pl.pallas_call(
        closing_kernel,
        out_shape=(struct((1, features), F32), struct((1, heads), F32)),
        in_specs=[VMEM] * 2,
        out_specs=(VMEM,) * 2,
        compiler_params=params(2),
        name="closing",
    )(grads, exchange(grads, shifts[-1]))
    return (teacher[None], student[None], grad_gain[0], grad_skip[0])


def solution(mesh):
    rows = P("dp", "ctx", "head")
    in_specs = (
        rows,
        rows,
        rows,
        P("dp", None),
        rows,
        rows,
        rows,
        rows,
        rows,
        P("head"),
        P("head"),
        P("head"),
        P("head"),
    )
    out_specs = (rows, rows, P("head"), P("head"))
    return jax.shard_map(body, mesh=mesh, in_specs=in_specs, out_specs=out_specs, check_vma=False)
```

```python
import functools
import math

import jax
import jax.numpy as jnp
from jax import lax
from jax.experimental import pallas as pl
from jax.experimental.pallas import tpu as pltpu
from jax.sharding import PartitionSpec as P

DH = 128
P_SIZE = 64
N = 128
EXTRA = 16
EPS = 1e-05
MASKED = -1e30
F32 = jnp.float32
BF16 = jnp.bfloat16
VMEM = pl.BlockSpec(memory_space=pltpu.VMEM)


def params(mib):
    return pltpu.CompilerParams(vmem_limit_bytes=mib << 20)


def cost(flops, size):
    return pl.CostEstimate(flops=flops, bytes_accessed=size, transcendentals=0)


def parts(v):
    hi = v.astype(BF16)
    return hi, (v - hi.astype(F32)).astype(BF16)


def spread_matrix(heads, width, first):
    row = lax.broadcasted_iota(jnp.int32, (heads, width), 0)
    lane = lax.broadcasted_iota(jnp.int32, (heads, width), 1)
    return jnp.where(row == (lane // P_SIZE) + first, 1.0, 0.0).astype(BF16)


def dot_nt(a, b):
    return lax.dot_general(a, b, (((1,), (1,)), ((), ())), preferred_element_type=F32)


def dot_tn(a, b):
    return lax.dot_general(a, b, (((0,), (0,)), ((), ())), preferred_element_type=F32)


def spread(v, matrix):
    return dot_tn(jnp.concatenate(parts(v), axis=0), jnp.concatenate([matrix, matrix], axis=0))


def doc_row(docs_ref, block, stretch):
    return docs_ref[:, pl.ds(pl.multiple_of(block * stretch, stretch), stretch)]


def as_column(row):
    size = row.shape[1]
    r = lax.broadcasted_iota(jnp.int32, (size, size), 0)
    c = lax.broadcasted_iota(jnp.int32, (size, size), 1)
    return jnp.sum(jnp.where(r == c, row.astype(F32), 0.0), axis=1, keepdims=True)


def lower_triangle(size):
    r = lax.broadcasted_iota(jnp.int32, (size, size), 0)
    c = lax.broadcasted_iota(jnp.int32, (size, size), 1)
    return r >= c


def prior_doc(docs_ref, block, stretch):
    before = doc_row(docs_ref, jnp.maximum(block - 1, 0), stretch)[:, stretch - 1 :]
    return jnp.where(block > 0, before, -1)


def own_block(index, count, half):
    return index if half == 0 else 2 * count - 1 - index


def ring_order(count):
    return [0] + list(range(1, count, 2)) + list(range(2, count, 2))[::-1]


def ring_source(index, count, steps):
    order = ring_order(count)
    source = jnp.int32(0)
    for place, member in enumerate(order):
        source = jnp.where(index == member, order[(place - steps) % count], source)
    return source


def put_state(ref, state):
    ref[:N, :] = state.astype(BF16)
    ref[N:, :] = jnp.zeros((EXTRA, ref.shape[1]), BF16)


def put_composite(ref, state, decay):
    hi, lo = parts(decay)
    ref[:N, :] = state.astype(BF16)
    ref[N:, :] = jnp.concatenate(
        [hi, lo, jnp.zeros((EXTRA - 2, ref.shape[1]), BF16)], axis=0
    )


def opening_kernel(
    count,
    groups,
    docs_ref,
    k_ref,
    v_ref,
    x_ref,
    b_ref,
    dt_ref,
    bias_ref,
    log_ref,
    kv_ref,
    ec_ref,
    *outs,
):
    xw_refs, dec_refs, f_refs, b_refs, send_refs = (
        outs[k * groups : (k + 1) * groups] for k in range(5)
    )
    heads, rows = dt_ref.shape
    stretch = rows // 2
    width = x_ref.shape[1] // groups
    kv_width = k_ref.shape[1]
    index = lax.axis_index("ctx")
    kv_ref[:, :kv_width] = k_ref[...]
    kv_ref[:, kv_width:] = v_ref[...]
    triangle = jnp.where(lower_triangle(stretch), 1.0, 0.0)
    slope = jnp.exp(as_column(log_ref[...]))
    bias = as_column(bias_ref[...])
    lane = lax.broadcasted_iota(jnp.int32, (heads, 8), 1)
    ends = jnp.zeros((heads, 8), F32)
    loads = []
    projs = []
    for half in range(2):
        block = own_block(index, count, half)
        sl = slice(half * stretch, (half + 1) * stretch)
        raw = dt_ref[:, sl] + bias
        dt = jnp.maximum(raw, 0.0) + jnp.log1p(jnp.exp(-jnp.abs(raw)))
        cum = lax.dot_general(
            -dt * slope,
            triangle,
            (((1,), (1,)), ((), ())),
            precision=lax.Precision.HIGHEST,
            preferred_element_type=F32,
        )
        ec_ref[:, sl] = jnp.exp(cum)
        loads.append(jnp.exp(-cum) * dt)
        final = jnp.exp(cum[:, stretch - 1 :])
        row = doc_row(docs_ref, block, stretch)
        last = row[:, stretch - 1 :]
        kept = jnp.where(last == prior_doc(docs_ref, block, stretch), 1.0, 0.0)
        ends = jnp.where(lane == half, final * kept, ends)
        ends = jnp.where(lane == 2 + half, final, ends)
        same = jnp.where(as_column(row) == last.astype(F32), 1.0, 0.0)
        projs.append((b_ref[sl, :].astype(F32) * same).astype(BF16))
    for g in range(groups):
        cols = slice(g * width, (g + 1) * width)
        matrix = spread_matrix(heads, width, g * (heads // groups))
        wide = spread(ends, matrix)
        dec_refs[g][...] = wide
        sums = []
        for half in range(2):
            sl = slice(half * stretch, (half + 1) * stretch)
            xw = (x_ref[sl, cols].astype(F32) * spread(loads[half], matrix)).astype(BF16)
            xw_refs[g][sl, :] = xw
            sums.append(dot_tn(projs[half][:, g * N : (g + 1) * N], xw) * wide[2 + half : 3 + half])
        f_refs[g][...] = sums[0].astype(BF16)
        b_refs[g][...] = sums[1].astype(BF16)

        @pl.when(index == 0)
        def _():
            put_state(send_refs[g], sums[0])

        @pl.when(index != 0)
        def _():
            put_composite(send_refs[g], wide[1:2] * sums[0] + sums[1], wide[0:1] * wide[1:2])


def chain_kernel(count, stage, got_ref, f_ref, b_ref, dec_ref, send_ref):
    index = lax.axis_index("ctx")

    @pl.when(index == stage)
    def _():
        state = dec_ref[0:1, :] * got_ref[:N, :].astype(F32) + f_ref[...].astype(F32)
        put_state(send_ref, state)

    @pl.when(index == count - 1 - stage)
    def _():
        decay = got_ref[N : N + 1, :].astype(F32) + got_ref[N + 1 : N + 2, :].astype(F32)
        inner = decay * f_ref[...].astype(F32) + got_ref[:N, :].astype(F32)
        state = dec_ref[1:2, :] * inner + b_ref[...].astype(F32)
        put_composite(send_ref, state, dec_ref[1:2, :] * decay * dec_ref[0:1, :])


def local_kernel(
    count, groups, docs_ref, x_ref, gate_ref, b_ref, c_ref, skip_ref, ec_ref, *refs
):
    xw_refs, pre_refs, reach_refs, sx_refs = (
        refs[k * groups : (k + 1) * groups] for k in range(4)
    )
    x_here, gate_here, sems = refs[4 * groups :]
    heads, rows = ec_ref.shape
    stretch = rows // 2
    width = x_ref.shape[1] // groups
    index = lax.axis_index("ctx")
    moves = []
    for g in range(groups):
        cols = pl.ds(g * width, width)
        moves.append(
            [
                pltpu.make_async_copy(x_ref.at[:, cols], x_here.at[g], sems.at[0, g]),
                pltpu.make_async_copy(gate_ref.at[:, cols], gate_here.at[g], sems.at[1, g]),
            ]
        )
        for move in moves[g]:
            move.start()
    triangle = lower_triangle(stretch)
    skip = as_column(skip_ref[...])
    step = 16
    masks = []
    for half in range(2):
        block = own_block(index, count, half)
        row = doc_row(docs_ref, block, stretch)
        column = as_column(row)
        reached = jnp.where(column == prior_doc(docs_ref, block, stretch).astype(F32), 1.0, 0.0)
        masks.append((triangle & (column == row.astype(F32)), reached))
    for g in range(groups):
        proj = slice(g * N, (g + 1) * N)
        matrix = spread_matrix(heads, width, g * (heads // groups))
        wide_skip = spread(skip, matrix)
        for half in range(2):
            sl = slice(half * stretch, (half + 1) * stretch)
            near, reached = masks[half]
            gram = dot_nt(c_ref[sl, proj], b_ref[sl, proj])
            gram = jnp.where(near, gram, 0.0).astype(BF16)
            wide = spread(ec_ref[:, sl], matrix)
            inner = jnp.dot(gram, xw_refs[g][sl, :], preferred_element_type=F32)
            if half == 0:
                for move in moves[g]:
                    move.wait()
            for k in range(0, stretch, step):
                at = slice(half * stretch + k, half * stretch + k + step)
                here = slice(k, k + step)
                x = x_here[g, at, :].astype(F32)
                gate = gate_here[g, at, :].astype(F32)
                silu = gate / (1.0 + jnp.exp(-gate))
                fade = wide[here] * silu
                sx = silu * x
                sx_refs[g][at, :] = sx
                pre_refs[g][at, :] = inner[here] * fade + wide_skip * sx
                reach_refs[g][at, :] = reached[here] * fade


def merge_kernel(count, state_ref, kv_ref, out_ref):
    index = lax.axis_index("ctx")
    outer = (index == 0) | (index == count - 1)
    rows, wide = kv_ref.shape
    stretch = rows // 2

    @pl.when(outer)
    def _():
        out_ref[...] = state_ref[...]

    @pl.when(jnp.logical_not(outer))
    def _():
        out_ref[:stretch, :wide] = kv_ref[:stretch, :]
        out_ref[:stretch, wide:] = kv_ref[stretch:, :]
        out_ref[stretch:, :] = jnp.zeros((out_ref.shape[0] - stretch, 2 * wide), BF16)


def arrivals(index, count, refs):
    if count != 4:
        return [(ring_source(index, count, r + 1), [(None, refs[r])]) for r in range(count - 1)]
    near, own_of_middle, next_of_middle, far, farther = refs
    middle = (index == 1) | (index == 2)
    low = index < 2
    return [
        (index ^ 1, [(None, near)]),
        (
            jnp.where(low, 2, 1),
            [(middle, own_of_middle), (jnp.logical_not(middle), far)],
        ),
        (
            jnp.where(low, 3, 0),
            [(middle, next_of_middle), (jnp.logical_not(middle), farther)],
        ),
    ]


def attention_kernel(count, per, stack, g, docs_ref, q_ref, k_ref, v_ref, *refs):
    others = count - 1
    sent = 5 if count == 4 else others
    out_ref, kt, vt, bias_f, bias_b, bias_a = refs[-6:]
    rows = q_ref.shape[0]
    stretch = rows // 2
    index = lax.axis_index("ctx")
    last = 2 * count - 1
    kv_width = refs[0].shape[1] // 2
    row_f = doc_row(docs_ref, index, stretch).astype(F32)
    row_b = doc_row(docs_ref, last - index, stretch).astype(F32)
    col_f = as_column(row_f)
    col_b = as_column(row_b)
    triangle = lower_triangle(stretch)

    def tile(k):
        return slice(k * stretch, (k + 1) * stretch)

    bias_f[...] = jnp.where(triangle & (col_f == row_f), 0.0, MASKED)
    bias_b[:, tile(0)] = jnp.where(col_b == row_f, 0.0, MASKED)
    bias_b[:, tile(1)] = jnp.where(triangle & (col_b == row_b), 0.0, MASKED)
    vt[:, DH:] = jnp.ones((vt.shape[0], DH), BF16)
    here = slice(g * DH, (g + 1) * DH)
    kt[tile(0), :] = k_ref[:stretch, here]
    vt[tile(0), :DH] = v_ref[:stretch, here]
    kt[tile(count), :] = k_ref[stretch:, here]
    vt[tile(count), :DH] = v_ref[stretch:, here]
    lower = []
    for r, (source, places) in enumerate(arrivals(index, count, refs[:sent])):
        lower.append(source < index)
        for condition, ref in places:

            def fetch(ref=ref, r=r):
                folded = ref.shape[1] > 2 * kv_width
                gap = jnp.where(lower[r], 0, 2 * kv_width if folded else stretch)
                for table, first in ((kt, g * DH), (vt, kv_width + g * DH)):
                    front = ref[:stretch, first : first + DH]
                    if folded:
                        own = ref[:stretch, pl.ds(pl.multiple_of(first + gap, DH), DH)]
                    else:
                        own = ref[pl.ds(pl.multiple_of(gap, stretch), stretch), first : first + DH]
                    table[tile(1 + r), :DH] = own
                    table[tile(count + 1 + r), :DH] = front

            if condition is None:
                fetch()
            else:
                pl.when(condition)(fetch)
        key_f = doc_row(docs_ref, source, stretch).astype(F32)
        key_a = doc_row(docs_ref, jnp.where(lower[r], source, last - source), stretch).astype(F32)
        bias_b[:, tile(2 + r)] = jnp.where(col_b == key_f, 0.0, MASKED)
        bias_a[:, tile(r)] = jnp.where(jnp.where(lower[r], col_f, col_b) == key_a, 0.0, MASKED)

    factor = math.log2(math.e) / math.sqrt(DH)
    tall = stack * stretch
    half_keys = count * stretch

    def stacked(first, base):
        return jnp.concatenate(
            [
                q_ref[base : base + stretch, (g * per + first + j) * DH : (g * per + first + j + 1) * DH]
                for j in range(stack)
            ],
            axis=0,
        )

    def biased(score, bias):
        size = score.shape[1]
        return (score.reshape(stack, stretch, size) + bias[None]).reshape(tall, size)

    for first in range(0, per, stack):
        s_f = dot_nt(stacked(first, 0), kt[:half_keys, :])
        s_b = dot_nt(stacked(first, stretch), kt[...])
        t_f = biased(s_f[:, tile(0)], bias_f[...])
        t_b = [biased(s_b[:, tile(0)], bias_b[:, tile(0)])]
        for k in range(1, count + 1):
            t_b.append(biased(s_b[:, tile(count + k - 1)], bias_b[:, tile(k)]))
        t_a = []
        for r in range(others):
            score = jnp.where(lower[r], s_f[:, tile(1 + r)], s_b[:, tile(1 + r)])
            t_a.append(biased(score, bias_a[:, tile(r)]))
        best_f = t_f
        best_b = functools.reduce(jnp.maximum, t_b)
        for r in range(others):
            best_f = jnp.maximum(best_f, jnp.where(lower[r], t_a[r], MASKED))
            best_b = jnp.maximum(best_b, jnp.where(lower[r], MASKED, t_a[r]))
        top_f = jnp.max(best_f, axis=1, keepdims=True)
        top_b = jnp.max(best_b, axis=1, keepdims=True)
        w_f = [jnp.exp2((t_f - top_f) * factor).astype(BF16)]
        w_b = [jnp.exp2((t - top_b) * factor).astype(BF16) for t in t_b]
        w_x = []
        for r in range(others):
            top = jnp.where(lower[r], top_f, top_b)
            w = jnp.exp2((t_a[r] - top) * factor)
            w_f.append(jnp.where(lower[r], w, 0.0).astype(BF16))
            w_x.append(jnp.where(lower[r], 0.0, w).astype(BF16))
        w_b = w_b[:1] + w_x + w_b[1:]
        out_f = jnp.dot(
            jnp.concatenate(w_f, axis=1), vt[:half_keys, :], preferred_element_type=F32
        )
        out_b = jnp.dot(jnp.concatenate(w_b, axis=1), vt[...], preferred_element_type=F32)
        for half, out in enumerate((out_f, out_b)):
            result = (out[:, :DH] / out[:, DH:]).astype(BF16)
            for j in range(stack):
                cols = slice((first + j) * DH, (first + j + 1) * DH)
                out_ref[tile(half), cols] = result[tile(j)]


def final_kernel(
    count,
    g,
    groups,
    loss_scale,
    pre_ref,
    reach_ref,
    sx_ref,
    c_ref,
    teacher_ref,
    gain_ref,
    f_ref,
    dec_ref,
    *refs,
):
    others = count - 1
    got = refs[:others]
    before = refs[others] if g else None
    proj = slice(g * N, (g + 1) * N)
    first_lane = g * pre_ref.shape[1]
    out_ref, grad_ref, front, back, flow, gated_ref, sums, gain_acc, skip_acc = refs[-9:]
    rows, width = pre_ref.shape
    stretch = rows // 2
    index = lax.axis_index("ctx")
    tile = 128
    step = 16

    @pl.when(index == 0)
    def _():
        front[...] = jnp.zeros_like(front)

    @pl.when(index == count - 1)
    def _():
        back[:N, :] = jnp.zeros((N, width), BF16)
        back[N:, :] = jnp.where(
            lax.broadcasted_iota(jnp.int32, (EXTRA, width), 0) == 0, 1.0, 0.0
        ).astype(BF16)

    for r in range(1, count):

        @pl.when(index == r)
        def _():
            front[...] = got[r - 1][:N, :]

        @pl.when(index == count - 1 - r)
        def _():
            back[...] = got[r - 1][...]

    d_in = back[N : N + 1, :].astype(F32) + back[N + 1 : N + 2, :].astype(F32)
    through = dec_ref[0:1, :] * front[...].astype(F32) + f_ref[...].astype(F32)
    entering = (d_in * through + back[:N, :].astype(F32)).astype(BF16)
    flow[:stretch, :] = jnp.dot(c_ref[:stretch, proj], front[...], preferred_element_type=F32)
    flow[stretch:, :] = jnp.dot(c_ref[stretch:, proj], entering, preferred_element_type=F32)
    gain_acc[...] = jnp.zeros_like(gain_acc)
    skip_acc[...] = jnp.zeros_like(skip_acc)

    @pl.loop(0, rows // step, unroll=2)
    def _(k):
        sl = pl.ds(pl.multiple_of(k * step, step), step)
        totals = [jnp.zeros((step, tile), F32)] * 3
        for j in range(0, width, tile):
            cols = slice(j, j + tile)
            gated = pre_ref[sl, cols] + reach_ref[sl, cols] * flow[sl, cols]
            gated_ref[sl, cols] = gated
            scaled = gated * gain_ref[:, first_lane + j : first_lane + j + tile]
            totals[0] += gated * gated
            totals[1] += scaled * scaled
            totals[2] += scaled * teacher_ref[sl, cols].astype(F32)
        for k3 in range(3):
            sums[sl, k3 * tile : (k3 + 1) * tile] = totals[k3]

    square, weighted, crossed = (
        jnp.sum(sums[:, k3 * tile : (k3 + 1) * tile], axis=1, keepdims=True) * (1.0 / width)
        for k3 in range(3)
    )
    scale = lax.rsqrt(square + EPS)
    push_scale = 2.0 * loss_scale
    mean = push_scale * scale * (scale * weighted - crossed)
    sums[:, :tile] = jnp.broadcast_to(scale, (rows, tile))
    sums[:, tile : 2 * tile] = jnp.broadcast_to(mean, (rows, tile))

    @pl.loop(0, rows // step, unroll=2)
    def _(k):
        sl = pl.ds(pl.multiple_of(k * step, step), step)
        scale = sums[sl, :tile]
        mean = sums[sl, tile : 2 * tile]
        for j in range(0, width, tile):
            cols = slice(j, j + tile)
            gain = gain_ref[:, first_lane + j : first_lane + j + tile]
            unit = gated_ref[sl, cols] * scale
            normed = unit * gain
            out_ref[sl, cols] = normed.astype(BF16)
            push = (normed - teacher_ref[sl, cols].astype(F32)) * push_scale
            by_gain = push * unit
            by_skip = (push * gain - unit * mean) * (scale * sx_ref[sl, cols])
            gain_acc[:, cols] += by_gain[:8] + by_gain[8:]
            skip_acc[:, cols] += by_skip[:8] + by_skip[8:]

    row = lax.broadcasted_iota(jnp.int32, (tile, width), 0)
    lane = lax.broadcasted_iota(jnp.int32, (tile, width), 1)
    matrix = jnp.where(row == lane // P_SIZE + g * (width // P_SIZE), 1.0, 0.0).astype(BF16)
    hi, lo = parts(skip_acc[...])
    by_head = jnp.sum(dot_nt(hi, matrix) + dot_nt(lo, matrix), axis=0, keepdims=True)
    grad_ref[...] = jnp.zeros_like(grad_ref)
    if g:
        grad_ref[:g, :] = before[:g, :]
        by_head += before[groups : groups + 1, :tile]
    grad_ref[g : g + 1, :] = jnp.sum(gain_acc[...], axis=0, keepdims=True)
    grad_ref[groups : groups + 1, :tile] = by_head


def writing_kernel(*refs):
    parts_in, out_ref, sems = refs[:-2], refs[-2], refs[-1]
    width = parts_in[0].shape[1]
    moves = [
        pltpu.make_async_copy(part, out_ref.at[:, pl.ds(k * width, width)], sems.at[k])
        for k, part in enumerate(parts_in)
    ]
    for move in moves:
        move.start()
    for move in moves:
        move.wait()


def closing_kernel(a_ref, b_ref, gain_ref, skip_ref):
    total = a_ref[...] + b_ref[...]
    groups, width = total.shape[0] - 1, total.shape[1]
    for g in range(groups):
        gain_ref[:, g * width : (g + 1) * width] = total[g : g + 1, :]
    skip_ref[...] = total[groups : groups + 1, : skip_ref.shape[1]]


def exchange(part, shift):
    axes = ("dp", "ctx")
    size = lax.axis_size(axes)
    return lax.ppermute(part, axes, [(d, d ^ shift) for d in range(size)])


def body(
    queries,
    keys,
    values,
    doc_ids,
    inputs,
    gate_input,
    b_input,
    c_input,
    dt_raw,
    dt_bias,
    decay_log,
    skip,
    gain,
):
    count = lax.axis_size("ctx")
    rows, features = queries.shape[1:]
    stretch = rows // 2
    kv_dev = keys.shape[2] // DH
    per_kv = queries.shape[2] // keys.shape[2]
    groups = b_input.shape[2] // N
    heads = features // P_SIZE
    width = features // groups
    length = doc_ids.shape[1]
    others = count - 1
    loss_scale = 1.0 / (lax.axis_size("dp") * count * rows)
    x, gate, bmat, cmat = inputs[0], gate_input[0], b_input[0], c_input[0]
    struct = jax.ShapeDtypeStruct

    def in_hbm(*arrays):
        return [pltpu.with_memory_space_constraint(array, pltpu.HBM) for array in arrays]

    def write(pieces):
        return pl.pallas_call(
            writing_kernel,
            out_shape=struct((rows, features), BF16),
            in_specs=[VMEM] * len(pieces),
            out_specs=pl.BlockSpec(memory_space=pl.ANY),
            scratch_shapes=[pltpu.SemaphoreType.DMA((len(pieces),))],
            compiler_params=params(2),
            cost_estimate=cost(0, 4 * rows * features),
            name="writing",
        )(*pieces)

    state = struct((N, width), BF16)
    payload = struct((N + EXTRA, width), BF16)
    outs = pl.pallas_call(
        functools.partial(opening_kernel, count, groups),
        out_shape=(
            struct((rows, 2 * kv_dev * DH), BF16),
            struct((heads, rows), F32),
            *([struct((rows, width), BF16)] * groups),
            *([struct((8, width), F32)] * groups),
            *([state] * (2 * groups)),
            *([payload] * groups),
        ),
        in_specs=[VMEM] * 8,
        out_specs=(VMEM,) * (2 + 5 * groups),
        compiler_params=params(16),
        cost_estimate=cost(4 * rows * features * N, 8 * rows * features),
        name="opening",
    )(
        *in_hbm(
            doc_ids,
            keys[0],
            values[0],
            x,
            bmat,
            dt_raw[0].T,
            dt_bias.reshape(1, heads),
            decay_log.reshape(1, heads),
        )
    )
    kv, ec = outs[:2]
    xw, dec, f_parts, b_parts, send = (
        outs[2 + k * groups : 2 + (k + 1) * groups] for k in range(5)
    )

    local = pl.pallas_call(
        functools.partial(local_kernel, count, groups),
        out_shape=(struct((rows, width), F32),) * (3 * groups),
        in_specs=[
            VMEM,
            *[pl.BlockSpec(memory_space=pl.ANY)] * 2,
            *[VMEM] * (4 + groups),
        ],
        out_specs=(VMEM,) * (3 * groups),
        scratch_shapes=[
            pltpu.VMEM((groups, rows, width), BF16),
            pltpu.VMEM((groups, rows, width), BF16),
            pltpu.SemaphoreType.DMA((2, groups)),
        ],
        compiler_params=params(16),
        cost_estimate=cost(2 * rows * features * N, 16 * rows * features),
        name="local",
    )(*in_hbm(doc_ids, x, gate, bmat, cmat, skip.reshape(1, heads)), ec, *xw)

    send = list(send)
    got = [[] for _ in range(groups)]
    if count == 4:
        inward, outward, across = [(0, 1), (3, 2)], [(1, 0), (2, 3)], [(1, 2), (2, 1)]
        near = lax.ppermute(kv, "ctx", inward + outward)
        middle = lax.ppermute(kv, "ctx", across)
        middle, *local = lax.optimization_barrier((middle, *local))
        beyond = lax.ppermute(near, "ctx", across)
        send[-1] = pl.pallas_call(
            functools.partial(merge_kernel, count),
            out_shape=payload,
            in_specs=[VMEM] * 2,
            out_specs=VMEM,
            compiler_params=params(4),
            cost_estimate=cost(0, 4 * N * width),
            name="merge",
        )(send[-1], middle)
        far = lax.ppermute(send[-1], "ctx", inward + outward)
        got[-1].append(far)
        farther = lax.ppermute(beyond, "ctx", outward)
        kv_got = [near, middle, beyond, far, farther]
    else:
        ring = ring_order(count)
        ring_pairs = [(ring[d], ring[(d + 1) % count]) for d in range(count)]
        kv_got = [kv]
        for _ in range(others):
            kv_got.append(lax.ppermute(kv_got[-1], "ctx", ring_pairs))
        kv_got = kv_got[1:]
    stack = 4 if per_kv % 4 == 0 and count <= 4 else 1
    targets = [
        pl.pallas_call(
            functools.partial(attention_kernel, count, per_kv, stack, g),
            out_shape=struct((rows, per_kv * DH), BF16),
            in_specs=[VMEM] * (4 + len(kv_got)),
            out_specs=VMEM,
            scratch_shapes=[
                pltpu.VMEM((2 * count * stretch, DH), BF16),
                pltpu.VMEM((2 * count * stretch, 2 * DH), BF16),
                pltpu.VMEM((stretch, stretch), F32),
                pltpu.VMEM((stretch, (count + 1) * stretch), F32),
                pltpu.VMEM((stretch, others * stretch), F32),
            ],
            compiler_params=params(24),
            cost_estimate=cost(
                4 * (2 * count + 1) * stretch * stretch * per_kv * DH, 8 * rows * per_kv * DH
            ),
            name="attention",
        )(doc_ids, queries[0], keys[0], values[0], *kv_got)
        for g in range(kv_dev)
    ]
    for r in range(1, count):
        for g in range(groups):
            if r == 3 and g == groups - 1:
                got[g][-1], targets[0] = lax.optimization_barrier((got[g][-1], targets[0]))
            if r > 1:
                send[g] = pl.pallas_call(
                    functools.partial(chain_kernel, count, r - 1),
                    out_shape=payload,
                    in_specs=[VMEM] * 4,
                    out_specs=VMEM,
                    compiler_params=params(4),
                    cost_estimate=cost(8 * N * width, 8 * N * width),
                    name="chain",
                )(got[g][-1], f_parts[g], b_parts[g], dec[g])
            if len(got[g]) < r:
                pairs = [(r - 1, r), (count - r, count - r - 1)]
                got[g].append(lax.ppermute(send[g], "ctx", pairs))

    normed, grads = [], None
    for g in range(groups):
        more = [] if grads is None else [grads]
        made, grads = pl.pallas_call(
            functools.partial(final_kernel, count, g, groups, loss_scale),
            out_shape=(struct((rows, width), BF16), struct((groups + 1, width), F32)),
            in_specs=[VMEM] * (8 + others + len(more)),
            out_specs=(VMEM,) * 2,
            scratch_shapes=[
                pltpu.VMEM((N, width), BF16),
                pltpu.VMEM((N + EXTRA, width), BF16),
                pltpu.VMEM((rows, width), F32),
                pltpu.VMEM((rows, width), F32),
                pltpu.VMEM((rows, 3 * 128), F32),
                pltpu.VMEM((8, width), F32),
                pltpu.VMEM((8, width), F32),
            ],
            compiler_params=params(16),
            cost_estimate=cost(2 * rows * width * N, 20 * rows * width),
            name="final",
        )(
            *local[g::groups],
            cmat,
            targets[g],
            gain.reshape(1, features),
            f_parts[g],
            dec[g],
            *got[g],
            *more,
        )
        normed.append(made)
    shifts = [1 << k for k in reversed(range(count.bit_length() - 1))]
    partner = exchange(grads, shifts[0])
    *targets, _ = lax.optimization_barrier((*targets, grads))
    teacher = write(targets)
    partner, teacher = lax.optimization_barrier((partner, teacher))
    student = write(normed)
    if lax.axis_size("dp") == 2:
        grads = (grads + partner) + (exchange(grads, count) + exchange(grads, count + shifts[0]))
    else:
        grads = grads + partner
    for shift in shifts[1:-1]:
        grads = grads + exchange(grads, shift)
    grad_gain, grad_skip = pl.pallas_call(
        closing_kernel,
        out_shape=(struct((1, features), F32), struct((1, heads), F32)),
        in_specs=[VMEM] * 2,
        out_specs=(VMEM,) * 2,
        compiler_params=params(2),
        name="closing",
    )(grads, exchange(grads, shifts[-1]))
    return (teacher[None], student[None], grad_gain[0], grad_skip[0])


def solution(mesh):
    rows = P("dp", "ctx", "head")
    in_specs = (
        rows,
        rows,
        rows,
        P("dp", None),
        rows,
        rows,
        rows,
        rows,
        rows,
        P("head"),
        P("head"),
        P("head"),
        P("head"),
    )
    out_specs = (rows, rows, P("head"), P("head"))
    return jax.shard_map(body, mesh=mesh, in_specs=in_specs, out_specs=out_specs, check_vma=False)
```

```python
import functools
import math

import jax
import jax.numpy as jnp
from jax import lax
from jax.experimental import pallas as pl
from jax.experimental.pallas import tpu as pltpu
from jax.sharding import PartitionSpec as P

DH = 128
P_SIZE = 64
N = 128
EXTRA = 16
EPS = 1e-05
MASKED = -1e30
F32 = jnp.float32
BF16 = jnp.bfloat16
VMEM = pl.BlockSpec(memory_space=pltpu.VMEM)


def params(mib):
    return pltpu.CompilerParams(vmem_limit_bytes=mib << 20)


def cost(flops, size):
    return pl.CostEstimate(flops=flops, bytes_accessed=size, transcendentals=0)


def parts(v):
    hi = v.astype(BF16)
    return hi, (v - hi.astype(F32)).astype(BF16)


def spread_matrix(heads, width, first):
    row = lax.broadcasted_iota(jnp.int32, (heads, width), 0)
    lane = lax.broadcasted_iota(jnp.int32, (heads, width), 1)
    return jnp.where(row == (lane // P_SIZE) + first, 1.0, 0.0).astype(BF16)


def dot_nt(a, b):
    return lax.dot_general(a, b, (((1,), (1,)), ((), ())), preferred_element_type=F32)


def dot_tn(a, b):
    return lax.dot_general(a, b, (((0,), (0,)), ((), ())), preferred_element_type=F32)


def spread(v, matrix):
    return dot_tn(jnp.concatenate(parts(v), axis=0), jnp.concatenate([matrix, matrix], axis=0))


def doc_row(docs_ref, block, stretch):
    return docs_ref[:, pl.ds(pl.multiple_of(block * stretch, stretch), stretch)]


def as_column(row):
    size = row.shape[1]
    r = lax.broadcasted_iota(jnp.int32, (size, size), 0)
    c = lax.broadcasted_iota(jnp.int32, (size, size), 1)
    return jnp.sum(jnp.where(r == c, row.astype(F32), 0.0), axis=1, keepdims=True)


def lower_triangle(size):
    r = lax.broadcasted_iota(jnp.int32, (size, size), 0)
    c = lax.broadcasted_iota(jnp.int32, (size, size), 1)
    return r >= c


def prior_doc(docs_ref, block, stretch):
    before = doc_row(docs_ref, jnp.maximum(block - 1, 0), stretch)[:, stretch - 1 :]
    return jnp.where(block > 0, before, -1)


def own_block(index, count, half):
    return index if half == 0 else 2 * count - 1 - index


def ring_order(count):
    return [0] + list(range(1, count, 2)) + list(range(2, count, 2))[::-1]


def ring_source(index, count, steps):
    order = ring_order(count)
    source = jnp.int32(0)
    for place, member in enumerate(order):
        source = jnp.where(index == member, order[(place - steps) % count], source)
    return source


def passed_decay(ref, first, heads, width, g):
    matrix = spread_matrix(heads, width, g * (width // P_SIZE))
    wide = jnp.dot(ref[first : first + EXTRA, :heads], matrix, preferred_element_type=F32)
    return wide[0:1] + wide[1:2]


def opening_kernel(
    count,
    groups,
    docs_ref,
    k_ref,
    v_ref,
    x_ref,
    b_ref,
    dt_ref,
    bias_ref,
    log_ref,
    kv_ref,
    ec_ref,
    *outs,
):
    xw_refs, dec_refs, f_refs, b_refs, send_refs = (
        outs[k * groups : (k + 1) * groups] for k in range(5)
    )
    heads, rows = dt_ref.shape
    stretch = rows // 2
    width = x_ref.shape[1] // groups
    kv_width = k_ref.shape[1]
    index = lax.axis_index("ctx")
    kv_ref[:rows, :kv_width] = k_ref[...]
    kv_ref[:rows, kv_width:] = v_ref[...]
    kv_ref[rows:, :] = jnp.zeros((EXTRA, 2 * kv_width), BF16)
    triangle = jnp.where(lower_triangle(stretch), 1.0, 0.0)
    slope = jnp.exp(as_column(log_ref[...]))
    bias = as_column(bias_ref[...])
    lane = lax.broadcasted_iota(jnp.int32, (heads, 8), 1)
    ends = jnp.zeros((heads, 8), F32)
    loads = []
    projs = []
    for half in range(2):
        block = own_block(index, count, half)
        sl = slice(half * stretch, (half + 1) * stretch)
        raw = dt_ref[:, sl] + bias
        dt = jnp.maximum(raw, 0.0) + jnp.log1p(jnp.exp(-jnp.abs(raw)))
        cum = lax.dot_general(
            -dt * slope,
            triangle,
            (((1,), (1,)), ((), ())),
            precision=lax.Precision.HIGHEST,
            preferred_element_type=F32,
        )
        ec_ref[:, sl] = jnp.exp(cum)
        loads.append(jnp.exp(-cum) * dt)
        final = jnp.exp(cum[:, stretch - 1 :])
        row = doc_row(docs_ref, block, stretch)
        last = row[:, stretch - 1 :]
        kept = jnp.where(last == prior_doc(docs_ref, block, stretch), 1.0, 0.0)
        ends = jnp.where(lane == half, final * kept, ends)
        ends = jnp.where(lane == 2 + half, final, ends)
        same = jnp.where(as_column(row) == last.astype(F32), 1.0, 0.0)
        projs.append((b_ref[sl, :].astype(F32) * same).astype(BF16))
    both = ends[:, 0:1] * ends[:, 1:2]
    r = lax.broadcasted_iota(jnp.int32, (heads, heads), 0)
    c = lax.broadcasted_iota(jnp.int32, (heads, heads), 1)
    hi, lo = parts(jnp.sum(jnp.where(r == c, both, 0.0), axis=0, keepdims=True))
    kv_ref[rows:, :heads] = jnp.concatenate(
        [hi, lo, jnp.zeros((EXTRA - 2, heads), BF16)], axis=0
    )
    for g in range(groups):
        cols = slice(g * width, (g + 1) * width)
        matrix = spread_matrix(heads, width, g * (heads // groups))
        wide = spread(ends, matrix)
        dec_refs[g][...] = wide
        sums = []
        for half in range(2):
            sl = slice(half * stretch, (half + 1) * stretch)
            xw = (x_ref[sl, cols].astype(F32) * spread(loads[half], matrix)).astype(BF16)
            xw_refs[g][sl, :] = xw
            sums.append(dot_tn(projs[half][:, g * N : (g + 1) * N], xw) * wide[2 + half : 3 + half])
        f_refs[g][...] = sums[0].astype(BF16)
        b_refs[g][...] = sums[1].astype(BF16)

        @pl.when(index == 0)
        def _():
            send_refs[g][...] = sums[0].astype(BF16)

        @pl.when(index != 0)
        def _():
            send_refs[g][...] = (wide[1:2] * sums[0] + sums[1]).astype(BF16)


def chain_kernel(count, stage, g, heads, got_ref, f_ref, b_ref, dec_ref, *refs):
    send_ref = refs[-1]
    width = f_ref.shape[1]
    index = lax.axis_index("ctx")

    @pl.when(index == stage)
    def _():
        state = dec_ref[0:1, :] * got_ref[:N, :].astype(F32) + f_ref[...].astype(F32)
        send_ref[...] = state.astype(BF16)

    @pl.when(index == count - 1 - stage)
    def _():
        decay = jnp.ones((1, width), F32)
        for r, ref in enumerate(refs[:-1]):
            one = passed_decay(ref, ref.shape[0] - EXTRA, heads, width, g)
            if count != 4:
                one = jnp.where(ring_source(index, count, r + 1) > index, one, 1.0)
            decay = decay * one
        inner = decay * f_ref[...].astype(F32) + got_ref[:N, :].astype(F32)
        send_ref[...] = (dec_ref[1:2, :] * inner + b_ref[...].astype(F32)).astype(BF16)


def local_kernel(
    count, groups, docs_ref, x_ref, gate_ref, b_ref, c_ref, skip_ref, ec_ref, *refs
):
    xw_refs, pre_refs, reach_refs, sx_refs = (
        refs[k * groups : (k + 1) * groups] for k in range(4)
    )
    x_here, gate_here, sems = refs[4 * groups :]
    heads, rows = ec_ref.shape
    stretch = rows // 2
    width = x_ref.shape[1] // groups
    index = lax.axis_index("ctx")
    moves = []
    for g in range(groups):
        cols = pl.ds(g * width, width)
        moves.append(
            [
                pltpu.make_async_copy(x_ref.at[:, cols], x_here.at[g], sems.at[0, g]),
                pltpu.make_async_copy(gate_ref.at[:, cols], gate_here.at[g], sems.at[1, g]),
            ]
        )
        for move in moves[g]:
            move.start()
    triangle = lower_triangle(stretch)
    skip = as_column(skip_ref[...])
    step = 16
    masks = []
    for half in range(2):
        block = own_block(index, count, half)
        row = doc_row(docs_ref, block, stretch)
        column = as_column(row)
        reached = jnp.where(column == prior_doc(docs_ref, block, stretch).astype(F32), 1.0, 0.0)
        masks.append((triangle & (column == row.astype(F32)), reached))
    for g in range(groups):
        proj = slice(g * N, (g + 1) * N)
        matrix = spread_matrix(heads, width, g * (heads // groups))
        wide_skip = spread(skip, matrix)
        for half in range(2):
            sl = slice(half * stretch, (half + 1) * stretch)
            near, reached = masks[half]
            gram = dot_nt(c_ref[sl, proj], b_ref[sl, proj])
            gram = jnp.where(near, gram, 0.0).astype(BF16)
            wide = spread(ec_ref[:, sl], matrix)
            inner = jnp.dot(gram, xw_refs[g][sl, :], preferred_element_type=F32)
            if half == 0:
                for move in moves[g]:
                    move.wait()
            for k in range(0, stretch, step):
                at = slice(half * stretch + k, half * stretch + k + step)
                here = slice(k, k + step)
                x = x_here[g, at, :].astype(F32)
                gate = gate_here[g, at, :].astype(F32)
                silu = gate / (1.0 + jnp.exp(-gate))
                fade = wide[here] * silu
                sx = silu * x
                sx_refs[g][at, :] = sx
                pre_refs[g][at, :] = inner[here] * fade + wide_skip * sx
                reach_refs[g][at, :] = reached[here] * fade


def merge_kernel(count, state_ref, kv_ref, out_ref):
    index = lax.axis_index("ctx")
    outer = (index == 0) | (index == count - 1)
    wide = kv_ref.shape[1]
    rows = kv_ref.shape[0] - EXTRA
    stretch = rows // 2

    @pl.when(outer)
    def _():
        out_ref[:N, :] = state_ref[...]
        out_ref[N:, :] = jnp.zeros((EXTRA, out_ref.shape[1]), BF16)

    @pl.when(jnp.logical_not(outer))
    def _():
        out_ref[:stretch, :wide] = kv_ref[:stretch, :]
        out_ref[:stretch, wide:] = kv_ref[stretch:rows, :]
        out_ref[stretch:, :wide] = kv_ref[rows:, :]
        out_ref[stretch:, wide:] = jnp.zeros((EXTRA, wide), BF16)


def arrivals(index, count, refs):
    if count != 4:
        return [(ring_source(index, count, r + 1), [(None, refs[r])]) for r in range(count - 1)]
    near, own_of_middle, next_of_middle, far, farther = refs
    middle = (index == 1) | (index == 2)
    low = index < 2
    return [
        (index ^ 1, [(None, near)]),
        (
            jnp.where(low, 2, 1),
            [(middle, own_of_middle), (jnp.logical_not(middle), far)],
        ),
        (
            jnp.where(low, 3, 0),
            [(middle, next_of_middle), (jnp.logical_not(middle), farther)],
        ),
    ]


def attention_kernel(count, per, stack, g, docs_ref, q_ref, k_ref, v_ref, *refs):
    others = count - 1
    sent = 5 if count == 4 else others
    out_ref, kt, vt, bias_f, bias_b, bias_a = refs[-6:]
    rows = q_ref.shape[0]
    stretch = rows // 2
    index = lax.axis_index("ctx")
    last = 2 * count - 1
    kv_width = refs[0].shape[1] // 2
    row_f = doc_row(docs_ref, index, stretch).astype(F32)
    row_b = doc_row(docs_ref, last - index, stretch).astype(F32)
    col_f = as_column(row_f)
    col_b = as_column(row_b)
    triangle = lower_triangle(stretch)

    def tile(k):
        return slice(k * stretch, (k + 1) * stretch)

    bias_f[...] = jnp.where(triangle & (col_f == row_f), 0.0, MASKED)
    bias_b[:, tile(0)] = jnp.where(col_b == row_f, 0.0, MASKED)
    bias_b[:, tile(1)] = jnp.where(triangle & (col_b == row_b), 0.0, MASKED)
    vt[:, DH:] = jnp.ones((vt.shape[0], DH), BF16)
    here = slice(g * DH, (g + 1) * DH)
    kt[tile(0), :] = k_ref[:stretch, here]
    vt[tile(0), :DH] = v_ref[:stretch, here]
    kt[tile(count), :] = k_ref[stretch:, here]
    vt[tile(count), :DH] = v_ref[stretch:, here]
    lower = []
    for r, (source, places) in enumerate(arrivals(index, count, refs[:sent])):
        lower.append(source < index)
        for condition, ref in places:

            def fetch(ref=ref, r=r):
                folded = ref.shape[1] > 2 * kv_width
                gap = jnp.where(lower[r], 0, 2 * kv_width if folded else stretch)
                for table, first in ((kt, g * DH), (vt, kv_width + g * DH)):
                    front = ref[:stretch, first : first + DH]
                    if folded:
                        own = ref[:stretch, pl.ds(pl.multiple_of(first + gap, DH), DH)]
                    else:
                        own = ref[pl.ds(pl.multiple_of(gap, stretch), stretch), first : first + DH]
                    table[tile(1 + r), :DH] = own
                    table[tile(count + 1 + r), :DH] = front

            if condition is None:
                fetch()
            else:
                pl.when(condition)(fetch)
        key_f = doc_row(docs_ref, source, stretch).astype(F32)
        key_a = doc_row(docs_ref, jnp.where(lower[r], source, last - source), stretch).astype(F32)
        bias_b[:, tile(2 + r)] = jnp.where(col_b == key_f, 0.0, MASKED)
        bias_a[:, tile(r)] = jnp.where(jnp.where(lower[r], col_f, col_b) == key_a, 0.0, MASKED)

    factor = math.log2(math.e) / math.sqrt(DH)
    tall = stack * stretch
    half_keys = count * stretch

    def stacked(first, base):
        return jnp.concatenate(
            [
                q_ref[base : base + stretch, (g * per + first + j) * DH : (g * per + first + j + 1) * DH]
                for j in range(stack)
            ],
            axis=0,
        )

    def biased(score, bias):
        size = score.shape[1]
        return (score.reshape(stack, stretch, size) + bias[None]).reshape(tall, size)

    for first in range(0, per, stack):
        s_f = dot_nt(stacked(first, 0), kt[:half_keys, :])
        s_b = dot_nt(stacked(first, stretch), kt[...])
        t_f = biased(s_f[:, tile(0)], bias_f[...])
        t_b = [biased(s_b[:, tile(0)], bias_b[:, tile(0)])]
        for k in range(1, count + 1):
            t_b.append(biased(s_b[:, tile(count + k - 1)], bias_b[:, tile(k)]))
        t_a = []
        for r in range(others):
            score = jnp.where(lower[r], s_f[:, tile(1 + r)], s_b[:, tile(1 + r)])
            t_a.append(biased(score, bias_a[:, tile(r)]))
        best_f = t_f
        best_b = functools.reduce(jnp.maximum, t_b)
        for r in range(others):
            best_f = jnp.maximum(best_f, jnp.where(lower[r], t_a[r], MASKED))
            best_b = jnp.maximum(best_b, jnp.where(lower[r], MASKED, t_a[r]))
        top_f = jnp.max(best_f, axis=1, keepdims=True)
        top_b = jnp.max(best_b, axis=1, keepdims=True)
        w_f = [jnp.exp2((t_f - top_f) * factor).astype(BF16)]
        w_b = [jnp.exp2((t - top_b) * factor).astype(BF16) for t in t_b]
        w_x = []
        for r in range(others):
            top = jnp.where(lower[r], top_f, top_b)
            w = jnp.exp2((t_a[r] - top) * factor)
            w_f.append(jnp.where(lower[r], w, 0.0).astype(BF16))
            w_x.append(jnp.where(lower[r], 0.0, w).astype(BF16))
        w_b = w_b[:1] + w_x + w_b[1:]
        out_f = jnp.dot(
            jnp.concatenate(w_f, axis=1), vt[:half_keys, :], preferred_element_type=F32
        )
        out_b = jnp.dot(jnp.concatenate(w_b, axis=1), vt[...], preferred_element_type=F32)
        for half, out in enumerate((out_f, out_b)):
            result = (out[:, :DH] / out[:, DH:]).astype(BF16)
            for j in range(stack):
                cols = slice((first + j) * DH, (first + j + 1) * DH)
                out_ref[tile(half), cols] = result[tile(j)]


def final_kernel(
    count,
    g,
    groups,
    loss_scale,
    heads,
    pre_ref,
    reach_ref,
    sx_ref,
    c_ref,
    teacher_ref,
    gain_ref,
    f_ref,
    dec_ref,
    *refs,
):
    others = count - 1
    got = refs[:others]
    sent = 5 if count == 4 else others
    kv_refs = refs[others : others + sent]
    before = refs[others + sent] if g else None
    proj = slice(g * N, (g + 1) * N)
    first_lane = g * pre_ref.shape[1]
    out_ref, grad_ref, front, back, flow, gated_ref, sums, gain_acc, skip_acc = refs[-9:]
    rows, width = pre_ref.shape
    stretch = rows // 2
    index = lax.axis_index("ctx")
    tile = 128
    step = 16

    @pl.when(index == 0)
    def _():
        front[...] = jnp.zeros_like(front)

    @pl.when(index == count - 1)
    def _():
        back[...] = jnp.zeros_like(back)

    for r in range(1, count):

        @pl.when(index == r)
        def _():
            front[...] = got[r - 1][:N, :]

        @pl.when(index == count - 1 - r)
        def _():
            back[...] = got[r - 1][:N, :]

    d_in = jnp.ones((1, width), F32)
    for source, places in arrivals(index, count, kv_refs):
        for condition, ref in places:
            used = source > index
            if condition is not None:
                used = used & condition
            one = passed_decay(ref, ref.shape[0] - EXTRA, heads, width, g)
            d_in = d_in * jnp.where(used, one, 1.0)
    through = dec_ref[0:1, :] * front[...].astype(F32) + f_ref[...].astype(F32)
    entering = (d_in * through + back[...].astype(F32)).astype(BF16)
    flow[:stretch, :] = jnp.dot(c_ref[:stretch, proj], front[...], preferred_element_type=F32)
    flow[stretch:, :] = jnp.dot(c_ref[stretch:, proj], entering, preferred_element_type=F32)
    gain_acc[...] = jnp.zeros_like(gain_acc)
    skip_acc[...] = jnp.zeros_like(skip_acc)

    @pl.loop(0, rows // step, unroll=2)
    def _(k):
        sl = pl.ds(pl.multiple_of(k * step, step), step)
        totals = [jnp.zeros((step, tile), F32)] * 3
        for j in range(0, width, tile):
            cols = slice(j, j + tile)
            gated = pre_ref[sl, cols] + reach_ref[sl, cols] * flow[sl, cols]
            gated_ref[sl, cols] = gated
            scaled = gated * gain_ref[:, first_lane + j : first_lane + j + tile]
            totals[0] += gated * gated
            totals[1] += scaled * scaled
            totals[2] += scaled * teacher_ref[sl, cols].astype(F32)
        for k3 in range(3):
            sums[sl, k3 * tile : (k3 + 1) * tile] = totals[k3]

    square, weighted, crossed = (
        jnp.sum(sums[:, k3 * tile : (k3 + 1) * tile], axis=1, keepdims=True) * (1.0 / width)
        for k3 in range(3)
    )
    scale = lax.rsqrt(square + EPS)
    push_scale = 2.0 * loss_scale
    mean = push_scale * scale * (scale * weighted - crossed)
    sums[:, :tile] = jnp.broadcast_to(scale, (rows, tile))
    sums[:, tile : 2 * tile] = jnp.broadcast_to(mean, (rows, tile))

    @pl.loop(0, rows // step, unroll=2)
    def _(k):
        sl = pl.ds(pl.multiple_of(k * step, step), step)
        scale = sums[sl, :tile]
        mean = sums[sl, tile : 2 * tile]
        for j in range(0, width, tile):
            cols = slice(j, j + tile)
            gain = gain_ref[:, first_lane + j : first_lane + j + tile]
            unit = gated_ref[sl, cols] * scale
            normed = unit * gain
            out_ref[sl, cols] = normed.astype(BF16)
            push = (normed - teacher_ref[sl, cols].astype(F32)) * push_scale
            by_gain = push * unit
            by_skip = (push * gain - unit * mean) * (scale * sx_ref[sl, cols])
            gain_acc[:, cols] += by_gain[:8] + by_gain[8:]
            skip_acc[:, cols] += by_skip[:8] + by_skip[8:]

    row = lax.broadcasted_iota(jnp.int32, (tile, width), 0)
    lane = lax.broadcasted_iota(jnp.int32, (tile, width), 1)
    matrix = jnp.where(row == lane // P_SIZE + g * (width // P_SIZE), 1.0, 0.0).astype(BF16)
    hi, lo = parts(skip_acc[...])
    by_head = jnp.sum(dot_nt(hi, matrix) + dot_nt(lo, matrix), axis=0, keepdims=True)
    grad_ref[...] = jnp.zeros_like(grad_ref)
    if g:
        grad_ref[:g, :] = before[:g, :]
        by_head += before[groups : groups + 1, :tile]
    grad_ref[g : g + 1, :] = jnp.sum(gain_acc[...], axis=0, keepdims=True)
    grad_ref[groups : groups + 1, :tile] = by_head


def writing_kernel(*refs):
    parts_in, out_ref, sems = refs[:-2], refs[-2], refs[-1]
    width = parts_in[0].shape[1]
    moves = [
        pltpu.make_async_copy(part, out_ref.at[:, pl.ds(k * width, width)], sems.at[k])
        for k, part in enumerate(parts_in)
    ]
    for move in moves:
        move.start()
    for move in moves:
        move.wait()


def closing_kernel(a_ref, b_ref, gain_ref, skip_ref):
    total = a_ref[...] + b_ref[...]
    groups, width = total.shape[0] - 1, total.shape[1]
    for g in range(groups):
        gain_ref[:, g * width : (g + 1) * width] = total[g : g + 1, :]
    skip_ref[...] = total[groups : groups + 1, : skip_ref.shape[1]]


def exchange(part, shift):
    axes = ("dp", "ctx")
    size = lax.axis_size(axes)
    return lax.ppermute(part, axes, [(d, d ^ shift) for d in range(size)])


def body(
    queries,
    keys,
    values,
    doc_ids,
    inputs,
    gate_input,
    b_input,
    c_input,
    dt_raw,
    dt_bias,
    decay_log,
    skip,
    gain,
):
    count = lax.axis_size("ctx")
    rows, features = queries.shape[1:]
    stretch = rows // 2
    kv_dev = keys.shape[2] // DH
    per_kv = queries.shape[2] // keys.shape[2]
    groups = b_input.shape[2] // N
    heads = features // P_SIZE
    width = features // groups
    length = doc_ids.shape[1]
    others = count - 1
    loss_scale = 1.0 / (lax.axis_size("dp") * count * rows)
    x, gate, bmat, cmat = inputs[0], gate_input[0], b_input[0], c_input[0]
    struct = jax.ShapeDtypeStruct

    def in_hbm(*arrays):
        return [pltpu.with_memory_space_constraint(array, pltpu.HBM) for array in arrays]

    def write(*pieces):
        return pl.pallas_call(
            writing_kernel,
            out_shape=struct((rows, features), BF16),
            in_specs=[VMEM] * len(pieces),
            out_specs=pl.BlockSpec(memory_space=pl.ANY),
            scratch_shapes=[pltpu.SemaphoreType.DMA((len(pieces),))],
            compiler_params=params(2),
            cost_estimate=cost(0, 4 * rows * features),
            name="writing",
        )(*pieces)

    state = struct((N, width), BF16)
    payload = struct((N + EXTRA, width), BF16)
    outs = pl.pallas_call(
        functools.partial(opening_kernel, count, groups),
        out_shape=(
            struct((rows + EXTRA, 2 * kv_dev * DH), BF16),
            struct((heads, rows), F32),
            *([struct((rows, width), BF16)] * groups),
            *([struct((8, width), F32)] * groups),
            *([state] * (2 * groups)),
            *([state] * groups),
        ),
        in_specs=[VMEM] * 8,
        out_specs=(VMEM,) * (2 + 5 * groups),
        compiler_params=params(16),
        cost_estimate=cost(4 * rows * features * N, 8 * rows * features),
        name="opening",
    )(
        *in_hbm(
            doc_ids,
            keys[0],
            values[0],
            x,
            bmat,
            dt_raw[0].T,
            dt_bias.reshape(1, heads),
            decay_log.reshape(1, heads),
        )
    )
    kv, ec = outs[:2]
    xw, dec, f_parts, b_parts, send = (
        outs[2 + k * groups : 2 + (k + 1) * groups] for k in range(5)
    )

    local = pl.pallas_call(
        functools.partial(local_kernel, count, groups),
        out_shape=(struct((rows, width), F32),) * (3 * groups),
        in_specs=[
            VMEM,
            *[pl.BlockSpec(memory_space=pl.ANY)] * 2,
            *[VMEM] * (4 + groups),
        ],
        out_specs=(VMEM,) * (3 * groups),
        scratch_shapes=[
            pltpu.VMEM((groups, rows, width), BF16),
            pltpu.VMEM((groups, rows, width), BF16),
            pltpu.SemaphoreType.DMA((2, groups)),
        ],
        compiler_params=params(16),
        cost_estimate=cost(2 * rows * features * N, 16 * rows * features),
        name="local",
    )(*in_hbm(doc_ids, x, gate, bmat, cmat, skip.reshape(1, heads)), ec, *xw)

    send = list(send)
    got = [[] for _ in range(groups)]
    def passed_on(g, stage, needed):
        return pl.pallas_call(
            functools.partial(chain_kernel, count, stage, g, heads),
            out_shape=state,
            in_specs=[VMEM] * (4 + len(needed)),
            out_specs=VMEM,
            compiler_params=params(6),
            cost_estimate=cost(16384 * N * width, 8 * N * width),
            name="chain",
        )(got[g][-1], f_parts[g], b_parts[g], dec[g], *needed)

    if count == 4:
        inward, outward, across = [(0, 1), (3, 2)], [(1, 0), (2, 3)], [(1, 2), (2, 1)]
        near = lax.ppermute(kv, "ctx", inward + outward)
        middle = lax.ppermute(kv, "ctx", across)
        middle, *local = lax.optimization_barrier((middle, *local))
        beyond = lax.ppermute(near, "ctx", across)
        send[-1] = pl.pallas_call(
            functools.partial(merge_kernel, count),
            out_shape=payload,
            in_specs=[VMEM] * 2,
            out_specs=VMEM,
            compiler_params=params(4),
            cost_estimate=cost(0, 4 * N * width),
            name="merge",
        )(send[-1], middle)
        far = lax.ppermute(send[-1], "ctx", inward + outward)
        got[-1].append(far)
        if groups > 1:
            got[0].append(lax.ppermute(send[0], "ctx", [(0, 1), (3, 2)]))
            send[0] = passed_on(0, 1, [near])
            beyond, _ = lax.optimization_barrier((beyond, send[0]))
            got[0].append(lax.ppermute(send[0], "ctx", across))
        farther = lax.ppermute(beyond, "ctx", outward)
        kv_got = [near, middle, beyond, far, farther]
    else:
        ring = ring_order(count)
        ring_pairs = [(ring[d], ring[(d + 1) % count]) for d in range(count)]
        kv_got = [kv]
        for _ in range(others):
            kv_got.append(lax.ppermute(kv_got[-1], "ctx", ring_pairs))
        kv_got = kv_got[1:]
    stack = 4 if per_kv % 4 == 0 and count <= 4 else 1
    targets = [
        pl.pallas_call(
            functools.partial(attention_kernel, count, per_kv, stack, g),
            out_shape=struct((rows, per_kv * DH), BF16),
            in_specs=[VMEM] * (4 + len(kv_got)),
            out_specs=VMEM,
            scratch_shapes=[
                pltpu.VMEM((2 * count * stretch, DH), BF16),
                pltpu.VMEM((2 * count * stretch, 2 * DH), BF16),
                pltpu.VMEM((stretch, stretch), F32),
                pltpu.VMEM((stretch, (count + 1) * stretch), F32),
                pltpu.VMEM((stretch, others * stretch), F32),
            ],
            compiler_params=params(24),
            cost_estimate=cost(
                4 * (2 * count + 1) * stretch * stretch * per_kv * DH, 8 * rows * per_kv * DH
            ),
            name="attention",
        )(doc_ids, queries[0], keys[0], values[0], *kv_got)
        for g in range(kv_dev)
    ]
    for r in range(1, count):
        for g in range(groups):
            if len(got[g]) >= r:
                continue
            if r == 3 and g == groups - 1:
                got[g][-1], targets[0] = lax.optimization_barrier((got[g][-1], targets[0]))
            if r > 1:
                if count == 4:
                    needed = [near] if r == 2 else [middle, beyond]
                else:
                    needed = kv_got
                send[g] = passed_on(g, r - 1, needed)
            pairs = [(r - 1, r), (count - r, count - r - 1)]
            got[g].append(lax.ppermute(send[g], "ctx", pairs))

    got[0][-1], *targets = lax.optimization_barrier((got[0][-1], *targets))
    normed, grads = [], None
    for g in range(groups):
        more = [] if grads is None else [grads]
        made, grads = pl.pallas_call(
            functools.partial(final_kernel, count, g, groups, loss_scale, heads),
            out_shape=(struct((rows, width), BF16), struct((groups + 1, width), F32)),
            in_specs=[VMEM] * (8 + others + len(kv_got) + len(more)),
            out_specs=(VMEM,) * 2,
            scratch_shapes=[
                pltpu.VMEM((N, width), BF16),
                pltpu.VMEM((N, width), BF16),
                pltpu.VMEM((rows, width), F32),
                pltpu.VMEM((rows, width), F32),
                pltpu.VMEM((rows, 3 * 128), F32),
                pltpu.VMEM((8, width), F32),
                pltpu.VMEM((8, width), F32),
            ],
            compiler_params=params(16),
            cost_estimate=cost(2 * rows * width * N, 20 * rows * width),
            name="final",
        )(
            *local[g::groups],
            cmat,
            targets[g],
            gain.reshape(1, features),
            f_parts[g],
            dec[g],
            *got[g],
            *kv_got,
            *more,
        )
        normed.append(made)
    teacher, student = write(*targets), write(*normed)
    shifts = [1 << k for k in reversed(range(count.bit_length() - 1))]
    partner = exchange(grads, shifts[0])
    if lax.axis_size("dp") == 2:
        grads = (grads + partner) + (exchange(grads, count) + exchange(grads, count + shifts[0]))
    else:
        grads = grads + partner
    for shift in shifts[1:-1]:
        grads = grads + exchange(grads, shift)
    grad_gain, grad_skip = pl.pallas_call(
        closing_kernel,
        out_shape=(struct((1, features), F32), struct((1, heads), F32)),
        in_specs=[VMEM] * 2,
        out_specs=(VMEM,) * 2,
        compiler_params=params(2),
        name="closing",
    )(grads, exchange(grads, shifts[-1]))
    return (teacher[None], student[None], grad_gain[0], grad_skip[0])


def solution(mesh):
    rows = P("dp", "ctx", "head")
    in_specs = (
        rows,
        rows,
        rows,
        P("dp", None),
        rows,
        rows,
        rows,
        rows,
        rows,
        P("head"),
        P("head"),
        P("head"),
        P("head"),
    )
    out_specs = (rows, rows, P("head"), P("head"))
    return jax.shard_map(body, mesh=mesh, in_specs=in_specs, out_specs=out_specs, check_vma=False)
```

```python
import functools
import math

import jax
import jax.numpy as jnp
from jax import lax
from jax.experimental import pallas as pl
from jax.experimental.pallas import tpu as pltpu
from jax.sharding import PartitionSpec as P

DH = 128
P_SIZE = 64
N = 128
EXTRA = 16
EPS = 1e-05
MASKED = -1e30
F32 = jnp.float32
BF16 = jnp.bfloat16
VMEM = pl.BlockSpec(memory_space=pltpu.VMEM)


def params(mib):
    return pltpu.CompilerParams(vmem_limit_bytes=mib << 20)


def cost(flops, size):
    return pl.CostEstimate(flops=flops, bytes_accessed=size, transcendentals=0)


def parts(v):
    hi = v.astype(BF16)
    return hi, (v - hi.astype(F32)).astype(BF16)


def spread_matrix(heads, width, first):
    row = lax.broadcasted_iota(jnp.int32, (heads, width), 0)
    lane = lax.broadcasted_iota(jnp.int32, (heads, width), 1)
    return jnp.where(row == (lane // P_SIZE) + first, 1.0, 0.0).astype(BF16)


def dot_nt(a, b):
    return lax.dot_general(a, b, (((1,), (1,)), ((), ())), preferred_element_type=F32)


def dot_tn(a, b):
    return lax.dot_general(a, b, (((0,), (0,)), ((), ())), preferred_element_type=F32)


def spread(v, matrix):
    return dot_tn(jnp.concatenate(parts(v), axis=0), jnp.concatenate([matrix, matrix], axis=0))


def doc_row(docs_ref, block, stretch):
    return docs_ref[:, pl.ds(pl.multiple_of(block * stretch, stretch), stretch)]


def as_column(row):
    size = row.shape[1]
    r = lax.broadcasted_iota(jnp.int32, (size, size), 0)
    c = lax.broadcasted_iota(jnp.int32, (size, size), 1)
    return jnp.sum(jnp.where(r == c, row.astype(F32), 0.0), axis=1, keepdims=True)


def lower_triangle(size):
    r = lax.broadcasted_iota(jnp.int32, (size, size), 0)
    c = lax.broadcasted_iota(jnp.int32, (size, size), 1)
    return r >= c


def prior_doc(docs_ref, block, stretch):
    before = doc_row(docs_ref, jnp.maximum(block - 1, 0), stretch)[:, stretch - 1 :]
    return jnp.where(block > 0, before, -1)


def own_block(index, count, half):
    return index if half == 0 else 2 * count - 1 - index


def ring_order(count):
    return [0] + list(range(1, count, 2)) + list(range(2, count, 2))[::-1]


def ring_source(index, count, steps):
    order = ring_order(count)
    source = jnp.int32(0)
    for place, member in enumerate(order):
        source = jnp.where(index == member, order[(place - steps) % count], source)
    return source


def passed_decay(ref, first, heads, width, g):
    matrix = spread_matrix(heads, width, g * (width // P_SIZE))
    wide = jnp.dot(ref[first : first + EXTRA, :heads], matrix, preferred_element_type=F32)
    return wide[0:1] + wide[1:2]


def opening_kernel(
    count,
    groups,
    docs_ref,
    k_ref,
    v_ref,
    x_ref,
    b_ref,
    dt_ref,
    bias_ref,
    log_ref,
    kv_ref,
    ec_ref,
    *outs,
):
    xw_refs, dec_refs, f_refs, b_refs, send_refs = (
        outs[k * groups : (k + 1) * groups] for k in range(5)
    )
    heads, rows = dt_ref.shape
    stretch = rows // 2
    width = x_ref.shape[1] // groups
    kv_width = k_ref.shape[1]
    index = lax.axis_index("ctx")
    kv_ref[:rows, :kv_width] = k_ref[...]
    kv_ref[:rows, kv_width:] = v_ref[...]
    kv_ref[rows:, :] = jnp.zeros((EXTRA, 2 * kv_width), BF16)
    triangle = jnp.where(lower_triangle(stretch), 1.0, 0.0)
    slope = jnp.exp(as_column(log_ref[...]))
    bias = as_column(bias_ref[...])
    lane = lax.broadcasted_iota(jnp.int32, (heads, 8), 1)
    ends = jnp.zeros((heads, 8), F32)
    loads = []
    projs = []
    for half in range(2):
        block = own_block(index, count, half)
        sl = slice(half * stretch, (half + 1) * stretch)
        raw = dt_ref[:, sl] + bias
        dt = jnp.maximum(raw, 0.0) + jnp.log1p(jnp.exp(-jnp.abs(raw)))
        cum = lax.dot_general(
            -dt * slope,
            triangle,
            (((1,), (1,)), ((), ())),
            precision=lax.Precision.HIGHEST,
            preferred_element_type=F32,
        )
        ec_ref[:, sl] = jnp.exp(cum)
        loads.append(jnp.exp(-cum) * dt)
        final = jnp.exp(cum[:, stretch - 1 :])
        row = doc_row(docs_ref, block, stretch)
        last = row[:, stretch - 1 :]
        kept = jnp.where(last == prior_doc(docs_ref, block, stretch), 1.0, 0.0)
        ends = jnp.where(lane == half, final * kept, ends)
        ends = jnp.where(lane == 2 + half, final, ends)
        same = jnp.where(as_column(row) == last.astype(F32), 1.0, 0.0)
        projs.append((b_ref[sl, :].astype(F32) * same).astype(BF16))
    both = ends[:, 0:1] * ends[:, 1:2]
    r = lax.broadcasted_iota(jnp.int32, (heads, heads), 0)
    c = lax.broadcasted_iota(jnp.int32, (heads, heads), 1)
    hi, lo = parts(jnp.sum(jnp.where(r == c, both, 0.0), axis=0, keepdims=True))
    kv_ref[rows:, :heads] = jnp.concatenate(
        [hi, lo, jnp.zeros((EXTRA - 2, heads), BF16)], axis=0
    )
    for g in range(groups):
        cols = slice(g * width, (g + 1) * width)
        matrix = spread_matrix(heads, width, g * (heads // groups))
        wide = spread(ends, matrix)
        dec_refs[g][...] = wide
        sums = []
        for half in range(2):
            sl = slice(half * stretch, (half + 1) * stretch)
            xw = (x_ref[sl, cols].astype(F32) * spread(loads[half], matrix)).astype(BF16)
            xw_refs[g][sl, :] = xw
            sums.append(dot_tn(projs[half][:, g * N : (g + 1) * N], xw) * wide[2 + half : 3 + half])
        f_refs[g][...] = sums[0].astype(BF16)
        b_refs[g][...] = sums[1].astype(BF16)

        @pl.when(index == 0)
        def _():
            send_refs[g][...] = sums[0].astype(BF16)

        @pl.when(index != 0)
        def _():
            send_refs[g][...] = (wide[1:2] * sums[0] + sums[1]).astype(BF16)


def chain_kernel(count, stage, g, heads, got_ref, f_ref, b_ref, dec_ref, *refs):
    send_ref = refs[-1]
    width = f_ref.shape[1]
    index = lax.axis_index("ctx")

    @pl.when(index == stage)
    def _():
        state = dec_ref[0:1, :] * got_ref[:N, :].astype(F32) + f_ref[...].astype(F32)
        send_ref[...] = state.astype(BF16)

    @pl.when(index == count - 1 - stage)
    def _():
        decay = jnp.ones((1, width), F32)
        for r, ref in enumerate(refs[:-1]):
            one = passed_decay(ref, ref.shape[0] - EXTRA, heads, width, g)
            if count != 4:
                one = jnp.where(ring_source(index, count, r + 1) > index, one, 1.0)
            decay = decay * one
        inner = decay * f_ref[...].astype(F32) + got_ref[:N, :].astype(F32)
        send_ref[...] = (dec_ref[1:2, :] * inner + b_ref[...].astype(F32)).astype(BF16)


def local_kernel(
    count, groups, docs_ref, x_ref, gate_ref, b_ref, c_ref, skip_ref, ec_ref, *refs
):
    xw_refs, pre_refs, reach_refs, sx_refs = (
        refs[k * groups : (k + 1) * groups] for k in range(4)
    )
    x_here, gate_here, sems = refs[4 * groups :]
    heads, rows = ec_ref.shape
    stretch = rows // 2
    width = x_ref.shape[1] // groups
    index = lax.axis_index("ctx")
    moves = []
    for g in range(groups):
        cols = pl.ds(g * width, width)
        moves.append(
            [
                pltpu.make_async_copy(x_ref.at[:, cols], x_here.at[g], sems.at[0, g]),
                pltpu.make_async_copy(gate_ref.at[:, cols], gate_here.at[g], sems.at[1, g]),
            ]
        )
        for move in moves[g]:
            move.start()
    triangle = lower_triangle(stretch)
    skip = as_column(skip_ref[...])
    step = 16
    masks = []
    for half in range(2):
        block = own_block(index, count, half)
        row = doc_row(docs_ref, block, stretch)
        column = as_column(row)
        reached = jnp.where(column == prior_doc(docs_ref, block, stretch).astype(F32), 1.0, 0.0)
        masks.append((triangle & (column == row.astype(F32)), reached))
    for g in range(groups):
        proj = slice(g * N, (g + 1) * N)
        matrix = spread_matrix(heads, width, g * (heads // groups))
        wide_skip = spread(skip, matrix)
        for half in range(2):
            sl = slice(half * stretch, (half + 1) * stretch)
            near, reached = masks[half]
            gram = dot_nt(c_ref[sl, proj], b_ref[sl, proj])
            gram = jnp.where(near, gram, 0.0).astype(BF16)
            wide = spread(ec_ref[:, sl], matrix)
            inner = jnp.dot(gram, xw_refs[g][sl, :], preferred_element_type=F32)
            if half == 0:
                for move in moves[g]:
                    move.wait()
            for k in range(0, stretch, step):
                at = slice(half * stretch + k, half * stretch + k + step)
                here = slice(k, k + step)
                x = x_here[g, at, :].astype(F32)
                gate = gate_here[g, at, :].astype(F32)
                silu = gate / (1.0 + jnp.exp(-gate))
                fade = wide[here] * silu
                sx = silu * x
                sx_refs[g][at, :] = sx
                pre_refs[g][at, :] = inner[here] * fade + wide_skip * sx
                reach_refs[g][at, :] = reached[here] * fade


def merge_kernel(count, state_ref, kv_ref, out_ref):
    index = lax.axis_index("ctx")
    outer = (index == 0) | (index == count - 1)
    wide = kv_ref.shape[1]
    rows = kv_ref.shape[0] - EXTRA
    stretch = rows // 2

    @pl.when(outer)
    def _():
        out_ref[:N, :] = state_ref[...]
        out_ref[N:, :] = jnp.zeros((EXTRA, out_ref.shape[1]), BF16)

    @pl.when(jnp.logical_not(outer))
    def _():
        out_ref[:stretch, :wide] = kv_ref[:stretch, :]
        out_ref[:stretch, wide:] = kv_ref[stretch:rows, :]
        out_ref[stretch:, :wide] = kv_ref[rows:, :]
        out_ref[stretch:, wide:] = jnp.zeros((EXTRA, wide), BF16)


def arrivals(index, count, refs):
    if count != 4:
        return [(ring_source(index, count, r + 1), [(None, refs[r])]) for r in range(count - 1)]
    near, own_of_middle, next_of_middle, far, farther = refs
    middle = (index == 1) | (index == 2)
    low = index < 2
    return [
        (index ^ 1, [(None, near)]),
        (
            jnp.where(low, 2, 1),
            [(middle, own_of_middle), (jnp.logical_not(middle), far)],
        ),
        (
            jnp.where(low, 3, 0),
            [(middle, next_of_middle), (jnp.logical_not(middle), farther)],
        ),
    ]


def attention_kernel(count, per, stack, g, docs_ref, q_ref, k_ref, v_ref, *refs):
    others = count - 1
    sent = 5 if count == 4 else others
    out_ref, kt, vt, bias_f, bias_b, bias_a = refs[-6:]
    rows = q_ref.shape[0]
    stretch = rows // 2
    index = lax.axis_index("ctx")
    last = 2 * count - 1
    kv_width = refs[0].shape[1] // 2
    row_f = doc_row(docs_ref, index, stretch).astype(F32)
    row_b = doc_row(docs_ref, last - index, stretch).astype(F32)
    col_f = as_column(row_f)
    col_b = as_column(row_b)
    triangle = lower_triangle(stretch)

    def tile(k):
        return slice(k * stretch, (k + 1) * stretch)

    bias_f[...] = jnp.where(triangle & (col_f == row_f), 0.0, MASKED)
    bias_b[:, tile(0)] = jnp.where(col_b == row_f, 0.0, MASKED)
    bias_b[:, tile(1)] = jnp.where(triangle & (col_b == row_b), 0.0, MASKED)
    vt[:, DH:] = jnp.ones((vt.shape[0], DH), BF16)
    here = slice(g * DH, (g + 1) * DH)
    kt[tile(0), :] = k_ref[:stretch, here]
    vt[tile(0), :DH] = v_ref[:stretch, here]
    kt[tile(count), :] = k_ref[stretch:, here]
    vt[tile(count), :DH] = v_ref[stretch:, here]
    lower = []
    for r, (source, places) in enumerate(arrivals(index, count, refs[:sent])):
        lower.append(source < index)
        for condition, ref in places:

            def fetch(ref=ref, r=r):
                folded = ref.shape[1] > 2 * kv_width
                gap = jnp.where(lower[r], 0, 2 * kv_width if folded else stretch)
                for table, first in ((kt, g * DH), (vt, kv_width + g * DH)):
                    front = ref[:stretch, first : first + DH]
                    if folded:
                        own = ref[:stretch, pl.ds(pl.multiple_of(first + gap, DH), DH)]
                    else:
                        own = ref[pl.ds(pl.multiple_of(gap, stretch), stretch), first : first + DH]
                    table[tile(1 + r), :DH] = own
                    table[tile(count + 1 + r), :DH] = front

            if condition is None:
                fetch()
            else:
                pl.when(condition)(fetch)
        key_f = doc_row(docs_ref, source, stretch).astype(F32)
        key_a = doc_row(docs_ref, jnp.where(lower[r], source, last - source), stretch).astype(F32)
        bias_b[:, tile(2 + r)] = jnp.where(col_b == key_f, 0.0, MASKED)
        bias_a[:, tile(r)] = jnp.where(jnp.where(lower[r], col_f, col_b) == key_a, 0.0, MASKED)

    factor = math.log2(math.e) / math.sqrt(DH)
    tall = stack * stretch
    half_keys = count * stretch

    def stacked(first, base):
        return jnp.concatenate(
            [
                q_ref[base : base + stretch, (g * per + first + j) * DH : (g * per + first + j + 1) * DH]
                for j in range(stack)
            ],
            axis=0,
        )

    def biased(score, bias):
        size = score.shape[1]
        return (score.reshape(stack, stretch, size) + bias[None]).reshape(tall, size)

    for first in range(0, per, stack):
        s_f = dot_nt(stacked(first, 0), kt[:half_keys, :])
        s_b = dot_nt(stacked(first, stretch), kt[...])
        t_f = biased(s_f[:, tile(0)], bias_f[...])
        t_b = [biased(s_b[:, tile(0)], bias_b[:, tile(0)])]
        for k in range(1, count + 1):
            t_b.append(biased(s_b[:, tile(count + k - 1)], bias_b[:, tile(k)]))
        t_a = []
        for r in range(others):
            score = jnp.where(lower[r], s_f[:, tile(1 + r)], s_b[:, tile(1 + r)])
            t_a.append(biased(score, bias_a[:, tile(r)]))
        best_f = t_f
        best_b = functools.reduce(jnp.maximum, t_b)
        for r in range(others):
            best_f = jnp.maximum(best_f, jnp.where(lower[r], t_a[r], MASKED))
            best_b = jnp.maximum(best_b, jnp.where(lower[r], MASKED, t_a[r]))
        top_f = jnp.max(best_f, axis=1, keepdims=True)
        top_b = jnp.max(best_b, axis=1, keepdims=True)
        w_f = [jnp.exp2((t_f - top_f) * factor).astype(BF16)]
        w_b = [jnp.exp2((t - top_b) * factor).astype(BF16) for t in t_b]
        w_x = []
        for r in range(others):
            top = jnp.where(lower[r], top_f, top_b)
            w = jnp.exp2((t_a[r] - top) * factor)
            w_f.append(jnp.where(lower[r], w, 0.0).astype(BF16))
            w_x.append(jnp.where(lower[r], 0.0, w).astype(BF16))
        w_b = w_b[:1] + w_x + w_b[1:]
        out_f = jnp.dot(
            jnp.concatenate(w_f, axis=1), vt[:half_keys, :], preferred_element_type=F32
        )
        out_b = jnp.dot(jnp.concatenate(w_b, axis=1), vt[...], preferred_element_type=F32)
        for half, out in enumerate((out_f, out_b)):
            result = (out[:, :DH] / out[:, DH:]).astype(BF16)
            for j in range(stack):
                cols = slice((first + j) * DH, (first + j + 1) * DH)
                out_ref[tile(half), cols] = result[tile(j)]


def final_kernel(
    count,
    g,
    groups,
    loss_scale,
    heads,
    pre_ref,
    reach_ref,
    sx_ref,
    c_ref,
    teacher_ref,
    gain_ref,
    f_ref,
    dec_ref,
    *refs,
):
    others = count - 1
    got = refs[:others]
    sent = 5 if count == 4 else others
    kv_refs = refs[others : others + sent]
    before = refs[others + sent] if g else None
    proj = slice(g * N, (g + 1) * N)
    first_lane = g * pre_ref.shape[1]
    out_ref, grad_ref, front, back, flow, gated_ref, sums, gain_acc, skip_acc = refs[-9:]
    rows, width = pre_ref.shape
    stretch = rows // 2
    index = lax.axis_index("ctx")
    tile = 128
    step = 16

    @pl.when(index == 0)
    def _():
        front[...] = jnp.zeros_like(front)

    @pl.when(index == count - 1)
    def _():
        back[...] = jnp.zeros_like(back)

    for r in range(1, count):

        @pl.when(index == r)
        def _():
            front[...] = got[r - 1][:N, :]

        @pl.when(index == count - 1 - r)
        def _():
            back[...] = got[r - 1][:N, :]

    sources, rows_in = [], []
    for source, places in arrivals(index, count, kv_refs):
        found = [ref[ref.shape[0] - EXTRA :, :heads].astype(F32) for _, ref in places]
        if len(found) == 2:
            found = [jnp.where(places[0][0], found[0], found[1])]
        sources.append(source)
        rows_in.append(found[0])
    spread_rows = spread_matrix(heads, width, g * (width // P_SIZE))
    wide = jnp.dot(
        jnp.concatenate(rows_in, axis=0).astype(BF16), spread_rows, preferred_element_type=F32
    )
    d_in = jnp.ones((1, width), F32)
    for r, source in enumerate(sources):
        one = wide[r * EXTRA : r * EXTRA + 1] + wide[r * EXTRA + 1 : r * EXTRA + 2]
        d_in = d_in * jnp.where(source > index, one, 1.0)
    through = dec_ref[0:1, :] * front[...].astype(F32) + f_ref[...].astype(F32)
    entering = (d_in * through + back[...].astype(F32)).astype(BF16)
    flow[:stretch, :] = jnp.dot(c_ref[:stretch, proj], front[...], preferred_element_type=F32)
    flow[stretch:, :] = jnp.dot(c_ref[stretch:, proj], entering, preferred_element_type=F32)
    gain_acc[...] = jnp.zeros_like(gain_acc)
    skip_acc[...] = jnp.zeros_like(skip_acc)

    @pl.loop(0, rows // step, unroll=2)
    def _(k):
        sl = pl.ds(pl.multiple_of(k * step, step), step)
        totals = [jnp.zeros((step, tile), F32)] * 3
        for j in range(0, width, tile):
            cols = slice(j, j + tile)
            gated = pre_ref[sl, cols] + reach_ref[sl, cols] * flow[sl, cols]
            gated_ref[sl, cols] = gated
            scaled = gated * gain_ref[:, first_lane + j : first_lane + j + tile]
            totals[0] += gated * gated
            totals[1] += scaled * scaled
            totals[2] += scaled * teacher_ref[sl, cols].astype(F32)
        for k3 in range(3):
            sums[sl, k3 * tile : (k3 + 1) * tile] = totals[k3]

    square, weighted, crossed = (
        jnp.sum(sums[:, k3 * tile : (k3 + 1) * tile], axis=1, keepdims=True) * (1.0 / width)
        for k3 in range(3)
    )
    scale = lax.rsqrt(square + EPS)
    push_scale = 2.0 * loss_scale
    mean = push_scale * scale * (scale * weighted - crossed)
    sums[:, :tile] = jnp.broadcast_to(scale, (rows, tile))
    sums[:, tile : 2 * tile] = jnp.broadcast_to(mean, (rows, tile))

    @pl.loop(0, rows // step, unroll=2)
    def _(k):
        sl = pl.ds(pl.multiple_of(k * step, step), step)
        scale = sums[sl, :tile]
        mean = sums[sl, tile : 2 * tile]
        for j in range(0, width, tile):
            cols = slice(j, j + tile)
            gain = gain_ref[:, first_lane + j : first_lane + j + tile]
            unit = gated_ref[sl, cols] * scale
            normed = unit * gain
            out_ref[sl, cols] = normed.astype(BF16)
            push = (normed - teacher_ref[sl, cols].astype(F32)) * push_scale
            by_gain = push * unit
            by_skip = (push * gain - unit * mean) * (scale * sx_ref[sl, cols])
            gain_acc[:, cols] += by_gain[:8] + by_gain[8:]
            skip_acc[:, cols] += by_skip[:8] + by_skip[8:]

    row = lax.broadcasted_iota(jnp.int32, (tile, width), 0)
    lane = lax.broadcasted_iota(jnp.int32, (tile, width), 1)
    matrix = jnp.where(row == lane // P_SIZE + g * (width // P_SIZE), 1.0, 0.0).astype(BF16)
    hi, lo = parts(skip_acc[...])
    by_head = jnp.sum(dot_nt(hi, matrix) + dot_nt(lo, matrix), axis=0, keepdims=True)
    grad_ref[...] = jnp.zeros_like(grad_ref)
    if g:
        grad_ref[:g, :] = before[:g, :]
        by_head += before[groups : groups + 1, :tile]
    grad_ref[g : g + 1, :] = jnp.sum(gain_acc[...], axis=0, keepdims=True)
    grad_ref[groups : groups + 1, :tile] = by_head


def writing_kernel(*refs):
    parts_in, out_ref, sems = refs[:-2], refs[-2], refs[-1]
    width = parts_in[0].shape[1]
    moves = [
        pltpu.make_async_copy(part, out_ref.at[:, pl.ds(k * width, width)], sems.at[k])
        for k, part in enumerate(parts_in)
    ]
    for move in moves:
        move.start()
    for move in moves:
        move.wait()


def closing_kernel(a_ref, b_ref, gain_ref, skip_ref):
    total = a_ref[...] + b_ref[...]
    groups, width = total.shape[0] - 1, total.shape[1]
    for g in range(groups):
        gain_ref[:, g * width : (g + 1) * width] = total[g : g + 1, :]
    skip_ref[...] = total[groups : groups + 1, : skip_ref.shape[1]]


def exchange(part, shift):
    axes = ("dp", "ctx")
    size = lax.axis_size(axes)
    return lax.ppermute(part, axes, [(d, d ^ shift) for d in range(size)])


def body(
    queries,
    keys,
    values,
    doc_ids,
    inputs,
    gate_input,
    b_input,
    c_input,
    dt_raw,
    dt_bias,
    decay_log,
    skip,
    gain,
):
    count = lax.axis_size("ctx")
    rows, features = queries.shape[1:]
    stretch = rows // 2
    kv_dev = keys.shape[2] // DH
    per_kv = queries.shape[2] // keys.shape[2]
    groups = b_input.shape[2] // N
    heads = features // P_SIZE
    width = features // groups
    length = doc_ids.shape[1]
    others = count - 1
    loss_scale = 1.0 / (lax.axis_size("dp") * count * rows)
    x, gate, bmat, cmat = inputs[0], gate_input[0], b_input[0], c_input[0]
    struct = jax.ShapeDtypeStruct

    def in_hbm(*arrays):
        return [pltpu.with_memory_space_constraint(array, pltpu.HBM) for array in arrays]

    def write(*pieces):
        return pl.pallas_call(
            writing_kernel,
            out_shape=struct((rows, features), BF16),
            in_specs=[VMEM] * len(pieces),
            out_specs=pl.BlockSpec(memory_space=pl.ANY),
            scratch_shapes=[pltpu.SemaphoreType.DMA((len(pieces),))],
            compiler_params=params(2),
            cost_estimate=cost(0, 4 * rows * features),
            name="writing",
        )(*pieces)

    state = struct((N, width), BF16)
    payload = struct((N + EXTRA, width), BF16)
    outs = pl.pallas_call(
        functools.partial(opening_kernel, count, groups),
        out_shape=(
            struct((rows + EXTRA, 2 * kv_dev * DH), BF16),
            struct((heads, rows), F32),
            *([struct((rows, width), BF16)] * groups),
            *([struct((8, width), F32)] * groups),
            *([state] * (2 * groups)),
            *([state] * groups),
        ),
        in_specs=[VMEM] * 8,
        out_specs=(VMEM,) * (2 + 5 * groups),
        compiler_params=params(16),
        cost_estimate=cost(4 * rows * features * N, 8 * rows * features),
        name="opening",
    )(
        *in_hbm(
            doc_ids,
            keys[0],
            values[0],
            x,
            bmat,
            dt_raw[0].T,
            dt_bias.reshape(1, heads),
            decay_log.reshape(1, heads),
        )
    )
    kv, ec = outs[:2]
    xw, dec, f_parts, b_parts, send = (
        outs[2 + k * groups : 2 + (k + 1) * groups] for k in range(5)
    )

    local = pl.pallas_call(
        functools.partial(local_kernel, count, groups),
        out_shape=(struct((rows, width), F32),) * (3 * groups),
        in_specs=[
            VMEM,
            *[pl.BlockSpec(memory_space=pl.ANY)] * 2,
            *[VMEM] * (4 + groups),
        ],
        out_specs=(VMEM,) * (3 * groups),
        scratch_shapes=[
            pltpu.VMEM((groups, rows, width), BF16),
            pltpu.VMEM((groups, rows, width), BF16),
            pltpu.SemaphoreType.DMA((2, groups)),
        ],
        compiler_params=params(16),
        cost_estimate=cost(2 * rows * features * N, 16 * rows * features),
        name="local",
    )(*in_hbm(doc_ids, x, gate, bmat, cmat, skip.reshape(1, heads)), ec, *xw)

    send = list(send)
    got = [[] for _ in range(groups)]
    def passed_on(g, stage, needed):
        return pl.pallas_call(
            functools.partial(chain_kernel, count, stage, g, heads),
            out_shape=state,
            in_specs=[VMEM] * (4 + len(needed)),
            out_specs=VMEM,
            compiler_params=params(6),
            cost_estimate=cost(16384 * N * width, 8 * N * width),
            name="chain",
        )(got[g][-1], f_parts[g], b_parts[g], dec[g], *needed)

    if count == 4:
        inward, outward, across = [(0, 1), (3, 2)], [(1, 0), (2, 3)], [(1, 2), (2, 1)]
        near = lax.ppermute(kv, "ctx", inward + outward)
        middle = lax.ppermute(kv, "ctx", across)
        middle, *local = lax.optimization_barrier((middle, *local))
        beyond = lax.ppermute(near, "ctx", across)
        send[-1] = pl.pallas_call(
            functools.partial(merge_kernel, count),
            out_shape=payload,
            in_specs=[VMEM] * 2,
            out_specs=VMEM,
            compiler_params=params(4),
            cost_estimate=cost(0, 4 * N * width),
            name="merge",
        )(send[-1], middle)
        far = lax.ppermute(send[-1], "ctx", inward + outward)
        got[-1].append(far)
        if groups > 1:
            got[0].append(lax.ppermute(send[0], "ctx", [(0, 1), (3, 2)]))
            send[0] = passed_on(0, 1, [near])
            beyond, _ = lax.optimization_barrier((beyond, send[0]))
            got[0].append(lax.ppermute(send[0], "ctx", across))
        farther = lax.ppermute(beyond, "ctx", outward)
        kv_got = [near, middle, beyond, far, farther]
    else:
        ring = ring_order(count)
        ring_pairs = [(ring[d], ring[(d + 1) % count]) for d in range(count)]
        kv_got = [kv]
        for _ in range(others):
            kv_got.append(lax.ppermute(kv_got[-1], "ctx", ring_pairs))
        kv_got = kv_got[1:]
    stack = 4 if per_kv % 4 == 0 and count <= 4 else 1
    targets = [
        pl.pallas_call(
            functools.partial(attention_kernel, count, per_kv, stack, g),
            out_shape=struct((rows, per_kv * DH), BF16),
            in_specs=[VMEM] * (4 + len(kv_got)),
            out_specs=VMEM,
            scratch_shapes=[
                pltpu.VMEM((2 * count * stretch, DH), BF16),
                pltpu.VMEM((2 * count * stretch, 2 * DH), BF16),
                pltpu.VMEM((stretch, stretch), F32),
                pltpu.VMEM((stretch, (count + 1) * stretch), F32),
                pltpu.VMEM((stretch, others * stretch), F32),
            ],
            compiler_params=params(24),
            cost_estimate=cost(
                4 * (2 * count + 1) * stretch * stretch * per_kv * DH, 8 * rows * per_kv * DH
            ),
            name="attention",
        )(doc_ids, queries[0], keys[0], values[0], *kv_got)
        for g in range(kv_dev)
    ]
    for r in range(1, count):
        for g in range(groups):
            if len(got[g]) >= r:
                continue
            if r == 3 and g == groups - 1:
                got[g][-1], targets[0] = lax.optimization_barrier((got[g][-1], targets[0]))
            if r > 1:
                if count == 4:
                    needed = [near] if r == 2 else [middle, beyond]
                else:
                    needed = kv_got
                send[g] = passed_on(g, r - 1, needed)
            pairs = [(r - 1, r), (count - r, count - r - 1)]
            got[g].append(lax.ppermute(send[g], "ctx", pairs))

    got[0][-1], *targets = lax.optimization_barrier((got[0][-1], *targets))
    normed, grads = [], None
    for g in range(groups):
        more = [] if grads is None else [grads]
        made, grads = pl.pallas_call(
            functools.partial(final_kernel, count, g, groups, loss_scale, heads),
            out_shape=(struct((rows, width), BF16), struct((groups + 1, width), F32)),
            in_specs=[VMEM] * (8 + others + len(kv_got) + len(more)),
            out_specs=(VMEM,) * 2,
            scratch_shapes=[
                pltpu.VMEM((N, width), BF16),
                pltpu.VMEM((N, width), BF16),
                pltpu.VMEM((rows, width), F32),
                pltpu.VMEM((rows, width), F32),
                pltpu.VMEM((rows, 3 * 128), F32),
                pltpu.VMEM((8, width), F32),
                pltpu.VMEM((8, width), F32),
            ],
            compiler_params=params(16),
            cost_estimate=cost(2 * rows * width * N, 20 * rows * width),
            name="final",
        )(
            *local[g::groups],
            cmat,
            targets[g],
            gain.reshape(1, features),
            f_parts[g],
            dec[g],
            *got[g],
            *kv_got,
            *more,
        )
        normed.append(made)
    teacher, student = write(*targets), write(*normed)
    shifts = [1 << k for k in range(count.bit_length() - 1)]
    partner = exchange(grads, shifts[0])
    if lax.axis_size("dp") == 2:
        grads = (grads + partner) + (exchange(grads, count) + exchange(grads, count + shifts[0]))
    else:
        grads = grads + partner
    for shift in shifts[1:-1]:
        grads = grads + exchange(grads, shift)
    grad_gain, grad_skip = pl.pallas_call(
        closing_kernel,
        out_shape=(struct((1, features), F32), struct((1, heads), F32)),
        in_specs=[VMEM] * 2,
        out_specs=(VMEM,) * 2,
        compiler_params=params(2),
        name="closing",
    )(grads, exchange(grads, shifts[-1]))
    return (teacher[None], student[None], grad_gain[0], grad_skip[0])


def solution(mesh):
    rows = P("dp", "ctx", "head")
    in_specs = (
        rows,
        rows,
        rows,
        P("dp", None),
        rows,
        rows,
        rows,
        rows,
        rows,
        P("head"),
        P("head"),
        P("head"),
        P("head"),
    )
    out_specs = (rows, rows, P("head"), P("head"))
    return jax.shard_map(body, mesh=mesh, in_specs=in_specs, out_specs=out_specs, check_vma=False)
```

```python
import functools
import math

import jax
import jax.numpy as jnp
from jax import lax
from jax.experimental import pallas as pl
from jax.experimental.pallas import tpu as pltpu
from jax.sharding import PartitionSpec as P

DH = 128
P_SIZE = 64
N = 128
EXTRA = 16
EPS = 1e-05
MASKED = -1e30
F32 = jnp.float32
BF16 = jnp.bfloat16
VMEM = pl.BlockSpec(memory_space=pltpu.VMEM)


def params(mib):
    return pltpu.CompilerParams(vmem_limit_bytes=mib << 20)


def cost(flops, size):
    return pl.CostEstimate(flops=flops, bytes_accessed=size, transcendentals=0)


def parts(v):
    hi = v.astype(BF16)
    return hi, (v - hi.astype(F32)).astype(BF16)


def spread_matrix(heads, width, first):
    row = lax.broadcasted_iota(jnp.int32, (heads, width), 0)
    lane = lax.broadcasted_iota(jnp.int32, (heads, width), 1)
    return jnp.where(row == (lane // P_SIZE) + first, 1.0, 0.0).astype(BF16)


def dot_nt(a, b):
    return lax.dot_general(a, b, (((1,), (1,)), ((), ())), preferred_element_type=F32)


def dot_tn(a, b):
    return lax.dot_general(a, b, (((0,), (0,)), ((), ())), preferred_element_type=F32)


def spread(v, matrix):
    return dot_tn(jnp.concatenate(parts(v), axis=0), jnp.concatenate([matrix, matrix], axis=0))


def doc_row(docs_ref, block, stretch):
    return docs_ref[:, pl.ds(pl.multiple_of(block * stretch, stretch), stretch)]


def as_column(row):
    size = row.shape[1]
    r = lax.broadcasted_iota(jnp.int32, (size, size), 0)
    c = lax.broadcasted_iota(jnp.int32, (size, size), 1)
    return jnp.sum(jnp.where(r == c, row.astype(F32), 0.0), axis=1, keepdims=True)


def lower_triangle(size):
    r = lax.broadcasted_iota(jnp.int32, (size, size), 0)
    c = lax.broadcasted_iota(jnp.int32, (size, size), 1)
    return r >= c


def prior_doc(docs_ref, block, stretch):
    before = doc_row(docs_ref, jnp.maximum(block - 1, 0), stretch)[:, stretch - 1 :]
    return jnp.where(block > 0, before, -1)


def own_block(index, count, half):
    return index if half == 0 else 2 * count - 1 - index


def ring_order(count):
    return [0] + list(range(1, count, 2)) + list(range(2, count, 2))[::-1]


def ring_source(index, count, steps):
    order = ring_order(count)
    source = jnp.int32(0)
    for place, member in enumerate(order):
        source = jnp.where(index == member, order[(place - steps) % count], source)
    return source


def passed_decay(ref, first, heads, width, g):
    matrix = spread_matrix(heads, width, g * (width // P_SIZE))
    wide = jnp.dot(ref[first : first + EXTRA, :heads], matrix, preferred_element_type=F32)
    return wide[0:1] + wide[1:2]


def opening_kernel(
    count,
    groups,
    docs_ref,
    k_ref,
    v_ref,
    x_ref,
    b_ref,
    dt_ref,
    bias_ref,
    log_ref,
    kv_ref,
    ec_ref,
    *outs,
):
    xw_refs, dec_refs, f_refs, b_refs, send_refs = (
        outs[k * groups : (k + 1) * groups] for k in range(5)
    )
    heads, rows = dt_ref.shape
    stretch = rows // 2
    width = x_ref.shape[1] // groups
    kv_width = k_ref.shape[1]
    index = lax.axis_index("ctx")
    kv_ref[:rows, :kv_width] = k_ref[...]
    kv_ref[:rows, kv_width:] = v_ref[...]
    kv_ref[rows:, :] = jnp.zeros((EXTRA, 2 * kv_width), BF16)
    triangle = jnp.where(lower_triangle(stretch), 1.0, 0.0)
    slope = jnp.exp(as_column(log_ref[...]))
    bias = as_column(bias_ref[...])
    lane = lax.broadcasted_iota(jnp.int32, (heads, 8), 1)
    ends = jnp.zeros((heads, 8), F32)
    loads = []
    projs = []
    for half in range(2):
        block = own_block(index, count, half)
        sl = slice(half * stretch, (half + 1) * stretch)
        raw = dt_ref[:, sl] + bias
        dt = jnp.maximum(raw, 0.0) + jnp.log1p(jnp.exp(-jnp.abs(raw)))
        cum = lax.dot_general(
            -dt * slope,
            triangle,
            (((1,), (1,)), ((), ())),
            precision=lax.Precision.HIGHEST,
            preferred_element_type=F32,
        )
        ec_ref[:, sl] = jnp.exp(cum)
        loads.append(jnp.exp(-cum) * dt)
        final = jnp.exp(cum[:, stretch - 1 :])
        row = doc_row(docs_ref, block, stretch)
        last = row[:, stretch - 1 :]
        kept = jnp.where(last == prior_doc(docs_ref, block, stretch), 1.0, 0.0)
        ends = jnp.where(lane == half, final * kept, ends)
        ends = jnp.where(lane == 2 + half, final, ends)
        same = jnp.where(as_column(row) == last.astype(F32), 1.0, 0.0)
        projs.append((b_ref[sl, :].astype(F32) * same).astype(BF16))
    both = ends[:, 0:1] * ends[:, 1:2]
    r = lax.broadcasted_iota(jnp.int32, (heads, heads), 0)
    c = lax.broadcasted_iota(jnp.int32, (heads, heads), 1)
    hi, lo = parts(jnp.sum(jnp.where(r == c, both, 0.0), axis=0, keepdims=True))
    kv_ref[rows:, :heads] = jnp.concatenate(
        [hi, lo, jnp.zeros((EXTRA - 2, heads), BF16)], axis=0
    )
    for g in range(groups):
        cols = slice(g * width, (g + 1) * width)
        matrix = spread_matrix(heads, width, g * (heads // groups))
        wide = spread(ends, matrix)
        dec_refs[g][...] = wide
        sums = []
        for half in range(2):
            sl = slice(half * stretch, (half + 1) * stretch)
            xw = (x_ref[sl, cols].astype(F32) * spread(loads[half], matrix)).astype(BF16)
            xw_refs[g][sl, :] = xw
            sums.append(dot_tn(projs[half][:, g * N : (g + 1) * N], xw) * wide[2 + half : 3 + half])
        f_refs[g][...] = sums[0].astype(BF16)
        b_refs[g][...] = sums[1].astype(BF16)

        @pl.when(index == 0)
        def _():
            send_refs[g][...] = sums[0].astype(BF16)

        @pl.when(index != 0)
        def _():
            send_refs[g][...] = (wide[1:2] * sums[0] + sums[1]).astype(BF16)


def chain_kernel(count, stage, g, heads, got_ref, f_ref, b_ref, dec_ref, *refs):
    send_ref = refs[-1]
    width = f_ref.shape[1]
    index = lax.axis_index("ctx")

    @pl.when(index == stage)
    def _():
        state = dec_ref[0:1, :] * got_ref[:N, :].astype(F32) + f_ref[...].astype(F32)
        send_ref[...] = state.astype(BF16)

    @pl.when(index == count - 1 - stage)
    def _():
        decay = jnp.ones((1, width), F32)
        for r, ref in enumerate(refs[:-1]):
            one = passed_decay(ref, ref.shape[0] - EXTRA, heads, width, g)
            if count != 4:
                one = jnp.where(ring_source(index, count, r + 1) > index, one, 1.0)
            decay = decay * one
        inner = decay * f_ref[...].astype(F32) + got_ref[:N, :].astype(F32)
        send_ref[...] = (dec_ref[1:2, :] * inner + b_ref[...].astype(F32)).astype(BF16)


def local_kernel(
    count, groups, docs_ref, x_ref, gate_ref, b_ref, c_ref, skip_ref, ec_ref, *refs
):
    xw_refs, pre_refs, reach_refs, sx_refs = (
        refs[k * groups : (k + 1) * groups] for k in range(4)
    )
    x_here, gate_here, sems = refs[4 * groups :]
    heads, rows = ec_ref.shape
    stretch = rows // 2
    width = x_ref.shape[1] // groups
    index = lax.axis_index("ctx")
    moves = []
    for g in range(groups):
        cols = pl.ds(g * width, width)
        moves.append(
            [
                pltpu.make_async_copy(x_ref.at[:, cols], x_here.at[g], sems.at[0, g]),
                pltpu.make_async_copy(gate_ref.at[:, cols], gate_here.at[g], sems.at[1, g]),
            ]
        )
        for move in moves[g]:
            move.start()
    triangle = lower_triangle(stretch)
    skip = as_column(skip_ref[...])
    step = 16
    masks = []
    for half in range(2):
        block = own_block(index, count, half)
        row = doc_row(docs_ref, block, stretch)
        column = as_column(row)
        reached = jnp.where(column == prior_doc(docs_ref, block, stretch).astype(F32), 1.0, 0.0)
        masks.append((triangle & (column == row.astype(F32)), reached))
    for g in range(groups):
        proj = slice(g * N, (g + 1) * N)
        matrix = spread_matrix(heads, width, g * (heads // groups))
        wide_skip = spread(skip, matrix)
        for half in range(2):
            sl = slice(half * stretch, (half + 1) * stretch)
            near, reached = masks[half]
            gram = dot_nt(c_ref[sl, proj], b_ref[sl, proj])
            gram = jnp.where(near, gram, 0.0).astype(BF16)
            wide = spread(ec_ref[:, sl], matrix)
            inner = jnp.dot(gram, xw_refs[g][sl, :], preferred_element_type=F32)
            if half == 0:
                for move in moves[g]:
                    move.wait()
            for k in range(0, stretch, step):
                at = slice(half * stretch + k, half * stretch + k + step)
                here = slice(k, k + step)
                x = x_here[g, at, :].astype(F32)
                gate = gate_here[g, at, :].astype(F32)
                silu = gate / (1.0 + jnp.exp(-gate))
                fade = wide[here] * silu
                sx = silu * x
                sx_refs[g][at, :] = sx
                pre_refs[g][at, :] = inner[here] * fade + wide_skip * sx
                reach_refs[g][at, :] = reached[here] * fade


def merge_kernel(count, state_ref, kv_ref, out_ref):
    index = lax.axis_index("ctx")
    outer = (index == 0) | (index == count - 1)
    wide = kv_ref.shape[1]
    rows = kv_ref.shape[0] - EXTRA
    stretch = rows // 2

    @pl.when(outer)
    def _():
        out_ref[:N, :] = state_ref[...]
        out_ref[N:, :] = jnp.zeros((EXTRA, out_ref.shape[1]), BF16)

    @pl.when(jnp.logical_not(outer))
    def _():
        out_ref[:stretch, :wide] = kv_ref[:stretch, :]
        out_ref[:stretch, wide:] = kv_ref[stretch:rows, :]
        out_ref[stretch:, :wide] = kv_ref[rows:, :]
        out_ref[stretch:, wide:] = jnp.zeros((EXTRA, wide), BF16)


def arrivals(index, count, refs):
    if count != 4:
        return [(ring_source(index, count, r + 1), [(None, refs[r])]) for r in range(count - 1)]
    near, own_of_middle, next_of_middle, far, farther = refs
    middle = (index == 1) | (index == 2)
    low = index < 2
    return [
        (index ^ 1, [(None, near)]),
        (
            jnp.where(low, 2, 1),
            [(middle, own_of_middle), (jnp.logical_not(middle), far)],
        ),
        (
            jnp.where(low, 3, 0),
            [(middle, next_of_middle), (jnp.logical_not(middle), farther)],
        ),
    ]


def attention_kernel(count, per, stack, g, docs_ref, q_ref, k_ref, v_ref, *refs):
    others = count - 1
    sent = 5 if count == 4 else others
    out_ref, kt, vt, bias_f, bias_b, bias_a = refs[-6:]
    rows = q_ref.shape[0]
    stretch = rows // 2
    index = lax.axis_index("ctx")
    last = 2 * count - 1
    kv_width = refs[0].shape[1] // 2
    row_f = doc_row(docs_ref, index, stretch).astype(F32)
    row_b = doc_row(docs_ref, last - index, stretch).astype(F32)
    col_f = as_column(row_f)
    col_b = as_column(row_b)
    triangle = lower_triangle(stretch)

    def tile(k):
        return slice(k * stretch, (k + 1) * stretch)

    bias_f[...] = jnp.where(triangle & (col_f == row_f), 0.0, MASKED)
    bias_b[:, tile(0)] = jnp.where(col_b == row_f, 0.0, MASKED)
    bias_b[:, tile(1)] = jnp.where(triangle & (col_b == row_b), 0.0, MASKED)
    vt[:, DH:] = jnp.ones((vt.shape[0], DH), BF16)
    here = slice(g * DH, (g + 1) * DH)
    kt[tile(0), :] = k_ref[:stretch, here]
    vt[tile(0), :DH] = v_ref[:stretch, here]
    kt[tile(count), :] = k_ref[stretch:, here]
    vt[tile(count), :DH] = v_ref[stretch:, here]
    lower = []
    for r, (source, places) in enumerate(arrivals(index, count, refs[:sent])):
        lower.append(source < index)
        for condition, ref in places:

            def fetch(ref=ref, r=r):
                folded = ref.shape[1] > 2 * kv_width
                gap = jnp.where(lower[r], 0, 2 * kv_width if folded else stretch)
                for table, first in ((kt, g * DH), (vt, kv_width + g * DH)):
                    front = ref[:stretch, first : first + DH]
                    if folded:
                        own = ref[:stretch, pl.ds(pl.multiple_of(first + gap, DH), DH)]
                    else:
                        own = ref[pl.ds(pl.multiple_of(gap, stretch), stretch), first : first + DH]
                    table[tile(1 + r), :DH] = own
                    table[tile(count + 1 + r), :DH] = front

            if condition is None:
                fetch()
            else:
                pl.when(condition)(fetch)
        key_f = doc_row(docs_ref, source, stretch).astype(F32)
        key_a = doc_row(docs_ref, jnp.where(lower[r], source, last - source), stretch).astype(F32)
        bias_b[:, tile(2 + r)] = jnp.where(col_b == key_f, 0.0, MASKED)
        bias_a[:, tile(r)] = jnp.where(jnp.where(lower[r], col_f, col_b) == key_a, 0.0, MASKED)

    factor = math.log2(math.e) / math.sqrt(DH)
    tall = stack * stretch
    half_keys = count * stretch

    def stacked(first, base):
        return jnp.concatenate(
            [
                q_ref[base : base + stretch, (g * per + first + j) * DH : (g * per + first + j + 1) * DH]
                for j in range(stack)
            ],
            axis=0,
        )

    def biased(score, bias):
        size = score.shape[1]
        return (score.reshape(stack, stretch, size) + bias[None]).reshape(tall, size)

    for first in range(0, per, stack):
        s_f = dot_nt(stacked(first, 0), kt[:half_keys, :])
        s_b = dot_nt(stacked(first, stretch), kt[...])
        t_f = biased(s_f[:, tile(0)], bias_f[...])
        t_b = [biased(s_b[:, tile(0)], bias_b[:, tile(0)])]
        for k in range(1, count + 1):
            t_b.append(biased(s_b[:, tile(count + k - 1)], bias_b[:, tile(k)]))
        t_a = []
        for r in range(others):
            score = jnp.where(lower[r], s_f[:, tile(1 + r)], s_b[:, tile(1 + r)])
            t_a.append(biased(score, bias_a[:, tile(r)]))
        best_f = t_f
        best_b = functools.reduce(jnp.maximum, t_b)
        for r in range(others):
            best_f = jnp.maximum(best_f, jnp.where(lower[r], t_a[r], MASKED))
            best_b = jnp.maximum(best_b, jnp.where(lower[r], MASKED, t_a[r]))
        top_f = jnp.max(best_f, axis=1, keepdims=True)
        top_b = jnp.max(best_b, axis=1, keepdims=True)
        w_f = [jnp.exp2((t_f - top_f) * factor).astype(BF16)]
        w_b = [jnp.exp2((t - top_b) * factor).astype(BF16) for t in t_b]
        w_x = []
        for r in range(others):
            top = jnp.where(lower[r], top_f, top_b)
            w = jnp.exp2((t_a[r] - top) * factor)
            w_f.append(jnp.where(lower[r], w, 0.0).astype(BF16))
            w_x.append(jnp.where(lower[r], 0.0, w).astype(BF16))
        w_b = w_b[:1] + w_x + w_b[1:]
        out_f = jnp.dot(
            jnp.concatenate(w_f, axis=1), vt[:half_keys, :], preferred_element_type=F32
        )
        out_b = jnp.dot(jnp.concatenate(w_b, axis=1), vt[...], preferred_element_type=F32)
        for half, out in enumerate((out_f, out_b)):
            result = (out[:, :DH] / out[:, DH:]).astype(BF16)
            for j in range(stack):
                cols = slice((first + j) * DH, (first + j + 1) * DH)
                out_ref[tile(half), cols] = result[tile(j)]


def final_kernel(
    count,
    g,
    groups,
    loss_scale,
    heads,
    pre_ref,
    reach_ref,
    sx_ref,
    c_ref,
    teacher_ref,
    gain_ref,
    f_ref,
    dec_ref,
    *refs,
):
    others = count - 1
    got = refs[:others]
    sent = 5 if count == 4 else others
    kv_refs = refs[others : others + sent]
    before = refs[others + sent] if g else None
    proj = slice(g * N, (g + 1) * N)
    first_lane = g * pre_ref.shape[1]
    out_ref, grad_ref, front, back, flow, gated_ref, sums, gain_acc, skip_acc = refs[-9:]
    rows, width = pre_ref.shape
    stretch = rows // 2
    index = lax.axis_index("ctx")
    tile = 128
    step = 16

    @pl.when(index == 0)
    def _():
        front[...] = jnp.zeros_like(front)

    @pl.when(index == count - 1)
    def _():
        back[...] = jnp.zeros_like(back)

    for r in range(1, count):

        @pl.when(index == r)
        def _():
            front[...] = got[r - 1][:N, :]

        @pl.when(index == count - 1 - r)
        def _():
            back[...] = got[r - 1][:N, :]

    sources, rows_in = [], []
    for source, places in arrivals(index, count, kv_refs):
        found = [ref[ref.shape[0] - EXTRA :, :heads].astype(F32) for _, ref in places]
        if len(found) == 2:
            found = [jnp.where(places[0][0], found[0], found[1])]
        sources.append(source)
        rows_in.append(found[0])
    spread_rows = spread_matrix(heads, width, g * (width // P_SIZE))
    wide = jnp.dot(
        jnp.concatenate(rows_in, axis=0).astype(BF16), spread_rows, preferred_element_type=F32
    )
    d_in = jnp.ones((1, width), F32)
    for r, source in enumerate(sources):
        one = wide[r * EXTRA : r * EXTRA + 1] + wide[r * EXTRA + 1 : r * EXTRA + 2]
        d_in = d_in * jnp.where(source > index, one, 1.0)
    through = dec_ref[0:1, :] * front[...].astype(F32) + f_ref[...].astype(F32)
    entering = (d_in * through + back[...].astype(F32)).astype(BF16)
    flow[:stretch, :] = jnp.dot(c_ref[:stretch, proj], front[...], preferred_element_type=F32)
    flow[stretch:, :] = jnp.dot(c_ref[stretch:, proj], entering, preferred_element_type=F32)
    gain_acc[...] = jnp.zeros_like(gain_acc)
    skip_acc[...] = jnp.zeros_like(skip_acc)

    @pl.loop(0, rows // step, unroll=2)
    def _(k):
        sl = pl.ds(pl.multiple_of(k * step, step), step)
        totals = [jnp.zeros((step, tile), F32)] * 3
        for j in range(0, width, tile):
            cols = slice(j, j + tile)
            gated = pre_ref[sl, cols] + reach_ref[sl, cols] * flow[sl, cols]
            gated_ref[sl, cols] = gated
            scaled = gated * gain_ref[:, first_lane + j : first_lane + j + tile]
            totals[0] += gated * gated
            totals[1] += scaled * scaled
            totals[2] += scaled * teacher_ref[sl, cols].astype(F32)
        for k3 in range(3):
            sums[sl, k3 * tile : (k3 + 1) * tile] = totals[k3]

    square, weighted, crossed = (
        jnp.sum(sums[:, k3 * tile : (k3 + 1) * tile], axis=1, keepdims=True) * (1.0 / width)
        for k3 in range(3)
    )
    scale = lax.rsqrt(square + EPS)
    push_scale = 2.0 * loss_scale
    mean = push_scale * scale * (scale * weighted - crossed)
    sums[:, :tile] = jnp.broadcast_to(scale, (rows, tile))
    sums[:, tile : 2 * tile] = jnp.broadcast_to(mean, (rows, tile))

    @pl.loop(0, rows // step, unroll=2)
    def _(k):
        sl = pl.ds(pl.multiple_of(k * step, step), step)
        scale = sums[sl, :tile]
        mean = sums[sl, tile : 2 * tile]
        for j in range(0, width, tile):
            cols = slice(j, j + tile)
            gain = gain_ref[:, first_lane + j : first_lane + j + tile]
            unit = gated_ref[sl, cols] * scale
            normed = unit * gain
            out_ref[sl, cols] = normed.astype(BF16)
            push = (normed - teacher_ref[sl, cols].astype(F32)) * push_scale
            by_gain = push * unit
            by_skip = (push * gain - unit * mean) * (scale * sx_ref[sl, cols])
            gain_acc[:, cols] += by_gain[:8] + by_gain[8:]
            skip_acc[:, cols] += by_skip[:8] + by_skip[8:]

    row = lax.broadcasted_iota(jnp.int32, (tile, width), 0)
    lane = lax.broadcasted_iota(jnp.int32, (tile, width), 1)
    matrix = jnp.where(row == lane // P_SIZE + g * (width // P_SIZE), 1.0, 0.0).astype(BF16)
    hi, lo = parts(skip_acc[...])
    by_head = jnp.sum(dot_nt(hi, matrix) + dot_nt(lo, matrix), axis=0, keepdims=True)
    grad_ref[...] = jnp.zeros_like(grad_ref)
    if g:
        grad_ref[:g, :] = before[:g, :]
        by_head += before[groups : groups + 1, :tile]
    grad_ref[g : g + 1, :] = jnp.sum(gain_acc[...], axis=0, keepdims=True)
    grad_ref[groups : groups + 1, :tile] = by_head


def writing_kernel(*refs):
    parts_in, out_ref, sems = refs[:-2], refs[-2], refs[-1]
    width = parts_in[0].shape[1]
    moves = [
        pltpu.make_async_copy(part, out_ref.at[:, pl.ds(k * width, width)], sems.at[k])
        for k, part in enumerate(parts_in)
    ]
    for move in moves:
        move.start()
    for move in moves:
        move.wait()


def closing_kernel(a_ref, b_ref, gain_ref, skip_ref):
    total = a_ref[...] + b_ref[...]
    groups, width = total.shape[0] - 1, total.shape[1]
    for g in range(groups):
        gain_ref[:, g * width : (g + 1) * width] = total[g : g + 1, :]
    skip_ref[...] = total[groups : groups + 1, : skip_ref.shape[1]]


def exchange(part, shift):
    axes = ("dp", "ctx")
    size = lax.axis_size(axes)
    return lax.ppermute(part, axes, [(d, d ^ shift) for d in range(size)])


def body(
    queries,
    keys,
    values,
    doc_ids,
    inputs,
    gate_input,
    b_input,
    c_input,
    dt_raw,
    dt_bias,
    decay_log,
    skip,
    gain,
):
    count = lax.axis_size("ctx")
    rows, features = queries.shape[1:]
    stretch = rows // 2
    kv_dev = keys.shape[2] // DH
    per_kv = queries.shape[2] // keys.shape[2]
    groups = b_input.shape[2] // N
    heads = features // P_SIZE
    width = features // groups
    length = doc_ids.shape[1]
    others = count - 1
    loss_scale = 1.0 / (lax.axis_size("dp") * count * rows)
    x, gate, bmat, cmat = inputs[0], gate_input[0], b_input[0], c_input[0]
    struct = jax.ShapeDtypeStruct

    def in_hbm(*arrays):
        return [pltpu.with_memory_space_constraint(array, pltpu.HBM) for array in arrays]

    def write(*pieces):
        return pl.pallas_call(
            writing_kernel,
            out_shape=struct((rows, features), BF16),
            in_specs=[VMEM] * len(pieces),
            out_specs=pl.BlockSpec(memory_space=pl.ANY),
            scratch_shapes=[pltpu.SemaphoreType.DMA((len(pieces),))],
            compiler_params=params(2),
            cost_estimate=cost(0, 4 * rows * features),
            name="writing",
        )(*pieces)

    state = struct((N, width), BF16)
    payload = struct((N + EXTRA, width), BF16)
    outs = pl.pallas_call(
        functools.partial(opening_kernel, count, groups),
        out_shape=(
            struct((rows + EXTRA, 2 * kv_dev * DH), BF16),
            struct((heads, rows), F32),
            *([struct((rows, width), BF16)] * groups),
            *([struct((8, width), F32)] * groups),
            *([state] * (2 * groups)),
            *([state] * groups),
        ),
        in_specs=[VMEM] * 8,
        out_specs=(VMEM,) * (2 + 5 * groups),
        compiler_params=params(16),
        cost_estimate=cost(4 * rows * features * N, 8 * rows * features),
        name="opening",
    )(
        *in_hbm(
            doc_ids,
            keys[0],
            values[0],
            x,
            bmat,
            dt_raw[0].T,
            dt_bias.reshape(1, heads),
            decay_log.reshape(1, heads),
        )
    )
    kv, ec = outs[:2]
    xw, dec, f_parts, b_parts, send = (
        outs[2 + k * groups : 2 + (k + 1) * groups] for k in range(5)
    )

    local = pl.pallas_call(
        functools.partial(local_kernel, count, groups),
        out_shape=(struct((rows, width), F32),) * (3 * groups),
        in_specs=[
            VMEM,
            *[pl.BlockSpec(memory_space=pl.ANY)] * 2,
            *[VMEM] * (4 + groups),
        ],
        out_specs=(VMEM,) * (3 * groups),
        scratch_shapes=[
            pltpu.VMEM((groups, rows, width), BF16),
            pltpu.VMEM((groups, rows, width), BF16),
            pltpu.SemaphoreType.DMA((2, groups)),
        ],
        compiler_params=params(16),
        cost_estimate=cost(2 * rows * features * N, 16 * rows * features),
        name="local",
    )(*in_hbm(doc_ids, x, gate, bmat, cmat, skip.reshape(1, heads)), ec, *xw)

    send = list(send)
    got = [[] for _ in range(groups)]
    def passed_on(g, stage, needed):
        return pl.pallas_call(
            functools.partial(chain_kernel, count, stage, g, heads),
            out_shape=state,
            in_specs=[VMEM] * (4 + len(needed)),
            out_specs=VMEM,
            compiler_params=params(6),
            cost_estimate=cost(16384 * N * width, 8 * N * width),
            name="chain",
        )(got[g][-1], f_parts[g], b_parts[g], dec[g], *needed)

    if count == 4:
        inward, outward, across = [(0, 1), (3, 2)], [(1, 0), (2, 3)], [(1, 2), (2, 1)]
        near = lax.ppermute(kv, "ctx", inward + outward)
        middle = lax.ppermute(kv, "ctx", across)
        middle, *local = lax.optimization_barrier((middle, *local))
        beyond = lax.ppermute(near, "ctx", across)
        send[-1] = pl.pallas_call(
            functools.partial(merge_kernel, count),
            out_shape=payload,
            in_specs=[VMEM] * 2,
            out_specs=VMEM,
            compiler_params=params(4),
            cost_estimate=cost(0, 4 * N * width),
            name="merge",
        )(send[-1], middle)
        far = lax.ppermute(send[-1], "ctx", inward + outward)
        got[-1].append(far)
        if groups > 1:
            got[0].append(lax.ppermute(send[0], "ctx", [(0, 1), (3, 2)]))
            send[0] = passed_on(0, 1, [near])
            beyond, _ = lax.optimization_barrier((beyond, send[0]))
            got[0].append(lax.ppermute(send[0], "ctx", across))
        farther = lax.ppermute(beyond, "ctx", outward)
        kv_got = [near, middle, beyond, far, farther]
    else:
        ring = ring_order(count)
        ring_pairs = [(ring[d], ring[(d + 1) % count]) for d in range(count)]
        kv_got = [kv]
        for _ in range(others):
            kv_got.append(lax.ppermute(kv_got[-1], "ctx", ring_pairs))
        kv_got = kv_got[1:]
    stack = 4 if per_kv % 4 == 0 and count <= 4 else 1
    targets = [
        pl.pallas_call(
            functools.partial(attention_kernel, count, per_kv, stack, g),
            out_shape=struct((rows, per_kv * DH), BF16),
            in_specs=[VMEM] * (4 + len(kv_got)),
            out_specs=VMEM,
            scratch_shapes=[
                pltpu.VMEM((2 * count * stretch, DH), BF16),
                pltpu.VMEM((2 * count * stretch, 2 * DH), BF16),
                pltpu.VMEM((stretch, stretch), F32),
                pltpu.VMEM((stretch, (count + 1) * stretch), F32),
                pltpu.VMEM((stretch, others * stretch), F32),
            ],
            compiler_params=params(24),
            cost_estimate=cost(
                4 * (2 * count + 1) * stretch * stretch * per_kv * DH, 8 * rows * per_kv * DH
            ),
            name="attention",
        )(doc_ids, queries[0], keys[0], values[0], *kv_got)
        for g in range(kv_dev)
    ]
    for r in range(1, count):
        for g in range(groups):
            if len(got[g]) >= r:
                continue
            if r == 3 and g == groups - 1:
                got[g][-1], targets[0] = lax.optimization_barrier((got[g][-1], targets[0]))
            if r > 1:
                if count == 4:
                    needed = [near] if r == 2 else [middle, beyond]
                else:
                    needed = kv_got
                send[g] = passed_on(g, r - 1, needed)
            pairs = [(r - 1, r), (count - r, count - r - 1)]
            got[g].append(lax.ppermute(send[g], "ctx", pairs))

    got[0][-1], *targets = lax.optimization_barrier((got[0][-1], *targets))
    normed, grads = [], None
    for g in range(groups):
        more = [] if grads is None else [grads]
        made, grads = pl.pallas_call(
            functools.partial(final_kernel, count, g, groups, loss_scale, heads),
            out_shape=(struct((rows, width), BF16), struct((groups + 1, width), F32)),
            in_specs=[VMEM] * (8 + others + len(kv_got) + len(more)),
            out_specs=(VMEM,) * 2,
            scratch_shapes=[
                pltpu.VMEM((N, width), BF16),
                pltpu.VMEM((N, width), BF16),
                pltpu.VMEM((rows, width), F32),
                pltpu.VMEM((rows, width), F32),
                pltpu.VMEM((rows, 3 * 128), F32),
                pltpu.VMEM((8, width), F32),
                pltpu.VMEM((8, width), F32),
            ],
            compiler_params=params(16),
            cost_estimate=cost(2 * rows * width * N, 20 * rows * width),
            name="final",
        )(
            *local[g::groups],
            cmat,
            targets[g],
            gain.reshape(1, features),
            f_parts[g],
            dec[g],
            *got[g],
            *kv_got,
            *more,
        )
        normed.append(made)
    teacher, student = write(*targets), write(*normed)
    shifts = [1 << k for k in range((lax.axis_size("dp") * count).bit_length() - 1)]
    if count >= 4:
        grads = (grads + exchange(grads, 1)) + (exchange(grads, 2) + exchange(grads, 3))
        shifts = shifts[2:]
    for shift in shifts[:-1]:
        grads = grads + exchange(grads, shift)
    grad_gain, grad_skip = pl.pallas_call(
        closing_kernel,
        out_shape=(struct((1, features), F32), struct((1, heads), F32)),
        in_specs=[VMEM] * 2,
        out_specs=(VMEM,) * 2,
        compiler_params=params(2),
        name="closing",
    )(grads, exchange(grads, shifts[-1]))
    return (teacher[None], student[None], grad_gain[0], grad_skip[0])


def solution(mesh):
    rows = P("dp", "ctx", "head")
    in_specs = (
        rows,
        rows,
        rows,
        P("dp", None),
        rows,
        rows,
        rows,
        rows,
        rows,
        P("head"),
        P("head"),
        P("head"),
        P("head"),
    )
    out_specs = (rows, rows, P("head"), P("head"))
    return jax.shard_map(body, mesh=mesh, in_specs=in_specs, out_specs=out_specs, check_vma=False)
```

```python
import functools
import math

import jax
import jax.numpy as jnp
from jax import lax
from jax.experimental import pallas as pl
from jax.experimental.pallas import tpu as pltpu
from jax.sharding import PartitionSpec as P

DH = 128
P_SIZE = 64
N = 128
EXTRA = 16
EPS = 1e-05
MASKED = -1e30
F32 = jnp.float32
BF16 = jnp.bfloat16
VMEM = pl.BlockSpec(memory_space=pltpu.VMEM)


def params(mib):
    return pltpu.CompilerParams(vmem_limit_bytes=mib << 20)


def cost(flops, size):
    return pl.CostEstimate(flops=flops, bytes_accessed=size, transcendentals=0)


def parts(v):
    hi = v.astype(BF16)
    return hi, (v - hi.astype(F32)).astype(BF16)


def spread_matrix(heads, width, first):
    row = lax.broadcasted_iota(jnp.int32, (heads, width), 0)
    lane = lax.broadcasted_iota(jnp.int32, (heads, width), 1)
    return jnp.where(row == (lane // P_SIZE) + first, 1.0, 0.0).astype(BF16)


def dot_nt(a, b):
    return lax.dot_general(a, b, (((1,), (1,)), ((), ())), preferred_element_type=F32)


def dot_tn(a, b):
    return lax.dot_general(a, b, (((0,), (0,)), ((), ())), preferred_element_type=F32)


def spread(v, matrix):
    return dot_tn(jnp.concatenate(parts(v), axis=0), jnp.concatenate([matrix, matrix], axis=0))


def doc_row(docs_ref, block, stretch):
    return docs_ref[:, pl.ds(pl.multiple_of(block * stretch, stretch), stretch)]


def as_column(row):
    size = row.shape[1]
    r = lax.broadcasted_iota(jnp.int32, (size, size), 0)
    c = lax.broadcasted_iota(jnp.int32, (size, size), 1)
    return jnp.sum(jnp.where(r == c, row.astype(F32), 0.0), axis=1, keepdims=True)


def lower_triangle(size):
    r = lax.broadcasted_iota(jnp.int32, (size, size), 0)
    c = lax.broadcasted_iota(jnp.int32, (size, size), 1)
    return r >= c


def prior_doc(docs_ref, block, stretch):
    before = doc_row(docs_ref, jnp.maximum(block - 1, 0), stretch)[:, stretch - 1 :]
    return jnp.where(block > 0, before, -1)


def own_block(index, count, half):
    return index if half == 0 else 2 * count - 1 - index


def ring_order(count):
    return [0] + list(range(1, count, 2)) + list(range(2, count, 2))[::-1]


def ring_source(index, count, steps):
    order = ring_order(count)
    source = jnp.int32(0)
    for place, member in enumerate(order):
        source = jnp.where(index == member, order[(place - steps) % count], source)
    return source


def passed_decay(ref, first, heads, width, g):
    matrix = spread_matrix(heads, width, g * (width // P_SIZE))
    wide = jnp.dot(ref[first : first + EXTRA, :heads], matrix, preferred_element_type=F32)
    return wide[0:1] + wide[1:2]


def opening_kernel(
    count,
    groups,
    docs_ref,
    k_ref,
    v_ref,
    x_ref,
    b_ref,
    dt_ref,
    bias_ref,
    log_ref,
    kv_ref,
    ec_ref,
    *outs,
):
    xw_refs, dec_refs, f_refs, b_refs, send_refs = (
        outs[k * groups : (k + 1) * groups] for k in range(5)
    )
    heads, rows = dt_ref.shape
    stretch = rows // 2
    width = x_ref.shape[1] // groups
    kv_width = k_ref.shape[1]
    index = lax.axis_index("ctx")
    kv_ref[:rows, :kv_width] = k_ref[...]
    kv_ref[:rows, kv_width:] = v_ref[...]
    kv_ref[rows:, :] = jnp.zeros((EXTRA, 2 * kv_width), BF16)
    triangle = jnp.where(lower_triangle(stretch), 1.0, 0.0)
    slope = jnp.exp(as_column(log_ref[...]))
    bias = as_column(bias_ref[...])
    lane = lax.broadcasted_iota(jnp.int32, (heads, 8), 1)
    ends = jnp.zeros((heads, 8), F32)
    loads = []
    projs = []
    for half in range(2):
        block = own_block(index, count, half)
        sl = slice(half * stretch, (half + 1) * stretch)
        raw = dt_ref[:, sl] + bias
        dt = jnp.maximum(raw, 0.0) + jnp.log1p(jnp.exp(-jnp.abs(raw)))
        cum = lax.dot_general(
            -dt * slope,
            triangle,
            (((1,), (1,)), ((), ())),
            precision=lax.Precision.HIGHEST,
            preferred_element_type=F32,
        )
        ec_ref[:, sl] = jnp.exp(cum)
        loads.append(jnp.exp(-cum) * dt)
        final = jnp.exp(cum[:, stretch - 1 :])
        row = doc_row(docs_ref, block, stretch)
        last = row[:, stretch - 1 :]
        kept = jnp.where(last == prior_doc(docs_ref, block, stretch), 1.0, 0.0)
        ends = jnp.where(lane == half, final * kept, ends)
        ends = jnp.where(lane == 2 + half, final, ends)
        same = jnp.where(as_column(row) == last.astype(F32), 1.0, 0.0)
        projs.append((b_ref[sl, :].astype(F32) * same).astype(BF16))
    both = ends[:, 0:1] * ends[:, 1:2]
    r = lax.broadcasted_iota(jnp.int32, (heads, heads), 0)
    c = lax.broadcasted_iota(jnp.int32, (heads, heads), 1)
    hi, lo = parts(jnp.sum(jnp.where(r == c, both, 0.0), axis=0, keepdims=True))
    kv_ref[rows:, :heads] = jnp.concatenate(
        [hi, lo, jnp.zeros((EXTRA - 2, heads), BF16)], axis=0
    )
    for g in range(groups):
        cols = slice(g * width, (g + 1) * width)
        matrix = spread_matrix(heads, width, g * (heads // groups))
        wide = spread(ends, matrix)
        dec_refs[g][...] = wide
        sums = []
        for half in range(2):
            sl = slice(half * stretch, (half + 1) * stretch)
            xw = (x_ref[sl, cols].astype(F32) * spread(loads[half], matrix)).astype(BF16)
            xw_refs[g][sl, :] = xw
            sums.append(dot_tn(projs[half][:, g * N : (g + 1) * N], xw) * wide[2 + half : 3 + half])
        f_refs[g][...] = sums[0].astype(BF16)
        b_refs[g][...] = sums[1].astype(BF16)

        @pl.when(index == 0)
        def _():
            send_refs[g][...] = sums[0].astype(BF16)

        @pl.when(index != 0)
        def _():
            send_refs[g][...] = (wide[1:2] * sums[0] + sums[1]).astype(BF16)


def chain_kernel(count, stage, g, heads, got_ref, f_ref, b_ref, dec_ref, *refs):
    send_ref = refs[-1]
    width = f_ref.shape[1]
    index = lax.axis_index("ctx")

    @pl.when(index == stage)
    def _():
        state = dec_ref[0:1, :] * got_ref[:N, :].astype(F32) + f_ref[...].astype(F32)
        send_ref[...] = state.astype(BF16)

    @pl.when(index == count - 1 - stage)
    def _():
        decay = jnp.ones((1, width), F32)
        for r, ref in enumerate(refs[:-1]):
            one = passed_decay(ref, ref.shape[0] - EXTRA, heads, width, g)
            if count != 4:
                one = jnp.where(ring_source(index, count, r + 1) > index, one, 1.0)
            decay = decay * one
        inner = decay * f_ref[...].astype(F32) + got_ref[:N, :].astype(F32)
        send_ref[...] = (dec_ref[1:2, :] * inner + b_ref[...].astype(F32)).astype(BF16)


def local_kernel(
    count, groups, docs_ref, x_ref, gate_ref, b_ref, c_ref, skip_ref, ec_ref, *refs
):
    xw_refs, pre_refs, reach_refs, sx_refs = (
        refs[k * groups : (k + 1) * groups] for k in range(4)
    )
    x_here, gate_here, sems = refs[4 * groups :]
    heads, rows = ec_ref.shape
    stretch = rows // 2
    width = x_ref.shape[1] // groups
    index = lax.axis_index("ctx")
    moves = []
    for g in range(groups):
        cols = pl.ds(g * width, width)
        moves.append(
            [
                pltpu.make_async_copy(x_ref.at[:, cols], x_here.at[g], sems.at[0, g]),
                pltpu.make_async_copy(gate_ref.at[:, cols], gate_here.at[g], sems.at[1, g]),
            ]
        )
        for move in moves[g]:
            move.start()
    triangle = lower_triangle(stretch)
    skip = as_column(skip_ref[...])
    step = 16
    masks = []
    for half in range(2):
        block = own_block(index, count, half)
        row = doc_row(docs_ref, block, stretch)
        column = as_column(row)
        reached = jnp.where(column == prior_doc(docs_ref, block, stretch).astype(F32), 1.0, 0.0)
        masks.append((triangle & (column == row.astype(F32)), reached))
    for g in range(groups):
        proj = slice(g * N, (g + 1) * N)
        matrix = spread_matrix(heads, width, g * (heads // groups))
        wide_skip = spread(skip, matrix)
        for half in range(2):
            sl = slice(half * stretch, (half + 1) * stretch)
            near, reached = masks[half]
            gram = dot_nt(c_ref[sl, proj], b_ref[sl, proj])
            gram = jnp.where(near, gram, 0.0).astype(BF16)
            wide = spread(ec_ref[:, sl], matrix)
            inner = jnp.dot(gram, xw_refs[g][sl, :], preferred_element_type=F32)
            if half == 0:
                for move in moves[g]:
                    move.wait()
            for k in range(0, stretch, step):
                at = slice(half * stretch + k, half * stretch + k + step)
                here = slice(k, k + step)
                x = x_here[g, at, :].astype(F32)
                gate = gate_here[g, at, :].astype(F32)
                silu = gate / (1.0 + jnp.exp(-gate))
                fade = wide[here] * silu
                sx = silu * x
                sx_refs[g][at, :] = sx
                pre_refs[g][at, :] = inner[here] * fade + wide_skip * sx
                reach_refs[g][at, :] = reached[here] * fade


def merge_kernel(count, state_ref, kv_ref, out_ref):
    index = lax.axis_index("ctx")
    outer = (index == 0) | (index == count - 1)
    wide = kv_ref.shape[1]
    rows = kv_ref.shape[0] - EXTRA
    stretch = rows // 2

    @pl.when(outer)
    def _():
        out_ref[:N, :] = state_ref[...]
        out_ref[N:, :] = jnp.zeros((EXTRA, out_ref.shape[1]), BF16)

    @pl.when(jnp.logical_not(outer))
    def _():
        out_ref[:stretch, :wide] = kv_ref[:stretch, :]
        out_ref[:stretch, wide:] = kv_ref[stretch:rows, :]
        out_ref[stretch:, :wide] = kv_ref[rows:, :]
        out_ref[stretch:, wide:] = jnp.zeros((EXTRA, wide), BF16)


def arrivals(index, count, refs):
    if count != 4:
        return [(ring_source(index, count, r + 1), [(None, refs[r])]) for r in range(count - 1)]
    near, own_of_middle, next_of_middle, far, farther = refs
    middle = (index == 1) | (index == 2)
    low = index < 2
    return [
        (index ^ 1, [(None, near)]),
        (
            jnp.where(low, 2, 1),
            [(middle, own_of_middle), (jnp.logical_not(middle), far)],
        ),
        (
            jnp.where(low, 3, 0),
            [(middle, next_of_middle), (jnp.logical_not(middle), farther)],
        ),
    ]


def attention_kernel(count, per, stack, g, docs_ref, q_ref, k_ref, v_ref, *refs):
    others = count - 1
    sent = 5 if count == 4 else others
    out_ref, kt, vt, bias_f, bias_b, bias_a = refs[-6:]
    rows = q_ref.shape[0]
    stretch = rows // 2
    index = lax.axis_index("ctx")
    last = 2 * count - 1
    kv_width = refs[0].shape[1] // 2
    row_f = doc_row(docs_ref, index, stretch).astype(F32)
    row_b = doc_row(docs_ref, last - index, stretch).astype(F32)
    col_f = as_column(row_f)
    col_b = as_column(row_b)
    triangle = lower_triangle(stretch)

    def tile(k):
        return slice(k * stretch, (k + 1) * stretch)

    bias_f[...] = jnp.where(triangle & (col_f == row_f), 0.0, MASKED)
    bias_b[:, tile(0)] = jnp.where(col_b == row_f, 0.0, MASKED)
    bias_b[:, tile(1)] = jnp.where(triangle & (col_b == row_b), 0.0, MASKED)
    vt[:, DH:] = jnp.ones((vt.shape[0], DH), BF16)
    here = slice(g * DH, (g + 1) * DH)
    kt[tile(0), :] = k_ref[:stretch, here]
    vt[tile(0), :DH] = v_ref[:stretch, here]
    kt[tile(count), :] = k_ref[stretch:, here]
    vt[tile(count), :DH] = v_ref[stretch:, here]
    lower = []
    for r, (source, places) in enumerate(arrivals(index, count, refs[:sent])):
        lower.append(source < index)
        for condition, ref in places:

            def fetch(ref=ref, r=r):
                folded = ref.shape[1] > 2 * kv_width
                gap = jnp.where(lower[r], 0, 2 * kv_width if folded else stretch)
                for table, first in ((kt, g * DH), (vt, kv_width + g * DH)):
                    front = ref[:stretch, first : first + DH]
                    if folded:
                        own = ref[:stretch, pl.ds(pl.multiple_of(first + gap, DH), DH)]
                    else:
                        own = ref[pl.ds(pl.multiple_of(gap, stretch), stretch), first : first + DH]
                    table[tile(1 + r), :DH] = own
                    table[tile(count + 1 + r), :DH] = front

            if condition is None:
                fetch()
            else:
                pl.when(condition)(fetch)
        key_f = doc_row(docs_ref, source, stretch).astype(F32)
        key_a = doc_row(docs_ref, jnp.where(lower[r], source, last - source), stretch).astype(F32)
        bias_b[:, tile(2 + r)] = jnp.where(col_b == key_f, 0.0, MASKED)
        bias_a[:, tile(r)] = jnp.where(jnp.where(lower[r], col_f, col_b) == key_a, 0.0, MASKED)

    factor = math.log2(math.e) / math.sqrt(DH)
    tall = stack * stretch
    half_keys = count * stretch

    def stacked(first, base):
        return jnp.concatenate(
            [
                q_ref[base : base + stretch, (g * per + first + j) * DH : (g * per + first + j + 1) * DH]
                for j in range(stack)
            ],
            axis=0,
        )

    def biased(score, bias):
        size = score.shape[1]
        return (score.reshape(stack, stretch, size) + bias[None]).reshape(tall, size)

    for first in range(0, per, stack):
        s_f = dot_nt(stacked(first, 0), kt[:half_keys, :])
        s_b = dot_nt(stacked(first, stretch), kt[...])
        t_f = biased(s_f[:, tile(0)], bias_f[...])
        t_b = [biased(s_b[:, tile(0)], bias_b[:, tile(0)])]
        for k in range(1, count + 1):
            t_b.append(biased(s_b[:, tile(count + k - 1)], bias_b[:, tile(k)]))
        t_a = []
        for r in range(others):
            score = jnp.where(lower[r], s_f[:, tile(1 + r)], s_b[:, tile(1 + r)])
            t_a.append(biased(score, bias_a[:, tile(r)]))
        best_f = t_f
        best_b = functools.reduce(jnp.maximum, t_b)
        for r in range(others):
            best_f = jnp.maximum(best_f, jnp.where(lower[r], t_a[r], MASKED))
            best_b = jnp.maximum(best_b, jnp.where(lower[r], MASKED, t_a[r]))
        top_f = jnp.max(best_f, axis=1, keepdims=True)
        top_b = jnp.max(best_b, axis=1, keepdims=True)
        w_f = [jnp.exp2((t_f - top_f) * factor).astype(BF16)]
        w_b = [jnp.exp2((t - top_b) * factor).astype(BF16) for t in t_b]
        w_x = []
        for r in range(others):
            top = jnp.where(lower[r], top_f, top_b)
            w = jnp.exp2((t_a[r] - top) * factor)
            w_f.append(jnp.where(lower[r], w, 0.0).astype(BF16))
            w_x.append(jnp.where(lower[r], 0.0, w).astype(BF16))
        w_b = w_b[:1] + w_x + w_b[1:]
        out_f = jnp.dot(
            jnp.concatenate(w_f, axis=1), vt[:half_keys, :], preferred_element_type=F32
        )
        out_b = jnp.dot(jnp.concatenate(w_b, axis=1), vt[...], preferred_element_type=F32)
        for half, out in enumerate((out_f, out_b)):
            result = (out[:, :DH] / out[:, DH:]).astype(BF16)
            for j in range(stack):
                cols = slice((first + j) * DH, (first + j + 1) * DH)
                out_ref[tile(half), cols] = result[tile(j)]


def final_kernel(
    count,
    g,
    groups,
    loss_scale,
    heads,
    pre_ref,
    reach_ref,
    sx_ref,
    c_ref,
    teacher_ref,
    gain_ref,
    f_ref,
    dec_ref,
    *refs,
):
    others = count - 1
    got = refs[:others]
    sent = 5 if count == 4 else others
    kv_refs = refs[others : others + sent]
    before = refs[others + sent] if g else None
    proj = slice(g * N, (g + 1) * N)
    first_lane = g * pre_ref.shape[1]
    out_ref, grad_ref, front, back, flow, gated_ref, sums, gain_acc, skip_acc = refs[-9:]
    rows, width = pre_ref.shape
    stretch = rows // 2
    index = lax.axis_index("ctx")
    tile = 128
    step = 16

    @pl.when(index == 0)
    def _():
        front[...] = jnp.zeros_like(front)

    @pl.when(index == count - 1)
    def _():
        back[...] = jnp.zeros_like(back)

    for r in range(1, count):

        @pl.when(index == r)
        def _():
            front[...] = got[r - 1][:N, :]

        @pl.when(index == count - 1 - r)
        def _():
            back[...] = got[r - 1][:N, :]

    sources, rows_in = [], []
    for source, places in arrivals(index, count, kv_refs):
        found = [ref[ref.shape[0] - EXTRA :, :heads].astype(F32) for _, ref in places]
        if len(found) == 2:
            found = [jnp.where(places[0][0], found[0], found[1])]
        sources.append(source)
        rows_in.append(found[0])
    spread_rows = spread_matrix(heads, width, g * (width // P_SIZE))
    wide = jnp.dot(
        jnp.concatenate(rows_in, axis=0).astype(BF16), spread_rows, preferred_element_type=F32
    )
    d_in = jnp.ones((1, width), F32)
    for r, source in enumerate(sources):
        one = wide[r * EXTRA : r * EXTRA + 1] + wide[r * EXTRA + 1 : r * EXTRA + 2]
        d_in = d_in * jnp.where(source > index, one, 1.0)
    through = dec_ref[0:1, :] * front[...].astype(F32) + f_ref[...].astype(F32)
    entering = (d_in * through + back[...].astype(F32)).astype(BF16)
    flow[:stretch, :] = jnp.dot(c_ref[:stretch, proj], front[...], preferred_element_type=F32)
    flow[stretch:, :] = jnp.dot(c_ref[stretch:, proj], entering, preferred_element_type=F32)
    gain_acc[...] = jnp.zeros_like(gain_acc)
    skip_acc[...] = jnp.zeros_like(skip_acc)

    @pl.loop(0, rows // step, unroll=2)
    def _(k):
        sl = pl.ds(pl.multiple_of(k * step, step), step)
        totals = [jnp.zeros((step, tile), F32)] * 3
        for j in range(0, width, tile):
            cols = slice(j, j + tile)
            gated = pre_ref[sl, cols] + reach_ref[sl, cols] * flow[sl, cols]
            gated_ref[sl, cols] = gated
            scaled = gated * gain_ref[:, first_lane + j : first_lane + j + tile]
            totals[0] += gated * gated
            totals[1] += scaled * scaled
            totals[2] += scaled * teacher_ref[sl, cols].astype(F32)
        for k3 in range(3):
            sums[sl, k3 * tile : (k3 + 1) * tile] = totals[k3]

    square, weighted, crossed = (
        jnp.sum(sums[:, k3 * tile : (k3 + 1) * tile], axis=1, keepdims=True) * (1.0 / width)
        for k3 in range(3)
    )
    scale = lax.rsqrt(square + EPS)
    push_scale = 2.0 * loss_scale
    mean = push_scale * scale * (scale * weighted - crossed)
    sums[:, :tile] = jnp.broadcast_to(scale, (rows, tile))
    sums[:, tile : 2 * tile] = jnp.broadcast_to(mean, (rows, tile))

    @pl.loop(0, rows // step, unroll=2)
    def _(k):
        sl = pl.ds(pl.multiple_of(k * step, step), step)
        scale = sums[sl, :tile]
        mean = sums[sl, tile : 2 * tile]
        for j in range(0, width, tile):
            cols = slice(j, j + tile)
            gain = gain_ref[:, first_lane + j : first_lane + j + tile]
            unit = gated_ref[sl, cols] * scale
            normed = unit * gain
            out_ref[sl, cols] = normed.astype(BF16)
            push = (normed - teacher_ref[sl, cols].astype(F32)) * push_scale
            by_gain = push * unit
            by_skip = (push * gain - unit * mean) * (scale * sx_ref[sl, cols])
            gain_acc[:, cols] += by_gain[:8] + by_gain[8:]
            skip_acc[:, cols] += by_skip[:8] + by_skip[8:]

    row = lax.broadcasted_iota(jnp.int32, (tile, width), 0)
    lane = lax.broadcasted_iota(jnp.int32, (tile, width), 1)
    matrix = jnp.where(row == lane // P_SIZE + g * (width // P_SIZE), 1.0, 0.0).astype(BF16)
    hi, lo = parts(skip_acc[...])
    by_head = jnp.sum(dot_nt(hi, matrix) + dot_nt(lo, matrix), axis=0, keepdims=True)
    grad_ref[...] = jnp.zeros_like(grad_ref)
    if g:
        grad_ref[:g, :] = before[:g, :]
        by_head += before[groups : groups + 1, :tile]
    grad_ref[g : g + 1, :] = jnp.sum(gain_acc[...], axis=0, keepdims=True)
    grad_ref[groups : groups + 1, :tile] = by_head


def writing_kernel(*refs):
    parts_in, out_ref, sems = refs[:-2], refs[-2], refs[-1]
    width = parts_in[0].shape[1]
    moves = [
        pltpu.make_async_copy(part, out_ref.at[:, pl.ds(k * width, width)], sems.at[k])
        for k, part in enumerate(parts_in)
    ]
    for move in moves:
        move.start()
    for move in moves:
        move.wait()


def closing_kernel(a_ref, b_ref, gain_ref, skip_ref):
    total = a_ref[...] + b_ref[...]
    groups, width = total.shape[0] - 1, total.shape[1]
    for g in range(groups):
        gain_ref[:, g * width : (g + 1) * width] = total[g : g + 1, :]
    skip_ref[...] = total[groups : groups + 1, : skip_ref.shape[1]]


def exchange(part, shift):
    axes = ("dp", "ctx")
    size = lax.axis_size(axes)
    return lax.ppermute(part, axes, [(d, d ^ shift) for d in range(size)])


def body(
    queries,
    keys,
    values,
    doc_ids,
    inputs,
    gate_input,
    b_input,
    c_input,
    dt_raw,
    dt_bias,
    decay_log,
    skip,
    gain,
):
    count = lax.axis_size("ctx")
    rows, features = queries.shape[1:]
    stretch = rows // 2
    kv_dev = keys.shape[2] // DH
    per_kv = queries.shape[2] // keys.shape[2]
    groups = b_input.shape[2] // N
    heads = features // P_SIZE
    width = features // groups
    length = doc_ids.shape[1]
    others = count - 1
    loss_scale = 1.0 / (lax.axis_size("dp") * count * rows)
    x, gate, bmat, cmat = inputs[0], gate_input[0], b_input[0], c_input[0]
    struct = jax.ShapeDtypeStruct

    def in_hbm(*arrays):
        return [pltpu.with_memory_space_constraint(array, pltpu.HBM) for array in arrays]

    def write(*pieces):
        return pl.pallas_call(
            writing_kernel,
            out_shape=struct((rows, features), BF16),
            in_specs=[VMEM] * len(pieces),
            out_specs=pl.BlockSpec(memory_space=pl.ANY),
            scratch_shapes=[pltpu.SemaphoreType.DMA((len(pieces),))],
            compiler_params=params(2),
            cost_estimate=cost(0, 4 * rows * features),
            name="writing",
        )(*pieces)

    state = struct((N, width), BF16)
    payload = struct((N + EXTRA, width), BF16)
    outs = pl.pallas_call(
        functools.partial(opening_kernel, count, groups),
        out_shape=(
            struct((rows + EXTRA, 2 * kv_dev * DH), BF16),
            struct((heads, rows), F32),
            *([struct((rows, width), BF16)] * groups),
            *([struct((8, width), F32)] * groups),
            *([state] * (2 * groups)),
            *([state] * groups),
        ),
        in_specs=[VMEM] * 8,
        out_specs=(VMEM,) * (2 + 5 * groups),
        compiler_params=params(16),
        cost_estimate=cost(4 * rows * features * N, 8 * rows * features),
        name="opening",
    )(
        *in_hbm(
            doc_ids,
            keys[0],
            values[0],
            x,
            bmat,
            dt_raw[0].T,
            dt_bias.reshape(1, heads),
            decay_log.reshape(1, heads),
        )
    )
    kv, ec = outs[:2]
    xw, dec, f_parts, b_parts, send = (
        outs[2 + k * groups : 2 + (k + 1) * groups] for k in range(5)
    )

    local = pl.pallas_call(
        functools.partial(local_kernel, count, groups),
        out_shape=(struct((rows, width), F32),) * (3 * groups),
        in_specs=[
            VMEM,
            *[pl.BlockSpec(memory_space=pl.ANY)] * 2,
            *[VMEM] * (4 + groups),
        ],
        out_specs=(VMEM,) * (3 * groups),
        scratch_shapes=[
            pltpu.VMEM((groups, rows, width), BF16),
            pltpu.VMEM((groups, rows, width), BF16),
            pltpu.SemaphoreType.DMA((2, groups)),
        ],
        compiler_params=params(16),
        cost_estimate=cost(2 * rows * features * N, 16 * rows * features),
        name="local",
    )(*in_hbm(doc_ids, x, gate, bmat, cmat, skip.reshape(1, heads)), ec, *xw)

    send = list(send)
    got = [[] for _ in range(groups)]
    def passed_on(g, stage, needed):
        return pl.pallas_call(
            functools.partial(chain_kernel, count, stage, g, heads),
            out_shape=state,
            in_specs=[VMEM] * (4 + len(needed)),
            out_specs=VMEM,
            compiler_params=params(6),
            cost_estimate=cost(16384 * N * width, 8 * N * width),
            name="chain",
        )(got[g][-1], f_parts[g], b_parts[g], dec[g], *needed)

    if count == 4:
        inward, outward, across = [(0, 1), (3, 2)], [(1, 0), (2, 3)], [(1, 2), (2, 1)]
        near = lax.ppermute(kv, "ctx", inward + outward)
        middle = lax.ppermute(kv, "ctx", across)
        middle, *local = lax.optimization_barrier((middle, *local))
        beyond = lax.ppermute(near, "ctx", across)
        send[-1] = pl.pallas_call(
            functools.partial(merge_kernel, count),
            out_shape=payload,
            in_specs=[VMEM] * 2,
            out_specs=VMEM,
            compiler_params=params(4),
            cost_estimate=cost(0, 4 * N * width),
            name="merge",
        )(send[-1], middle)
        far = lax.ppermute(send[-1], "ctx", inward + outward)
        got[-1].append(far)
        if groups > 1:
            got[0].append(lax.ppermute(send[0], "ctx", [(0, 1), (3, 2)]))
            send[0] = passed_on(0, 1, [near])
            beyond, _ = lax.optimization_barrier((beyond, send[0]))
            got[0].append(lax.ppermute(send[0], "ctx", across))
        farther = lax.ppermute(beyond, "ctx", outward)
        kv_got = [near, middle, beyond, far, farther]
    else:
        ring = ring_order(count)
        ring_pairs = [(ring[d], ring[(d + 1) % count]) for d in range(count)]
        kv_got = [kv]
        for _ in range(others):
            kv_got.append(lax.ppermute(kv_got[-1], "ctx", ring_pairs))
        kv_got = kv_got[1:]
    stack = 4 if per_kv % 4 == 0 and count <= 4 else 1
    targets = [
        pl.pallas_call(
            functools.partial(attention_kernel, count, per_kv, stack, g),
            out_shape=struct((rows, per_kv * DH), BF16),
            in_specs=[VMEM] * (4 + len(kv_got)),
            out_specs=VMEM,
            scratch_shapes=[
                pltpu.VMEM((2 * count * stretch, DH), BF16),
                pltpu.VMEM((2 * count * stretch, 2 * DH), BF16),
                pltpu.VMEM((stretch, stretch), F32),
                pltpu.VMEM((stretch, (count + 1) * stretch), F32),
                pltpu.VMEM((stretch, others * stretch), F32),
            ],
            compiler_params=params(24),
            cost_estimate=cost(
                4 * (2 * count + 1) * stretch * stretch * per_kv * DH, 8 * rows * per_kv * DH
            ),
            name="attention",
        )(doc_ids, queries[0], keys[0], values[0], *kv_got)
        for g in range(kv_dev)
    ]
    for r in range(1, count):
        for g in range(groups):
            if len(got[g]) >= r:
                continue
            if r == 3 and g == groups - 1:
                got[g][-1], targets[0] = lax.optimization_barrier((got[g][-1], targets[0]))
            if r > 1:
                if count == 4:
                    needed = [near] if r == 2 else [middle, beyond]
                else:
                    needed = kv_got
                send[g] = passed_on(g, r - 1, needed)
            pairs = [(r - 1, r), (count - r, count - r - 1)]
            got[g].append(lax.ppermute(send[g], "ctx", pairs))

    got[0][-1], *targets = lax.optimization_barrier((got[0][-1], *targets))
    teacher = write(*targets)
    normed, grads = [], None
    for g in range(groups):
        more = [] if grads is None else [grads]
        if g == groups - 1:
            got[g][-1], teacher = lax.optimization_barrier((got[g][-1], teacher))
        made, grads = pl.pallas_call(
            functools.partial(final_kernel, count, g, groups, loss_scale, heads),
            out_shape=(struct((rows, width), BF16), struct((groups + 1, width), F32)),
            in_specs=[VMEM] * (8 + others + len(kv_got) + len(more)),
            out_specs=(VMEM,) * 2,
            scratch_shapes=[
                pltpu.VMEM((N, width), BF16),
                pltpu.VMEM((N, width), BF16),
                pltpu.VMEM((rows, width), F32),
                pltpu.VMEM((rows, width), F32),
                pltpu.VMEM((rows, 3 * 128), F32),
                pltpu.VMEM((8, width), F32),
                pltpu.VMEM((8, width), F32),
            ],
            compiler_params=params(16),
            cost_estimate=cost(2 * rows * width * N, 20 * rows * width),
            name="final",
        )(
            *local[g::groups],
            cmat,
            targets[g],
            gain.reshape(1, features),
            f_parts[g],
            dec[g],
            *got[g],
            *kv_got,
            *more,
        )
        normed.append(made)
    student = write(*normed)
    shifts = [1 << k for k in range((lax.axis_size("dp") * count).bit_length() - 1)]
    if count >= 4:
        grads = (grads + exchange(grads, 1)) + (exchange(grads, 2) + exchange(grads, 3))
        shifts = shifts[2:]
    for shift in shifts[:-1]:
        grads = grads + exchange(grads, shift)
    grad_gain, grad_skip = pl.pallas_call(
        closing_kernel,
        out_shape=(struct((1, features), F32), struct((1, heads), F32)),
        in_specs=[VMEM] * 2,
        out_specs=(VMEM,) * 2,
        compiler_params=params(2),
        name="closing",
    )(grads, exchange(grads, shifts[-1]))
    return (teacher[None], student[None], grad_gain[0], grad_skip[0])


def solution(mesh):
    rows = P("dp", "ctx", "head")
    in_specs = (
        rows,
        rows,
        rows,
        P("dp", None),
        rows,
        rows,
        rows,
        rows,
        rows,
        P("head"),
        P("head"),
        P("head"),
        P("head"),
    )
    out_specs = (rows, rows, P("head"), P("head"))
    return jax.shard_map(body, mesh=mesh, in_specs=in_specs, out_specs=out_specs, check_vma=False)
```

```python
import functools
import math

import jax
import jax.numpy as jnp
from jax import lax
from jax.experimental import pallas as pl
from jax.experimental.pallas import tpu as pltpu
from jax.sharding import PartitionSpec as P

DH = 128
P_SIZE = 64
N = 128
EXTRA = 16
EPS = 1e-05
MASKED = -1e30
F32 = jnp.float32
BF16 = jnp.bfloat16
VMEM = pl.BlockSpec(memory_space=pltpu.VMEM)


def params(mib):
    return pltpu.CompilerParams(vmem_limit_bytes=mib << 20)


def cost(flops, size):
    return pl.CostEstimate(flops=flops, bytes_accessed=size, transcendentals=0)


def parts(v):
    hi = v.astype(BF16)
    return hi, (v - hi.astype(F32)).astype(BF16)


def spread_matrix(heads, width, first):
    row = lax.broadcasted_iota(jnp.int32, (heads, width), 0)
    lane = lax.broadcasted_iota(jnp.int32, (heads, width), 1)
    return jnp.where(row == (lane // P_SIZE) + first, 1.0, 0.0).astype(BF16)


def dot_nt(a, b):
    return lax.dot_general(a, b, (((1,), (1,)), ((), ())), preferred_element_type=F32)


def dot_tn(a, b):
    return lax.dot_general(a, b, (((0,), (0,)), ((), ())), preferred_element_type=F32)


def spread(v, matrix):
    return dot_tn(jnp.concatenate(parts(v), axis=0), jnp.concatenate([matrix, matrix], axis=0))


def doc_row(docs_ref, block, stretch):
    return docs_ref[:, pl.ds(pl.multiple_of(block * stretch, stretch), stretch)]


def as_column(row):
    size = row.shape[1]
    r = lax.broadcasted_iota(jnp.int32, (size, size), 0)
    c = lax.broadcasted_iota(jnp.int32, (size, size), 1)
    return jnp.sum(jnp.where(r == c, row.astype(F32), 0.0), axis=1, keepdims=True)


def lower_triangle(size):
    r = lax.broadcasted_iota(jnp.int32, (size, size), 0)
    c = lax.broadcasted_iota(jnp.int32, (size, size), 1)
    return r >= c


def prior_doc(docs_ref, block, stretch):
    before = doc_row(docs_ref, jnp.maximum(block - 1, 0), stretch)[:, stretch - 1 :]
    return jnp.where(block > 0, before, -1)


def own_block(index, count, half):
    return index if half == 0 else 2 * count - 1 - index


def ring_order(count):
    return [0] + list(range(1, count, 2)) + list(range(2, count, 2))[::-1]


def ring_source(index, count, steps):
    order = ring_order(count)
    source = jnp.int32(0)
    for place, member in enumerate(order):
        source = jnp.where(index == member, order[(place - steps) % count], source)
    return source


def passed_decay(ref, first, heads, width, g):
    matrix = spread_matrix(heads, width, g * (width // P_SIZE))
    wide = jnp.dot(ref[first : first + EXTRA, :heads], matrix, preferred_element_type=F32)
    return wide[0:1] + wide[1:2]


def opening_kernel(
    count,
    groups,
    docs_ref,
    k_ref,
    v_ref,
    x_ref,
    b_ref,
    dt_ref,
    bias_ref,
    log_ref,
    kv_ref,
    ec_ref,
    *outs,
):
    xw_refs, dec_refs, f_refs, b_refs, send_refs = (
        outs[k * groups : (k + 1) * groups] for k in range(5)
    )
    heads, rows = dt_ref.shape
    stretch = rows // 2
    width = x_ref.shape[1] // groups
    kv_width = k_ref.shape[1]
    index = lax.axis_index("ctx")
    kv_ref[:rows, :kv_width] = k_ref[...]
    kv_ref[:rows, kv_width:] = v_ref[...]
    kv_ref[rows:, :] = jnp.zeros((EXTRA, 2 * kv_width), BF16)
    slope = jnp.exp(as_column(log_ref[...]))
    bias = as_column(bias_ref[...])
    lane = lax.broadcasted_iota(jnp.int32, (heads, 8), 1)
    ends = jnp.zeros((heads, 8), F32)
    loads = []
    projs = []
    raw = jnp.concatenate([dt_ref[:, :stretch] + bias, dt_ref[:, stretch:] + bias], axis=0)
    dt_both = jnp.maximum(raw, 0.0) + jnp.log1p(jnp.exp(-jnp.abs(raw)))
    rate = -dt_both * jnp.concatenate([slope, slope], axis=0)
    hi, lo = parts(rate)
    rest = (rate - hi.astype(F32) - lo.astype(F32)).astype(BF16)
    triangle = jnp.where(lower_triangle(stretch), 1.0, 0.0).astype(BF16)
    cum_both = dot_nt(
        jnp.concatenate([hi, lo, rest], axis=1), jnp.concatenate([triangle] * 3, axis=1)
    )
    grown = jnp.exp(cum_both)
    load_both = jnp.exp(-cum_both) * dt_both
    for half in range(2):
        block = own_block(index, count, half)
        sl = slice(half * stretch, (half + 1) * stretch)
        here = slice(half * heads, (half + 1) * heads)
        ec_ref[:, sl] = grown[here]
        loads.append(load_both[here])
        final = grown[here, stretch - 1 :]
        row = doc_row(docs_ref, block, stretch)
        last = row[:, stretch - 1 :]
        kept = jnp.where(last == prior_doc(docs_ref, block, stretch), 1.0, 0.0)
        ends = jnp.where(lane == half, final * kept, ends)
        ends = jnp.where(lane == 2 + half, final, ends)
        same = jnp.where(as_column(row) == last.astype(F32), 1.0, 0.0)
        projs.append((b_ref[sl, :].astype(F32) * same).astype(BF16))
    both = ends[:, 0:1] * ends[:, 1:2]
    r = lax.broadcasted_iota(jnp.int32, (heads, heads), 0)
    c = lax.broadcasted_iota(jnp.int32, (heads, heads), 1)
    hi, lo = parts(jnp.sum(jnp.where(r == c, both, 0.0), axis=0, keepdims=True))
    kv_ref[rows:, :heads] = jnp.concatenate(
        [hi, lo, jnp.zeros((EXTRA - 2, heads), BF16)], axis=0
    )
    for g in range(groups):
        cols = slice(g * width, (g + 1) * width)
        matrix = spread_matrix(heads, width, g * (heads // groups))
        wide = spread(ends, matrix)
        dec_refs[g][...] = wide
        sums = []
        for half in range(2):
            sl = slice(half * stretch, (half + 1) * stretch)
            xw = (x_ref[sl, cols].astype(F32) * spread(loads[half], matrix)).astype(BF16)
            xw_refs[g][sl, :] = xw
            sums.append(dot_tn(projs[half][:, g * N : (g + 1) * N], xw) * wide[2 + half : 3 + half])
        f_refs[g][...] = sums[0].astype(BF16)
        b_refs[g][...] = sums[1].astype(BF16)

        @pl.when(index == 0)
        def _():
            send_refs[g][...] = sums[0].astype(BF16)

        @pl.when(index != 0)
        def _():
            send_refs[g][...] = (wide[1:2] * sums[0] + sums[1]).astype(BF16)


def chain_kernel(count, stage, g, heads, got_ref, f_ref, b_ref, dec_ref, *refs):
    send_ref = refs[-1]
    width = f_ref.shape[1]
    index = lax.axis_index("ctx")

    @pl.when(index == stage)
    def _():
        state = dec_ref[0:1, :] * got_ref[:N, :].astype(F32) + f_ref[...].astype(F32)
        send_ref[...] = state.astype(BF16)

    @pl.when(index == count - 1 - stage)
    def _():
        decay = jnp.ones((1, width), F32)
        for r, ref in enumerate(refs[:-1]):
            one = passed_decay(ref, ref.shape[0] - EXTRA, heads, width, g)
            if count != 4:
                one = jnp.where(ring_source(index, count, r + 1) > index, one, 1.0)
            decay = decay * one
        inner = decay * f_ref[...].astype(F32) + got_ref[:N, :].astype(F32)
        send_ref[...] = (dec_ref[1:2, :] * inner + b_ref[...].astype(F32)).astype(BF16)


def local_kernel(
    count, groups, docs_ref, x_ref, gate_ref, b_ref, c_ref, skip_ref, ec_ref, *refs
):
    xw_refs, pre_refs, reach_refs, sx_refs = (
        refs[k * groups : (k + 1) * groups] for k in range(4)
    )
    x_here, gate_here, sems = refs[4 * groups :]
    heads, rows = ec_ref.shape
    stretch = rows // 2
    width = x_ref.shape[1] // groups
    index = lax.axis_index("ctx")
    moves = []
    for g in range(groups):
        cols = pl.ds(g * width, width)
        moves.append(
            [
                pltpu.make_async_copy(x_ref.at[:, cols], x_here.at[g], sems.at[0, g]),
                pltpu.make_async_copy(gate_ref.at[:, cols], gate_here.at[g], sems.at[1, g]),
            ]
        )
        for move in moves[g]:
            move.start()
    triangle = lower_triangle(stretch)
    skip = as_column(skip_ref[...])
    step = 16
    masks = []
    for half in range(2):
        block = own_block(index, count, half)
        row = doc_row(docs_ref, block, stretch)
        column = as_column(row)
        reached = jnp.where(column == prior_doc(docs_ref, block, stretch).astype(F32), 1.0, 0.0)
        masks.append((triangle & (column == row.astype(F32)), reached))
    for g in range(groups):
        proj = slice(g * N, (g + 1) * N)
        matrix = spread_matrix(heads, width, g * (heads // groups))
        wide_skip = spread(skip, matrix)
        for half in range(2):
            sl = slice(half * stretch, (half + 1) * stretch)
            near, reached = masks[half]
            gram = dot_nt(c_ref[sl, proj], b_ref[sl, proj])
            gram = jnp.where(near, gram, 0.0).astype(BF16)
            wide = spread(ec_ref[:, sl], matrix)
            inner = jnp.dot(gram, xw_refs[g][sl, :], preferred_element_type=F32)
            if half == 0:
                for move in moves[g]:
                    move.wait()
            for k in range(0, stretch, step):
                at = slice(half * stretch + k, half * stretch + k + step)
                here = slice(k, k + step)
                x = x_here[g, at, :].astype(F32)
                gate = gate_here[g, at, :].astype(F32)
                silu = gate / (1.0 + jnp.exp(-gate))
                fade = wide[here] * silu
                sx = silu * x
                sx_refs[g][at, :] = sx
                pre_refs[g][at, :] = inner[here] * fade + wide_skip * sx
                reach_refs[g][at, :] = reached[here] * fade


def merge_kernel(count, state_ref, kv_ref, out_ref):
    index = lax.axis_index("ctx")
    outer = (index == 0) | (index == count - 1)
    wide = kv_ref.shape[1]
    rows = kv_ref.shape[0] - EXTRA
    stretch = rows // 2

    @pl.when(outer)
    def _():
        out_ref[:N, :] = state_ref[...]
        out_ref[N:, :] = jnp.zeros((EXTRA, out_ref.shape[1]), BF16)

    @pl.when(jnp.logical_not(outer))
    def _():
        out_ref[:stretch, :wide] = kv_ref[:stretch, :]
        out_ref[:stretch, wide:] = kv_ref[stretch:rows, :]
        out_ref[stretch:, :wide] = kv_ref[rows:, :]
        out_ref[stretch:, wide:] = jnp.zeros((EXTRA, wide), BF16)


def arrivals(index, count, refs):
    if count != 4:
        return [(ring_source(index, count, r + 1), [(None, refs[r])]) for r in range(count - 1)]
    near, own_of_middle, next_of_middle, far, farther = refs
    middle = (index == 1) | (index == 2)
    low = index < 2
    return [
        (index ^ 1, [(None, near)]),
        (
            jnp.where(low, 2, 1),
            [(middle, own_of_middle), (jnp.logical_not(middle), far)],
        ),
        (
            jnp.where(low, 3, 0),
            [(middle, next_of_middle), (jnp.logical_not(middle), farther)],
        ),
    ]


def attention_kernel(count, per, stack, g, docs_ref, q_ref, k_ref, v_ref, *refs):
    others = count - 1
    sent = 5 if count == 4 else others
    out_ref, kt, vt, bias_f, bias_b, bias_a = refs[-6:]
    rows = q_ref.shape[0]
    stretch = rows // 2
    index = lax.axis_index("ctx")
    last = 2 * count - 1
    kv_width = refs[0].shape[1] // 2
    row_f = doc_row(docs_ref, index, stretch).astype(F32)
    row_b = doc_row(docs_ref, last - index, stretch).astype(F32)
    col_f = as_column(row_f)
    col_b = as_column(row_b)
    triangle = lower_triangle(stretch)

    def tile(k):
        return slice(k * stretch, (k + 1) * stretch)

    bias_f[...] = jnp.where(triangle & (col_f == row_f), 0.0, MASKED)
    bias_b[:, tile(0)] = jnp.where(col_b == row_f, 0.0, MASKED)
    bias_b[:, tile(1)] = jnp.where(triangle & (col_b == row_b), 0.0, MASKED)
    vt[:, DH:] = jnp.ones((vt.shape[0], DH), BF16)
    here = slice(g * DH, (g + 1) * DH)
    kt[tile(0), :] = k_ref[:stretch, here]
    vt[tile(0), :DH] = v_ref[:stretch, here]
    kt[tile(count), :] = k_ref[stretch:, here]
    vt[tile(count), :DH] = v_ref[stretch:, here]
    lower = []
    for r, (source, places) in enumerate(arrivals(index, count, refs[:sent])):
        lower.append(source < index)
        for condition, ref in places:

            def fetch(ref=ref, r=r):
                folded = ref.shape[1] > 2 * kv_width
                gap = jnp.where(lower[r], 0, 2 * kv_width if folded else stretch)
                for table, first in ((kt, g * DH), (vt, kv_width + g * DH)):
                    front = ref[:stretch, first : first + DH]
                    if folded:
                        own = ref[:stretch, pl.ds(pl.multiple_of(first + gap, DH), DH)]
                    else:
                        own = ref[pl.ds(pl.multiple_of(gap, stretch), stretch), first : first + DH]
                    table[tile(1 + r), :DH] = own
                    table[tile(count + 1 + r), :DH] = front

            if condition is None:
                fetch()
            else:
                pl.when(condition)(fetch)
        key_f = doc_row(docs_ref, source, stretch).astype(F32)
        key_a = doc_row(docs_ref, jnp.where(lower[r], source, last - source), stretch).astype(F32)
        bias_b[:, tile(2 + r)] = jnp.where(col_b == key_f, 0.0, MASKED)
        bias_a[:, tile(r)] = jnp.where(jnp.where(lower[r], col_f, col_b) == key_a, 0.0, MASKED)

    factor = math.log2(math.e) / math.sqrt(DH)
    tall = stack * stretch
    half_keys = count * stretch

    def stacked(first, base):
        return jnp.concatenate(
            [
                q_ref[base : base + stretch, (g * per + first + j) * DH : (g * per + first + j + 1) * DH]
                for j in range(stack)
            ],
            axis=0,
        )

    def biased(score, bias):
        size = score.shape[1]
        return (score.reshape(stack, stretch, size) + bias[None]).reshape(tall, size)

    for first in range(0, per, stack):
        s_f = dot_nt(stacked(first, 0), kt[:half_keys, :])
        s_b = dot_nt(stacked(first, stretch), kt[...])
        t_f = biased(s_f[:, tile(0)], bias_f[...])
        t_b = [biased(s_b[:, tile(0)], bias_b[:, tile(0)])]
        for k in range(1, count + 1):
            t_b.append(biased(s_b[:, tile(count + k - 1)], bias_b[:, tile(k)]))
        t_a = []
        for r in range(others):
            score = jnp.where(lower[r], s_f[:, tile(1 + r)], s_b[:, tile(1 + r)])
            t_a.append(biased(score, bias_a[:, tile(r)]))
        best_f = t_f
        best_b = functools.reduce(jnp.maximum, t_b)
        for r in range(others):
            best_f = jnp.maximum(best_f, jnp.where(lower[r], t_a[r], MASKED))
            best_b = jnp.maximum(best_b, jnp.where(lower[r], MASKED, t_a[r]))
        top_f = jnp.max(best_f, axis=1, keepdims=True)
        top_b = jnp.max(best_b, axis=1, keepdims=True)
        w_f = [jnp.exp2((t_f - top_f) * factor).astype(BF16)]
        w_b = [jnp.exp2((t - top_b) * factor).astype(BF16) for t in t_b]
        w_x = []
        for r in range(others):
            top = jnp.where(lower[r], top_f, top_b)
            w = jnp.exp2((t_a[r] - top) * factor)
            w_f.append(jnp.where(lower[r], w, 0.0).astype(BF16))
            w_x.append(jnp.where(lower[r], 0.0, w).astype(BF16))
        w_b = w_b[:1] + w_x + w_b[1:]
        out_f = jnp.dot(
            jnp.concatenate(w_f, axis=1), vt[:half_keys, :], preferred_element_type=F32
        )
        out_b = jnp.dot(jnp.concatenate(w_b, axis=1), vt[...], preferred_element_type=F32)
        for half, out in enumerate((out_f, out_b)):
            result = (out[:, :DH] / out[:, DH:]).astype(BF16)
            for j in range(stack):
                cols = slice((first + j) * DH, (first + j + 1) * DH)
                out_ref[tile(half), cols] = result[tile(j)]


def final_kernel(
    count,
    g,
    groups,
    loss_scale,
    heads,
    pre_ref,
    reach_ref,
    sx_ref,
    c_ref,
    teacher_ref,
    gain_ref,
    f_ref,
    dec_ref,
    *refs,
):
    others = count - 1
    got = refs[:others]
    sent = 5 if count == 4 else others
    kv_refs = refs[others : others + sent]
    before = refs[others + sent] if g else None
    proj = slice(g * N, (g + 1) * N)
    first_lane = g * pre_ref.shape[1]
    out_ref, grad_ref, front, back, flow, gated_ref, sums, gain_acc, skip_acc = refs[-9:]
    rows, width = pre_ref.shape
    stretch = rows // 2
    index = lax.axis_index("ctx")
    tile = 128
    step = 16

    @pl.when(index == 0)
    def _():
        front[...] = jnp.zeros_like(front)

    @pl.when(index == count - 1)
    def _():
        back[...] = jnp.zeros_like(back)

    for r in range(1, count):

        @pl.when(index == r)
        def _():
            front[...] = got[r - 1][:N, :]

        @pl.when(index == count - 1 - r)
        def _():
            back[...] = got[r - 1][:N, :]

    sources, rows_in = [], []
    for source, places in arrivals(index, count, kv_refs):
        found = [ref[ref.shape[0] - EXTRA :, :heads].astype(F32) for _, ref in places]
        if len(found) == 2:
            found = [jnp.where(places[0][0], found[0], found[1])]
        sources.append(source)
        rows_in.append(found[0])
    spread_rows = spread_matrix(heads, width, g * (width // P_SIZE))
    wide = jnp.dot(
        jnp.concatenate(rows_in, axis=0).astype(BF16), spread_rows, preferred_element_type=F32
    )
    d_in = jnp.ones((1, width), F32)
    for r, source in enumerate(sources):
        one = wide[r * EXTRA : r * EXTRA + 1] + wide[r * EXTRA + 1 : r * EXTRA + 2]
        d_in = d_in * jnp.where(source > index, one, 1.0)
    through = dec_ref[0:1, :] * front[...].astype(F32) + f_ref[...].astype(F32)
    entering = (d_in * through + back[...].astype(F32)).astype(BF16)
    flow[:stretch, :] = jnp.dot(c_ref[:stretch, proj], front[...], preferred_element_type=F32)
    flow[stretch:, :] = jnp.dot(c_ref[stretch:, proj], entering, preferred_element_type=F32)
    gain_acc[...] = jnp.zeros_like(gain_acc)
    skip_acc[...] = jnp.zeros_like(skip_acc)

    @pl.loop(0, rows // step, unroll=2)
    def _(k):
        sl = pl.ds(pl.multiple_of(k * step, step), step)
        totals = [jnp.zeros((step, tile), F32)] * 3
        for j in range(0, width, tile):
            cols = slice(j, j + tile)
            gated = pre_ref[sl, cols] + reach_ref[sl, cols] * flow[sl, cols]
            gated_ref[sl, cols] = gated
            scaled = gated * gain_ref[:, first_lane + j : first_lane + j + tile]
            totals[0] += gated * gated
            totals[1] += scaled * scaled
            totals[2] += scaled * teacher_ref[sl, cols].astype(F32)
        for k3 in range(3):
            sums[sl, k3 * tile : (k3 + 1) * tile] = totals[k3]

    square, weighted, crossed = (
        jnp.sum(sums[:, k3 * tile : (k3 + 1) * tile], axis=1, keepdims=True) * (1.0 / width)
        for k3 in range(3)
    )
    scale = lax.rsqrt(square + EPS)
    push_scale = 2.0 * loss_scale
    mean = push_scale * scale * (scale * weighted - crossed)
    sums[:, :tile] = jnp.broadcast_to(scale, (rows, tile))
    sums[:, tile : 2 * tile] = jnp.broadcast_to(mean, (rows, tile))

    @pl.loop(0, rows // step, unroll=2)
    def _(k):
        sl = pl.ds(pl.multiple_of(k * step, step), step)
        scale = sums[sl, :tile]
        mean = sums[sl, tile : 2 * tile]
        for j in range(0, width, tile):
            cols = slice(j, j + tile)
            gain = gain_ref[:, first_lane + j : first_lane + j + tile]
            unit = gated_ref[sl, cols] * scale
            normed = unit * gain
            out_ref[sl, cols] = normed.astype(BF16)
            push = (normed - teacher_ref[sl, cols].astype(F32)) * push_scale
            by_gain = push * unit
            by_skip = (push * gain - unit * mean) * (scale * sx_ref[sl, cols])
            gain_acc[:, cols] += by_gain[:8] + by_gain[8:]
            skip_acc[:, cols] += by_skip[:8] + by_skip[8:]

    row = lax.broadcasted_iota(jnp.int32, (tile, width), 0)
    lane = lax.broadcasted_iota(jnp.int32, (tile, width), 1)
    matrix = jnp.where(row == lane // P_SIZE + g * (width // P_SIZE), 1.0, 0.0).astype(BF16)
    hi, lo = parts(skip_acc[...])
    by_head = jnp.sum(dot_nt(hi, matrix) + dot_nt(lo, matrix), axis=0, keepdims=True)
    grad_ref[...] = jnp.zeros_like(grad_ref)
    if g:
        grad_ref[:g, :] = before[:g, :]
        by_head += before[groups : groups + 1, :tile]
    grad_ref[g : g + 1, :] = jnp.sum(gain_acc[...], axis=0, keepdims=True)
    grad_ref[groups : groups + 1, :tile] = by_head


def writing_kernel(*refs):
    parts_in, out_ref, sems = refs[:-2], refs[-2], refs[-1]
    width = parts_in[0].shape[1]
    moves = [
        pltpu.make_async_copy(part, out_ref.at[:, pl.ds(k * width, width)], sems.at[k])
        for k, part in enumerate(parts_in)
    ]
    for move in moves:
        move.start()
    for move in moves:
        move.wait()


def closing_kernel(a_ref, b_ref, gain_ref, skip_ref):
    total = a_ref[...] + b_ref[...]
    groups, width = total.shape[0] - 1, total.shape[1]
    for g in range(groups):
        gain_ref[:, g * width : (g + 1) * width] = total[g : g + 1, :]
    skip_ref[...] = total[groups : groups + 1, : skip_ref.shape[1]]


def exchange(part, shift):
    axes = ("dp", "ctx")
    size = lax.axis_size(axes)
    return lax.ppermute(part, axes, [(d, d ^ shift) for d in range(size)])


def body(
    queries,
    keys,
    values,
    doc_ids,
    inputs,
    gate_input,
    b_input,
    c_input,
    dt_raw,
    dt_bias,
    decay_log,
    skip,
    gain,
):
    count = lax.axis_size("ctx")
    rows, features = queries.shape[1:]
    stretch = rows // 2
    kv_dev = keys.shape[2] // DH
    per_kv = queries.shape[2] // keys.shape[2]
    groups = b_input.shape[2] // N
    heads = features // P_SIZE
    width = features // groups
    length = doc_ids.shape[1]
    others = count - 1
    loss_scale = 1.0 / (lax.axis_size("dp") * count * rows)
    x, gate, bmat, cmat = inputs[0], gate_input[0], b_input[0], c_input[0]
    struct = jax.ShapeDtypeStruct

    def in_hbm(*arrays):
        return [pltpu.with_memory_space_constraint(array, pltpu.HBM) for array in arrays]

    def write(*pieces):
        return pl.pallas_call(
            writing_kernel,
            out_shape=struct((rows, features), BF16),
            in_specs=[VMEM] * len(pieces),
            out_specs=pl.BlockSpec(memory_space=pl.ANY),
            scratch_shapes=[pltpu.SemaphoreType.DMA((len(pieces),))],
            compiler_params=params(2),
            cost_estimate=cost(0, 4 * rows * features),
            name="writing",
        )(*pieces)

    state = struct((N, width), BF16)
    payload = struct((N + EXTRA, width), BF16)
    outs = pl.pallas_call(
        functools.partial(opening_kernel, count, groups),
        out_shape=(
            struct((rows + EXTRA, 2 * kv_dev * DH), BF16),
            struct((heads, rows), F32),
            *([struct((rows, width), BF16)] * groups),
            *([struct((8, width), F32)] * groups),
            *([state] * (2 * groups)),
            *([state] * groups),
        ),
        in_specs=[VMEM] * 8,
        out_specs=(VMEM,) * (2 + 5 * groups),
        compiler_params=params(16),
        cost_estimate=cost(4 * rows * features * N, 8 * rows * features),
        name="opening",
    )(
        *in_hbm(
            doc_ids,
            keys[0],
            values[0],
            x,
            bmat,
            dt_raw[0].T,
            dt_bias.reshape(1, heads),
            decay_log.reshape(1, heads),
        )
    )
    kv, ec = outs[:2]
    xw, dec, f_parts, b_parts, send = (
        outs[2 + k * groups : 2 + (k + 1) * groups] for k in range(5)
    )

    local = pl.pallas_call(
        functools.partial(local_kernel, count, groups),
        out_shape=(struct((rows, width), F32),) * (3 * groups),
        in_specs=[
            VMEM,
            *[pl.BlockSpec(memory_space=pl.ANY)] * 2,
            *[VMEM] * (4 + groups),
        ],
        out_specs=(VMEM,) * (3 * groups),
        scratch_shapes=[
            pltpu.VMEM((groups, rows, width), BF16),
            pltpu.VMEM((groups, rows, width), BF16),
            pltpu.SemaphoreType.DMA((2, groups)),
        ],
        compiler_params=params(16),
        cost_estimate=cost(2 * rows * features * N, 16 * rows * features),
        name="local",
    )(*in_hbm(doc_ids, x, gate, bmat, cmat, skip.reshape(1, heads)), ec, *xw)

    send = list(send)
    got = [[] for _ in range(groups)]
    def passed_on(g, stage, needed):
        return pl.pallas_call(
            functools.partial(chain_kernel, count, stage, g, heads),
            out_shape=state,
            in_specs=[VMEM] * (4 + len(needed)),
            out_specs=VMEM,
            compiler_params=params(6),
            cost_estimate=cost(16384 * N * width, 8 * N * width),
            name="chain",
        )(got[g][-1], f_parts[g], b_parts[g], dec[g], *needed)

    if count == 4:
        inward, outward, across = [(0, 1), (3, 2)], [(1, 0), (2, 3)], [(1, 2), (2, 1)]
        near = lax.ppermute(kv, "ctx", inward + outward)
        middle = lax.ppermute(kv, "ctx", across)
        middle, *local = lax.optimization_barrier((middle, *local))
        beyond = lax.ppermute(near, "ctx", across)
        send[-1] = pl.pallas_call(
            functools.partial(merge_kernel, count),
            out_shape=payload,
            in_specs=[VMEM] * 2,
            out_specs=VMEM,
            compiler_params=params(4),
            cost_estimate=cost(0, 4 * N * width),
            name="merge",
        )(send[-1], middle)
        far = lax.ppermute(send[-1], "ctx", inward + outward)
        got[-1].append(far)
        if groups > 1:
            got[0].append(lax.ppermute(send[0], "ctx", [(0, 1), (3, 2)]))
            send[0] = passed_on(0, 1, [near])
            beyond, _ = lax.optimization_barrier((beyond, send[0]))
            got[0].append(lax.ppermute(send[0], "ctx", across))
        farther = lax.ppermute(beyond, "ctx", outward)
        kv_got = [near, middle, beyond, far, farther]
    else:
        ring = ring_order(count)
        ring_pairs = [(ring[d], ring[(d + 1) % count]) for d in range(count)]
        kv_got = [kv]
        for _ in range(others):
            kv_got.append(lax.ppermute(kv_got[-1], "ctx", ring_pairs))
        kv_got = kv_got[1:]
    stack = 4 if per_kv % 4 == 0 and count <= 4 else 1
    targets = [
        pl.pallas_call(
            functools.partial(attention_kernel, count, per_kv, stack, g),
            out_shape=struct((rows, per_kv * DH), BF16),
            in_specs=[VMEM] * (4 + len(kv_got)),
            out_specs=VMEM,
            scratch_shapes=[
                pltpu.VMEM((2 * count * stretch, DH), BF16),
                pltpu.VMEM((2 * count * stretch, 2 * DH), BF16),
                pltpu.VMEM((stretch, stretch), F32),
                pltpu.VMEM((stretch, (count + 1) * stretch), F32),
                pltpu.VMEM((stretch, others * stretch), F32),
            ],
            compiler_params=params(24),
            cost_estimate=cost(
                4 * (2 * count + 1) * stretch * stretch * per_kv * DH, 8 * rows * per_kv * DH
            ),
            name="attention",
        )(doc_ids, queries[0], keys[0], values[0], *kv_got)
        for g in range(kv_dev)
    ]
    for r in range(1, count):
        for g in range(groups):
            if len(got[g]) >= r:
                continue
            if r == 3 and g == groups - 1:
                got[g][-1], targets[0] = lax.optimization_barrier((got[g][-1], targets[0]))
            if r > 1:
                if count == 4:
                    needed = [near] if r == 2 else [middle, beyond]
                else:
                    needed = kv_got
                send[g] = passed_on(g, r - 1, needed)
            pairs = [(r - 1, r), (count - r, count - r - 1)]
            got[g].append(lax.ppermute(send[g], "ctx", pairs))

    got[0][-1], *targets = lax.optimization_barrier((got[0][-1], *targets))
    normed, grads = [], None
    for g in range(groups):
        more = [] if grads is None else [grads]
        made, grads = pl.pallas_call(
            functools.partial(final_kernel, count, g, groups, loss_scale, heads),
            out_shape=(struct((rows, width), BF16), struct((groups + 1, width), F32)),
            in_specs=[VMEM] * (8 + others + len(kv_got) + len(more)),
            out_specs=(VMEM,) * 2,
            scratch_shapes=[
                pltpu.VMEM((N, width), BF16),
                pltpu.VMEM((N, width), BF16),
                pltpu.VMEM((rows, width), F32),
                pltpu.VMEM((rows, width), F32),
                pltpu.VMEM((rows, 3 * 128), F32),
                pltpu.VMEM((8, width), F32),
                pltpu.VMEM((8, width), F32),
            ],
            compiler_params=params(16),
            cost_estimate=cost(2 * rows * width * N, 20 * rows * width),
            name="final",
        )(
            *local[g::groups],
            cmat,
            targets[g],
            gain.reshape(1, features),
            f_parts[g],
            dec[g],
            *got[g],
            *kv_got,
            *more,
        )
        normed.append(made)
    teacher, student = write(*targets), write(*normed)
    shifts = [1 << k for k in range((lax.axis_size("dp") * count).bit_length() - 1)]
    if count >= 4:
        grads = (grads + exchange(grads, 1)) + (exchange(grads, 2) + exchange(grads, 3))
        shifts = shifts[2:]
    for shift in shifts[:-1]:
        grads = grads + exchange(grads, shift)
    grad_gain, grad_skip = pl.pallas_call(
        closing_kernel,
        out_shape=(struct((1, features), F32), struct((1, heads), F32)),
        in_specs=[VMEM] * 2,
        out_specs=(VMEM,) * 2,
        compiler_params=params(2),
        name="closing",
    )(grads, exchange(grads, shifts[-1]))
    return (teacher[None], student[None], grad_gain[0], grad_skip[0])


def solution(mesh):
    rows = P("dp", "ctx", "head")
    in_specs = (
        rows,
        rows,
        rows,
        P("dp", None),
        rows,
        rows,
        rows,
        rows,
        rows,
        P("head"),
        P("head"),
        P("head"),
        P("head"),
    )
    out_specs = (rows, rows, P("head"), P("head"))
    return jax.shard_map(body, mesh=mesh, in_specs=in_specs, out_specs=out_specs, check_vma=False)
```

```python
import functools
import math

import jax
import jax.numpy as jnp
from jax import lax
from jax.experimental import pallas as pl
from jax.experimental.pallas import tpu as pltpu
from jax.sharding import PartitionSpec as P

DH = 128
P_SIZE = 64
N = 128
EXTRA = 16
EPS = 1e-05
MASKED = -1e30
F32 = jnp.float32
BF16 = jnp.bfloat16
VMEM = pl.BlockSpec(memory_space=pltpu.VMEM)


def params(mib):
    return pltpu.CompilerParams(vmem_limit_bytes=mib << 20)


def cost(flops, size):
    return pl.CostEstimate(flops=flops, bytes_accessed=size, transcendentals=0)


def parts(v):
    hi = v.astype(BF16)
    return hi, (v - hi.astype(F32)).astype(BF16)


def spread_matrix(heads, width, first):
    row = lax.broadcasted_iota(jnp.int32, (heads, width), 0)
    lane = lax.broadcasted_iota(jnp.int32, (heads, width), 1)
    return jnp.where(row == (lane // P_SIZE) + first, 1.0, 0.0).astype(BF16)


def dot_nt(a, b):
    return lax.dot_general(a, b, (((1,), (1,)), ((), ())), preferred_element_type=F32)


def dot_tn(a, b):
    return lax.dot_general(a, b, (((0,), (0,)), ((), ())), preferred_element_type=F32)


def spread(v, matrix):
    return dot_tn(jnp.concatenate(parts(v), axis=0), jnp.concatenate([matrix, matrix], axis=0))


def doc_row(docs_ref, block, stretch):
    return docs_ref[:, pl.ds(pl.multiple_of(block * stretch, stretch), stretch)]


def as_column(row):
    size = row.shape[1]
    r = lax.broadcasted_iota(jnp.int32, (size, size), 0)
    c = lax.broadcasted_iota(jnp.int32, (size, size), 1)
    return jnp.sum(jnp.where(r == c, row.astype(F32), 0.0), axis=1, keepdims=True)


def lower_triangle(size):
    r = lax.broadcasted_iota(jnp.int32, (size, size), 0)
    c = lax.broadcasted_iota(jnp.int32, (size, size), 1)
    return r >= c


def prior_doc(docs_ref, block, stretch):
    before = doc_row(docs_ref, jnp.maximum(block - 1, 0), stretch)[:, stretch - 1 :]
    return jnp.where(block > 0, before, -1)


def own_block(index, count, half):
    return index if half == 0 else 2 * count - 1 - index


def ring_order(count):
    return [0] + list(range(1, count, 2)) + list(range(2, count, 2))[::-1]


def ring_source(index, count, steps):
    order = ring_order(count)
    source = jnp.int32(0)
    for place, member in enumerate(order):
        source = jnp.where(index == member, order[(place - steps) % count], source)
    return source


def passed_decay(ref, first, heads, width, g):
    matrix = spread_matrix(heads, width, g * (width // P_SIZE))
    wide = jnp.dot(ref[first : first + EXTRA, :heads], matrix, preferred_element_type=F32)
    return wide[0:1] + wide[1:2]


def opening_kernel(
    count,
    groups,
    docs_ref,
    k_ref,
    v_ref,
    x_ref,
    b_ref,
    dt_ref,
    bias_ref,
    log_ref,
    kv_ref,
    ec_ref,
    *outs,
):
    xw_refs, dec_refs, f_refs, b_refs, send_refs = (
        outs[k * groups : (k + 1) * groups] for k in range(5)
    )
    heads, rows = dt_ref.shape
    stretch = rows // 2
    width = x_ref.shape[1] // groups
    kv_width = k_ref.shape[1]
    index = lax.axis_index("ctx")
    kv_ref[:rows, :kv_width] = k_ref[...]
    kv_ref[:rows, kv_width:] = v_ref[...]
    kv_ref[rows:, :] = jnp.zeros((EXTRA, 2 * kv_width), BF16)
    slope = jnp.exp(as_column(log_ref[...]))
    bias = as_column(bias_ref[...])
    lane = lax.broadcasted_iota(jnp.int32, (heads, 8), 1)
    ends = jnp.zeros((heads, 8), F32)
    loads = []
    projs = []
    raw = jnp.concatenate([dt_ref[:, :stretch] + bias, dt_ref[:, stretch:] + bias], axis=0)
    dt_both = jnp.maximum(raw, 0.0) + jnp.log1p(jnp.exp(-jnp.abs(raw)))
    rate = -dt_both * jnp.concatenate([slope, slope], axis=0)
    hi, lo = parts(rate)
    rest = (rate - hi.astype(F32) - lo.astype(F32)).astype(BF16)
    triangle = jnp.where(lower_triangle(stretch), 1.0, 0.0).astype(BF16)
    cum_both = dot_nt(
        jnp.concatenate([hi, lo, rest], axis=1), jnp.concatenate([triangle] * 3, axis=1)
    )
    grown = jnp.exp(cum_both)
    load_both = jnp.exp(-cum_both) * dt_both
    for half in range(2):
        block = own_block(index, count, half)
        sl = slice(half * stretch, (half + 1) * stretch)
        here = slice(half * heads, (half + 1) * heads)
        ec_ref[:, sl] = grown[here]
        loads.append(load_both[here])
        final = grown[here, stretch - 1 :]
        row = doc_row(docs_ref, block, stretch)
        last = row[:, stretch - 1 :]
        kept = jnp.where(last == prior_doc(docs_ref, block, stretch), 1.0, 0.0)
        ends = jnp.where(lane == half, final * kept, ends)
        ends = jnp.where(lane == 2 + half, final, ends)
        same = jnp.where(as_column(row) == last.astype(F32), 1.0, 0.0)
        projs.append((b_ref[sl, :].astype(F32) * same).astype(BF16))
    both = ends[:, 0:1] * ends[:, 1:2]
    r = lax.broadcasted_iota(jnp.int32, (heads, heads), 0)
    c = lax.broadcasted_iota(jnp.int32, (heads, heads), 1)
    hi, lo = parts(jnp.sum(jnp.where(r == c, both, 0.0), axis=0, keepdims=True))
    kv_ref[rows:, :heads] = jnp.concatenate(
        [hi, lo, jnp.zeros((EXTRA - 2, heads), BF16)], axis=0
    )
    for g in range(groups):
        cols = slice(g * width, (g + 1) * width)
        matrix = spread_matrix(heads, width, g * (heads // groups))
        wide = spread(ends, matrix)
        dec_refs[g][...] = wide
        sums = []
        for half in range(2):
            sl = slice(half * stretch, (half + 1) * stretch)
            xw = (x_ref[sl, cols].astype(F32) * spread(loads[half], matrix)).astype(BF16)
            xw_refs[g][sl, :] = xw
            sums.append(dot_tn(projs[half][:, g * N : (g + 1) * N], xw) * wide[2 + half : 3 + half])
        f_refs[g][...] = sums[0].astype(BF16)
        b_refs[g][...] = sums[1].astype(BF16)

        @pl.when(index == 0)
        def _():
            send_refs[g][...] = sums[0].astype(BF16)

        @pl.when(index != 0)
        def _():
            send_refs[g][...] = (wide[1:2] * sums[0] + sums[1]).astype(BF16)


def chain_kernel(count, stage, g, heads, got_ref, f_ref, b_ref, dec_ref, *refs):
    send_ref = refs[-1]
    width = f_ref.shape[1]
    index = lax.axis_index("ctx")

    @pl.when(index == stage)
    def _():
        state = dec_ref[0:1, :] * got_ref[:N, :].astype(F32) + f_ref[...].astype(F32)
        send_ref[...] = state.astype(BF16)

    @pl.when(index == count - 1 - stage)
    def _():
        decay = jnp.ones((1, width), F32)
        for r, ref in enumerate(refs[:-1]):
            one = passed_decay(ref, ref.shape[0] - EXTRA, heads, width, g)
            if count != 4:
                one = jnp.where(ring_source(index, count, r + 1) > index, one, 1.0)
            decay = decay * one
        inner = decay * f_ref[...].astype(F32) + got_ref[:N, :].astype(F32)
        send_ref[...] = (dec_ref[1:2, :] * inner + b_ref[...].astype(F32)).astype(BF16)


def local_kernel(
    count, groups, docs_ref, x_ref, gate_ref, b_ref, c_ref, skip_ref, ec_ref, *refs
):
    xw_refs, pre_refs, reach_refs, sx_refs = (
        refs[k * groups : (k + 1) * groups] for k in range(4)
    )
    x_here, gate_here, sems = refs[4 * groups :]
    heads, rows = ec_ref.shape
    stretch = rows // 2
    width = x_ref.shape[1] // groups
    index = lax.axis_index("ctx")
    moves = []
    for g in range(groups):
        cols = pl.ds(g * width, width)
        moves.append(
            [
                pltpu.make_async_copy(x_ref.at[:, cols], x_here.at[g], sems.at[0, g]),
                pltpu.make_async_copy(gate_ref.at[:, cols], gate_here.at[g], sems.at[1, g]),
            ]
        )
        for move in moves[g]:
            move.start()
    triangle = lower_triangle(stretch)
    skip = as_column(skip_ref[...])
    step = 16
    masks = []
    for half in range(2):
        block = own_block(index, count, half)
        row = doc_row(docs_ref, block, stretch)
        column = as_column(row)
        reached = jnp.where(column == prior_doc(docs_ref, block, stretch).astype(F32), 1.0, 0.0)
        masks.append((triangle & (column == row.astype(F32)), reached))
    for g in range(groups):
        proj = slice(g * N, (g + 1) * N)
        matrix = spread_matrix(heads, width, g * (heads // groups))
        wide_skip = spread(skip, matrix)
        for half in range(2):
            sl = slice(half * stretch, (half + 1) * stretch)
            near, reached = masks[half]
            gram = dot_nt(c_ref[sl, proj], b_ref[sl, proj])
            gram = jnp.where(near, gram, 0.0).astype(BF16)
            wide = spread(ec_ref[:, sl], matrix)
            inner = jnp.dot(gram, xw_refs[g][sl, :], preferred_element_type=F32)
            if half == 0:
                for move in moves[g]:
                    move.wait()
            for k in range(0, stretch, step):
                at = slice(half * stretch + k, half * stretch + k + step)
                here = slice(k, k + step)
                x = x_here[g, at, :].astype(F32)
                gate = gate_here[g, at, :].astype(F32)
                silu = gate / (1.0 + jnp.exp(-gate))
                fade = wide[here] * silu
                sx = silu * x
                sx_refs[g][at, :] = sx
                pre_refs[g][at, :] = inner[here] * fade + wide_skip * sx
                reach_refs[g][at, :] = reached[here] * fade


def merge_kernel(count, state_ref, kv_ref, out_ref):
    index = lax.axis_index("ctx")
    outer = (index == 0) | (index == count - 1)
    wide = kv_ref.shape[1]
    rows = kv_ref.shape[0] - EXTRA
    stretch = rows // 2

    @pl.when(outer)
    def _():
        out_ref[:N, :] = state_ref[...]
        out_ref[N:, :] = jnp.zeros((EXTRA, out_ref.shape[1]), BF16)

    @pl.when(jnp.logical_not(outer))
    def _():
        out_ref[:stretch, :wide] = kv_ref[:stretch, :]
        out_ref[:stretch, wide:] = kv_ref[stretch:rows, :]
        out_ref[stretch:, :wide] = kv_ref[rows:, :]
        out_ref[stretch:, wide:] = jnp.zeros((EXTRA, wide), BF16)


def arrivals(index, count, refs):
    if count != 4:
        return [(ring_source(index, count, r + 1), [(None, refs[r])]) for r in range(count - 1)]
    near, own_of_middle, next_of_middle, far, farther = refs
    middle = (index == 1) | (index == 2)
    low = index < 2
    return [
        (index ^ 1, [(None, near)]),
        (
            jnp.where(low, 2, 1),
            [(middle, own_of_middle), (jnp.logical_not(middle), far)],
        ),
        (
            jnp.where(low, 3, 0),
            [(middle, next_of_middle), (jnp.logical_not(middle), farther)],
        ),
    ]


def attention_kernel(count, per, stack, g, docs_ref, q_ref, k_ref, v_ref, *refs):
    others = count - 1
    sent = 5 if count == 4 else others
    out_ref, kt, vt, vf, bias_f, bias_b, bias_a = refs[-7:]
    rows = q_ref.shape[0]
    stretch = rows // 2
    index = lax.axis_index("ctx")
    last = 2 * count - 1
    kv_width = refs[0].shape[1] // 2
    row_f = doc_row(docs_ref, index, stretch).astype(F32)
    row_b = doc_row(docs_ref, last - index, stretch).astype(F32)
    col_f = as_column(row_f)
    col_b = as_column(row_b)
    triangle = lower_triangle(stretch)

    def tile(k):
        return slice(k * stretch, (k + 1) * stretch)

    bias_f[...] = jnp.where(triangle & (col_f == row_f), 0.0, MASKED)
    bias_b[:, tile(0)] = jnp.where(col_b == row_f, 0.0, MASKED)
    bias_b[:, tile(1)] = jnp.where(triangle & (col_b == row_b), 0.0, MASKED)
    vt[:, DH:] = jnp.ones((vt.shape[0], DH), BF16)
    here = slice(g * DH, (g + 1) * DH)
    kt[tile(0), :] = k_ref[:stretch, here]
    vt[tile(0), :DH] = v_ref[:stretch, here]
    kt[tile(count), :] = k_ref[stretch:, here]
    vt[tile(count), :DH] = v_ref[stretch:, here]
    lower = []
    for r, (source, places) in enumerate(arrivals(index, count, refs[:sent])):
        lower.append(source < index)
        for condition, ref in places:

            def fetch(ref=ref, r=r):
                folded = ref.shape[1] > 2 * kv_width
                gap = jnp.where(lower[r], 0, 2 * kv_width if folded else stretch)
                for table, first in ((kt, g * DH), (vt, kv_width + g * DH)):
                    front = ref[:stretch, first : first + DH]
                    if folded:
                        own = ref[:stretch, pl.ds(pl.multiple_of(first + gap, DH), DH)]
                    else:
                        own = ref[pl.ds(pl.multiple_of(gap, stretch), stretch), first : first + DH]
                    table[tile(1 + r), :DH] = own
                    table[tile(count + 1 + r), :DH] = front

            if condition is None:
                fetch()
            else:
                pl.when(condition)(fetch)
        key_f = doc_row(docs_ref, source, stretch).astype(F32)
        key_a = doc_row(docs_ref, jnp.where(lower[r], source, last - source), stretch).astype(F32)
        bias_b[:, tile(2 + r)] = jnp.where(col_b == key_f, 0.0, MASKED)
        bias_a[:, tile(r)] = jnp.where(jnp.where(lower[r], col_f, col_b) == key_a, 0.0, MASKED)

    vf[...] = vt[: count * stretch, :]
    for r in range(others):

        @pl.when(lower[r])
        def _():
            vt[tile(1 + r), :] = jnp.zeros((stretch, 2 * DH), BF16)

        @pl.when(jnp.logical_not(lower[r]))
        def _():
            vf[tile(1 + r), :] = jnp.zeros((stretch, 2 * DH), BF16)

    factor = math.log2(math.e) / math.sqrt(DH)
    tall = stack * stretch
    half_keys = count * stretch

    def stacked(first, base):
        return jnp.concatenate(
            [
                q_ref[base : base + stretch, (g * per + first + j) * DH : (g * per + first + j + 1) * DH]
                for j in range(stack)
            ],
            axis=0,
        )

    def biased(score, bias):
        size = score.shape[1]
        return (score.reshape(stack, stretch, size) + bias[None]).reshape(tall, size)

    for first in range(0, per, stack):
        s_f = dot_nt(stacked(first, 0), kt[:half_keys, :])
        s_b = dot_nt(stacked(first, stretch), kt[...])
        t_f = biased(s_f[:, tile(0)], bias_f[...])
        t_b = [biased(s_b[:, tile(0)], bias_b[:, tile(0)])]
        for k in range(1, count + 1):
            t_b.append(biased(s_b[:, tile(count + k - 1)], bias_b[:, tile(k)]))
        t_a = []
        for r in range(others):
            score = jnp.where(lower[r], s_f[:, tile(1 + r)], s_b[:, tile(1 + r)])
            t_a.append(biased(score, bias_a[:, tile(r)]))
        best_f = t_f
        best_b = functools.reduce(jnp.maximum, t_b)
        for r in range(others):
            best_f = jnp.maximum(best_f, jnp.where(lower[r], t_a[r], MASKED))
            best_b = jnp.maximum(best_b, jnp.where(lower[r], MASKED, t_a[r]))
        top_f = jnp.max(best_f, axis=1, keepdims=True)
        top_b = jnp.max(best_b, axis=1, keepdims=True)
        w_f = [jnp.exp2((t_f - top_f) * factor).astype(BF16)]
        w_b = [jnp.exp2((t - top_b) * factor).astype(BF16) for t in t_b]
        w_x = []
        for r in range(others):
            top = jnp.where(lower[r], top_f, top_b)
            w = jnp.exp2((t_a[r] - top) * factor).astype(BF16)
            w_f.append(w)
            w_x.append(w)
        w_b = w_b[:1] + w_x + w_b[1:]
        out_f = jnp.dot(
            jnp.concatenate(w_f, axis=1), vf[...], preferred_element_type=F32
        )
        out_b = jnp.dot(jnp.concatenate(w_b, axis=1), vt[...], preferred_element_type=F32)
        for half, out in enumerate((out_f, out_b)):
            result = (out[:, :DH] / out[:, DH:]).astype(BF16)
            for j in range(stack):
                cols = slice((first + j) * DH, (first + j + 1) * DH)
                out_ref[tile(half), cols] = result[tile(j)]


def final_kernel(
    count,
    g,
    groups,
    loss_scale,
    heads,
    pre_ref,
    reach_ref,
    sx_ref,
    c_ref,
    teacher_ref,
    gain_ref,
    f_ref,
    dec_ref,
    *refs,
):
    others = count - 1
    got = refs[:others]
    sent = 5 if count == 4 else others
    kv_refs = refs[others : others + sent]
    before = refs[others + sent] if g else None
    proj = slice(g * N, (g + 1) * N)
    first_lane = g * pre_ref.shape[1]
    out_ref, grad_ref, front, back, flow, gated_ref, sums, gain_acc, skip_acc = refs[-9:]
    rows, width = pre_ref.shape
    stretch = rows // 2
    index = lax.axis_index("ctx")
    tile = 128
    step = 16

    @pl.when(index == 0)
    def _():
        front[...] = jnp.zeros_like(front)

    @pl.when(index == count - 1)
    def _():
        back[...] = jnp.zeros_like(back)

    for r in range(1, count):

        @pl.when(index == r)
        def _():
            front[...] = got[r - 1][:N, :]

        @pl.when(index == count - 1 - r)
        def _():
            back[...] = got[r - 1][:N, :]

    sources, rows_in = [], []
    for source, places in arrivals(index, count, kv_refs):
        found = [ref[ref.shape[0] - EXTRA :, :heads].astype(F32) for _, ref in places]
        if len(found) == 2:
            found = [jnp.where(places[0][0], found[0], found[1])]
        sources.append(source)
        rows_in.append(found[0])
    spread_rows = spread_matrix(heads, width, g * (width // P_SIZE))
    wide = jnp.dot(
        jnp.concatenate(rows_in, axis=0).astype(BF16), spread_rows, preferred_element_type=F32
    )
    d_in = jnp.ones((1, width), F32)
    for r, source in enumerate(sources):
        one = wide[r * EXTRA : r * EXTRA + 1] + wide[r * EXTRA + 1 : r * EXTRA + 2]
        d_in = d_in * jnp.where(source > index, one, 1.0)
    through = dec_ref[0:1, :] * front[...].astype(F32) + f_ref[...].astype(F32)
    entering = (d_in * through + back[...].astype(F32)).astype(BF16)
    flow[:stretch, :] = jnp.dot(c_ref[:stretch, proj], front[...], preferred_element_type=F32)
    flow[stretch:, :] = jnp.dot(c_ref[stretch:, proj], entering, preferred_element_type=F32)
    gain_acc[...] = jnp.zeros_like(gain_acc)
    skip_acc[...] = jnp.zeros_like(skip_acc)

    @pl.loop(0, rows // step, unroll=2)
    def _(k):
        sl = pl.ds(pl.multiple_of(k * step, step), step)
        totals = [jnp.zeros((step, tile), F32)] * 3
        for j in range(0, width, tile):
            cols = slice(j, j + tile)
            gated = pre_ref[sl, cols] + reach_ref[sl, cols] * flow[sl, cols]
            gated_ref[sl, cols] = gated
            scaled = gated * gain_ref[:, first_lane + j : first_lane + j + tile]
            totals[0] += gated * gated
            totals[1] += scaled * scaled
            totals[2] += scaled * teacher_ref[sl, cols].astype(F32)
        for k3 in range(3):
            sums[sl, k3 * tile : (k3 + 1) * tile] = totals[k3]

    square, weighted, crossed = (
        jnp.sum(sums[:, k3 * tile : (k3 + 1) * tile], axis=1, keepdims=True) * (1.0 / width)
        for k3 in range(3)
    )
    scale = lax.rsqrt(square + EPS)
    push_scale = 2.0 * loss_scale
    mean = push_scale * scale * (scale * weighted - crossed)
    sums[:, :tile] = jnp.broadcast_to(scale, (rows, tile))
    sums[:, tile : 2 * tile] = jnp.broadcast_to(mean, (rows, tile))

    @pl.loop(0, rows // step, unroll=2)
    def _(k):
        sl = pl.ds(pl.multiple_of(k * step, step), step)
        scale = sums[sl, :tile]
        mean = sums[sl, tile : 2 * tile]
        for j in range(0, width, tile):
            cols = slice(j, j + tile)
            gain = gain_ref[:, first_lane + j : first_lane + j + tile]
            unit = gated_ref[sl, cols] * scale
            normed = unit * gain
            out_ref[sl, cols] = normed.astype(BF16)
            push = (normed - teacher_ref[sl, cols].astype(F32)) * push_scale
            by_gain = push * unit
            by_skip = (push * gain - unit * mean) * (scale * sx_ref[sl, cols])
            gain_acc[:, cols] += by_gain[:8] + by_gain[8:]
            skip_acc[:, cols] += by_skip[:8] + by_skip[8:]

    row = lax.broadcasted_iota(jnp.int32, (tile, width), 0)
    lane = lax.broadcasted_iota(jnp.int32, (tile, width), 1)
    matrix = jnp.where(row == lane // P_SIZE + g * (width // P_SIZE), 1.0, 0.0).astype(BF16)
    hi, lo = parts(skip_acc[...])
    by_head = jnp.sum(dot_nt(hi, matrix) + dot_nt(lo, matrix), axis=0, keepdims=True)
    grad_ref[...] = jnp.zeros_like(grad_ref)
    if g:
        grad_ref[:g, :] = before[:g, :]
        by_head += before[groups : groups + 1, :tile]
    grad_ref[g : g + 1, :] = jnp.sum(gain_acc[...], axis=0, keepdims=True)
    grad_ref[groups : groups + 1, :tile] = by_head


def writing_kernel(*refs):
    parts_in, out_ref, sems = refs[:-2], refs[-2], refs[-1]
    width = parts_in[0].shape[1]
    moves = [
        pltpu.make_async_copy(part, out_ref.at[:, pl.ds(k * width, width)], sems.at[k])
        for k, part in enumerate(parts_in)
    ]
    for move in moves:
        move.start()
    for move in moves:
        move.wait()


def closing_kernel(a_ref, b_ref, gain_ref, skip_ref):
    total = a_ref[...] + b_ref[...]
    groups, width = total.shape[0] - 1, total.shape[1]
    for g in range(groups):
        gain_ref[:, g * width : (g + 1) * width] = total[g : g + 1, :]
    skip_ref[...] = total[groups : groups + 1, : skip_ref.shape[1]]


def exchange(part, shift):
    axes = ("dp", "ctx")
    size = lax.axis_size(axes)
    return lax.ppermute(part, axes, [(d, d ^ shift) for d in range(size)])


def body(
    queries,
    keys,
    values,
    doc_ids,
    inputs,
    gate_input,
    b_input,
    c_input,
    dt_raw,
    dt_bias,
    decay_log,
    skip,
    gain,
):
    count = lax.axis_size("ctx")
    rows, features = queries.shape[1:]
    stretch = rows // 2
    kv_dev = keys.shape[2] // DH
    per_kv = queries.shape[2] // keys.shape[2]
    groups = b_input.shape[2] // N
    heads = features // P_SIZE
    width = features // groups
    length = doc_ids.shape[1]
    others = count - 1
    loss_scale = 1.0 / (lax.axis_size("dp") * count * rows)
    x, gate, bmat, cmat = inputs[0], gate_input[0], b_input[0], c_input[0]
    struct = jax.ShapeDtypeStruct

    def in_hbm(*arrays):
        return [pltpu.with_memory_space_constraint(array, pltpu.HBM) for array in arrays]

    def write(*pieces):
        return pl.pallas_call(
            writing_kernel,
            out_shape=struct((rows, features), BF16),
            in_specs=[VMEM] * len(pieces),
            out_specs=pl.BlockSpec(memory_space=pl.ANY),
            scratch_shapes=[pltpu.SemaphoreType.DMA((len(pieces),))],
            compiler_params=params(2),
            cost_estimate=cost(0, 4 * rows * features),
            name="writing",
        )(*pieces)

    state = struct((N, width), BF16)
    payload = struct((N + EXTRA, width), BF16)
    outs = pl.pallas_call(
        functools.partial(opening_kernel, count, groups),
        out_shape=(
            struct((rows + EXTRA, 2 * kv_dev * DH), BF16),
            struct((heads, rows), F32),
            *([struct((rows, width), BF16)] * groups),
            *([struct((8, width), F32)] * groups),
            *([state] * (2 * groups)),
            *([state] * groups),
        ),
        in_specs=[VMEM] * 8,
        out_specs=(VMEM,) * (2 + 5 * groups),
        compiler_params=params(16),
        cost_estimate=cost(4 * rows * features * N, 8 * rows * features),
        name="opening",
    )(
        *in_hbm(
            doc_ids,
            keys[0],
            values[0],
            x,
            bmat,
            dt_raw[0].T,
            dt_bias.reshape(1, heads),
            decay_log.reshape(1, heads),
        )
    )
    kv, ec = outs[:2]
    xw, dec, f_parts, b_parts, send = (
        outs[2 + k * groups : 2 + (k + 1) * groups] for k in range(5)
    )

    local = pl.pallas_call(
        functools.partial(local_kernel, count, groups),
        out_shape=(struct((rows, width), F32),) * (3 * groups),
        in_specs=[
            VMEM,
            *[pl.BlockSpec(memory_space=pl.ANY)] * 2,
            *[VMEM] * (4 + groups),
        ],
        out_specs=(VMEM,) * (3 * groups),
        scratch_shapes=[
            pltpu.VMEM((groups, rows, width), BF16),
            pltpu.VMEM((groups, rows, width), BF16),
            pltpu.SemaphoreType.DMA((2, groups)),
        ],
        compiler_params=params(16),
        cost_estimate=cost(2 * rows * features * N, 16 * rows * features),
        name="local",
    )(*in_hbm(doc_ids, x, gate, bmat, cmat, skip.reshape(1, heads)), ec, *xw)

    send = list(send)
    got = [[] for _ in range(groups)]
    def passed_on(g, stage, needed):
        return pl.pallas_call(
            functools.partial(chain_kernel, count, stage, g, heads),
            out_shape=state,
            in_specs=[VMEM] * (4 + len(needed)),
            out_specs=VMEM,
            compiler_params=params(6),
            cost_estimate=cost(16384 * N * width, 8 * N * width),
            name="chain",
        )(got[g][-1], f_parts[g], b_parts[g], dec[g], *needed)

    if count == 4:
        inward, outward, across = [(0, 1), (3, 2)], [(1, 0), (2, 3)], [(1, 2), (2, 1)]
        near = lax.ppermute(kv, "ctx", inward + outward)
        middle = lax.ppermute(kv, "ctx", across)
        middle, *local = lax.optimization_barrier((middle, *local))
        beyond = lax.ppermute(near, "ctx", across)
        send[-1] = pl.pallas_call(
            functools.partial(merge_kernel, count),
            out_shape=payload,
            in_specs=[VMEM] * 2,
            out_specs=VMEM,
            compiler_params=params(4),
            cost_estimate=cost(0, 4 * N * width),
            name="merge",
        )(send[-1], middle)
        far = lax.ppermute(send[-1], "ctx", inward + outward)
        got[-1].append(far)
        if groups > 1:
            got[0].append(lax.ppermute(send[0], "ctx", [(0, 1), (3, 2)]))
            send[0] = passed_on(0, 1, [near])
            beyond, _ = lax.optimization_barrier((beyond, send[0]))
            got[0].append(lax.ppermute(send[0], "ctx", across))
        farther = lax.ppermute(beyond, "ctx", outward)
        kv_got = [near, middle, beyond, far, farther]
    else:
        ring = ring_order(count)
        ring_pairs = [(ring[d], ring[(d + 1) % count]) for d in range(count)]
        kv_got = [kv]
        for _ in range(others):
            kv_got.append(lax.ppermute(kv_got[-1], "ctx", ring_pairs))
        kv_got = kv_got[1:]
    stack = 4 if per_kv % 4 == 0 and count <= 4 else 1
    targets = [
        pl.pallas_call(
            functools.partial(attention_kernel, count, per_kv, stack, g),
            out_shape=struct((rows, per_kv * DH), BF16),
            in_specs=[VMEM] * (4 + len(kv_got)),
            out_specs=VMEM,
            scratch_shapes=[
                pltpu.VMEM((2 * count * stretch, DH), BF16),
                pltpu.VMEM((2 * count * stretch, 2 * DH), BF16),
                pltpu.VMEM((count * stretch, 2 * DH), BF16),
                pltpu.VMEM((stretch, stretch), F32),
                pltpu.VMEM((stretch, (count + 1) * stretch), F32),
                pltpu.VMEM((stretch, others * stretch), F32),
            ],
            compiler_params=params(24),
            cost_estimate=cost(
                4 * (2 * count + 1) * stretch * stretch * per_kv * DH, 8 * rows * per_kv * DH
            ),
            name="attention",
        )(doc_ids, queries[0], keys[0], values[0], *kv_got)
        for g in range(kv_dev)
    ]
    for r in range(1, count):
        for g in range(groups):
            if len(got[g]) >= r:
                continue
            if r == 3 and g == groups - 1:
                got[g][-1], targets[0] = lax.optimization_barrier((got[g][-1], targets[0]))
            if r > 1:
                if count == 4:
                    needed = [near] if r == 2 else [middle, beyond]
                else:
                    needed = kv_got
                send[g] = passed_on(g, r - 1, needed)
            pairs = [(r - 1, r), (count - r, count - r - 1)]
            got[g].append(lax.ppermute(send[g], "ctx", pairs))

    got[0][-1], *targets = lax.optimization_barrier((got[0][-1], *targets))
    normed, grads = [], None
    for g in range(groups):
        more = [] if grads is None else [grads]
        made, grads = pl.pallas_call(
            functools.partial(final_kernel, count, g, groups, loss_scale, heads),
            out_shape=(struct((rows, width), BF16), struct((groups + 1, width), F32)),
            in_specs=[VMEM] * (8 + others + len(kv_got) + len(more)),
            out_specs=(VMEM,) * 2,
            scratch_shapes=[
                pltpu.VMEM((N, width), BF16),
                pltpu.VMEM((N, width), BF16),
                pltpu.VMEM((rows, width), F32),
                pltpu.VMEM((rows, width), F32),
                pltpu.VMEM((rows, 3 * 128), F32),
                pltpu.VMEM((8, width), F32),
                pltpu.VMEM((8, width), F32),
            ],
            compiler_params=params(16),
            cost_estimate=cost(2 * rows * width * N, 20 * rows * width),
            name="final",
        )(
            *local[g::groups],
            cmat,
            targets[g],
            gain.reshape(1, features),
            f_parts[g],
            dec[g],
            *got[g],
            *kv_got,
            *more,
        )
        normed.append(made)
    teacher, student = write(*targets), write(*normed)
    shifts = [1 << k for k in range((lax.axis_size("dp") * count).bit_length() - 1)]
    if count >= 4:
        grads = (grads + exchange(grads, 1)) + (exchange(grads, 2) + exchange(grads, 3))
        shifts = shifts[2:]
    for shift in shifts[:-1]:
        grads = grads + exchange(grads, shift)
    grad_gain, grad_skip = pl.pallas_call(
        closing_kernel,
        out_shape=(struct((1, features), F32), struct((1, heads), F32)),
        in_specs=[VMEM] * 2,
        out_specs=(VMEM,) * 2,
        compiler_params=params(2),
        name="closing",
    )(grads, exchange(grads, shifts[-1]))
    return (teacher[None], student[None], grad_gain[0], grad_skip[0])


def solution(mesh):
    rows = P("dp", "ctx", "head")
    in_specs = (
        rows,
        rows,
        rows,
        P("dp", None),
        rows,
        rows,
        rows,
        rows,
        rows,
        P("head"),
        P("head"),
        P("head"),
        P("head"),
    )
    out_specs = (rows, rows, P("head"), P("head"))
    return jax.shard_map(body, mesh=mesh, in_specs=in_specs, out_specs=out_specs, check_vma=False)
```
